32 devices in a mesh: gx: 8 (over y, x, core), gy: 4 (over z).
Axes of the slice: x: 2, y: 2, z: 4, core: 2. Of those that a mesh axis runs over, the one named last changes fastest.
Arguments:
- right_side: float32 [128, 64, 256], P('gx', 'gy'), may hold values from -24 to 24
- solution: float32 [128, 64, 256], P('gx', 'gy'), may hold values from -6 to 6
- phase: int32 [128, 64, 256], P('gx', 'gy'), may hold values from 0 to 2
- permeability: float32 [3], replicated, may hold values from 1 to 30
Outputs:
- solution_next: float32 [128, 64, 256], P('gx', 'gy')
The draws below stay inside these ranges and needn't reach their ends.
Inputs may be any that keep to these rules, and one draw needn't show every extreme that they name: `phase`: material id of each cell.
All inputs are finite; a program needn't handle non-finite values.
Results may differ from the reference program's by a relative error of at most 0.0003.
Values sent between devices are 32-bit elements; how exact they have to be, the bound alone decides.
No kernel may reach another device: no remote copies, remote signals or barrier semaphores. Data moves between devices by JAX's collectives and lax.ppermute only.
A program may use at most 128 MiB of HBM per device.

```python
import math
import jax
import jax.numpy as jnp

DEG = 4
CYCLES = 2
LEVELS = 4
COARSE_SWEEPS = 4
NX = 128
NY = 64
NZ = 256


def touch_ends(entries, own_key, low, largest):
    longest = entries.shape.index(max(entries.shape))
    spots = []
    for shift in (0, 1):
        where = [jax.random.randint(jax.random.fold_in(own_key, axis), (), 0, length) for axis, length in enumerate(entries.shape)]
        where[longest] = (where[longest] + shift) % entries.shape[longest]
        spots.append(tuple(where))
    return entries.at[spots[0]].set(low).at[spots[1]].set(largest)


def levels(rng, dims, split, smallest, high):
    factor_of, own = 1.0, jax.random.fold_in(rng, 6)
    for dim, shards_of in split:
        draws = jnp.exp(jax.random.uniform(jax.random.fold_in(own, dim), (shards_of,), jnp.float32, smallest / len(split), high / len(split)))
        factor_of = factor_of * jnp.repeat(draws, dims[dim] // shards_of).reshape([-1 if axis == dim else 1 for axis in range(len(dims))])
    return factor_of


def gaussian(key, extent, spread, bound, cuts=(), held_as=jnp.bfloat16):
    factor_of = levels(key, extent, cuts, -0.22, 0.18) if cuts else 1.0
    drawn = jax.random.normal(key, extent, jnp.float32) * spread * factor_of
    return jnp.minimum(jnp.maximum(drawn, -bound), bound).astype(held_as)


def setup_inputs(seed: int = 0) -> dict:
    key_list = jax.random.split(jax.random.key(seed), 5)
    right_side = gaussian(key_list[0], (NX, NY, NZ), 4.0, 24.0, ((0, 8), (1, 4)), jnp.float32)
    solution = gaussian(key_list[1], (NX, NY, NZ), 1.0, 6.0, ((0, 8), (1, 4)), jnp.float32)
    phase = touch_ends(jax.random.randint(key_list[2], (NX, NY, NZ), 0, 3), jax.random.fold_in(key_list[2], 1), 0, 2).astype(jnp.int32)
    permeability = jnp.clip(jnp.exp(jax.random.uniform(key_list[3], (3,), jnp.float32, math.log(1.0), math.log(30.0))), 1.0, 30.0)
    return {"right_side": right_side, "solution": solution, "phase": phase, "permeability": permeability}


THETA = 1.15
DELTA = 0.85
SIGMA = 1.15 / 0.85
DAMPING = 0.6


def shift_lower(field):
    return jnp.concatenate([jnp.zeros_like(field[:, :, :1]), field[:, :, :-1]], axis=2)


def shift_upper(field):
    return jnp.concatenate([field[:, :, 1:], jnp.zeros_like(field[:, :, :1])], axis=2)


def face_weights(padded):
    centre = padded[1:-1, 1:-1]
    inside = (centre > 0).astype(jnp.float32)

    def weight(other):
        other = jnp.where(other > 0, other, centre)
        return 2.0 * centre * other / (centre + other + 1.0 - inside)

    return (weight(padded[:-2, 1:-1]), weight(padded[2:, 1:-1]), weight(padded[1:-1, :-2]),
            weight(padded[1:-1, 2:]), weight(shift_lower(centre)), weight(shift_upper(centre)))


def inverse_diagonal(weights, scale):
    diagonal = scale * (weights[0] + weights[1] + weights[2] + weights[3] + weights[4] + weights[5])
    inside = (diagonal > 0).astype(jnp.float32)
    return inside / (diagonal + 1.0 - inside)


def apply_operator(padded, weights, scale):
    field = padded[1:-1, 1:-1]
    total = weights[0] * (field - padded[:-2, 1:-1])
    total = total + weights[1] * (field - padded[2:, 1:-1])
    total = total + weights[2] * (field - padded[1:-1, :-2])
    total = total + weights[3] * (field - padded[1:-1, 2:])
    total = total + weights[4] * (field - shift_lower(field))
    total = total + weights[5] * (field - shift_upper(field))
    return scale * total


def restrict(field):
    shape = field.shape
    blocks = field.reshape(shape[0] // 2, 2, shape[1] // 2, 2, shape[2] // 2, 2)
    return jnp.mean(blocks, axis=(1, 3, 5))


def prolong(field):
    return jnp.repeat(jnp.repeat(jnp.repeat(field, 2, axis=0), 2, axis=1), 2, axis=2)


def border(field):
    return jnp.pad(field, ((1, 1), (1, 1), (0, 0)))


def jacobi(source, operate, inverse, sweeps):
    correction = DAMPING * inverse * source
    for sweep in range(sweeps - 1):
        correction = correction + DAMPING * inverse * (source - operate(correction))
    return correction


def reference(right_side, solution, phase, permeability):
    material = jnp.where(phase == 0, permeability[0], jnp.where(phase == 1, permeability[1], permeability[2]))
    weights = face_weights(border(material))
    inverse = inverse_diagonal(weights, 1.0)

    def fine_op(field):
        return apply_operator(border(field), weights, 1.0)

    residual = right_side - fine_op(solution)
    rho = 1.0 / SIGMA
    direction = inverse * residual / THETA
    smoothed = direction
    for step in range(DEG - 1):
        rho_next = 1.0 / (2.0 * SIGMA - rho)
        image = fine_op(smoothed)
        direction = rho_next * rho * direction + (2.0 * rho_next / DELTA) * inverse * (residual - image)
        smoothed = smoothed + direction
        rho = rho_next

    tables = []
    material_level = material
    for level in range(1, LEVELS + 1):
        material_level = restrict(material_level)
        scale = 0.25 ** level
        level_weights = face_weights(border(material_level))
        tables.append((level_weights, inverse_diagonal(level_weights, scale), scale))

    def level_op(level, field):
        level_weights, level_inverse, scale = tables[level - 1]
        return apply_operator(border(field), level_weights, scale)

    def vcycle(level, source):
        level_inverse = tables[level - 1][1]
        if level == LEVELS:
            return jacobi(source, lambda f: level_op(level, f), level_inverse, COARSE_SWEEPS)
        correction = DAMPING * level_inverse * source
        remainder = source - level_op(level, correction)
        correction = correction + prolong(vcycle(level + 1, restrict(remainder)))
        correction = correction + DAMPING * level_inverse * (source - level_op(level, correction))
        return correction

    coarse_source = restrict(residual)
    coarse = vcycle(1, coarse_source)
    for cycle in range(CYCLES - 1):
        coarse = coarse + vcycle(1, coarse_source - level_op(1, coarse))
    return solution + smoothed + prolong(coarse)
```

```python
import functools
import math

import jax
import jax.numpy as jnp
from jax import lax
from jax.experimental import pallas as pl
from jax.experimental.pallas import tpu as pltpu
from jax.sharding import PartitionSpec as P

DEG = 4
COARSE_SWEEPS = 4
THETA = 1.15
DELTA = 0.85
SIGMA = 1.15 / 0.85
DAMPING = 0.6
KEPT = 1.0 - DAMPING
F32 = jnp.float32
LANES = 128
MIB = 1024 * 1024
HELD = 4 * MIB


def iota(shape, axis):
    return lax.broadcasted_iota(jnp.int32, shape, axis)


def invert(x):
    guess = pl.reciprocal(x, approx=True)
    return guess * (2.0 - x * guess)


def harmonic(a, b, scale):
    return (2.0 * scale) * a * b * invert(jnp.maximum(a + b, 1e-3))


def pair_matrix(size, offset=0):
    column = iota((size, LANES), 1)
    return ((column >= offset) & (iota((size, LANES), 0) // 2 == column - offset)).astype(jnp.bfloat16)


def spread_matrix(width):
    return (iota((LANES, width), 1) // 2 == iota((LANES, width), 0)).astype(jnp.bfloat16)


def select(values, matrix):
    high = values.astype(jnp.bfloat16)
    rest = values - high.astype(F32)
    middle = rest.astype(jnp.bfloat16)
    low = (rest - middle.astype(F32)).astype(jnp.bfloat16)
    out = jnp.dot(high, matrix, preferred_element_type=F32)
    out = out + jnp.dot(middle, matrix, preferred_element_type=F32)
    return out + jnp.dot(low, matrix, preferred_element_type=F32)


def roll(x, shift, axis):
    return pltpu.roll(x, shift % x.shape[axis], axis)


def lower(x, axis):
    return roll(x, 1, axis)


def upper(x, axis):
    return roll(x, x.shape[axis] - 1, axis)


def faces_kernel(place, permeability, potential, phase, material, inner, outer, even, odd):
    low_x, low_y = place[0] == 1, place[1] == 1
    count, rows = potential.shape[:2]
    ids = phase[...]
    p0, p1, p2 = permeability[0], permeability[1], permeability[2]
    material[...] = jnp.where(ids == 0, p0, jnp.where(ids == 1, p1, p2))
    last = count - 1
    first = jnp.where(low_x, 0, last)
    second = jnp.where(low_x, 1, last - 1)
    inner[0] = potential[first]
    inner[1] = material[first]
    inner[2] = material[second]
    outer[0] = potential[last - first]
    outer[1] = material[last - first]
    outer[2] = material[last - second]
    for i in range(count):
        for slot, (ref, a, b) in enumerate(((potential, 0, rows - 1), (material, 0, rows - 1), (material, 1, rows - 2))):
            low, high = ref[i, a : a + 1, :], ref[i, b : b + 1, :]
            even[slot, i : i + 1, :] = jnp.where(low_y, low, high)
            odd[slot, i : i + 1, :] = jnp.where(low_y, high, low)


def residual_kernel(
    place, source, potential, material, inner, outer, even, odd,
    residual, payload, source1, material1, strip_even, strip_odd,
    mat, pot, wide, narrow, coarse, wide2, narrow2,
):
    low_x, low_y = place[0] == 1, place[1] == 1
    count, rows, depth = source.shape
    c1, r1, d1 = count // 2, rows // 2, depth // 2
    c2, r2 = c1 // 2, r1 // 2

    def ordered(flag, a, b):
        return jnp.where(flag, a, b), jnp.where(flag, b, a)

    x_low, x_high = ordered(low_x, inner[...], outer[...])
    y_low, y_high = ordered(low_y, even[...], odd[...])
    mat[0], mat[count + 1] = x_low[1], x_high[1]
    pot[0], pot[count + 1] = x_low[0], x_high[0]
    mat[pl.ds(1, count)] = material[...]
    pot[pl.ds(1, count)] = potential[...]
    row, lane = iota((rows, depth), 0), iota((rows, depth), 1)

    def neighbours(a, low, high):
        below = jnp.where(row == 0, low, lower(a, 0))
        above = jnp.where(row == rows - 1, high, upper(a, 0))
        return below, above

    face = harmonic(mat[0], mat[1], 1.0)
    for i in range(count):
        a, v = mat[i + 1], pot[i + 1]
        m_down, m_up = neighbours(a, y_low[1, i : i + 1], y_high[1, i : i + 1])
        v_down, v_up = neighbours(v, y_low[0, i : i + 1], y_high[0, i : i + 1])
        m_back = jnp.where(lane == 0, 0.0, lower(a, 1))
        m_front = jnp.where(lane == depth - 1, 0.0, upper(a, 1))
        next_face = harmonic(a, mat[i + 2], 1.0)
        weights = [face, next_face] + [harmonic(a, b, 1.0) for b in (m_down, m_up, m_back, m_front)]
        others = (mat[i], mat[i + 2], m_down, m_up, m_back, m_front)
        fields = (pot[i], pot[i + 2], v_down, v_up, lower(v, 1), upper(v, 1))
        diagonal = sum(jnp.where(b > 0.0, w, a) for w, b in zip(weights, others))
        off = sum(w * f for w, f in zip(weights, fields))
        left = source[i] - (diagonal * v - off)
        residual[i] = left
        face = next_face
        at = (i // 2) * rows
        if i % 2 == 0:
            kept_left, kept_a = left, a
        else:
            wide[at : at + rows] = kept_left + left
            wide[count // 2 * rows + at : count // 2 * rows + at + rows] = kept_a + a
        low = jnp.concatenate([left[:4], a[:4]], axis=0)
        high = jnp.concatenate([left[rows - 4 :], a[rows - 4 :]], axis=0)
        for ref, strip in ((strip_even, jnp.where(low_y, low, high)), (strip_odd, jnp.where(low_y, high, low))):
            for piece in range(depth // LANES):
                ref[i * (depth // LANES) + piece] = strip[:, piece * LANES : (piece + 1) * LANES]
    base = 2 * c1 * rows
    for n, both in enumerate((x_low[1] + x_low[2], x_high[1] + x_high[2], y_low[1] + y_low[2], y_high[1] + y_high[2])):
        wide[base + n * rows : base + (n + 1) * rows] = both
    narrow[...] = select(wide[...], pair_matrix(depth)) * 0.125
    half = narrow.shape[0] // 2
    coarse[...] = narrow[pl.ds(0, half, 2)] + narrow[pl.ds(1, half, 2)]

    s = [coarse[k * r1 : (k + 1) * r1] for k in range(c1)]
    m = [coarse[c1 * r1 + k * r1 : c1 * r1 + (k + 1) * r1] for k in range(c1)]
    base = 2 * c1 * r1
    m_xlow, m_xhigh, m_ylow, m_yhigh = (coarse[base + n * r1 : base + (n + 1) * r1] for n in range(4))
    row, lane = iota((r1, d1), 0), iota((r1, d1), 1)
    around = [m_xlow] + m + [m_xhigh]
    errors, tables = [], []
    face = harmonic(around[0], around[1], 0.25)
    for k in range(c1):
        a = m[k]
        down = jnp.where(row == 0, m_ylow[k : k + 1], lower(a, 0))
        up = jnp.where(row == r1 - 1, m_yhigh[k : k + 1], upper(a, 0))
        back = jnp.where(lane == 0, 0.0, lower(a, 1))
        front = jnp.where(lane == d1 - 1, 0.0, upper(a, 1))
        next_face = harmonic(a, around[k + 2], 0.25)
        weights = [face, next_face] + [harmonic(a, b, 0.25) for b in (down, up, back, front)]
        others = (around[k], around[k + 2], down, up, back, front)
        diagonal = sum(jnp.where(b > 0.0, w, 0.25 * a) for w, b in zip(weights, others))
        errors.append(DAMPING * s[k] * invert(diagonal))
        tables.append(weights)
        face = next_face
        source1[k] = s[k]
        material1[k] = a
        low = jnp.concatenate([s[k][:4], a[:4]], axis=0)
        high = jnp.concatenate([s[k][r1 - 4 :], a[r1 - 4 :]], axis=0)
        at = count * (depth // LANES) + k
        strip_even[at] = jnp.where(low_y, low, high)
        strip_odd[at] = jnp.where(low_y, high, low)
    for k in range(c1):
        e, w = errors[k], tables[k]
        t = KEPT * s[k] + w[4] * lower(e, 1) + w[5] * upper(e, 1)
        t = t + w[2] * jnp.where(row == 0, 0.0, lower(e, 0)) + w[3] * jnp.where(row == r1 - 1, 0.0, upper(e, 0))
        if k > 0:
            t = t + w[0] * errors[k - 1]
        if k < c1 - 1:
            t = t + w[1] * errors[k + 1]
        at = (k // 2) * r1
        if k % 2 == 0:
            kept = t
        else:
            wide2[0, at : at + r1] = kept + t
            wide2[1, at : at + r1] = m[k - 1] + m[k]
        base = c2 * r1
        wide2[1, base + k : base + k + 1] = (w[2] * e)[:1]
        wide2[1, base + r1 + k : base + r1 + k + 1] = (w[3] * e)[r1 - 1 :]
    wide2[0, base : base + r1] = tables[0][0] * errors[0]
    wide2[0, base + r1 : base + 2 * r1] = tables[c1 - 1][1] * errors[c1 - 1]
    narrow2[...] = (select(wide2[0], pair_matrix(d1)) + select(wide2[1], pair_matrix(d1, LANES // 2))) * 0.125
    half = narrow2.shape[0] // 2
    block = narrow2[pl.ds(0, half, 2)] + narrow2[pl.ds(1, half, 2)]
    payload[...] = jnp.broadcast_to(block[None], payload.shape)


def strips_kernel(
    place, residual, material, source1, material1, even, odd,
    inner, outer, long_r, long_m, long_s1, long_m1,
):
    low_x, low_y = place[0] == 1, place[1] == 1
    count, rows, depth = residual.shape
    pieces = depth // LANES
    c1 = source1.shape[0]

    def sides(at):
        a, b = even[at], odd[at]
        return jnp.where(low_y, a, b), jnp.where(low_y, b, a)

    for i in range(count):
        for piece in range(pieces):
            low, high = sides(i * pieces + piece)
            z = slice(piece * LANES, (piece + 1) * LANES)
            long_r[i, :, z] = jnp.concatenate([low[:4], residual[i, :, z], high[:4]], axis=0)
            long_m[i, :, z] = jnp.concatenate([low[4:], material[i, :, z], high[4:]], axis=0)
    for k in range(c1):
        low, high = sides(count * pieces + k)
        long_s1[k] = jnp.concatenate([low[:4], source1[k], high[:4]], axis=0)
        long_m1[k] = jnp.concatenate([low[4:], material1[k], high[4:]], axis=0)

    def pack(out, flag):
        at = 0
        for ref, planes in ((long_r, 3), (long_m, 4), (long_s1, 3), (long_m1, 4)):
            start = jnp.where(flag, 0, ref.shape[0] - planes)
            for n in range(planes):
                for tile in range(ref.shape[1] // 8):
                    for piece in range(ref.shape[2] // LANES):
                        out[at] = ref[start + n, tile * 8 : tile * 8 + 8, piece * LANES : (piece + 1) * LANES]
                        at += 1

    pack(inner, low_x)
    pack(outer, jnp.logical_not(low_x))


def unpack(source, flag, out, start, planes, tiles, pieces, at):
    for n in range(planes):
        for tile in range(tiles):
            for piece in range(pieces):
                value = jnp.where(flag, source[0][at], source[1][at])
                out[start + n, tile * 8 : tile * 8 + 8, piece * LANES : (piece + 1) * LANES] = value
                at += 1
    return at


def smooth_kernel(place, potential, long_r, long_m, inner, outer, out, mat, res, x, d, fx, fy, fz, inv):
    low_x = place[0] == 1
    count, rows, depth = potential.shape
    pieces, tiles = depth // LANES, long_r.shape[1] // 8
    both = (inner, outer)
    flags = (low_x, jnp.logical_not(low_x))
    n_r = 3 * tiles * pieces
    for flag, start_r, start_m in ((flags[0], 1, 0), (flags[1], count + 4, count + 4)):
        at = unpack(both, flag, res, start_r, 3, tiles, pieces, 0)
        unpack(both, flag, mat, start_m, 4, tiles, pieces, at)
    res[pl.ds(4, count)] = long_r[...]
    mat[pl.ds(4, count)] = long_m[...]
    total = count + 8
    length = rows + 8
    lane = iota((length, depth), 1)

    def weigh(i, previous):
        a, ahead = mat[i], mat[i + 1]
        f = harmonic(a, ahead, 1.0)
        fx[i + 1] = f
        down = lower(a, 0)
        back = jnp.where(lane == 0, 0.0, lower(a, 1))
        w_down, w_back = harmonic(a, down, 1.0), harmonic(a, back, 1.0)
        fy[i], fz[i] = w_down, w_back
        w_up, w_front = upper(w_down, 0), upper(w_back, 1)
        pairs = (
            (previous, mat[i - 1]), (f, ahead), (w_down, down), (w_up, upper(a, 0)), (w_back, back),
            (w_front, jnp.where(lane == depth - 1, 0.0, upper(a, 1))),
        )
        diagonal = sum(jnp.where(b > 0.0, w, a) for w, b in pairs)
        inverse = jnp.where(a > 0.0, invert(jnp.maximum(diagonal, 1e-3)), 0.0)
        inv[i] = inverse
        res[i] = inverse * res[i]
        start = res[i] * (1.0 / THETA)
        x[0, i] = start
        d[i] = start
        return f

    first = harmonic(mat[0], mat[1], 1.0)
    fx[1] = first
    lax.fori_loop(1, total - 1, weigh, first)
    rho = 1.0 / SIGMA
    for step in range(DEG - 1):
        ahead = 1.0 / (2.0 * SIGMA - rho)
        old, new = step % 2, (step + 1) % 2
        final = step == DEG - 2

        def sweep(i, _):
            v = x[old, i]
            w_down, w_back = fy[i], fz[i]
            off = fx[i] * x[old, i - 1] + fx[i + 1] * x[old, i + 1]
            off = off + w_down * lower(v, 0) + upper(w_down * v, 0)
            off = off + w_back * lower(v, 1) + upper(w_back * v, 1)
            change = ahead * rho * d[i] + (2.0 * ahead / DELTA) * (res[i] - v + inv[i] * off)
            if final:
                out[i - 4] = potential[i - 4] + (v + change)[4 : 4 + rows]
            else:
                d[i] = change
                x[new, i] = v + change
            return 0

        lax.fori_loop(2 + step, total - 2 - step, sweep, 0)
        rho = ahead


def chunk_of(count):
    return min(count, 8)


def tables_of(mat, table, scale, valid_rows, valid_lanes):
    count, rows = mat.shape[0] - 2, mat.shape[1]
    step = chunk_of(count)
    shape = (step, rows, LANES)
    row, lane = iota(shape, 1), iota(shape, 2)

    def body(n, _):
        at = n * step
        a, before, ahead = mat[pl.ds(at + 1, step)], mat[pl.ds(at, step)], mat[pl.ds(at + 2, step)]
        down = jnp.where(row == 0, 0.0, lower(a, 1))
        back = jnp.where(lane == 0, 0.0, lower(a, 2))
        up = jnp.where(row == rows - 1, 0.0, upper(a, 1))
        front = jnp.where(lane == LANES - 1, 0.0, upper(a, 2))
        w = [harmonic(a, b, scale) for b in (before, ahead, down, back)]
        w += [upper(w[2], 1), upper(w[3], 2)]
        diagonal = sum(jnp.where(b > 0.0, f, scale * a) for f, b in zip(w, (before, ahead, down, back, up, front)))
        table[0, pl.ds(at, step)] = w[0]
        table[1, pl.ds(at, step)] = w[2]
        table[2, pl.ds(at, step)] = w[3]
        table[3, pl.ds(at, step)] = jnp.where(a > 0.0, invert(jnp.maximum(diagonal, 1e-4)), 0.0)
        return 0

    lax.fori_loop(0, count // step, body, 0)
    table[0, count] = jnp.zeros((rows, LANES), F32)


def off_diagonal(e, table, at, step):
    v = e[pl.ds(at + 1, step)]
    total = table[0, pl.ds(at, step)] * e[pl.ds(at, step)] + table[0, pl.ds(at + 1, step)] * e[pl.ds(at + 2, step)]
    fy, fz = table[1, pl.ds(at, step)], table[2, pl.ds(at, step)]
    total = total + fy * lower(v, 1) + upper(fy * v, 1)
    return v, total + fz * lower(v, 2) + upper(fz * v, 2)


def each(count, body):
    step = chunk_of(count)

    def run(n, _):
        body(n * step, step)
        return 0

    lax.fori_loop(0, count // step, run, 0)


def halve(fine, out, first, temp, count, rows, rows_out):
    step = chunk_of(count // 2)
    padded = fine.shape[1]

    def add(at, step):
        a = fine[pl.ds(first + 2 * at, 2 * step)].reshape(step, 2, padded, LANES)
        sums = (a[:, 0] + a[:, 1]).reshape(step * padded, LANES)
        temp[pl.ds(pl.multiple_of(at * padded, 8), step * padded)] = select(sums, pair_matrix(LANES)) * 0.125

    each(count // 2, add)
    keep = rows // 2

    def fold(k, _):
        base = pl.multiple_of(k * padded, 8)
        value = temp[pl.ds(base, padded // 2, 2)] + temp[pl.ds(base + 1, padded // 2, 2)]
        out[k + 1, 0 : padded // 2, :] = value
        return 0

    lax.fori_loop(0, count // 2, fold, 0)


def widen(coarse, temp, out, count, rows):
    padded = coarse.shape[1]
    step = chunk_of(count)

    def lanes(at, step):
        values = coarse[pl.ds(at + 1, step)].reshape(step * padded, LANES)
        temp[pl.ds(pl.multiple_of(at * padded, 8), step * padded)] = select(values, spread_matrix(LANES))

    each(count, lanes)
    keep = out.shape[0] // count // 2

    def fold(k, _):
        value = temp[pl.ds(pl.multiple_of(k * padded, 8), keep)]
        base = pl.multiple_of(k * 2 * keep, 8)
        out[pl.ds(base, keep, 2)] = value
        out[pl.ds(base + 1, keep, 2)] = value
        return 0

    lax.fori_loop(0, count, fold, 0)


def cycle(s, e, tables, work, dims):
    for ref in e:
        zero = jnp.zeros(ref.shape[1:], F32)
        ref[0] = zero
        ref[ref.shape[0] - 1] = zero
    temp, spread, rest = work
    for level in range(2):
        count, rows, padded = dims[level]
        s_l, e_l, table, t = s[level], e[level], tables[level], rest[level]

        def start(at, step):
            e_l[pl.ds(at + 1, step)] = DAMPING * s_l[pl.ds(at + 1, step)] * table[3, pl.ds(at, step)]

        each(count, start)

        def remainder(at, step):
            _, off = off_diagonal(e_l, table, at, step)
            t[pl.ds(at, step)] = KEPT * s_l[pl.ds(at + 1, step)] + off

        each(count, remainder)
        halve(t, s[level + 1], 0, temp, count, rows, dims[level + 1][2])
    count, rows, padded = dims[2]
    s_l, e_l, table = s[2], e[2], tables[2]

    def start(at, step):
        e_l[pl.ds(at + 1, step)] = DAMPING * s_l[pl.ds(at + 1, step)] * table[3, pl.ds(at, step)]

    def relax(s_l, e_l, table, t, count):
        def sweep(at, step):
            v, off = off_diagonal(e_l, table, at, step)
            t[pl.ds(at, step)] = KEPT * v + DAMPING * table[3, pl.ds(at, step)] * (s_l[pl.ds(at + 1, step)] + off)

        def back(at, step):
            e_l[pl.ds(at + 1, step)] = t[pl.ds(at, step)]

        each(count, sweep)
        each(count, back)

    each(count, start)
    for _ in range(COARSE_SWEEPS - 1):
        relax(s_l, e_l, table, rest[2], count)
    for level in (1, 0):
        count, rows, padded = dims[level]
        s_l, e_l, table, t = s[level], e[level], tables[level], rest[level]
        up = spread[level]
        widen(e[level + 1], temp, up, dims[level + 1][0], dims[level + 1][1])

        def correct(at, step):
            more = up[pl.ds(pl.multiple_of(at * padded, 8), step * padded)].reshape(step, 1, padded, LANES)
            now = e_l[pl.ds(2 * at + 1, 2 * step)].reshape(step, 2, padded, LANES)
            e_l[pl.ds(2 * at + 1, 2 * step)] = (now + more).reshape(2 * step, padded, LANES)

        each(count // 2, correct)
        relax(s_l, e_l, table, t, count)


def window(e, place, out, c2, r2, pad):
    count, rows = e.shape[0] - 2, e.shape[1]
    pad[...] = jnp.zeros(pad.shape, F32)
    planes = c2 + 4
    for n in range(planes):
        at = place[2] * c2 + n - 2
        inside = (at >= 0) & (at < count)
        value = e[jnp.clip(at, 0, count - 1) + 1]
        pad[n, 8 : 8 + rows, :] = jnp.where(inside, value, 0.0)
    for n in range(planes):
        out[n] = pad[n, pl.ds(place[3] * r2 + 6, r2 + 4), :]


def level_shapes(count, rows, depth):
    return [(count // k, rows // k, max(rows // k, 8)) for k in (1, 2, 4)]


def work_shapes(dims):
    out = []
    for count, _, padded in dims:
        out.append(pltpu.VMEM((count + 2, padded, LANES), F32))
    for count, _, padded in dims:
        out.append(pltpu.VMEM((count + 2, padded, LANES), F32))
    for count, _, padded in dims:
        out.append(pltpu.VMEM((count + 2, padded, LANES), F32))
    out.append(pltpu.VMEM((dims[0][0] // 2 * dims[0][2], LANES), F32))
    for count, _, padded in dims[:2]:
        out.append(pltpu.VMEM((count // 2 * padded, LANES), F32))
    return out


def first_cycle_kernel(dims, grid, c2, r2, place, blocks, out, table2, table3, table4, *scratch):
    s, e, rest = scratch[0:3], scratch[3:6], scratch[6:9]
    temp, spread = scratch[9], scratch[10:12]
    mats, pad = scratch[12:15], scratch[15]
    face_y, face_x = e[0], rest[0]
    tables = (table2, table3, table4)
    gx, gy = grid
    count, rows, _ = dims[0]
    for ref in (*s, *mats, face_y, face_x):
        ref[...] = jnp.zeros(ref.shape, F32)
    lane = iota((c2 * r2, LANES), 1)
    half = LANES // 2

    def place_column(i, _):
        for j in range(gy):
            block = blocks[i * gy + j]
            turned = roll(block, half, 1)
            own = jnp.where(lane < half, block[: c2 * r2], 0.0)
            own_m = jnp.where(lane < half, turned[: c2 * r2], 0.0)
            x_faces = jnp.where(lane[: 2 * r2] < half, block[c2 * r2 :], 0.0)
            y_faces = jnp.where(lane[: 2 * c2] < half, turned[c2 * r2 :], 0.0)
            for k in range(c2):
                at = i * c2 + k + 1
                s[0][at, j * r2 : (j + 1) * r2, :] = own[k * r2 : (k + 1) * r2]
                mats[0][at, j * r2 : (j + 1) * r2, :] = own_m[k * r2 : (k + 1) * r2]
                if j > 0:
                    face_y[at, j * r2 - 1 : j * r2, :] = y_faces[k : k + 1]
                if j < gy - 1:
                    face_y[at, (j + 1) * r2 : (j + 1) * r2 + 1, :] = y_faces[c2 + k : c2 + k + 1]
            face_x[i * c2, j * r2 : (j + 1) * r2, :] = x_faces[:r2]
            face_x[(i + 1) * c2 + 1, j * r2 : (j + 1) * r2, :] = x_faces[r2:]
        return 0

    lax.fori_loop(0, gx, place_column, 0)

    def join(at, step):
        now = pl.ds(at + 1, step)
        s[0][now] = s[0][now] + face_x[now] + face_y[now]

    each(count, join)
    scale = 0.0625
    for level in range(3):
        if level:
            count, rows, padded = dims[level - 1]
            halve(mats[level - 1], mats[level], 1, temp, count, rows, dims[level][2])
        tables_of(mats[level], tables[level], scale, None, None)
        scale *= 0.25
    cycle(s, e, tables, (temp, spread, rest), dims)
    window(e[0], place, out, c2, r2, pad)


def shifted(a):
    zero = jnp.zeros_like(a[:1])
    return jnp.concatenate([zero, a[:-1]], axis=0), jnp.concatenate([a[1:], zero], axis=0)


def apply_off(e, fx, fy, fz):
    before, ahead = shifted(e)
    out = fx[:-1] * before + fx[1:] * ahead
    out = out + fy * lower(e, 1) + upper(fy * e, 1)
    return out + fz * lower(e, 2) + upper(fz * e, 2)


def raise_window(window_ref, flat, out):
    planes, rows, _ = window_ref.shape
    values = select(window_ref[...].reshape(planes * rows, LANES), spread_matrix(LANES))
    flat[pl.ds(0, planes * rows, 2)] = values
    flat[pl.ds(1, planes * rows, 2)] = values
    v = flat[...].reshape(planes, 1, 2 * rows, LANES)
    out[...] = jnp.broadcast_to(v, (planes, 2, 2 * rows, LANES)).reshape(2 * planes, 2 * rows, LANES)


def level1_kernel(
    offset, place, long_s1, long_m1, inner, outer, window1,
    payload, first, error2, source2, faces,
    src, mat, flat, prolonged, wide, narrow,
):
    low_x = place[0] == 1
    count, length, depth = long_s1.shape
    rows = length - 8
    both = (inner, outer)
    zero = jnp.zeros((length, depth), F32)
    src[0] = zero
    src[count + 7] = zero
    for flag, start_s, start_m in ((low_x, 1, 0), (jnp.logical_not(low_x), count + 4, count + 4)):
        at = unpack(both, flag, src, start_s, 3, length // 8, 1, offset)
        unpack(both, flag, mat, start_m, 4, length // 8, 1, at)
    src[pl.ds(4, count)] = long_s1[...]
    mat[pl.ds(4, count)] = long_m1[...]
    raise_window(window1, flat, prolonged)
    a = mat[...]
    lane = iota(a.shape, 2)
    before, ahead = shifted(a)
    down, up = lower(a, 1), upper(a, 1)
    back = jnp.where(lane == 0, 0.0, lower(a, 2))
    front = jnp.where(lane == depth - 1, 0.0, upper(a, 2))
    w_x, w_y, w_z = (harmonic(a, b, 0.25) for b in (before, down, back))
    _, w_ahead = shifted(w_x)
    pairs = ((w_x, before), (w_ahead, ahead), (w_y, down), (upper(w_y, 1), up), (w_z, back), (upper(w_z, 2), front))
    diagonal = sum(jnp.where(b > 0.0, w, 0.25 * a) for w, b in pairs)
    inverse = jnp.where(a > 0.0, invert(jnp.maximum(diagonal, 1e-4)), 0.0)
    w_x = jnp.concatenate([w_x, zero[None]], axis=0)
    faces[0] = w_x[:-1]
    faces[1] = w_y
    faces[2] = w_z
    faces[3] = inverse
    s = src[...]
    e = DAMPING * inverse * s + prolonged[...]
    c = KEPT * e + DAMPING * inverse * (s + apply_off(e, w_x, w_y, w_z))
    s2 = s - diagonal * c + apply_off(c, w_x, w_y, w_z)
    e2 = DAMPING * inverse * s2
    t = KEPT * s2 + apply_off(e2, w_x, w_y, w_z)
    first[...] = c
    error2[...] = e2
    source2[...] = s2
    wide[...] = t[4 : 4 + count, 4 : 4 + rows].reshape(count // 2, 2, rows, depth).sum(axis=1).reshape(count // 2 * rows, depth)
    part = count // 4 * rows
    narrow[...] = (select(wide[:part], pair_matrix(depth)) + select(wide[part:], pair_matrix(depth, LANES // 2))) * 0.125
    block = narrow[pl.ds(0, part // 2, 2)] + narrow[pl.ds(1, part // 2, 2)]
    payload[...] = jnp.broadcast_to(block[None], payload.shape)


def last_cycle_kernel(
    dims, grid, c2, r2, place, blocks, table2, table3, table4, first, error2, source2, faces, partial,
    out, *scratch,
):
    s, e, rest = scratch[0:3], scratch[3:6], scratch[6:9]
    temp, spread = scratch[9], scratch[10:12]
    pad, view, flat, prolonged, tall = scratch[12:17]
    gx, gy = grid
    for ref in s:
        ref[...] = jnp.zeros(ref.shape, F32)
    half = LANES // 2
    lane = iota((c2 // 2 * r2, LANES), 1)

    def place_column(i, _):
        for j in range(gy):
            block = blocks[i * gy + j]
            turned = roll(block, half, 1)
            parts = (jnp.where(lane < half, block, 0.0), jnp.where(lane < half, turned, 0.0))
            for k in range(c2):
                n = k % (c2 // 2)
                s[0][i * c2 + k + 1, j * r2 : (j + 1) * r2, :] = parts[k // (c2 // 2)][n * r2 : (n + 1) * r2]
        return 0

    lax.fori_loop(0, gx, place_column, 0)
    cycle(s, e, (table2, table3, table4), (temp, spread, rest), dims)
    window(e[0], place, view, c2, r2, pad)
    raise_window(view, flat, prolonged)
    count, rows, depth = partial.shape
    c1, r1 = count // 2, rows // 2
    ext = first.shape[0]
    w_x = jnp.concatenate([faces[0], jnp.zeros_like(faces[0, :1])], axis=0)
    v = error2[...] + prolonged[...]
    v = KEPT * v + DAMPING * faces[3] * (source2[...] + apply_off(v, w_x, faces[1], faces[2]))
    coarse = (first[...] + v)[4 : 4 + c1, 4 : 4 + r1].reshape(c1 * r1, LANES)
    values = select(coarse, spread_matrix(depth))
    for piece in range(depth // LANES):
        z = slice(piece * LANES, (piece + 1) * LANES)
        tall[piece, pl.ds(0, c1 * r1, 2)] = values[:, z]
        tall[piece, pl.ds(1, c1 * r1, 2)] = values[:, z]
        v = tall[piece].reshape(c1, 1, rows, LANES)
        v = jnp.broadcast_to(v, (c1, 2, rows, LANES)).reshape(count, rows, LANES)
        out[:, :, z] = partial[:, :, z] + v


def size_of(shape):
    lead = math.prod(shape[:-2])
    return 4 * lead * (-(-shape[-2] // 8) * 8) * (-(-shape[-1] // LANES) * LANES)


def call(kernel, name, inputs, outputs, scratch=()):
    streamed = 0

    def held(x):
        nonlocal streamed
        if x.ndim == 1:
            return x
        if size_of(x.shape) <= HELD:
            return pltpu.with_memory_space_constraint(x, pltpu.VMEM)
        streamed += size_of(x.shape)
        return x

    def result(shape):
        nonlocal streamed
        if size_of(shape) <= HELD:
            return pltpu.VMEM(shape, F32)
        streamed += size_of(shape)
        return jax.ShapeDtypeStruct(shape, F32)

    inputs = [held(x) for x in inputs]
    results = [result(shape) for shape in outputs]
    need = streamed + sum(size_of(x.shape) for x in scratch) + 6 * MIB
    return pl.pallas_call(
        kernel,
        out_shape=results,
        in_specs=[pl.BlockSpec(memory_space=pltpu.SMEM if x.ndim == 1 else pltpu.VMEM) for x in inputs],
        out_specs=[pl.BlockSpec(memory_space=pltpu.VMEM) for _ in outputs],
        scratch_shapes=list(scratch),
        compiler_params=pltpu.CompilerParams(vmem_limit_bytes=max(need, 16 * MIB)),
        name=name,
    )(*inputs)


def swaps(count):
    inner = [(i, i + 1) for i in range(0, count - 1, 2)]
    outer = [(i, i + 1) for i in range(1, count - 1, 2)]
    return [pairs + [(b, a) for a, b in pairs] for pairs in (inner, outer)]


def local(right_side, potential, phase, permeability):
    gx, gy = lax.axis_size("gx"), lax.axis_size("gy")
    devices = gx * gy
    here_x, here_y = lax.axis_index("gx"), lax.axis_index("gy")
    place = jnp.stack([here_x % 2, here_y % 2, here_x, here_y]).astype(jnp.int32)
    count, rows, depth = right_side.shape
    c1, r1, d1 = count // 2, rows // 2, depth // 2
    c2, r2 = c1 // 2, r1 // 2
    pieces = depth // LANES
    swap_x, swap_y = swaps(gx), swaps(gy)
    VM = lambda *shape: pltpu.VMEM(shape, F32)

    brick = (count, rows, depth)
    face = (3, rows, depth)
    material, inner, outer, even, odd = call(
        faces_kernel, "faces", (place, permeability, potential, phase), (brick, face, face, (3, count, depth), (3, count, depth))
    )
    even = lax.ppermute(even, "gy", swap_y[0])
    odd = lax.ppermute(odd, "gy", swap_y[1])
    outer = lax.ppermute(outer, "gx", swap_x[1])
    inner = lax.ppermute(inner, "gx", swap_x[0])

    strip = (count * pieces + c1, 8, LANES)
    block = (devices, c2 * r2 + 2 * r2, LANES)
    total = 2 * c1 * rows + 4 * rows
    small = c2 * r1 + 2 * r1
    residual, payload, source1, material1, even, odd = call(
        residual_kernel, "residual",
        (place, right_side, potential, material, inner, outer, even, odd),
        (brick, block, (c1, r1, d1), (c1, r1, d1), strip, strip),
        (
            VM(count + 2, rows, depth), VM(count + 2, rows, depth), VM(total, depth), VM(total, LANES), VM(total // 2, LANES),
            VM(2, small, d1), VM(small, LANES),
        ),
    )
    blocks = lax.all_to_all(payload, ("gx", "gy"), 0, 0)
    even = lax.ppermute(even, "gy", swap_y[0])
    odd = lax.ppermute(odd, "gy", swap_y[1])
    tiles, tiles1 = (rows + 8) // 8, (r1 + 8) // 8
    strip = (7 * tiles * pieces + 7 * tiles1, 8, LANES)
    long, long1 = (count, rows + 8, depth), (c1, r1 + 8, d1)
    inner, outer, long_r, long_m, long_s1, long_m1 = call(
        strips_kernel, "strips",
        (place, residual, material, source1, material1, even, odd),
        (strip, strip, long, long, long1, long1),
    )
    outer = lax.ppermute(outer, "gx", swap_x[1])
    inner = lax.ppermute(inner, "gx", swap_x[0])

    dims = level_shapes(gx * c2, gy * r2, d1 // 2)
    work = work_shapes(dims)
    view = (c2 + 4, r2 + 4, LANES)
    pad = VM(c2 + 4, dims[0][2] + 16, LANES)
    mats = [VM(n + 2, padded, LANES) for n, _, padded in dims]
    table_shapes = [(4, n + 1, padded, LANES) for n, _, padded in dims]
    window1, table2, table3, table4 = call(
        functools.partial(first_cycle_kernel, dims, (gx, gy), c2, r2), "cycle1",
        (place, blocks), (view, *table_shapes), (*work, *mats, pad),
    )
    frame = (c1 + 8, r1 + 8, d1)
    flat = VM((c2 + 4) * (r2 + 4) * 2, LANES)
    payload, first, error2, source2, faces = call(
        functools.partial(level1_kernel, 7 * tiles * pieces), "level1",
        (place, long_s1, long_m1, inner, outer, window1),
        ((devices, c2 // 2 * r2, LANES), frame, frame, frame, (4, *frame)),
        (VM(*frame), VM(*frame), flat, VM(*frame), VM(c1 // 2 * r1, d1), VM(c1 // 4 * r1, LANES)),
    )
    blocks = lax.all_to_all(payload, ("gx", "gy"), 0, 0)
    wide = (count + 8, rows + 8, depth)
    (partial,) = call(
        smooth_kernel, "smooth", (place, potential, long_r, long_m, inner, outer), (brick,),
        (
            VM(*wide), VM(*wide), VM(2, *wide), VM(*wide), VM(count + 9, rows + 8, depth), VM(*wide), VM(*wide), VM(*wide),
        ),
    )
    (out,) = call(
        functools.partial(last_cycle_kernel, dims, (gx, gy), c2, r2), "cycle2",
        (place, blocks, table2, table3, table4, first, error2, source2, faces, partial), (brick,),
        (*work, pad, VM(*view), flat, VM(*frame), VM(pieces, count // 2 * rows, LANES)),
    )
    return out


def solution(mesh):
    placed = (P("gx", "gy", None), P("gx", "gy", None), P("gx", "gy", None), P())
    return jax.shard_map(local, mesh=mesh, in_specs=placed, out_specs=P("gx", "gy", None), check_vma=False)
```

```python
import functools
import math

import jax
import jax.numpy as jnp
from jax import lax
from jax.experimental import pallas as pl
from jax.experimental.pallas import tpu as pltpu
from jax.sharding import PartitionSpec as P

DEG = 4
COARSE_SWEEPS = 4
THETA = 1.15
DELTA = 0.85
SIGMA = 1.15 / 0.85
DAMPING = 0.6
KEPT = 1.0 - DAMPING
F32 = jnp.float32
LANES = 128
MIB = 1024 * 1024
HELD = 4 * MIB


def iota(shape, axis):
    return lax.broadcasted_iota(jnp.int32, shape, axis)


def invert(x):
    guess = pl.reciprocal(x, approx=True)
    return guess * (2.0 - x * guess)


def harmonic(a, b, scale):
    return (2.0 * scale) * a * b * invert(jnp.maximum(a + b, 1e-3))


def pair_matrix(size, offset=0):
    column = iota((size, LANES), 1)
    return ((column >= offset) & (iota((size, LANES), 0) // 2 == column - offset)).astype(jnp.bfloat16)


def spread_matrix(width):
    return (iota((LANES, width), 1) // 2 == iota((LANES, width), 0)).astype(jnp.bfloat16)


def select(values, matrix):
    high = values.astype(jnp.bfloat16)
    rest = (values - high.astype(F32)).astype(jnp.bfloat16)
    return jnp.dot(high, matrix, preferred_element_type=F32) + jnp.dot(rest, matrix, preferred_element_type=F32)


def lower(x, axis, stride=1):
    return pltpu.roll(x, stride, axis)


def upper(x, axis, stride=1):
    return pltpu.roll(x, x.shape[axis] - stride, axis)


def as_float(condition):
    return jnp.where(condition, 1.0, 0.0)


def faces_kernel(
    place, permeability, potential, phase, source,
    material, pot, src, inner, outer, even, odd,
    ids, values, semaphores,
):
    arriving = [
        pltpu.make_async_copy(a, b, semaphores.at[n])
        for n, (a, b) in enumerate(((permeability, values), (phase, ids), (potential, pot), (source, src)))
    ]
    for copy in arriving:
        copy.start()
    low_x, low_y = place[0] == 1, place[1] == 1
    count, rows = pot.shape[:2]
    arriving[0].wait()
    arriving[1].wait()
    p0, p1, p2 = values[0], values[1], values[2]
    for i in range(count):
        here = ids[i]
        material[i] = jnp.where(here == 0, p0, jnp.where(here == 1, p1, p2))
    last = count - 1
    first = jnp.where(low_x, 0, last)
    second = jnp.where(low_x, 1, last - 1)
    inner[1] = material[first]
    inner[2] = material[second]
    outer[1] = material[last - first]
    outer[2] = material[last - second]

    def edge(slot, ref, a, b):
        for i in range(count):
            low, high = ref[i, a : a + 1, :], ref[i, b : b + 1, :]
            even[slot, i : i + 1, :] = jnp.where(low_y, low, high)
            odd[slot, i : i + 1, :] = jnp.where(low_y, high, low)

    edge(1, material, 0, rows - 1)
    edge(2, material, 1, rows - 2)
    arriving[2].wait()
    inner[0] = pot[first]
    outer[0] = pot[last - first]
    edge(0, pot, 0, rows - 1)
    arriving[3].wait()


def residual_kernel(
    place, source, potential, material, inner, outer, even, odd,
    residual, coarse, strip_even, strip_odd,
    wide, narrow, y_faces,
):
    low_x, low_y = place[0] == 1, place[1] == 1
    count, rows, depth = source.shape
    c1, r1 = count // 2, rows // 2
    pieces = depth // LANES

    def ordered(flag, a, b):
        return jnp.where(flag, a, b), jnp.where(flag, b, a)

    x_low, x_high = ordered(low_x, inner[...], outer[...])
    y_low, y_high = ordered(low_y, even[...], odd[...])
    row, lane = iota((rows, depth), 0), iota((rows, depth), 1)
    first, last = row == 0, row == rows - 1
    y_faces[0], y_faces[1] = y_low[0], y_high[0]
    y_faces[2], y_faces[3] = y_low[1], y_high[1]
    outside = as_float(lane == 0) + as_float(lane == depth - 1)

    def edge_count(faces):
        return as_float(faces[:1, :1] <= 0.0)

    outside_y = outside + jnp.where(first, edge_count(y_low[1]), 0.0) + jnp.where(last, edge_count(y_high[1]), 0.0)
    face = harmonic(x_low[1], material[0], 1.0)
    for i in range(count):
        a, v = material[i], potential[i]
        v_before = potential[i - 1] if i else x_low[0]
        v_ahead = potential[i + 1] if i < count - 1 else x_high[0]
        next_face = harmonic(a, material[i + 1] if i < count - 1 else x_high[1], 1.0)
        down = jnp.where(first, y_faces[2, i : i + 1], lower(a, 0))
        w_down = harmonic(a, down, 1.0)
        w_top = harmonic(a[rows - 1 :], y_faces[3, i : i + 1], 1.0)
        w_up = jnp.where(last, w_top, upper(w_down, 0))
        w_back = jnp.where(lane == 0, 0.0, harmonic(a, lower(a, 1), 1.0))
        w_front = upper(w_back, 1)
        v_down = jnp.where(first, y_faces[0, i : i + 1], lower(v, 0))
        v_up = jnp.where(last, y_faces[1, i : i + 1], upper(v, 0))
        outer_faces = outside_y
        if i == 0:
            outer_faces = outer_faces + edge_count(x_low[1])
        if i == count - 1:
            outer_faces = outer_faces + edge_count(x_high[1])
        diagonal = face + next_face + w_down + w_up + w_back + w_front + a * outer_faces
        off = face * v_before + next_face * v_ahead + w_down * v_down + w_up * v_up
        off = off + w_back * lower(v, 1) + w_front * upper(v, 1)
        left = source[i] - diagonal * v + off
        residual[i] = left
        face = next_face
        at = (i // 2) * rows
        if i % 2 == 0:
            kept_left, kept_a = left, a
        else:
            wide[at : at + rows] = kept_left + left
            wide[c1 * rows + at : c1 * rows + at + rows] = kept_a + a
        low = jnp.concatenate([left[:4], a[:4]], axis=0)
        high = jnp.concatenate([left[rows - 4 :], a[rows - 4 :]], axis=0)
        for ref, strip in ((strip_even, jnp.where(low_y, low, high)), (strip_odd, jnp.where(low_y, high, low))):
            for piece in range(pieces):
                ref[i * pieces + piece] = strip[:, piece * LANES : (piece + 1) * LANES]
    base = 2 * c1 * rows
    for n, both in enumerate((x_low[1] + x_low[2], x_high[1] + x_high[2], y_low[1] + y_low[2], y_high[1] + y_high[2])):
        wide[base + n * rows : base + (n + 1) * rows] = both
    narrow[...] = select(wide[...], pair_matrix(depth)) * 0.125
    half = narrow.shape[0] // 2
    coarse[...] = narrow[pl.ds(0, half, 2)] + narrow[pl.ds(1, half, 2)]
    for k in range(c1):
        s, m = coarse[k * r1 : (k + 1) * r1], coarse[(c1 + k) * r1 : (c1 + k + 1) * r1]
        low = jnp.concatenate([s[:4], m[:4]], axis=0)
        high = jnp.concatenate([s[r1 - 4 :], m[r1 - 4 :]], axis=0)
        strip_even[count * pieces + k] = jnp.where(low_y, low, high)
        strip_odd[count * pieces + k] = jnp.where(low_y, high, low)


def payload_kernel(c1, r1, coarse, payload, wide, narrow):
    c2 = c1 // 2
    depth = coarse.shape[1]
    s = [coarse[k * r1 : (k + 1) * r1] for k in range(c1)]
    m = [coarse[(c1 + k) * r1 : (c1 + k + 1) * r1] for k in range(c1)]
    base = 2 * c1 * r1
    m_xlow, m_xhigh, m_ylow, m_yhigh = (coarse[base + n * r1 : base + (n + 1) * r1] for n in range(4))
    row, lane = iota((r1, depth), 0), iota((r1, depth), 1)
    first, last = row == 0, row == r1 - 1
    around = [m_xlow] + m + [m_xhigh]
    errors, tables = [], []
    face = harmonic(around[0], around[1], 0.25)
    for k in range(c1):
        a = m[k]
        down = jnp.where(first, m_ylow[k : k + 1], lower(a, 0))
        up = jnp.where(last, m_yhigh[k : k + 1], upper(a, 0))
        next_face = harmonic(a, around[k + 2], 0.25)
        w_down = harmonic(a, down, 0.25)
        w_up = jnp.where(last, harmonic(a, up, 0.25), upper(w_down, 0))
        w_back = jnp.where(lane == 0, 0.0, harmonic(a, lower(a, 1), 0.25))
        w_front = upper(w_back, 1)
        outside = as_float(lane == 0) + as_float(lane == depth - 1)
        outside = outside + as_float(down <= 0.0) + as_float(up <= 0.0)
        outside = outside + as_float(around[k] <= 0.0) + as_float(around[k + 2] <= 0.0)
        diagonal = face + next_face + w_down + w_up + w_back + w_front + 0.25 * a * outside
        errors.append(DAMPING * s[k] * invert(diagonal))
        tables.append((face, next_face, w_down, w_up, w_back, w_front))
        face = next_face
    base = c2 * r1
    for k in range(c1):
        e, w = errors[k], tables[k]
        t = KEPT * s[k] + w[4] * lower(e, 1) + w[5] * upper(e, 1)
        t = t + jnp.where(first, 0.0, w[2] * lower(e, 0)) + jnp.where(last, 0.0, w[3] * upper(e, 0))
        if k > 0:
            t = t + w[0] * errors[k - 1]
        if k < c1 - 1:
            t = t + w[1] * errors[k + 1]
        at = (k // 2) * r1
        if k % 2 == 0:
            kept = t
        else:
            wide[0, at : at + r1] = kept + t
            wide[1, at : at + r1] = m[k - 1] + m[k]
        wide[1, base + k : base + k + 1] = (w[2] * e)[:1]
        wide[1, base + r1 + k : base + r1 + k + 1] = (w[3] * e)[r1 - 1 :]
    wide[0, base : base + r1] = tables[0][0] * errors[0]
    wide[0, base + r1 : base + 2 * r1] = tables[c1 - 1][1] * errors[c1 - 1]
    narrow[...] = (select(wide[0], pair_matrix(depth)) + select(wide[1], pair_matrix(depth, LANES // 2))) * 0.125
    half = narrow.shape[0] // 2
    block = narrow[pl.ds(0, half, 2)] + narrow[pl.ds(1, half, 2)]
    payload[...] = jnp.broadcast_to(block[None], payload.shape)


def strips_kernel(place, residual, material, coarse, even, odd, inner, outer, long):
    low_x, low_y = place[0] == 1, place[1] == 1
    count, rows, depth = residual.shape
    pieces = depth // LANES
    c1, r1 = count // 2, rows // 2
    base = count * pieces

    def sides(at):
        a, b = even[at], odd[at]
        return jnp.where(low_y, a, b), jnp.where(low_y, b, a)

    for i in range(count):
        for piece in range(pieces):
            low, high = sides(i * pieces + piece)
            z = slice(piece * LANES, (piece + 1) * LANES)
            long[0, i, :, z] = jnp.concatenate([low[:4], residual[i, :, z], high[:4]], axis=0)
            long[1, i, :, z] = jnp.concatenate([low[4:], material[i, :, z], high[4:]], axis=0)
    for k in range(c1):
        low, high = sides(base + k)
        s, m = coarse[k * r1 : (k + 1) * r1], coarse[(c1 + k) * r1 : (c1 + k + 1) * r1]
        i, z = count + k // 2, slice(k % 2 * LANES, (k % 2 + 1) * LANES)
        long[0, i, : r1 + 8, z] = jnp.concatenate([low[:4], s, high[:4]], axis=0)
        long[1, i, : r1 + 8, z] = jnp.concatenate([low[4:], m, high[4:]], axis=0)

    def pack(out, flag):
        at = 0
        for n, planes in ((0, 3), (1, 4)):
            start = jnp.where(flag, 0, count - planes)
            for k in range(planes):
                for tile in range((rows + 8) // 8):
                    for piece in range(pieces):
                        out[at] = long[n, start + k, tile * 8 : tile * 8 + 8, piece * LANES : (piece + 1) * LANES]
                        at += 1
        for n, planes in ((0, 3), (1, 4)):
            for k in range(planes):
                low, high = k, c1 - planes + k
                for tile in range((r1 + 8) // 8):
                    y = slice(tile * 8, tile * 8 + 8)
                    a = long[n, count + low // 2, y, low % 2 * LANES : (low % 2 + 1) * LANES]
                    b = long[n, count + high // 2, y, high % 2 * LANES : (high % 2 + 1) * LANES]
                    out[at] = jnp.where(flag, a, b)
                    at += 1

    pack(inner, low_x)
    pack(outer, jnp.logical_not(low_x))


def unpack(source, flag, out, start, planes, tiles, pieces, at):
    for n in range(planes):
        for tile in range(tiles):
            for piece in range(pieces):
                value = jnp.where(flag, source[0][at], source[1][at])
                out[start + n, tile * 8 : tile * 8 + 8, piece * LANES : (piece + 1) * LANES] = value
                at += 1
    return at


def smooth_kernel(ends, place, potential, long, inner, outer, out, mat, res, x, d, fx, fy, fz, inv):
    low_x = place[0] == 1
    count, rows, depth = potential.shape
    pieces, tiles = depth // LANES, (rows + 8) // 8
    both = (inner, outer)
    for flag, start_r, start_m in ((low_x, 1, 0), (jnp.logical_not(low_x), count + 4, count + 4)):
        at = unpack(both, flag, res, start_r, 3, tiles, pieces, 0)
        unpack(both, flag, mat, start_m, 4, tiles, pieces, at)
    res[pl.ds(4, count)] = long[0, :count]
    mat[pl.ds(4, count)] = long[1, :count]
    total, length = count + 8, rows + 8
    row, lane = iota((length, depth), 0), iota((length, depth), 1)
    outside = as_float(lane == 0) + as_float(lane == depth - 1)
    outside = outside + as_float((row == 4) & (place[3] == 0)) + as_float((row == rows + 3) & (place[3] == ends[1] - 1))
    low_end, high_end = place[2] == 0, place[2] == ends[0] - 1

    def weigh(at, step, previous):
        for n in range(step):
            i = at + n
            a, ahead = mat[i], mat[i + 1]
            f = harmonic(a, ahead, 1.0)
            w_down = harmonic(a, lower(a, 0), 1.0)
            w_back = jnp.where(lane == 0, 0.0, harmonic(a, lower(a, 1), 1.0))
            edges = as_float((i == 4) & low_end) + as_float((i == count + 3) & high_end)
            diagonal = previous + f + w_down + upper(w_down, 0) + w_back + upper(w_back, 1) + a * (outside + edges)
            inverse = jnp.where(a > 0.0, invert(jnp.maximum(diagonal, 1e-3)), 0.0)
            fx[i + 1], fy[i], fz[i], inv[i] = f, w_down, w_back, inverse
            scaled = inverse * res[i]
            res[i] = scaled
            x[0, i] = scaled * (1.0 / THETA)
            previous = f
        return previous

    first = harmonic(mat[0], mat[1], 1.0)
    fx[1] = first
    step = 2
    lax.fori_loop(0, (total - 2) // step, lambda n, f: weigh(1 + n * step, step, f), first)
    rho = 1.0 / SIGMA
    for turn in range(DEG - 1):
        following = 1.0 / (2.0 * SIGMA - rho)
        old, new = turn % 2, (turn + 1) % 2
        keep, gain = following * rho, 2.0 * following / DELTA

        def sweep(n, _):
            for k in range(step):
                i = 2 + turn + n * step + k
                v = x[old, i]
                w_down, w_back = fy[i], fz[i]
                off = fx[i] * x[old, i - 1] + fx[i + 1] * x[old, i + 1]
                off = off + w_down * lower(v, 0) + upper(w_down * v, 0)
                off = off + w_back * lower(v, 1) + upper(w_back * v, 1)
                before = v * keep if turn == 0 else d[i] * keep
                change = before + gain * (res[i] - v + inv[i] * off)
                if turn == DEG - 2:
                    out[i - 4] = potential[i - 4] + (v + change)[4 : 4 + rows]
                else:
                    d[i] = change
                    x[new, i] = v + change
            return 0

        lax.fori_loop(0, (total - 4 - 2 * turn) // step, sweep, 0)
        rho = following


def each(count, body, most=8):
    step = min(count, most)
    if count // step <= 4:
        for n in range(count // step):
            body(n * step, step)
        return

    def run(n, _):
        body(n * step, step)
        return 0

    lax.fori_loop(0, count // step, run, 0)


def fill_table(mat, table, level, count, base, width):
    stride, scale = 2**level, 0.25 ** (level + 2)
    rows = mat.shape[1]

    def body(at, step):
        shape = (step, rows, LANES)
        plane, row, lane = (iota(shape, axis) for axis in range(3))
        a, before, ahead = mat[pl.ds(at + 1, step)], mat[pl.ds(at, step)], mat[pl.ds(at + 2, step)]
        w_before, w_ahead = harmonic(a, before, scale), harmonic(a, ahead, scale)
        w_down = jnp.where(row < stride, 0.0, harmonic(a, lower(a, 1, stride), scale))
        w_back = jnp.where(lane < stride, 0.0, harmonic(a, lower(a, 2, stride), scale))
        outside = as_float(row == 0) + as_float(row == rows - stride) + as_float(lane == 0) + as_float(lane == width - stride)
        outside = outside + as_float(plane == -at) + as_float(plane == count - 1 - at)
        diagonal = w_before + w_ahead + w_down + upper(w_down, 1, stride) + w_back + upper(w_back, 2, stride)
        diagonal = diagonal + scale * a * outside
        table[0, pl.ds(base + at, step)] = w_before
        table[1, pl.ds(base + at, step)] = w_down
        table[2, pl.ds(base + at, step)] = w_back
        table[3, pl.ds(base + at, step)] = jnp.where(a > 0.0, invert(jnp.maximum(diagonal, 1e-4)), 0.0)

    each(count, body, 4)
    table[0, base + count] = jnp.zeros((rows, LANES), F32)


def fold(t, stride):
    a = t.reshape(t.shape[0] // 2, 2, *t.shape[1:])
    a = a[:, 0] + a[:, 1]
    a = a + upper(a, 1, stride)
    return a + upper(a, 2, stride)


def unfold(e, stride):
    e = e + lower(e, 1, stride)
    e = e + lower(e, 2, stride)
    return jnp.broadcast_to(e[:, None], (e.shape[0], 2, *e.shape[1:])).reshape(2 * e.shape[0], *e.shape[1:])


def off_diagonal(e, table, base, at, step, stride):
    v = e[pl.ds(at + 1, step)]
    total = table[0, pl.ds(base + at, step)] * e[pl.ds(at, step)]
    total = total + table[0, pl.ds(base + at + 1, step)] * e[pl.ds(at + 2, step)]
    fy, fz = table[1, pl.ds(base + at, step)], table[2, pl.ds(base + at, step)]
    total = total + fy * lower(v, 1, stride) + upper(fy * v, 1, stride)
    return v, total + fz * lower(v, 2, stride) + upper(fz * v, 2, stride)


def cycle(s, e, t, table, counts, bases, place, out, c2, r2, pad):
    zero = jnp.zeros(t.shape[1:], F32)
    for ref, count in zip(e, counts):
        ref[0] = zero
        ref[count + 1] = zero
    for level, (count, base) in enumerate(zip(counts, bases)):
        s_l, e_l, stride = s[level], e[level], 2**level

        def start(at, step):
            e_l[pl.ds(at + 1, step)] = DAMPING * s_l[pl.ds(at + 1, step)] * table[3, pl.ds(base + at, step)]

        each(count, start)
        if level == len(counts) - 1:
            break

        def remainder(at, step):
            _, off = off_diagonal(e_l, table, base, at, step, stride)
            left = KEPT * s_l[pl.ds(at + 1, step)] + off
            s[level + 1][pl.ds(at // 2 + 1, step // 2)] = 0.125 * fold(left, stride)

        each(count, remainder)

    def relax(s_l, source, target, base, count, stride):
        def sweep(at, step):
            v, off = off_diagonal(source, table, base, at, step, stride)
            inverse = table[3, pl.ds(base + at, step)]
            target[pl.ds(at + 1, step)] = KEPT * v + DAMPING * inverse * (s_l[pl.ds(at + 1, step)] + off)

        each(count, sweep)

    t[0] = zero
    t[counts[2] + 1] = zero
    now, other = e[2], t
    for _ in range(COARSE_SWEEPS - 1):
        relax(s[2], now, other, bases[2], counts[2], 4)
        now, other = other, now

    def add(at, step):
        e[1][pl.ds(2 * at + 1, 2 * step)] = e[1][pl.ds(2 * at + 1, 2 * step)] + unfold(now[pl.ds(at + 1, step)], 2)

    each(counts[2], add, 4)
    if now is t:
        now = e[2] = s[1]
    relax(s[1], e[1], t, bases[1], counts[1], 2)

    planes = c2 + 4
    begin = place[2] * c2 - 2
    inside = jnp.clip(begin, 0, counts[0] - planes)
    coarse = jnp.clip(place[2] * c2 // 2 - 2, 0, counts[1] - planes // 2 - 2)
    number = planes // 2 + 2
    at = pl.ds(2 * coarse + 1, 2 * number)
    e[0][at] = e[0][at] + unfold(t[pl.ds(coarse + 1, number)], 1)
    v, off = off_diagonal(e[0], table, bases[0], inside, planes, 1)
    inverse = table[3, pl.ds(bases[0] + inside, planes)]
    pad[...] = jnp.zeros(pad.shape, F32)
    rows = t.shape[1]
    value = KEPT * v + DAMPING * inverse * (s[0][pl.ds(inside + 1, planes)] + off)
    pad[pl.ds(2 + inside - begin, planes), 8 : 8 + rows, :] = value
    for n in range(planes):
        out[n] = pad[n + 2, pl.ds(place[3] * r2 + 6, r2 + 4), :]


def cycle_shapes(counts, rows, c2):
    out = [pltpu.VMEM((count + 2, rows, LANES), F32) for count in (*counts, *counts, counts[0])]
    return out + [pltpu.VMEM((c2 + 8, rows + 16, LANES), F32)]


def first_cycle_kernel(counts, bases, grid, c2, r2, width, place, blocks, out, table, *scratch):
    s, e, t, pad = scratch[0:3], list(scratch[3:6]), scratch[6], scratch[7]
    gx, gy = grid
    zero = jnp.zeros(t.shape[1:], F32)
    for ref, count in zip((t, *s), (counts[0], *counts)):
        ref[0] = zero
        ref[count + 1] = zero
    half = LANES // 2
    rows = gy * r2
    own = c2 * r2
    face_y = e[0]
    edge = iota((rows, LANES), 0) % r2
    edge = (edge == 0) | (edge == r2 - 1)
    valid = iota((own, LANES), 1) < half
    for n in range(counts[0] + 2):
        face_y[n, 0:8] = jnp.zeros((8, LANES), F32)
        face_y[n, rows - 8 : rows] = jnp.zeros((8, LANES), F32)

    def column(i, _):
        for j in range(gy):
            block = blocks[i * gy + j]
            turned = pltpu.roll(block, half, 1)
            values = jnp.where(valid, block[:own], 0.0)
            materials = jnp.where(valid, turned[:own], 0.0)
            y_faces = jnp.where(valid[: 2 * c2], turned[own:], 0.0)
            for k in range(c2):
                at = i * c2 + k + 1
                s[0][at, j * r2 : (j + 1) * r2, :] = values[k * r2 : (k + 1) * r2]
                t[at, j * r2 : (j + 1) * r2, :] = materials[k * r2 : (k + 1) * r2]
                if j > 0:
                    face_y[at, j * r2 - 1 : j * r2, :] = y_faces[k : k + 1]
                if j < gy - 1:
                    face_y[at, (j + 1) * r2 : (j + 1) * r2 + 1, :] = y_faces[c2 + k : c2 + k + 1]
        return 0

    lax.fori_loop(0, gx, column, 0)

    def sides(i, _):
        low = [blocks[i * gy + j, own : own + r2] for j in range(gy)]
        high = [blocks[i * gy + j, own + r2 :] for j in range(gy)]
        keep = iota((rows, LANES), 1) < half
        for parts, at in ((low, i * c2), (high, (i + 1) * c2 + 1)):
            s[0][at] = s[0][at] + jnp.where(keep, jnp.concatenate(parts, axis=0), 0.0)
        return 0

    lax.fori_loop(0, gx, sides, 0)

    def join(at, step):
        now = pl.ds(at + 1, step)
        s[0][now] = s[0][now] + jnp.where(edge, face_y[now], 0.0)

    each(counts[0], join)
    s[0][0] = zero
    s[0][counts[0] + 1] = zero
    mats = (t, s[1], s[2])
    for level, (count, base) in enumerate(zip(counts, bases)):
        if level:

            def coarsen(at, step):
                shape = (step // 2, rows, LANES)
                whole = (iota(shape, 1) % 2**level == 0) & (iota(shape, 2) % 2**level == 0)
                mean = 0.125 * fold(mats[level - 1][pl.ds(at + 1, step)], 2 ** (level - 1))
                mats[level][pl.ds(at // 2 + 1, step // 2)] = jnp.where(whole, mean, 0.0)

            each(counts[level - 1], coarsen)
        fill_table(mats[level], table, level, count, base, width)
    cycle(s, e, t, table, counts, bases, place, out, c2, r2, pad)


def shifted(a):
    zero = jnp.zeros_like(a[:1])
    return jnp.concatenate([zero, a[:-1]], axis=0), jnp.concatenate([a[1:], zero], axis=0)


def apply_off(e, fx, fy, fz):
    before, ahead = shifted(e)
    out = fx[:-1] * before + fx[1:] * ahead
    out = out + fy * lower(e, 1) + upper(fy * e, 1)
    return out + fz * lower(e, 2) + upper(fz * e, 2)


def raise_window(window_ref, flat, out):
    planes, rows, _ = window_ref.shape
    values = select(window_ref[...].reshape(planes * rows, LANES), spread_matrix(LANES))
    flat[pl.ds(0, planes * rows, 2)] = values
    flat[pl.ds(1, planes * rows, 2)] = values
    v = flat[...].reshape(planes, 1, 2 * rows, LANES)
    out[...] = jnp.broadcast_to(v, (planes, 2, 2 * rows, LANES)).reshape(2 * planes, 2 * rows, LANES)


def level1_kernel(offset, place, long, inner, outer, window1, payload, state, src, mat, flat, prolonged, wide, narrow):
    low_x = place[0] == 1
    total, length, depth = src.shape
    count, rows = total - 8, length - 8
    both = (inner, outer)
    zero = jnp.zeros((length, depth), F32)
    src[0] = zero
    src[total - 1] = zero
    for flag, start_s, start_m in ((low_x, 1, 0), (jnp.logical_not(low_x), count + 4, count + 4)):
        at = unpack(both, flag, src, start_s, 3, length // 8, 1, offset)
        unpack(both, flag, mat, start_m, 4, length // 8, 1, at)
    for n, ref in enumerate((src, mat)):
        for k in range(count):
            ref[4 + k] = long[n, 2 * count + k // 2, :length, k % 2 * LANES : (k % 2 + 1) * LANES]
    raise_window(window1, flat, prolonged)
    a = mat[...]
    lane = iota(a.shape, 2)
    before, ahead = shifted(a)
    down, up = lower(a, 1), upper(a, 1)
    w_x, w_y = harmonic(a, before, 0.25), harmonic(a, down, 0.25)
    w_z = jnp.where(lane == 0, 0.0, harmonic(a, lower(a, 2), 0.25))
    _, w_ahead = shifted(w_x)
    outside = as_float(lane == 0) + as_float(lane == depth - 1)
    for b in (before, ahead, down, up):
        outside = outside + as_float(b <= 0.0)
    diagonal = w_x + w_ahead + w_y + upper(w_y, 1) + w_z + upper(w_z, 2) + 0.25 * a * outside
    inverse = jnp.where(a > 0.0, invert(jnp.maximum(diagonal, 1e-4)), 0.0)
    state[0], state[1], state[2], state[3] = w_x, w_y, w_z, inverse
    w_x = jnp.concatenate([w_x, zero[None]], axis=0)
    s = src[...]
    e = DAMPING * inverse * s + prolonged[...]
    c = KEPT * e + DAMPING * inverse * (s + apply_off(e, w_x, w_y, w_z))
    s2 = s - diagonal * c + apply_off(c, w_x, w_y, w_z)
    e2 = DAMPING * inverse * s2
    t = KEPT * s2 + apply_off(e2, w_x, w_y, w_z)
    state[4], state[5], state[6] = c, s2, e2
    own = t[4 : 4 + count, 4 : 4 + rows].reshape(count // 2, 2, rows, depth)
    wide[...] = (own[:, 0] + own[:, 1]).reshape(count // 2 * rows, depth)
    part = count // 4 * rows
    narrow[...] = (select(wide[:part], pair_matrix(depth)) + select(wide[part:], pair_matrix(depth, LANES // 2))) * 0.125
    block = narrow[pl.ds(0, part // 2, 2)] + narrow[pl.ds(1, part // 2, 2)]
    payload[...] = jnp.broadcast_to(block[None], payload.shape)


def last_cycle_kernel(counts, bases, grid, c2, r2, place, blocks, table, state, partial, out, *scratch):
    s, e, t, pad = scratch[0:3], list(scratch[3:6]), scratch[6], scratch[7]
    view, flat, prolonged, tall = scratch[8:12]
    gx, gy = grid
    half = LANES // 2
    valid = iota((c2 // 2 * r2, LANES), 1) < half

    def column(i, _):
        for j in range(gy):
            block = blocks[i * gy + j]
            parts = (jnp.where(valid, block, 0.0), jnp.where(valid, pltpu.roll(block, half, 1), 0.0))
            for k in range(c2):
                n = k % (c2 // 2)
                s[0][i * c2 + k + 1, j * r2 : (j + 1) * r2, :] = parts[k // (c2 // 2)][n * r2 : (n + 1) * r2]
        return 0

    lax.fori_loop(0, gx, column, 0)
    cycle(s, e, t, table, counts, bases, place, view, c2, r2, pad)
    raise_window(view, flat, prolonged)
    count, rows, depth = partial.shape
    c1, r1 = count // 2, rows // 2
    near = slice(3, c1 + 5)
    own = slice(4, 4 + c1)
    v = state[6, near] + prolonged[near]
    w_x, w_y, w_z = state[0, 4 : c1 + 5], state[1, own], state[2, own]
    here = v[1:-1]
    off = w_x[:-1] * v[:-2] + w_x[1:] * v[2:]
    off = off + w_y * lower(here, 1) + upper(w_y * here, 1) + w_z * lower(here, 2) + upper(w_z * here, 2)
    here = KEPT * here + DAMPING * state[3, own] * (state[5, own] + off)
    coarse = (state[4, own] + here)[:, 4 : 4 + r1].reshape(c1 * r1, LANES)
    values = select(coarse, spread_matrix(depth))
    for piece in range(depth // LANES):
        z = slice(piece * LANES, (piece + 1) * LANES)
        tall[piece, pl.ds(0, c1 * r1, 2)] = values[:, z]
        tall[piece, pl.ds(1, c1 * r1, 2)] = values[:, z]
        for k in range(c1):
            more = tall[piece, k * rows : (k + 1) * rows]
            out[2 * k, :, z] = partial[2 * k, :, z] + more
            out[2 * k + 1, :, z] = partial[2 * k + 1, :, z] + more


def size_of(shape):
    lead = math.prod(shape[:-2])
    return 4 * lead * (-(-shape[-2] // 8) * 8) * (-(-shape[-1] // LANES) * LANES)


def call(kernel, name, inputs, outputs, scratch=(), apart=()):
    streamed = 0

    def held(n, x):
        nonlocal streamed
        if x.ndim == 1 or n in apart:
            return x
        if size_of(x.shape) <= HELD:
            return pltpu.with_memory_space_constraint(x, pltpu.VMEM)
        streamed += size_of(x.shape)
        return x

    def result(shape):
        nonlocal streamed
        if isinstance(shape, jax.ShapeDtypeStruct):
            streamed += size_of(shape.shape)
            return shape
        if size_of(shape) <= HELD:
            return pltpu.VMEM(shape, F32)
        streamed += size_of(shape)
        return jax.ShapeDtypeStruct(shape, F32)

    def space(n, x):
        return pl.ANY if n in apart else pltpu.SMEM if x.ndim == 1 else pltpu.VMEM

    specs = [pl.BlockSpec(memory_space=space(n, x)) for n, x in enumerate(inputs)]
    inputs = [held(n, x) for n, x in enumerate(inputs)]
    results = [result(shape) for shape in outputs]
    need = streamed + sum(size_of(x.shape) for x in scratch if len(x.shape) > 1) + 3 * MIB
    return pl.pallas_call(
        kernel,
        out_shape=results,
        in_specs=specs,
        out_specs=[pl.BlockSpec(memory_space=pltpu.VMEM) for _ in outputs],
        scratch_shapes=list(scratch),
        compiler_params=pltpu.CompilerParams(vmem_limit_bytes=max(need, 8 * MIB)),
        name=name,
    )(*inputs)


def swaps(count):
    inner = [(i, i + 1) for i in range(0, count - 1, 2)]
    outer = [(i, i + 1) for i in range(1, count - 1, 2)]
    return [pairs + [(b, a) for a, b in pairs] for pairs in (inner, outer)]


def local(right_side, potential, phase, permeability):
    gx, gy = lax.axis_size("gx"), lax.axis_size("gy")
    devices = gx * gy
    here_x, here_y = lax.axis_index("gx"), lax.axis_index("gy")
    place = jnp.stack([here_x % 2, here_y % 2, here_x, here_y]).astype(jnp.int32)
    count, rows, depth = right_side.shape
    c1, r1, d1 = count // 2, rows // 2, depth // 2
    c2, r2 = c1 // 2, r1 // 2
    pieces = depth // LANES
    swap_x, swap_y = swaps(gx), swaps(gy)
    VM = lambda *shape: pltpu.VMEM(shape, F32)

    brick = (count, rows, depth)
    face = (3, rows, depth)
    material, potential_here, source_here, inner, outer, even, odd = call(
        faces_kernel, "faces", (place, permeability, potential, phase, right_side),
        (brick, brick, brick, face, face, (3, count, depth), (3, count, depth)),
        (pltpu.VMEM(brick, jnp.int32), pltpu.SMEM(permeability.shape, F32), pltpu.SemaphoreType.DMA((4,))),
        apart=(1, 2, 3, 4),
    )
    even = lax.ppermute(even, "gy", swap_y[0])
    odd = lax.ppermute(odd, "gy", swap_y[1])
    outer = lax.ppermute(outer, "gx", swap_x[1])
    inner = lax.ppermute(inner, "gx", swap_x[0])

    strip = (count * pieces + c1, 8, LANES)
    total = 2 * c1 * rows + 4 * rows
    residual, coarse, even, odd = call(
        residual_kernel, "residual", (place, source_here, potential_here, material, inner, outer, even, odd),
        (brick, (total // 2, LANES), strip, strip),
        (VM(total, depth), VM(total, LANES), VM(4, count, depth)),
    )
    even = lax.ppermute(even, "gy", swap_y[0])
    odd = lax.ppermute(odd, "gy", swap_y[1])
    small = c2 * r1 + 2 * r1
    (payload,) = call(
        functools.partial(payload_kernel, c1, r1), "payload", (coarse,), ((devices, c2 * r2 + 2 * r2, LANES),),
        (VM(2, small, d1), VM(small, LANES)),
    )
    blocks = lax.all_to_all(payload, ("gx", "gy"), 0, 0)
    tiles, tiles1 = (rows + 8) // 8, (r1 + 8) // 8
    strip = (7 * tiles * pieces + 7 * tiles1, 8, LANES)
    inner, outer, long = call(
        strips_kernel, "strips", (place, residual, material, coarse, even, odd),
        (strip, strip, (2, count + c1 // 2, rows + 8, depth)),
    )
    outer = lax.ppermute(outer, "gx", swap_x[1])
    inner = lax.ppermute(inner, "gx", swap_x[0])

    counts = tuple(gx * c2 // k for k in (1, 2, 4))
    bases = (0, counts[0] + 1, counts[0] + counts[1] + 2)
    work = cycle_shapes(counts, gy * r2, c2)
    view = (c2 + 4, r2 + 4, LANES)
    window1, table = call(
        functools.partial(first_cycle_kernel, counts, bases, (gx, gy), c2, r2, d1 // 2), "cycle1", (place, blocks),
        (view, (4, sum(counts) + 3, gy * r2, LANES)), work,
    )
    frame = (c1 + 8, r1 + 8, d1)
    flat = VM((c2 + 4) * (r2 + 4) * 2, LANES)
    payload, state = call(
        functools.partial(level1_kernel, 7 * tiles * pieces), "level1", (place, long, inner, outer, window1),
        ((devices, c2 // 2 * r2, LANES), (7, *frame)),
        (VM(*frame), VM(*frame), flat, VM(*frame), VM(c1 // 2 * r1, d1), VM(c1 // 4 * r1, LANES)),
    )
    blocks = lax.all_to_all(payload, ("gx", "gy"), 0, 0)
    wide = (count + 8, rows + 8, depth)
    (partial,) = call(
        functools.partial(smooth_kernel, (gx, gy)), "smooth", (place, potential, long, inner, outer), (brick,),
        (VM(*wide), VM(*wide), VM(2, *wide), VM(*wide), VM(count + 9, rows + 8, depth), VM(*wide), VM(*wide), VM(*wide)),
    )
    (out,) = call(
        functools.partial(last_cycle_kernel, counts, bases, (gx, gy), c2, r2), "cycle2",
        (place, blocks, table, state, partial), (jax.ShapeDtypeStruct(brick, F32),),
        (*work, VM(*view), flat, VM(*frame), VM(pieces, count // 2 * rows, LANES)),
    )
    return out


def solution(mesh):
    placed = (P("gx", "gy", None), P("gx", "gy", None), P("gx", "gy", None), P())
    return jax.shard_map(local, mesh=mesh, in_specs=placed, out_specs=P("gx", "gy", None), check_vma=False)
```

```python
import functools
import math

import jax
import jax.numpy as jnp
from jax import lax
from jax.experimental import pallas as pl
from jax.experimental.pallas import tpu as pltpu
from jax.sharding import PartitionSpec as P

DEG = 4
COARSE_SWEEPS = 4
THETA = 1.15
DELTA = 0.85
SIGMA = 1.15 / 0.85
DAMPING = 0.6
KEPT = 1.0 - DAMPING
F32 = jnp.float32
LANES = 128
MIB = 1024 * 1024
HELD = 4 * MIB


def iota(shape, axis):
    return lax.broadcasted_iota(jnp.int32, shape, axis)


def invert(x):
    guess = pl.reciprocal(x, approx=True)
    return guess * (2.0 - x * guess)


def harmonic(a, b, scale):
    return (2.0 * scale) * a * b * invert(jnp.maximum(a + b, 1e-3))


def pair_matrix(size, offset=0):
    column = iota((size, LANES), 1)
    return ((column >= offset) & (iota((size, LANES), 0) // 2 == column - offset)).astype(jnp.bfloat16)


def spread_matrix(width):
    return (iota((LANES, width), 1) // 2 == iota((LANES, width), 0)).astype(jnp.bfloat16)


def select(values, matrix):
    high = values.astype(jnp.bfloat16)
    rest = (values - high.astype(F32)).astype(jnp.bfloat16)
    return jnp.dot(high, matrix, preferred_element_type=F32) + jnp.dot(rest, matrix, preferred_element_type=F32)


def lower(x, axis, stride=1):
    return pltpu.roll(x, stride, axis)


def upper(x, axis, stride=1):
    return pltpu.roll(x, x.shape[axis] - stride, axis)


def split(plane, out, at):
    for tile in range(plane.shape[0] // 8):
        for piece in range(plane.shape[1] // LANES):
            out[at] = plane[tile * 8 : tile * 8 + 8, piece * LANES : (piece + 1) * LANES]
            at += 1
    return at


def as_float(condition):
    return jnp.where(condition, 1.0, 0.0)


def faces_kernel(
    place, permeability, potential, phase, source,
    material, pot, src, inner, outer, even, odd,
    ids, values, semaphores,
):
    arriving = [
        pltpu.make_async_copy(a, b, semaphores.at[n])
        for n, (a, b) in enumerate(((permeability, values), (phase, ids), (potential, pot), (source, src)))
    ]
    for copy in arriving:
        copy.start()
    low_x, low_y = place[0] == 1, place[1] == 1
    count, rows = pot.shape[:2]
    arriving[0].wait()
    arriving[1].wait()
    p0, p1, p2 = values[0], values[1], values[2]
    for i in range(count):
        here = ids[i]
        material[i] = jnp.where(here == 0, p0, jnp.where(here == 1, p1, p2))
    last = count - 1
    first = jnp.where(low_x, 0, last)
    second = jnp.where(low_x, 1, last - 1)
    inner[1] = material[first]
    inner[2] = material[second]
    outer[1] = material[last - first]
    outer[2] = material[last - second]

    def edge(slot, ref, a, b):
        for i in range(count):
            low, high = ref[i, a : a + 1, :], ref[i, b : b + 1, :]
            even[slot, i : i + 1, :] = jnp.where(low_y, low, high)
            odd[slot, i : i + 1, :] = jnp.where(low_y, high, low)

    edge(1, material, 0, rows - 1)
    edge(2, material, 1, rows - 2)
    arriving[2].wait()
    inner[0] = pot[first]
    outer[0] = pot[last - first]
    edge(0, pot, 0, rows - 1)
    arriving[3].wait()


def residual_kernel(
    place, source, potential, material, inner, outer, even, odd,
    residual, coarse, strip_inner, strip_outer,
    wide, narrow, y_faces,
):
    low_x, low_y = place[0] == 1, place[1] == 1
    count, rows, depth = source.shape
    c1, r1 = count // 2, rows // 2

    def ordered(flag, a, b):
        return jnp.where(flag, a, b), jnp.where(flag, b, a)

    x_low, x_high = ordered(low_x, inner[...], outer[...])
    y_low, y_high = ordered(low_y, even[...], odd[...])
    row, lane = iota((rows, depth), 0), iota((rows, depth), 1)
    first, last = row == 0, row == rows - 1
    y_faces[0], y_faces[1] = y_low[0], y_high[0]
    y_faces[2], y_faces[3] = y_low[1], y_high[1]
    outside = as_float(lane == 0) + as_float(lane == depth - 1)

    def edge_count(faces):
        return as_float(faces[:1, :1] <= 0.0)

    outside_y = outside + jnp.where(first, edge_count(y_low[1]), 0.0) + jnp.where(last, edge_count(y_high[1]), 0.0)
    face = harmonic(x_low[1], material[0], 1.0)
    for i in range(count):
        a, v = material[i], potential[i]
        v_before = potential[i - 1] if i else x_low[0]
        v_ahead = potential[i + 1] if i < count - 1 else x_high[0]
        next_face = harmonic(a, material[i + 1] if i < count - 1 else x_high[1], 1.0)
        down = jnp.where(first, y_faces[2, i : i + 1], lower(a, 0))
        w_down = harmonic(a, down, 1.0)
        w_top = harmonic(a[rows - 1 :], y_faces[3, i : i + 1], 1.0)
        w_up = jnp.where(last, w_top, upper(w_down, 0))
        w_back = jnp.where(lane == 0, 0.0, harmonic(a, lower(a, 1), 1.0))
        w_front = upper(w_back, 1)
        v_down = jnp.where(first, y_faces[0, i : i + 1], lower(v, 0))
        v_up = jnp.where(last, y_faces[1, i : i + 1], upper(v, 0))
        outer_faces = outside_y
        if i == 0:
            outer_faces = outer_faces + edge_count(x_low[1])
        if i == count - 1:
            outer_faces = outer_faces + edge_count(x_high[1])
        diagonal = face + next_face + w_down + w_up + w_back + w_front + a * outer_faces
        off = face * v_before + next_face * v_ahead + w_down * v_down + w_up * v_up
        off = off + w_back * lower(v, 1) + w_front * upper(v, 1)
        left = source[i] - diagonal * v + off
        residual[i] = left
        face = next_face
        at = (i // 2) * rows
        if i % 2 == 0:
            kept_left, kept_a = left, a
        else:
            wide[at : at + rows] = kept_left + left
            wide[c1 * rows + at : c1 * rows + at + rows] = kept_a + a
    base = 2 * c1 * rows
    for n, both in enumerate((x_low[1] + x_low[2], x_high[1] + x_high[2], y_low[1] + y_low[2], y_high[1] + y_high[2])):
        wide[base + n * rows : base + (n + 1) * rows] = both
    narrow[...] = select(wide[...], pair_matrix(depth)) * 0.125
    half = narrow.shape[0] // 2
    coarse[...] = narrow[pl.ds(0, half, 2)] + narrow[pl.ds(1, half, 2)]
    for strip, flag in ((strip_inner, low_x), (strip_outer, jnp.logical_not(low_x))):
        at = 0
        for ref, planes in ((residual, 3), (material, 4)):
            start = jnp.where(flag, 0, count - planes)
            for k in range(planes):
                at = split(ref[start + k], strip, at)
        for first_row, planes in ((0, 3), (c1 * r1, 4)):
            for k in range(planes):
                low, high = first_row + k * r1, first_row + (c1 - planes + k) * r1
                strip[at] = jnp.where(flag, coarse[low : low + r1], coarse[high : high + r1])
                at += 1


def payload_kernel(c1, r1, coarse, payload, wide, narrow):
    c2 = c1 // 2
    depth = coarse.shape[1]
    s = [coarse[k * r1 : (k + 1) * r1] for k in range(c1)]
    m = [coarse[(c1 + k) * r1 : (c1 + k + 1) * r1] for k in range(c1)]
    base = 2 * c1 * r1
    m_xlow, m_xhigh, m_ylow, m_yhigh = (coarse[base + n * r1 : base + (n + 1) * r1] for n in range(4))
    row, lane = iota((r1, depth), 0), iota((r1, depth), 1)
    first, last = row == 0, row == r1 - 1
    around = [m_xlow] + m + [m_xhigh]
    errors, tables = [], []
    face = harmonic(around[0], around[1], 0.25)
    for k in range(c1):
        a = m[k]
        down = jnp.where(first, m_ylow[k : k + 1], lower(a, 0))
        up = jnp.where(last, m_yhigh[k : k + 1], upper(a, 0))
        next_face = harmonic(a, around[k + 2], 0.25)
        w_down = harmonic(a, down, 0.25)
        w_up = jnp.where(last, harmonic(a, up, 0.25), upper(w_down, 0))
        w_back = jnp.where(lane == 0, 0.0, harmonic(a, lower(a, 1), 0.25))
        w_front = upper(w_back, 1)
        outside = as_float(lane == 0) + as_float(lane == depth - 1)
        outside = outside + as_float(down <= 0.0) + as_float(up <= 0.0)
        outside = outside + as_float(around[k] <= 0.0) + as_float(around[k + 2] <= 0.0)
        diagonal = face + next_face + w_down + w_up + w_back + w_front + 0.25 * a * outside
        errors.append(DAMPING * s[k] * invert(diagonal))
        tables.append((face, next_face, w_down, w_up, w_back, w_front))
        face = next_face
    base = c2 * r1
    for k in range(c1):
        e, w = errors[k], tables[k]
        t = KEPT * s[k] + w[4] * lower(e, 1) + w[5] * upper(e, 1)
        t = t + jnp.where(first, 0.0, w[2] * lower(e, 0)) + jnp.where(last, 0.0, w[3] * upper(e, 0))
        if k > 0:
            t = t + w[0] * errors[k - 1]
        if k < c1 - 1:
            t = t + w[1] * errors[k + 1]
        at = (k // 2) * r1
        if k % 2 == 0:
            kept = t
        else:
            wide[0, at : at + r1] = kept + t
            wide[1, at : at + r1] = m[k - 1] + m[k]
        wide[1, base + k : base + k + 1] = (w[2] * e)[:1]
        wide[1, base + r1 + k : base + r1 + k + 1] = (w[3] * e)[r1 - 1 :]
    wide[0, base : base + r1] = tables[0][0] * errors[0]
    wide[0, base + r1 : base + 2 * r1] = tables[c1 - 1][1] * errors[c1 - 1]
    narrow[...] = (select(wide[0], pair_matrix(depth)) + select(wide[1], pair_matrix(depth, LANES // 2))) * 0.125
    half = narrow.shape[0] // 2
    block = narrow[pl.ds(0, half, 2)] + narrow[pl.ds(1, half, 2)]
    payload[...] = jnp.broadcast_to(block[None], payload.shape)


def fine_planes(rows, depth):
    return (rows // 8) * (depth // LANES)


def level1_place(k, count, r1):
    return count + 8 + k // 4, slice(k % 4 // 2 * r1, (k % 4 // 2 + 1) * r1), slice(k % 2 * LANES, (k % 2 + 1) * LANES)


def strips_kernel(place, residual, material, coarse, inner, outer, even, odd, long):
    low_x, low_y = place[0] == 1, place[1] == 1
    count, rows, depth = residual.shape
    pieces = depth // LANES
    c1, r1 = count // 2, rows // 2
    both = (inner, outer)
    empty = jnp.zeros((rows, depth), F32)
    long[0, 0] = empty
    long[0, count + 7] = empty
    per = fine_planes(rows, depth)

    def fetch(flag, at):
        return jnp.where(flag, both[0][at], both[1][at])

    for n, ref in enumerate((residual, material)):
        for k in range(count):
            long[n, 4 + k] = ref[k]
    nothing = jnp.zeros((r1, LANES), F32)
    for k in (0, c1 + 7):
        plane, y, z = level1_place(k, count, r1)
        long[0, plane, y, z] = nothing
    for n in range(2):
        for k in range(c1):
            plane, y, z = level1_place(k + 4, count, r1)
            at = (n * c1 + k) * r1
            long[n, plane, y, z] = coarse[at : at + r1]
    for flag, starts, starts1 in (
        (low_x, (1, 0), (1, 0)),
        (jnp.logical_not(low_x), (count + 4, count + 4), (c1 + 4, c1 + 4)),
    ):
        at = 0
        for n, planes in enumerate((3, 4)):
            for k in range(planes):
                for tile in range(rows // 8):
                    for piece in range(pieces):
                        z = slice(piece * LANES, (piece + 1) * LANES)
                        long[n, starts[n] + k, tile * 8 : tile * 8 + 8, z] = fetch(flag, at)
                        at += 1
        for n, planes in enumerate((3, 4)):
            for k in range(planes):
                plane, y, z = level1_place(starts1[n] + k, count, r1)
                long[n, plane, y, z] = fetch(flag, at)
                at += 1

    def send(at, a, b):
        last = a.shape[0] - 4
        low = jnp.concatenate([a[:4], b[:4]], axis=0)
        high = jnp.concatenate([a[last:], b[last:]], axis=0)
        even[at] = jnp.where(low_y, low, high)
        odd[at] = jnp.where(low_y, high, low)

    for i in range(count + 8):
        for piece in range(pieces):
            z = slice(piece * LANES, (piece + 1) * LANES)
            send(i * pieces + piece, long[0, i, :, z], long[1, i, :, z])
    for k in range(c1 + 8):
        plane, y, z = level1_place(k, count, r1)
        send((count + 8) * pieces + k, long[0, plane, y, z], long[1, plane, y, z])


def extend(low_y, even, odd, at, a, b):
    first, second = even[at], odd[at]
    low, high = jnp.where(low_y, first, second), jnp.where(low_y, second, first)
    return jnp.concatenate([low[:4], a, high[:4]], axis=0), jnp.concatenate([low[4:], b, high[4:]], axis=0)


def smooth_kernel(ends, place, potential_far, long, even, odd, out, mat, res, x, d, fx, fy, fz, inv, potential, semaphore):
    arriving = pltpu.make_async_copy(potential_far, potential, semaphore)
    arriving.start()
    low_y = place[1] == 1
    count, rows, depth = potential.shape
    pieces = depth // LANES
    for i in range(count + 8):
        for piece in range(pieces):
            z = slice(piece * LANES, (piece + 1) * LANES)
            at = i * pieces + piece
            res[i, :, z], mat[i, :, z] = extend(low_y, even, odd, at, long[0, i, :, z], long[1, i, :, z])
    total, length = count + 8, rows + 8
    row, lane = iota((length, depth), 0), iota((length, depth), 1)
    outside = as_float(lane == 0) + as_float(lane == depth - 1)
    outside = outside + as_float((row == 4) & (place[3] == 0)) + as_float((row == rows + 3) & (place[3] == ends[1] - 1))
    low_end, high_end = place[2] == 0, place[2] == ends[0] - 1

    def weigh(at, step, previous):
        for n in range(step):
            i = at + n
            a, ahead = mat[i], mat[i + 1]
            f = harmonic(a, ahead, 1.0)
            w_down = harmonic(a, lower(a, 0), 1.0)
            w_back = jnp.where(lane == 0, 0.0, harmonic(a, lower(a, 1), 1.0))
            edges = as_float((i == 4) & low_end) + as_float((i == count + 3) & high_end)
            diagonal = previous + f + w_down + upper(w_down, 0) + w_back + upper(w_back, 1) + a * (outside + edges)
            inverse = jnp.where(a > 0.0, invert(jnp.maximum(diagonal, 1e-3)), 0.0)
            fx[i + 1], fy[i], fz[i], inv[i] = f, w_down, w_back, inverse
            scaled = inverse * res[i]
            res[i] = scaled
            x[0, i] = scaled * (1.0 / THETA)
            previous = f
        return previous

    first = harmonic(mat[0], mat[1], 1.0)
    fx[1] = first
    step = 2
    lax.fori_loop(0, (total - 2) // step, lambda n, f: weigh(1 + n * step, step, f), first)
    rho = 1.0 / SIGMA
    for turn in range(DEG - 1):
        if turn == DEG - 2:
            arriving.wait()
        following = 1.0 / (2.0 * SIGMA - rho)
        old, new = turn % 2, (turn + 1) % 2
        keep, gain = following * rho, 2.0 * following / DELTA

        def sweep(n, _):
            for k in range(step):
                i = 2 + turn + n * step + k
                v = x[old, i]
                w_down, w_back = fy[i], fz[i]
                off = fx[i] * x[old, i - 1] + fx[i + 1] * x[old, i + 1]
                off = off + w_down * lower(v, 0) + upper(w_down * v, 0)
                off = off + w_back * lower(v, 1) + upper(w_back * v, 1)
                before = v * keep if turn == 0 else d[i] * keep
                change = before + gain * (res[i] - v + inv[i] * off)
                if turn == DEG - 2:
                    out[i - 4] = potential[i - 4] + (v + change)[4 : 4 + rows]
                else:
                    d[i] = change
                    x[new, i] = v + change
            return 0

        lax.fori_loop(0, (total - 4 - 2 * turn) // step, sweep, 0)
        rho = following


def each(count, body, most=8):
    step = min(count, most)
    if count // step <= 4:
        for n in range(count // step):
            body(n * step, step)
        return

    def run(n, _):
        body(n * step, step)
        return 0

    lax.fori_loop(0, count // step, run, 0)


def fill_table(mat, table, level, count, base, width):
    stride, scale = 2**level, 0.25 ** (level + 2)
    rows = mat.shape[1]

    def body(at, step):
        shape = (step, rows, LANES)
        plane, row, lane = (iota(shape, axis) for axis in range(3))
        a, before, ahead = mat[pl.ds(at + 1, step)], mat[pl.ds(at, step)], mat[pl.ds(at + 2, step)]
        w_before, w_ahead = harmonic(a, before, scale), harmonic(a, ahead, scale)
        w_down = jnp.where(row < stride, 0.0, harmonic(a, lower(a, 1, stride), scale))
        w_back = jnp.where(lane < stride, 0.0, harmonic(a, lower(a, 2, stride), scale))
        outside = as_float(row == 0) + as_float(row == rows - stride) + as_float(lane == 0) + as_float(lane == width - stride)
        outside = outside + as_float(plane == -at) + as_float(plane == count - 1 - at)
        diagonal = w_before + w_ahead + w_down + upper(w_down, 1, stride) + w_back + upper(w_back, 2, stride)
        diagonal = diagonal + scale * a * outside
        table[0, pl.ds(base + at, step)] = w_before
        table[1, pl.ds(base + at, step)] = w_down
        table[2, pl.ds(base + at, step)] = w_back
        table[3, pl.ds(base + at, step)] = jnp.where(a > 0.0, invert(jnp.maximum(diagonal, 1e-4)), 0.0)

    each(count, body, 4)
    table[0, base + count] = jnp.zeros((rows, LANES), F32)


def fold(t, stride):
    a = t.reshape(t.shape[0] // 2, 2, *t.shape[1:])
    a = a[:, 0] + a[:, 1]
    a = a + upper(a, 1, stride)
    return a + upper(a, 2, stride)


def unfold(e, stride):
    e = e + lower(e, 1, stride)
    e = e + lower(e, 2, stride)
    return jnp.broadcast_to(e[:, None], (e.shape[0], 2, *e.shape[1:])).reshape(2 * e.shape[0], *e.shape[1:])


def off_diagonal(e, table, base, at, step, stride):
    v = e[pl.ds(at + 1, step)]
    total = table[0, pl.ds(base + at, step)] * e[pl.ds(at, step)]
    total = total + table[0, pl.ds(base + at + 1, step)] * e[pl.ds(at + 2, step)]
    fy, fz = table[1, pl.ds(base + at, step)], table[2, pl.ds(base + at, step)]
    total = total + fy * lower(v, 1, stride) + upper(fy * v, 1, stride)
    return v, total + fz * lower(v, 2, stride) + upper(fz * v, 2, stride)


def cycle(s, e, t, table, counts, bases, place, out, c2, r2, pad):
    zero = jnp.zeros(t.shape[1:], F32)
    for ref, count in zip(e, counts):
        ref[0] = zero
        ref[count + 1] = zero
    for level, (count, base) in enumerate(zip(counts, bases)):
        s_l, e_l, stride = s[level], e[level], 2**level

        def start(at, step):
            e_l[pl.ds(at + 1, step)] = DAMPING * s_l[pl.ds(at + 1, step)] * table[3, pl.ds(base + at, step)]

        each(count, start)
        if level == len(counts) - 1:
            break

        def remainder(at, step):
            _, off = off_diagonal(e_l, table, base, at, step, stride)
            left = KEPT * s_l[pl.ds(at + 1, step)] + off
            s[level + 1][pl.ds(at // 2 + 1, step // 2)] = 0.125 * fold(left, stride)

        each(count, remainder)

    def relax(s_l, source, target, base, count, stride):
        def sweep(at, step):
            v, off = off_diagonal(source, table, base, at, step, stride)
            inverse = table[3, pl.ds(base + at, step)]
            target[pl.ds(at + 1, step)] = KEPT * v + DAMPING * inverse * (s_l[pl.ds(at + 1, step)] + off)

        each(count, sweep)

    t[0] = zero
    t[counts[2] + 1] = zero
    now, other = e[2], t
    for _ in range(COARSE_SWEEPS - 1):
        relax(s[2], now, other, bases[2], counts[2], 4)
        now, other = other, now

    def add(at, step):
        e[1][pl.ds(2 * at + 1, 2 * step)] = e[1][pl.ds(2 * at + 1, 2 * step)] + unfold(now[pl.ds(at + 1, step)], 2)

    each(counts[2], add, 4)
    if now is t:
        now = e[2] = s[1]
    relax(s[1], e[1], t, bases[1], counts[1], 2)

    planes = c2 + 4
    begin = place[2] * c2 - 2
    inside = jnp.clip(begin, 0, counts[0] - planes)
    coarse = jnp.clip(place[2] * c2 // 2 - 2, 0, counts[1] - planes // 2 - 2)
    number = planes // 2 + 2
    at = pl.ds(2 * coarse + 1, 2 * number)
    e[0][at] = e[0][at] + unfold(t[pl.ds(coarse + 1, number)], 1)
    v, off = off_diagonal(e[0], table, bases[0], inside, planes, 1)
    inverse = table[3, pl.ds(bases[0] + inside, planes)]
    pad[...] = jnp.zeros(pad.shape, F32)
    rows = t.shape[1]
    value = KEPT * v + DAMPING * inverse * (s[0][pl.ds(inside + 1, planes)] + off)
    pad[pl.ds(2 + inside - begin, planes), 8 : 8 + rows, :] = value
    for n in range(planes):
        out[n] = pad[n + 2, pl.ds(place[3] * r2 + 6, r2 + 4), :]


def cycle_shapes(counts, rows, c2):
    out = [pltpu.VMEM((count + 2, rows, LANES), F32) for count in (*counts, *counts, counts[0])]
    return out + [pltpu.VMEM((c2 + 8, rows + 16, LANES), F32)]


def first_cycle_kernel(counts, bases, grid, c2, r2, width, place, blocks, out, table, *scratch):
    s, e, t, pad = scratch[0:3], list(scratch[3:6]), scratch[6], scratch[7]
    gx, gy = grid
    zero = jnp.zeros(t.shape[1:], F32)
    for ref, count in zip((t, *s), (counts[0], *counts)):
        ref[0] = zero
        ref[count + 1] = zero
    half = LANES // 2
    rows = gy * r2
    own = c2 * r2
    face_y = e[0]
    edge = iota((rows, LANES), 0) % r2
    edge = (edge == 0) | (edge == r2 - 1)
    valid = iota((own, LANES), 1) < half
    for n in range(counts[0] + 2):
        face_y[n, 0:8] = jnp.zeros((8, LANES), F32)
        face_y[n, rows - 8 : rows] = jnp.zeros((8, LANES), F32)

    def column(i, _):
        for j in range(gy):
            block = blocks[i * gy + j]
            turned = pltpu.roll(block, half, 1)
            values = jnp.where(valid, block[:own], 0.0)
            materials = jnp.where(valid, turned[:own], 0.0)
            y_faces = jnp.where(valid[: 2 * c2], turned[own:], 0.0)
            for k in range(c2):
                at = i * c2 + k + 1
                s[0][at, j * r2 : (j + 1) * r2, :] = values[k * r2 : (k + 1) * r2]
                t[at, j * r2 : (j + 1) * r2, :] = materials[k * r2 : (k + 1) * r2]
                if j > 0:
                    face_y[at, j * r2 - 1 : j * r2, :] = y_faces[k : k + 1]
                if j < gy - 1:
                    face_y[at, (j + 1) * r2 : (j + 1) * r2 + 1, :] = y_faces[c2 + k : c2 + k + 1]
        return 0

    lax.fori_loop(0, gx, column, 0)

    def sides(i, _):
        low = [blocks[i * gy + j, own : own + r2] for j in range(gy)]
        high = [blocks[i * gy + j, own + r2 :] for j in range(gy)]
        keep = iota((rows, LANES), 1) < half
        for parts, at in ((low, i * c2), (high, (i + 1) * c2 + 1)):
            s[0][at] = s[0][at] + jnp.where(keep, jnp.concatenate(parts, axis=0), 0.0)
        return 0

    lax.fori_loop(0, gx, sides, 0)

    def join(at, step):
        now = pl.ds(at + 1, step)
        s[0][now] = s[0][now] + jnp.where(edge, face_y[now], 0.0)

    each(counts[0], join)
    s[0][0] = zero
    s[0][counts[0] + 1] = zero
    mats = (t, s[1], s[2])
    for level, (count, base) in enumerate(zip(counts, bases)):
        if level:

            def coarsen(at, step):
                shape = (step // 2, rows, LANES)
                whole = (iota(shape, 1) % 2**level == 0) & (iota(shape, 2) % 2**level == 0)
                mean = 0.125 * fold(mats[level - 1][pl.ds(at + 1, step)], 2 ** (level - 1))
                mats[level][pl.ds(at // 2 + 1, step // 2)] = jnp.where(whole, mean, 0.0)

            each(counts[level - 1], coarsen)
        fill_table(mats[level], table, level, count, base, width)
    cycle(s, e, t, table, counts, bases, place, out, c2, r2, pad)


def shifted(a):
    zero = jnp.zeros_like(a[:1])
    return jnp.concatenate([zero, a[:-1]], axis=0), jnp.concatenate([a[1:], zero], axis=0)


def apply_off(e, fx, fy, fz):
    before, ahead = shifted(e)
    out = fx[:-1] * before + fx[1:] * ahead
    out = out + fy * lower(e, 1) + upper(fy * e, 1)
    return out + fz * lower(e, 2) + upper(fz * e, 2)


def raise_window(window_ref, flat, out):
    planes, rows, _ = window_ref.shape
    values = select(window_ref[...].reshape(planes * rows, LANES), spread_matrix(LANES))
    flat[pl.ds(0, planes * rows, 2)] = values
    flat[pl.ds(1, planes * rows, 2)] = values
    v = flat[...].reshape(planes, 1, 2 * rows, LANES)
    out[...] = jnp.broadcast_to(v, (planes, 2, 2 * rows, LANES)).reshape(2 * planes, 2 * rows, LANES)


def level1_kernel(place, long, even, odd, window1, payload, state_far, src, mat, flat, prolonged, wide, narrow, state, semaphore):
    low_y = place[1] == 1
    total, length, depth = src.shape
    count, rows = total - 8, length - 8
    base = (long.shape[1] - total // 4) * (long.shape[3] // LANES)
    zero = jnp.zeros((length, depth), F32)
    for k in range(total):
        plane, y, z = level1_place(k, 2 * count, rows)
        src[k], mat[k] = extend(low_y, even, odd, base + k, long[0, plane, y, z], long[1, plane, y, z])
    raise_window(window1, flat, prolonged)
    a = mat[...]
    lane = iota(a.shape, 2)
    before, ahead = shifted(a)
    down, up = lower(a, 1), upper(a, 1)
    w_x, w_y = harmonic(a, before, 0.25), harmonic(a, down, 0.25)
    w_z = jnp.where(lane == 0, 0.0, harmonic(a, lower(a, 2), 0.25))
    _, w_ahead = shifted(w_x)
    outside = as_float(lane == 0) + as_float(lane == depth - 1)
    for b in (before, ahead, down, up):
        outside = outside + as_float(b <= 0.0)
    diagonal = w_x + w_ahead + w_y + upper(w_y, 1) + w_z + upper(w_z, 2) + 0.25 * a * outside
    inverse = jnp.where(a > 0.0, invert(jnp.maximum(diagonal, 1e-4)), 0.0)
    state[0], state[1], state[2], state[3] = w_x, w_y, w_z, inverse
    w_x = jnp.concatenate([w_x, zero[None]], axis=0)
    s = src[...]
    e = DAMPING * inverse * s + prolonged[...]
    c = KEPT * e + DAMPING * inverse * (s + apply_off(e, w_x, w_y, w_z))
    s2 = s - diagonal * c + apply_off(c, w_x, w_y, w_z)
    e2 = DAMPING * inverse * s2
    t = KEPT * s2 + apply_off(e2, w_x, w_y, w_z)
    state[4], state[5], state[6] = c, s2, e2
    leaving = pltpu.make_async_copy(state, state_far, semaphore)
    leaving.start()
    own = t[4 : 4 + count, 4 : 4 + rows].reshape(count // 2, 2, rows, depth)
    wide[...] = (own[:, 0] + own[:, 1]).reshape(count // 2 * rows, depth)
    part = count // 4 * rows
    narrow[...] = (select(wide[:part], pair_matrix(depth)) + select(wide[part:], pair_matrix(depth, LANES // 2))) * 0.125
    block = narrow[pl.ds(0, part // 2, 2)] + narrow[pl.ds(1, part // 2, 2)]
    payload[...] = jnp.broadcast_to(block[None], payload.shape)
    leaving.wait()


def last_cycle_kernel(counts, bases, grid, c2, r2, place, blocks, table, state_far, partial, out, *scratch):
    s, e, t, pad = scratch[0:3], list(scratch[3:6]), scratch[6], scratch[7]
    view, flat, prolonged, tall, state, semaphore = scratch[8:14]
    arriving = pltpu.make_async_copy(state_far, state, semaphore)
    arriving.start()
    gx, gy = grid
    half = LANES // 2
    valid = iota((c2 // 2 * r2, LANES), 1) < half

    def column(i, _):
        for j in range(gy):
            block = blocks[i * gy + j]
            parts = (jnp.where(valid, block, 0.0), jnp.where(valid, pltpu.roll(block, half, 1), 0.0))
            for k in range(c2):
                n = k % (c2 // 2)
                s[0][i * c2 + k + 1, j * r2 : (j + 1) * r2, :] = parts[k // (c2 // 2)][n * r2 : (n + 1) * r2]
        return 0

    lax.fori_loop(0, gx, column, 0)
    cycle(s, e, t, table, counts, bases, place, view, c2, r2, pad)
    raise_window(view, flat, prolonged)
    count, rows, depth = partial.shape
    c1, r1 = count // 2, rows // 2
    arriving.wait()
    near = slice(3, c1 + 5)
    own = slice(4, 4 + c1)
    v = state[6, near] + prolonged[near]
    w_x, w_y, w_z = state[0, 4 : c1 + 5], state[1, own], state[2, own]
    here = v[1:-1]
    off = w_x[:-1] * v[:-2] + w_x[1:] * v[2:]
    off = off + w_y * lower(here, 1) + upper(w_y * here, 1) + w_z * lower(here, 2) + upper(w_z * here, 2)
    here = KEPT * here + DAMPING * state[3, own] * (state[5, own] + off)
    coarse = (state[4, own] + here)[:, 4 : 4 + r1].reshape(c1 * r1, LANES)
    values = select(coarse, spread_matrix(depth))
    for piece in range(depth // LANES):
        z = slice(piece * LANES, (piece + 1) * LANES)
        tall[piece, pl.ds(0, c1 * r1, 2)] = values[:, z]
        tall[piece, pl.ds(1, c1 * r1, 2)] = values[:, z]
        for k in range(c1):
            more = tall[piece, k * rows : (k + 1) * rows]
            out[2 * k, :, z] = partial[2 * k, :, z] + more
            out[2 * k + 1, :, z] = partial[2 * k + 1, :, z] + more


def size_of(shape):
    lead = math.prod(shape[:-2])
    return 4 * lead * (-(-shape[-2] // 8) * 8) * (-(-shape[-1] // LANES) * LANES)


def call(kernel, name, inputs, outputs, scratch=(), apart=()):
    streamed = 0

    def held(n, x):
        nonlocal streamed
        if n in apart:
            return pltpu.with_memory_space_constraint(x, pltpu.HBM)
        if x.ndim == 1:
            return x
        if size_of(x.shape) <= HELD:
            return pltpu.with_memory_space_constraint(x, pltpu.VMEM)
        streamed += size_of(x.shape)
        return x

    def result(shape):
        nonlocal streamed
        if isinstance(shape, jax.ShapeDtypeStruct):
            streamed += size_of(shape.shape)
            return shape
        if far(shape):
            return pltpu.HBM(shape[1], F32)
        if size_of(shape) <= HELD:
            return pltpu.VMEM(shape, F32)
        streamed += size_of(shape)
        return jax.ShapeDtypeStruct(shape, F32)

    def far(x):
        return isinstance(x, tuple) and x[0] == "far"

    def space(n, x):
        return pltpu.HBM if n in apart else pltpu.SMEM if x.ndim == 1 else pltpu.VMEM

    specs = [pl.BlockSpec(memory_space=space(n, x)) for n, x in enumerate(inputs)]
    inputs = [held(n, x) for n, x in enumerate(inputs)]
    results = [result(shape) for shape in outputs]
    need = streamed + sum(size_of(x.shape) for x in scratch if len(getattr(x, "shape", ())) > 1) + 3 * MIB
    return pl.pallas_call(
        kernel,
        out_shape=results,
        in_specs=specs,
        out_specs=[pl.BlockSpec(memory_space=pltpu.HBM if far(x) else pltpu.VMEM) for x in outputs],
        scratch_shapes=list(scratch),
        compiler_params=pltpu.CompilerParams(vmem_limit_bytes=max(need, 8 * MIB)),
        name=name,
    )(*inputs)


def swaps(count):
    inner = [(i, i + 1) for i in range(0, count - 1, 2)]
    outer = [(i, i + 1) for i in range(1, count - 1, 2)]
    return [pairs + [(b, a) for a, b in pairs] for pairs in (inner, outer)]


def local(right_side, potential, phase, permeability):
    gx, gy = lax.axis_size("gx"), lax.axis_size("gy")
    devices = gx * gy
    here_x, here_y = lax.axis_index("gx"), lax.axis_index("gy")
    place = jnp.stack([here_x % 2, here_y % 2, here_x, here_y]).astype(jnp.int32)
    count, rows, depth = right_side.shape
    c1, r1, d1 = count // 2, rows // 2, depth // 2
    c2, r2 = c1 // 2, r1 // 2
    pieces = depth // LANES
    swap_x, swap_y = swaps(gx), swaps(gy)
    VM = lambda *shape: pltpu.VMEM(shape, F32)

    brick = (count, rows, depth)
    face = (3, rows, depth)
    material, potential_here, source_here, inner, outer, even, odd = call(
        faces_kernel, "faces", (place, permeability, potential, phase, right_side),
        (brick, brick, brick, face, face, (3, count, depth), (3, count, depth)),
        (pltpu.VMEM(brick, jnp.int32), pltpu.SMEM(permeability.shape, F32), pltpu.SemaphoreType.DMA((4,))),
        apart=(1, 2, 3, 4),
    )
    even = lax.ppermute(even, "gy", swap_y[0])
    odd = lax.ppermute(odd, "gy", swap_y[1])
    outer = lax.ppermute(outer, "gx", swap_x[1])
    inner = lax.ppermute(inner, "gx", swap_x[0])

    strip = (7 * fine_planes(rows, depth) + 7, 8, LANES)
    total = 2 * c1 * rows + 4 * rows
    residual, coarse, inner, outer = call(
        residual_kernel, "residual", (place, source_here, potential_here, material, inner, outer, even, odd),
        (brick, (total // 2, LANES), strip, strip),
        (VM(total, depth), VM(total, LANES), VM(4, count, depth)),
    )
    outer = lax.ppermute(outer, "gx", swap_x[1])
    inner = lax.ppermute(inner, "gx", swap_x[0])
    small = c2 * r1 + 2 * r1
    (payload,) = call(
        functools.partial(payload_kernel, c1, r1), "payload", (coarse,), ((devices, c2 * r2 + 2 * r2, LANES),),
        (VM(2, small, d1), VM(small, LANES)),
    )
    blocks = lax.all_to_all(payload, ("gx", "gy"), 0, 0)
    strip = ((count + 8) * pieces + c1 + 8, 8, LANES)
    even, odd, long = call(
        strips_kernel, "strips", (place, residual, material, coarse, inner, outer),
        (strip, strip, (2, count + 8 + (c1 + 8) // 4, rows, depth)),
    )
    even = lax.ppermute(even, "gy", swap_y[0])
    odd = lax.ppermute(odd, "gy", swap_y[1])

    counts = tuple(gx * c2 // k for k in (1, 2, 4))
    bases = (0, counts[0] + 1, counts[0] + counts[1] + 2)
    work = cycle_shapes(counts, gy * r2, c2)
    view = (c2 + 4, r2 + 4, LANES)
    window1, table = call(
        functools.partial(first_cycle_kernel, counts, bases, (gx, gy), c2, r2, d1 // 2), "cycle1", (place, blocks),
        (view, (4, sum(counts) + 3, gy * r2, LANES)), work,
    )
    frame = (c1 + 8, r1 + 8, d1)
    flat = VM((c2 + 4) * (r2 + 4) * 2, LANES)
    payload, state = call(
        level1_kernel, "level1", (place, long, even, odd, window1),
        ((devices, c2 // 2 * r2, LANES), ("far", (7, *frame))),
        (
            VM(*frame), VM(*frame), flat, VM(*frame), VM(c1 // 2 * r1, d1), VM(c1 // 4 * r1, LANES), VM(7, *frame),
            pltpu.SemaphoreType.DMA,
        ),
    )
    blocks = lax.all_to_all(payload, ("gx", "gy"), 0, 0)
    wide = (count + 8, rows + 8, depth)
    (partial,) = call(
        functools.partial(smooth_kernel, (gx, gy)), "smooth", (place, potential, long, even, odd), (brick,),
        (
            VM(*wide), VM(*wide), VM(2, *wide), VM(*wide), VM(count + 9, rows + 8, depth), VM(*wide), VM(*wide), VM(*wide),
            VM(*brick), pltpu.SemaphoreType.DMA,
        ),
        apart=(1,),
    )
    (out,) = call(
        functools.partial(last_cycle_kernel, counts, bases, (gx, gy), c2, r2), "cycle2",
        (place, blocks, table, state, partial), (jax.ShapeDtypeStruct(brick, F32),),
        (*work, VM(*view), flat, VM(*frame), VM(pieces, count // 2 * rows, LANES), VM(7, *frame), pltpu.SemaphoreType.DMA),
        apart=(3,),
    )
    return out


def solution(mesh):
    placed = (P("gx", "gy", None), P("gx", "gy", None), P("gx", "gy", None), P())
    return jax.shard_map(local, mesh=mesh, in_specs=placed, out_specs=P("gx", "gy", None), check_vma=False)
```

```python
import functools
import math

import jax
import jax.numpy as jnp
from jax import lax
from jax.experimental import pallas as pl
from jax.experimental.pallas import tpu as pltpu
from jax.sharding import PartitionSpec as P

DEG = 4
COARSE_SWEEPS = 4
THETA = 1.15
DELTA = 0.85
SIGMA = 1.15 / 0.85
DAMPING = 0.6
KEPT = 1.0 - DAMPING
F32 = jnp.float32
LANES = 128
MIB = 1024 * 1024
HELD = 4 * MIB


def iota(shape, axis):
    return lax.broadcasted_iota(jnp.int32, shape, axis)


def invert(x):
    guess = pl.reciprocal(x, approx=True)
    return guess * (2.0 - x * guess)


def harmonic(a, b, scale):
    return (2.0 * scale) * a * b * invert(jnp.maximum(a + b, 1e-3))


def pair_matrix(size, offset=0):
    column = iota((size, LANES), 1)
    return ((column >= offset) & (iota((size, LANES), 0) // 2 == column - offset)).astype(jnp.bfloat16)


def spread_matrix(width):
    return (iota((LANES, width), 1) // 2 == iota((LANES, width), 0)).astype(jnp.bfloat16)


def select(values, matrix):
    high = values.astype(jnp.bfloat16)
    rest = (values - high.astype(F32)).astype(jnp.bfloat16)
    return jnp.dot(high, matrix, preferred_element_type=F32) + jnp.dot(rest, matrix, preferred_element_type=F32)


def lower(x, axis, stride=1):
    return pltpu.roll(x, stride, axis)


def upper(x, axis, stride=1):
    return pltpu.roll(x, x.shape[axis] - stride, axis)


def as_float(condition):
    return jnp.where(condition, 1.0, 0.0)


def faces_kernel(
    place, permeability, potential, phase, source,
    material, pot, src, inner, outer, even, odd, payload,
    ids, values, semaphores, wide, narrow, folded, narrow1, sheet,
):
    arriving = [
        pltpu.make_async_copy(a, b, semaphores.at[n])
        for n, (a, b) in enumerate(((permeability, values), (phase, ids), (potential, pot), (source, src)))
    ]
    for copy in arriving:
        copy.start()
    low_x, low_y = place[0] == 1, place[1] == 1
    count, rows = pot.shape[:2]
    arriving[0].wait()
    arriving[1].wait()
    p0, p1, p2 = values[0], values[1], values[2]
    for i in range(count):
        here = ids[i]
        material[i] = jnp.where(here == 0, p0, jnp.where(here == 1, p1, p2))
    c1, r1 = count // 2, rows // 2
    for k in range(c1):
        wide[k * rows : (k + 1) * rows] = material[2 * k] + material[2 * k + 1]
    narrow[...] = select(wide[...], pair_matrix(wide.shape[1])) * 0.125
    half = c1 * r1
    finer = narrow[pl.ds(0, half, 2)] + narrow[pl.ds(1, half, 2)]
    for k in range(c1 // 2):
        folded[k * r1 : (k + 1) * r1] = finer[2 * k * r1 : (2 * k + 1) * r1] + finer[(2 * k + 1) * r1 : (2 * k + 2) * r1]
    part = folded.shape[0] // 2
    sheet[...] = jnp.broadcast_to(packed(folded[:part], folded[part:], narrow1)[None], sheet.shape)
    leaving = pltpu.make_async_copy(sheet, payload, semaphores.at[4])
    leaving.start()
    last = count - 1
    first = jnp.where(low_x, 0, last)
    second = jnp.where(low_x, 1, last - 1)
    inner[1] = material[first]
    inner[2] = material[second]
    outer[1] = material[last - first]
    outer[2] = material[last - second]

    def edge(slot, ref, a, b):
        for i in range(count):
            low, high = ref[i, a : a + 1, :], ref[i, b : b + 1, :]
            even[slot, i : i + 1, :] = jnp.where(low_y, low, high)
            odd[slot, i : i + 1, :] = jnp.where(low_y, high, low)

    edge(1, material, 0, rows - 1)
    edge(2, material, 1, rows - 2)
    arriving[2].wait()
    inner[0] = pot[first]
    outer[0] = pot[last - first]
    edge(0, pot, 0, rows - 1)
    leaving.wait()
    arriving[3].wait()


def residual_kernel(
    place, source, potential, material, inner, outer, even, odd,
    residual, coarse, strip_even, strip_odd,
    wide, narrow, y_faces,
):
    low_x, low_y = place[0] == 1, place[1] == 1
    count, rows, depth = source.shape
    c1, r1 = count // 2, rows // 2
    pieces = depth // LANES

    def ordered(flag, a, b):
        return jnp.where(flag, a, b), jnp.where(flag, b, a)

    x_low, x_high = ordered(low_x, inner[...], outer[...])
    y_low, y_high = ordered(low_y, even[...], odd[...])
    row, lane = iota((rows, depth), 0), iota((rows, depth), 1)
    first, last = row == 0, row == rows - 1
    y_faces[0], y_faces[1] = y_low[0], y_high[0]
    y_faces[2], y_faces[3] = y_low[1], y_high[1]
    outside = as_float(lane == 0) + as_float(lane == depth - 1)

    def edge_count(faces):
        return as_float(faces[:1, :1] <= 0.0)

    outside_y = outside + jnp.where(first, edge_count(y_low[1]), 0.0) + jnp.where(last, edge_count(y_high[1]), 0.0)
    face = harmonic(x_low[1], material[0], 1.0)
    for i in range(count):
        a, v = material[i], potential[i]
        v_before = potential[i - 1] if i else x_low[0]
        v_ahead = potential[i + 1] if i < count - 1 else x_high[0]
        next_face = harmonic(a, material[i + 1] if i < count - 1 else x_high[1], 1.0)
        down = jnp.where(first, y_faces[2, i : i + 1], lower(a, 0))
        w_down = harmonic(a, down, 1.0)
        w_top = harmonic(a[rows - 1 :], y_faces[3, i : i + 1], 1.0)
        w_up = jnp.where(last, w_top, upper(w_down, 0))
        w_back = jnp.where(lane == 0, 0.0, harmonic(a, lower(a, 1), 1.0))
        w_front = upper(w_back, 1)
        v_down = jnp.where(first, y_faces[0, i : i + 1], lower(v, 0))
        v_up = jnp.where(last, y_faces[1, i : i + 1], upper(v, 0))
        outer_faces = outside_y
        if i == 0:
            outer_faces = outer_faces + edge_count(x_low[1])
        if i == count - 1:
            outer_faces = outer_faces + edge_count(x_high[1])
        diagonal = face + next_face + w_down + w_up + w_back + w_front + a * outer_faces
        off = face * v_before + next_face * v_ahead + w_down * v_down + w_up * v_up
        off = off + w_back * lower(v, 1) + w_front * upper(v, 1)
        left = source[i] - diagonal * v + off
        residual[i] = left
        face = next_face
        at = (i // 2) * rows
        if i % 2 == 0:
            kept_left, kept_a = left, a
        else:
            wide[at : at + rows] = kept_left + left
            wide[c1 * rows + at : c1 * rows + at + rows] = kept_a + a
        low = jnp.concatenate([left[:4], a[:4]], axis=0)
        high = jnp.concatenate([left[rows - 4 :], a[rows - 4 :]], axis=0)
        for ref, strip in ((strip_even, jnp.where(low_y, low, high)), (strip_odd, jnp.where(low_y, high, low))):
            for piece in range(pieces):
                ref[i * pieces + piece] = strip[:, piece * LANES : (piece + 1) * LANES]
    base = 2 * c1 * rows
    for n, both in enumerate((x_low[1] + x_low[2], x_high[1] + x_high[2], y_low[1] + y_low[2], y_high[1] + y_high[2])):
        wide[base + n * rows : base + (n + 1) * rows] = both
    narrow[...] = select(wide[...], pair_matrix(depth)) * 0.125
    half = narrow.shape[0] // 2
    coarse[...] = narrow[pl.ds(0, half, 2)] + narrow[pl.ds(1, half, 2)]
    for k in range(c1):
        s, m = coarse[k * r1 : (k + 1) * r1], coarse[(c1 + k) * r1 : (c1 + k + 1) * r1]
        low = jnp.concatenate([s[:4], m[:4]], axis=0)
        high = jnp.concatenate([s[r1 - 4 :], m[r1 - 4 :]], axis=0)
        strip_even[count * pieces + k] = jnp.where(low_y, low, high)
        strip_odd[count * pieces + k] = jnp.where(low_y, high, low)


def payload_kernel(c1, r1, coarse, payload, wide, narrow, sheet, semaphore):
    c2 = c1 // 2
    depth = coarse.shape[1]
    s = [coarse[k * r1 : (k + 1) * r1] for k in range(c1)]
    m = [coarse[(c1 + k) * r1 : (c1 + k + 1) * r1] for k in range(c1)]
    base = 2 * c1 * r1
    m_xlow, m_xhigh, m_ylow, m_yhigh = (coarse[base + n * r1 : base + (n + 1) * r1] for n in range(4))
    row, lane = iota((r1, depth), 0), iota((r1, depth), 1)
    first, last = row == 0, row == r1 - 1
    around = [m_xlow] + m + [m_xhigh]
    errors, tables = [], []
    face = harmonic(around[0], around[1], 0.25)
    for k in range(c1):
        a = m[k]
        down = jnp.where(first, m_ylow[k : k + 1], lower(a, 0))
        up = jnp.where(last, m_yhigh[k : k + 1], upper(a, 0))
        next_face = harmonic(a, around[k + 2], 0.25)
        w_down = harmonic(a, down, 0.25)
        w_up = jnp.where(last, harmonic(a, up, 0.25), upper(w_down, 0))
        w_back = jnp.where(lane == 0, 0.0, harmonic(a, lower(a, 1), 0.25))
        w_front = upper(w_back, 1)
        outside = as_float(lane == 0) + as_float(lane == depth - 1)
        outside = outside + as_float(down <= 0.0) + as_float(up <= 0.0)
        outside = outside + as_float(around[k] <= 0.0) + as_float(around[k + 2] <= 0.0)
        diagonal = face + next_face + w_down + w_up + w_back + w_front + 0.25 * a * outside
        errors.append(DAMPING * s[k] * invert(diagonal))
        tables.append((face, next_face, w_down, w_up, w_back, w_front))
        face = next_face
    base = c2 // 2 * r1
    for k in range(c1):
        e, w = errors[k], tables[k]
        t = KEPT * s[k] + w[4] * lower(e, 1) + w[5] * upper(e, 1)
        t = t + jnp.where(first, 0.0, w[2] * lower(e, 0)) + jnp.where(last, 0.0, w[3] * upper(e, 0))
        if k > 0:
            t = t + w[0] * errors[k - 1]
        if k < c1 - 1:
            t = t + w[1] * errors[k + 1]
        at = k // 2 * r1
        if k % 2 == 0:
            kept = t
        else:
            wide[at // base, at % base : at % base + r1] = kept + t
        wide[1, base + k : base + k + 1] = (w[2] * e)[:1]
        wide[1, base + r1 + k : base + r1 + k + 1] = (w[3] * e)[r1 - 1 :]
    wide[0, base : base + r1] = tables[0][0] * errors[0]
    wide[0, base + r1 : base + 2 * r1] = tables[c1 - 1][1] * errors[c1 - 1]
    publish(wide[0], wide[1], narrow, sheet, payload, semaphore)


def packed(low, high, narrow):
    narrow[...] = (select(low, pair_matrix(LANES)) + select(high, pair_matrix(LANES, LANES // 2))) * 0.125
    half = narrow.shape[0] // 2
    return narrow[pl.ds(0, half, 2)] + narrow[pl.ds(1, half, 2)]


def publish(low, high, narrow, sheet, payload, semaphore):
    sheet[...] = jnp.broadcast_to(packed(low, high, narrow)[None], sheet.shape)
    leaving = pltpu.make_async_copy(sheet, payload, semaphore)
    leaving.start()
    leaving.wait()


def strips_kernel(place, residual, material, coarse, even, odd, inner, outer, long):
    low_x, low_y = place[0] == 1, place[1] == 1
    count, rows, depth = residual.shape
    pieces = depth // LANES
    c1, r1 = count // 2, rows // 2
    base = count * pieces

    def sides(at):
        a, b = even[at], odd[at]
        return jnp.where(low_y, a, b), jnp.where(low_y, b, a)

    for i in range(count):
        for piece in range(pieces):
            low, high = sides(i * pieces + piece)
            z = slice(piece * LANES, (piece + 1) * LANES)
            long[0, i, :, z] = jnp.concatenate([low[:4], residual[i, :, z], high[:4]], axis=0)
            long[1, i, :, z] = jnp.concatenate([low[4:], material[i, :, z], high[4:]], axis=0)
    for k in range(c1):
        low, high = sides(base + k)
        s, m = coarse[k * r1 : (k + 1) * r1], coarse[(c1 + k) * r1 : (c1 + k + 1) * r1]
        i, z = count + k // 2, slice(k % 2 * LANES, (k % 2 + 1) * LANES)
        long[0, i, : r1 + 8, z] = jnp.concatenate([low[:4], s, high[:4]], axis=0)
        long[1, i, : r1 + 8, z] = jnp.concatenate([low[4:], m, high[4:]], axis=0)

    def pack(out, flag):
        at = 0
        for n, planes in ((0, 3), (1, 4)):
            start = jnp.where(flag, 0, count - planes)
            for k in range(planes):
                for tile in range((rows + 8) // 8):
                    for piece in range(pieces):
                        out[at] = long[n, start + k, tile * 8 : tile * 8 + 8, piece * LANES : (piece + 1) * LANES]
                        at += 1
        for n, planes in ((0, 3), (1, 4)):
            for k in range(planes):
                low, high = k, c1 - planes + k
                for tile in range((r1 + 8) // 8):
                    y = slice(tile * 8, tile * 8 + 8)
                    a = long[n, count + low // 2, y, low % 2 * LANES : (low % 2 + 1) * LANES]
                    b = long[n, count + high // 2, y, high % 2 * LANES : (high % 2 + 1) * LANES]
                    out[at] = jnp.where(flag, a, b)
                    at += 1

    pack(inner, low_x)
    pack(outer, jnp.logical_not(low_x))


def unpack(source, flag, out, start, planes, tiles, pieces, at):
    for n in range(planes):
        for tile in range(tiles):
            for piece in range(pieces):
                value = jnp.where(flag, source[0][at], source[1][at])
                out[start + n, tile * 8 : tile * 8 + 8, piece * LANES : (piece + 1) * LANES] = value
                at += 1
    return at


def smooth_kernel(ends, place, potential_far, long, inner, outer, out, mat, res, x, d, fx, fy, fz, inv, potential, semaphore):
    arriving = pltpu.make_async_copy(potential_far, potential, semaphore)
    arriving.start()
    low_x = place[0] == 1
    count, rows, depth = potential.shape
    pieces, tiles = depth // LANES, (rows + 8) // 8
    both = (inner, outer)
    for flag, start_r, start_m in ((low_x, 1, 0), (jnp.logical_not(low_x), count + 4, count + 4)):
        at = unpack(both, flag, res, start_r, 3, tiles, pieces, 0)
        unpack(both, flag, mat, start_m, 4, tiles, pieces, at)
    res[pl.ds(4, count)] = long[0, :count]
    mat[pl.ds(4, count)] = long[1, :count]
    total, length = count + 8, rows + 8
    row, lane = iota((length, depth), 0), iota((length, depth), 1)
    outside = as_float(lane == 0) + as_float(lane == depth - 1)
    outside = outside + as_float((row == 4) & (place[3] == 0)) + as_float((row == rows + 3) & (place[3] == ends[1] - 1))
    low_end, high_end = place[2] == 0, place[2] == ends[0] - 1

    def weigh(at, step, previous):
        for n in range(step):
            i = at + n
            a, ahead = mat[i], mat[i + 1]
            f = harmonic(a, ahead, 1.0)
            w_down = harmonic(a, lower(a, 0), 1.0)
            w_back = jnp.where(lane == 0, 0.0, harmonic(a, lower(a, 1), 1.0))
            edges = as_float((i == 4) & low_end) + as_float((i == count + 3) & high_end)
            diagonal = previous + f + w_down + upper(w_down, 0) + w_back + upper(w_back, 1) + a * (outside + edges)
            inverse = jnp.where(a > 0.0, invert(jnp.maximum(diagonal, 1e-3)), 0.0)
            fx[i + 1], fy[i], fz[i], inv[i] = f, w_down, w_back, inverse
            scaled = inverse * res[i]
            res[i] = scaled
            x[0, i] = scaled * (1.0 / THETA)
            previous = f
        return previous

    first = harmonic(mat[0], mat[1], 1.0)
    fx[1] = first
    step = 2
    lax.fori_loop(0, (total - 2) // step, lambda n, f: weigh(1 + n * step, step, f), first)
    rho = 1.0 / SIGMA
    for turn in range(DEG - 1):
        if turn == DEG - 2:
            arriving.wait()
        following = 1.0 / (2.0 * SIGMA - rho)
        old, new = turn % 2, (turn + 1) % 2
        keep, gain = following * rho, 2.0 * following / DELTA

        def sweep(n, _):
            for k in range(step):
                i = 2 + turn + n * step + k
                v = x[old, i]
                w_down, w_back = fy[i], fz[i]
                off = fx[i] * x[old, i - 1] + fx[i + 1] * x[old, i + 1]
                off = off + w_down * lower(v, 0) + upper(w_down * v, 0)
                off = off + w_back * lower(v, 1) + upper(w_back * v, 1)
                before = v * keep if turn == 0 else d[i] * keep
                change = before + gain * (res[i] - v + inv[i] * off)
                if turn == DEG - 2:
                    out[i - 4] = potential[i - 4] + (v + change)[4 : 4 + rows]
                else:
                    d[i] = change
                    x[new, i] = v + change
            return 0

        lax.fori_loop(0, (total - 4 - 2 * turn) // step, sweep, 0)
        rho = following


def each(count, body, most=8):
    step = min(count, most)
    if count // step <= 4:
        for n in range(count // step):
            body(n * step, step)
        return

    def run(n, _):
        body(n * step, step)
        return 0

    lax.fori_loop(0, count // step, run, 0)


def fill_table(mat, table, level, count, base, width):
    stride, scale = 2**level, 0.25 ** (level + 2)
    rows = mat.shape[1]

    def body(at, step):
        shape = (step, rows, LANES)
        plane, row, lane = (iota(shape, axis) for axis in range(3))
        a, before, ahead = mat[pl.ds(at + 1, step)], mat[pl.ds(at, step)], mat[pl.ds(at + 2, step)]
        w_before, w_ahead = harmonic(a, before, scale), harmonic(a, ahead, scale)
        w_down = jnp.where(row < stride, 0.0, harmonic(a, lower(a, 1, stride), scale))
        w_back = jnp.where(lane < stride, 0.0, harmonic(a, lower(a, 2, stride), scale))
        outside = as_float(row == 0) + as_float(row == rows - stride) + as_float(lane == 0) + as_float(lane == width - stride)
        outside = outside + as_float(plane == -at) + as_float(plane == count - 1 - at)
        diagonal = w_before + w_ahead + w_down + upper(w_down, 1, stride) + w_back + upper(w_back, 2, stride)
        diagonal = diagonal + scale * a * outside
        table[0, pl.ds(base + at, step)] = w_before
        table[1, pl.ds(base + at, step)] = w_down
        table[2, pl.ds(base + at, step)] = w_back
        table[3, pl.ds(base + at, step)] = jnp.where(a > 0.0, invert(jnp.maximum(diagonal, 1e-4)), 0.0)

    each(count, body, 4)
    table[0, base + count] = jnp.zeros((rows, LANES), F32)


def fold(t, stride):
    a = t.reshape(t.shape[0] // 2, 2, *t.shape[1:])
    a = a[:, 0] + a[:, 1]
    a = a + upper(a, 1, stride)
    return a + upper(a, 2, stride)


def unfold(e, stride):
    e = e + lower(e, 1, stride)
    e = e + lower(e, 2, stride)
    return jnp.broadcast_to(e[:, None], (e.shape[0], 2, *e.shape[1:])).reshape(2 * e.shape[0], *e.shape[1:])


def off_diagonal(e, table, base, at, step, stride):
    v = e[pl.ds(at + 1, step)]
    total = table[0, pl.ds(base + at, step)] * e[pl.ds(at, step)]
    total = total + table[0, pl.ds(base + at + 1, step)] * e[pl.ds(at + 2, step)]
    fy, fz = table[1, pl.ds(base + at, step)], table[2, pl.ds(base + at, step)]
    total = total + fy * lower(v, 1, stride) + upper(fy * v, 1, stride)
    return v, total + fz * lower(v, 2, stride) + upper(fz * v, 2, stride)


def cycle(s, e, t, table, counts, bases, place, out, c2, r2, pad):
    zero = jnp.zeros(t.shape[1:], F32)
    for ref, count in zip(e, counts):
        ref[0] = zero
        ref[count + 1] = zero
    for level, (count, base) in enumerate(zip(counts, bases)):
        s_l, e_l, stride = s[level], e[level], 2**level

        def start(at, step):
            e_l[pl.ds(at + 1, step)] = DAMPING * s_l[pl.ds(at + 1, step)] * table[3, pl.ds(base + at, step)]

        each(count, start)
        if level == len(counts) - 1:
            break

        def remainder(at, step):
            _, off = off_diagonal(e_l, table, base, at, step, stride)
            left = KEPT * s_l[pl.ds(at + 1, step)] + off
            s[level + 1][pl.ds(at // 2 + 1, step // 2)] = 0.125 * fold(left, stride)

        each(count, remainder)

    def relax(s_l, source, target, base, count, stride):
        def sweep(at, step):
            v, off = off_diagonal(source, table, base, at, step, stride)
            inverse = table[3, pl.ds(base + at, step)]
            target[pl.ds(at + 1, step)] = KEPT * v + DAMPING * inverse * (s_l[pl.ds(at + 1, step)] + off)

        each(count, sweep)

    t[0] = zero
    t[counts[2] + 1] = zero
    now, other = e[2], t
    for _ in range(COARSE_SWEEPS - 1):
        relax(s[2], now, other, bases[2], counts[2], 4)
        now, other = other, now

    def add(at, step):
        e[1][pl.ds(2 * at + 1, 2 * step)] = e[1][pl.ds(2 * at + 1, 2 * step)] + unfold(now[pl.ds(at + 1, step)], 2)

    each(counts[2], add, 4)
    if now is t:
        now = e[2] = s[1]
    relax(s[1], e[1], t, bases[1], counts[1], 2)

    planes = c2 + 4
    begin = place[2] * c2 - 2
    inside = jnp.clip(begin, 0, counts[0] - planes)
    coarse = jnp.clip(place[2] * c2 // 2 - 2, 0, counts[1] - planes // 2 - 2)
    number = planes // 2 + 2
    at = pl.ds(2 * coarse + 1, 2 * number)
    e[0][at] = e[0][at] + unfold(t[pl.ds(coarse + 1, number)], 1)
    v, off = off_diagonal(e[0], table, bases[0], inside, planes, 1)
    inverse = table[3, pl.ds(bases[0] + inside, planes)]
    pad[...] = jnp.zeros(pad.shape, F32)
    rows = t.shape[1]
    value = KEPT * v + DAMPING * inverse * (s[0][pl.ds(inside + 1, planes)] + off)
    pad[pl.ds(2 + inside - begin, planes), 8 : 8 + rows, :] = value
    for n in range(planes):
        out[n] = pad[n + 2, pl.ds(place[3] * r2 + 6, r2 + 4), :]


def cycle_shapes(counts, rows, c2):
    out = [pltpu.VMEM((count + 2, rows, LANES), F32) for count in (*counts, *counts, counts[0])]
    return out + [pltpu.VMEM((c2 + 8, rows + 16, LANES), F32)]


def spread_blocks(blocks, out, grid, c2, r2):
    gx, gy = grid
    length = c2 // 2 * r2
    low = iota((length, LANES), 1) < LANES // 2

    def column(i, _):
        for j in range(gy):
            block = blocks[i * gy + j, :length]
            parts = (jnp.where(low, block, 0.0), jnp.where(low, pltpu.roll(block, LANES // 2, 1), 0.0))
            for k in range(c2):
                n = k % (c2 // 2)
                out[i * c2 + k + 1, j * r2 : (j + 1) * r2, :] = parts[k // (c2 // 2)][n * r2 : (n + 1) * r2]
        return 0

    lax.fori_loop(0, gx, column, 0)


def clear_ends(refs, counts):
    for ref, count in zip(refs, counts):
        zero = jnp.zeros(ref.shape[1:], F32)
        ref[0] = zero
        ref[count + 1] = zero


def tables_kernel(counts, bases, grid, c2, r2, width, blocks, table, *mats):
    rows = grid[1] * r2
    clear_ends(mats, counts)
    spread_blocks(blocks, mats[0], grid, c2, r2)
    for level, (count, base) in enumerate(zip(counts, bases)):
        if level:

            def coarsen(at, step):
                shape = (step // 2, rows, LANES)
                whole = (iota(shape, 1) % 2**level == 0) & (iota(shape, 2) % 2**level == 0)
                mean = 0.125 * fold(mats[level - 1][pl.ds(at + 1, step)], 2 ** (level - 1))
                mats[level][pl.ds(at // 2 + 1, step // 2)] = jnp.where(whole, mean, 0.0)

            each(counts[level - 1], coarsen)
        fill_table(mats[level], table, level, count, base, width)


def first_cycle_kernel(counts, bases, grid, c2, r2, place, blocks, table, out, *scratch):
    s, e, t, pad = scratch[0:3], list(scratch[3:6]), scratch[6], scratch[7]
    gx, gy = grid
    rows = gy * r2
    half = LANES // 2
    own = c2 // 2 * r2
    clear_ends(s, counts)
    spread_blocks(blocks, s[0], grid, c2, r2)
    face_y = e[0]
    low = iota((2 * c2, LANES), 1) < half

    def edges(i, _):
        for j in range(gy):
            faces = blocks[i * gy + j, own:]
            x_faces = jnp.where(low, faces, 0.0)
            y_faces = jnp.where(low, pltpu.roll(faces, half, 1), 0.0)
            here = slice(j * r2, (j + 1) * r2)
            s[0][i * c2, here, :] = s[0][i * c2, here, :] + x_faces[:r2]
            s[0][(i + 1) * c2 + 1, here, :] = s[0][(i + 1) * c2 + 1, here, :] + x_faces[r2:]
            for k in range(c2):
                at = i * c2 + k + 1
                if j > 0:
                    face_y[at, j * r2 - 1 : j * r2, :] = y_faces[k : k + 1]
                if j < gy - 1:
                    face_y[at, (j + 1) * r2 : (j + 1) * r2 + 1, :] = y_faces[c2 + k : c2 + k + 1]
        return 0

    lax.fori_loop(0, gx, edges, 0)

    def join(at, step):
        now = pl.ds(at + 1, step)
        row = iota((step, rows, LANES), 1)
        edge = ((row % r2 == 0) & (row > 0)) | ((row % r2 == r2 - 1) & (row < rows - 1))
        s[0][now] = s[0][now] + jnp.where(edge, face_y[now], 0.0)

    each(counts[0], join)
    clear_ends(s[:1], counts)
    cycle(s, e, t, table, counts, bases, place, out, c2, r2, pad)


def shifted(a):
    zero = jnp.zeros_like(a[:1])
    return jnp.concatenate([zero, a[:-1]], axis=0), jnp.concatenate([a[1:], zero], axis=0)


def apply_off(e, fx, fy, fz):
    before, ahead = shifted(e)
    out = fx[:-1] * before + fx[1:] * ahead
    out = out + fy * lower(e, 1) + upper(fy * e, 1)
    return out + fz * lower(e, 2) + upper(fz * e, 2)


def raise_window(window_ref, flat, out):
    planes, rows, _ = window_ref.shape
    values = select(window_ref[...].reshape(planes * rows, LANES), spread_matrix(LANES))
    flat[pl.ds(0, planes * rows, 2)] = values
    flat[pl.ds(1, planes * rows, 2)] = values
    v = flat[...].reshape(planes, 1, 2 * rows, LANES)
    out[...] = jnp.broadcast_to(v, (planes, 2, 2 * rows, LANES)).reshape(2 * planes, 2 * rows, LANES)


def level1_kernel(
    offset, place, long, inner, outer, window1, payload, state_far,
    src, mat, flat, prolonged, fx, fy, fz, diag, inv, err, c, state, wide, narrow, sheet, semaphores,
):
    low_x = place[0] == 1
    total, length, depth = src.shape
    count, rows = total - 8, length - 8
    both = (inner, outer)
    zero = jnp.zeros((length, depth), F32)
    src[0] = zero
    src[total - 1] = zero
    for flag, start_s, start_m in ((low_x, 1, 0), (jnp.logical_not(low_x), count + 4, count + 4)):
        at = unpack(both, flag, src, start_s, 3, length // 8, 1, offset)
        unpack(both, flag, mat, start_m, 4, length // 8, 1, at)
    for n, ref in enumerate((src, mat)):
        for k in range(count):
            ref[4 + k] = long[n, 2 * count + k // 2, :length, k % 2 * LANES : (k % 2 + 1) * LANES]
    raise_window(window1, flat, prolonged)
    row, lane = iota((length, depth), 0), iota((length, depth), 1)
    ends = as_float(lane == 0) + as_float(lane == depth - 1)
    fx[1] = harmonic(mat[0], mat[1], 0.25)
    for k in range(1, total - 1):
        a, before, ahead = mat[k], mat[k - 1], mat[k + 1]
        down, up = lower(a, 0), upper(a, 0)
        f = harmonic(a, ahead, 0.25)
        w_y = harmonic(a, down, 0.25)
        w_z = jnp.where(lane == 0, 0.0, harmonic(a, lower(a, 1), 0.25))
        outside = ends + as_float(before <= 0.0) + as_float(ahead <= 0.0) + as_float(down <= 0.0) + as_float(up <= 0.0)
        diagonal = fx[k] + f + w_y + upper(w_y, 0) + w_z + upper(w_z, 1) + 0.25 * a * outside
        inverse = jnp.where(a > 0.0, invert(jnp.maximum(diagonal, 1e-4)), 0.0)
        fx[k + 1], fy[k], fz[k], diag[k], inv[k] = f, w_y, w_z, diagonal, inverse
        err[k] = DAMPING * inverse * src[k] + prolonged[k]

    def off(v, k):
        here = v[k]
        w_y, w_z = fy[k], fz[k]
        out = fx[k] * v[k - 1] + fx[k + 1] * v[k + 1] + w_y * lower(here, 0) + upper(w_y * here, 0)
        return here, out + w_z * lower(here, 1) + upper(w_z * here, 1)

    for k in range(2, total - 2):
        here, more = off(err, k)
        c[k] = KEPT * here + DAMPING * inv[k] * (src[k] + more)
    for k in range(3, total - 3):
        here, more = off(c, k)
        left = src[k] - diag[k] * here + more
        src[k] = left
        value = DAMPING * inv[k] * left
        err[k] = value
        state[k - 3] = value
    base = count + 2
    for k in range(count + 1):
        state[base + k] = fx[k + 4]
    base += count + 1
    for n, ref in enumerate((fy, fz, inv, c, src)):
        for k in range(count):
            state[base + n * count + k] = ref[k + 4]
    leaving = pltpu.make_async_copy(state, state_far, semaphores.at[0])
    leaving.start()
    for k in range(4, count + 4):
        _, more = off(err, k)
        t = (KEPT * src[k] + more)[4 : 4 + rows]
        if k % 2 == 0:
            kept = t
        else:
            at = (k - 5) // 2 * rows
            wide[at : at + rows] = kept + t
    half = wide.shape[0] // 2
    publish(wide[:half], wide[half:], narrow, sheet, payload, semaphores.at[1])
    leaving.wait()


def last_cycle_kernel(counts, bases, grid, c2, r2, place, blocks, table, state_far, partial, out, *scratch):
    s, e, t, pad = scratch[0:3], list(scratch[3:6]), scratch[6], scratch[7]
    view, flat, prolonged, tall, coarse, state, semaphore = scratch[8:15]
    arriving = pltpu.make_async_copy(state_far, state, semaphore)
    arriving.start()
    spread_blocks(blocks, s[0], grid, c2, r2)
    clear_ends(s, counts)
    cycle(s, e, t, table, counts, bases, place, view, c2, r2, pad)
    raise_window(view, flat, prolonged)
    count, rows, depth = partial.shape
    c1, r1 = count // 2, rows // 2
    arriving.wait()
    for k in range(c1 + 2):
        prolonged[k + 3] = prolonged[k + 3] + state[k]
    base = 2 * c1 + 3
    for k in range(c1):
        here = prolonged[k + 4]
        w_y, w_z, inverse, before, left = (state[base + n * c1 + k] for n in range(5))
        off = state[c1 + 2 + k] * prolonged[k + 3] + state[c1 + 3 + k] * prolonged[k + 5]
        off = off + w_y * lower(here, 0) + upper(w_y * here, 0) + w_z * lower(here, 1) + upper(w_z * here, 1)
        total = before + KEPT * here + DAMPING * inverse * (left + off)
        coarse[k * r1 : (k + 1) * r1] = total[4 : 4 + r1]
    values = select(coarse[...], spread_matrix(depth))
    for piece in range(depth // LANES):
        z = slice(piece * LANES, (piece + 1) * LANES)
        tall[piece, pl.ds(0, c1 * r1, 2)] = values[:, z]
        tall[piece, pl.ds(1, c1 * r1, 2)] = values[:, z]
        for k in range(c1):
            more = tall[piece, k * rows : (k + 1) * rows]
            out[2 * k, :, z] = partial[2 * k, :, z] + more
            out[2 * k + 1, :, z] = partial[2 * k + 1, :, z] + more


def size_of(shape):
    lead = math.prod(shape[:-2])
    return 4 * lead * (-(-shape[-2] // 8) * 8) * (-(-shape[-1] // LANES) * LANES)


def call(kernel, name, inputs, outputs, scratch=(), apart=(), cost=None):
    streamed = 0

    def held(n, x):
        nonlocal streamed
        if n in apart:
            return pltpu.with_memory_space_constraint(x, pltpu.HBM)
        if x.ndim == 1:
            return x
        if size_of(x.shape) <= HELD:
            return pltpu.with_memory_space_constraint(x, pltpu.VMEM)
        streamed += size_of(x.shape)
        return x

    def result(shape):
        nonlocal streamed
        if isinstance(shape, jax.ShapeDtypeStruct):
            streamed += size_of(shape.shape)
            return shape
        if far(shape):
            return pltpu.HBM(shape[1], F32)
        if size_of(shape) <= HELD:
            return pltpu.VMEM(shape, F32)
        streamed += size_of(shape)
        return jax.ShapeDtypeStruct(shape, F32)

    def far(x):
        return isinstance(x, tuple) and x[0] == "far"

    def space(n, x):
        return pltpu.HBM if n in apart else pltpu.SMEM if x.ndim == 1 else pltpu.VMEM

    specs = [pl.BlockSpec(memory_space=space(n, x)) for n, x in enumerate(inputs)]
    inputs = [held(n, x) for n, x in enumerate(inputs)]
    results = [result(shape) for shape in outputs]
    need = streamed + sum(size_of(x.shape) for x in scratch if len(getattr(x, "shape", ())) > 1) + 3 * MIB
    return pl.pallas_call(
        kernel,
        out_shape=results,
        in_specs=specs,
        out_specs=[pl.BlockSpec(memory_space=pltpu.HBM if far(x) else pltpu.VMEM) for x in outputs],
        scratch_shapes=list(scratch),
        compiler_params=pltpu.CompilerParams(vmem_limit_bytes=max(need, 8 * MIB)),
        name=name,
        cost_estimate=None if cost is None else pl.CostEstimate(flops=cost, bytes_accessed=0, transcendentals=0),
    )(*inputs)


def swaps(count):
    inner = [(i, i + 1) for i in range(0, count - 1, 2)]
    outer = [(i, i + 1) for i in range(1, count - 1, 2)]
    return [pairs + [(b, a) for a, b in pairs] for pairs in (inner, outer)]


def local(right_side, potential, phase, permeability):
    gx, gy = lax.axis_size("gx"), lax.axis_size("gy")
    devices = gx * gy
    here_x, here_y = lax.axis_index("gx"), lax.axis_index("gy")
    place = jnp.stack([here_x % 2, here_y % 2, here_x, here_y]).astype(jnp.int32)
    count, rows, depth = right_side.shape
    c1, r1, d1 = count // 2, rows // 2, depth // 2
    c2, r2 = c1 // 2, r1 // 2
    pieces = depth // LANES
    swap_x, swap_y = swaps(gx), swaps(gy)
    VM = lambda *shape: pltpu.VMEM(shape, F32)

    brick = (count, rows, depth)
    face = (3, rows, depth)
    DMA = pltpu.SemaphoreType.DMA
    sheet = (devices, c2 // 2 * r2, LANES)
    sheet2 = (devices, c2 // 2 * r2 + 2 * r2, LANES)
    material, potential_here, source_here, inner, outer, even, odd, materials = call(
        faces_kernel, "faces", (place, permeability, potential, phase, right_side),
        (brick, brick, brick, face, face, (3, count, depth), (3, count, depth), ("far", sheet)),
        (
            pltpu.VMEM(brick, jnp.int32), pltpu.SMEM(permeability.shape, F32), pltpu.SemaphoreType.DMA((5,)),
            VM(c1 * rows, depth), VM(c1 * rows, LANES), VM(c2 * r1, LANES), VM(c2 // 2 * r1, LANES), VM(*sheet),
        ),
        apart=(1, 2, 3, 4),
    )
    materials = lax.all_to_all(materials, ("gx", "gy"), 0, 0)
    even = lax.ppermute(even, "gy", swap_y[0])
    odd = lax.ppermute(odd, "gy", swap_y[1])
    outer = lax.ppermute(outer, "gx", swap_x[1])
    inner = lax.ppermute(inner, "gx", swap_x[0])

    strip = (count * pieces + c1, 8, LANES)
    total = 2 * c1 * rows + 4 * rows
    residual, coarse, even, odd = call(
        residual_kernel, "residual", (place, source_here, potential_here, material, inner, outer, even, odd),
        (brick, (total // 2, LANES), strip, strip),
        (VM(total, depth), VM(total, LANES), VM(4, count, depth)), cost=10**10,
    )
    even = lax.ppermute(even, "gy", swap_y[0])
    odd = lax.ppermute(odd, "gy", swap_y[1])
    small = c2 // 2 * r1 + 2 * r1
    (payload,) = call(
        functools.partial(payload_kernel, c1, r1), "payload", (coarse,), (("far", sheet2),),
        (VM(2, small, d1), VM(small, LANES), VM(*sheet2), DMA),
    )
    blocks = lax.all_to_all(payload, ("gx", "gy"), 0, 0)
    tiles, tiles1 = (rows + 8) // 8, (r1 + 8) // 8
    strip = (7 * tiles * pieces + 7 * tiles1, 8, LANES)
    inner, outer, long = call(
        strips_kernel, "strips", (place, residual, material, coarse, even, odd),
        (strip, strip, (2, count + c1 // 2, rows + 8, depth)), cost=10**11,
    )
    outer = lax.ppermute(outer, "gx", swap_x[1])
    inner = lax.ppermute(inner, "gx", swap_x[0])

    counts = tuple(gx * c2 // k for k in (1, 2, 4))
    bases = (0, counts[0] + 1, counts[0] + counts[1] + 2)
    work = cycle_shapes(counts, gy * r2, c2)
    view = (c2 + 4, r2 + 4, LANES)
    planes = [VM(n + 2, gy * r2, LANES) for n in counts]
    (table,) = call(
        functools.partial(tables_kernel, counts, bases, (gx, gy), c2, r2, d1 // 2), "tables", (materials,),
        ((4, sum(counts) + 3, gy * r2, LANES),), planes,
    )
    (window1,) = call(
        functools.partial(first_cycle_kernel, counts, bases, (gx, gy), c2, r2), "cycle1", (place, blocks, table), (view,), work,
    )
    frame = (c1 + 8, r1 + 8, d1)
    flat = VM((c2 + 4) * (r2 + 4) * 2, LANES)
    state = (7 * c1 + 3, r1 + 8, d1)
    tall = VM(c1 + 9, r1 + 8, d1)
    payload, held = call(
        functools.partial(level1_kernel, 7 * tiles * pieces), "level1", (place, long, inner, outer, window1), (("far", sheet), ("far", state)),
        (
            VM(*frame), VM(*frame), flat, VM(*frame), tall, VM(*frame), VM(*frame), VM(*frame), VM(*frame), VM(*frame),
            VM(*frame), VM(*state), VM(c1 // 2 * r1, d1), VM(c1 // 4 * r1, LANES), VM(*sheet), pltpu.SemaphoreType.DMA((2,)),
        ),
    )
    blocks = lax.all_to_all(payload, ("gx", "gy"), 0, 0)
    wide = (count + 8, rows + 8, depth)
    (partial,) = call(
        functools.partial(smooth_kernel, (gx, gy)), "smooth", (place, potential, long, inner, outer), (brick,),
        (
            VM(*wide), VM(*wide), VM(2, *wide), VM(*wide), VM(count + 9, rows + 8, depth), VM(*wide), VM(*wide), VM(*wide),
            VM(*brick), pltpu.SemaphoreType.DMA,
        ),
        apart=(1,),
    )
    (out,) = call(
        functools.partial(last_cycle_kernel, counts, bases, (gx, gy), c2, r2), "cycle2",
        (place, blocks, table, held, partial), (jax.ShapeDtypeStruct(brick, F32),),
        (*work, VM(*view), flat, VM(*frame), VM(pieces, c1 * rows, LANES), VM(c1 * r1, LANES), VM(*state), DMA),
        apart=(3,),
    )
    return out


def solution(mesh):
    placed = (P("gx", "gy", None), P("gx", "gy", None), P("gx", "gy", None), P())
    return jax.shard_map(local, mesh=mesh, in_specs=placed, out_specs=P("gx", "gy", None), check_vma=False)
```

```python
import functools
import math

import jax
import jax.numpy as jnp
from jax import lax
from jax.experimental import pallas as pl
from jax.experimental.pallas import tpu as pltpu
from jax.sharding import PartitionSpec as P

DEG = 4
COARSE_SWEEPS = 4
THETA = 1.15
DELTA = 0.85
SIGMA = 1.15 / 0.85
DAMPING = 0.6
KEPT = 1.0 - DAMPING
F32 = jnp.float32
LANES = 128
MIB = 1024 * 1024
HELD = 4 * MIB
SMOOTH_STEP = 4
LEVEL1_STEP = 7


def iota(shape, axis):
    return lax.broadcasted_iota(jnp.int32, shape, axis)


def invert(x):
    guess = pl.reciprocal(x, approx=True)
    return guess * (2.0 - x * guess)


def harmonic(a, b, scale):
    return (2.0 * scale) * a * b * invert(jnp.maximum(a + b, 1e-3))


def pair_matrix(size, offset=0):
    column = iota((size, LANES), 1)
    return ((column >= offset) & (iota((size, LANES), 0) // 2 == column - offset)).astype(jnp.bfloat16)


def spread_matrix(width):
    return (iota((LANES, width), 1) // 2 == iota((LANES, width), 0)).astype(jnp.bfloat16)


def select(values, matrix):
    high = values.astype(jnp.bfloat16)
    rest = (values - high.astype(F32)).astype(jnp.bfloat16)
    return jnp.dot(high, matrix, preferred_element_type=F32) + jnp.dot(rest, matrix, preferred_element_type=F32)


def lower(x, axis, stride=1):
    return pltpu.roll(x, stride, axis)


def upper(x, axis, stride=1):
    return pltpu.roll(x, x.shape[axis] - stride, axis)


def as_float(condition):
    return jnp.where(condition, 1.0, 0.0)


def faces_kernel(
    place, permeability, potential, phase, source,
    material, pot, src, inner, outer, even, odd,
    ids, values, semaphores,
):
    arriving = [
        pltpu.make_async_copy(a, b, semaphores.at[n])
        for n, (a, b) in enumerate(((permeability, values), (phase, ids), (potential, pot), (source, src)))
    ]
    for copy in arriving:
        copy.start()
    low_x, low_y = place[0] == 1, place[1] == 1
    count, rows = pot.shape[:2]
    arriving[0].wait()
    arriving[1].wait()
    p0, p1, p2 = values[0], values[1], values[2]
    for i in range(count):
        here = ids[i]
        material[i] = jnp.where(here == 0, p0, jnp.where(here == 1, p1, p2))
    last = count - 1
    first = jnp.where(low_x, 0, last)
    second = jnp.where(low_x, 1, last - 1)
    inner[1] = material[first]
    inner[2] = material[second]
    outer[1] = material[last - first]
    outer[2] = material[last - second]

    def edge(slot, ref, a, b):
        for i in range(count):
            low, high = ref[i, a : a + 1, :], ref[i, b : b + 1, :]
            even[slot, i : i + 1, :] = jnp.where(low_y, low, high)
            odd[slot, i : i + 1, :] = jnp.where(low_y, high, low)

    edge(1, material, 0, rows - 1)
    edge(2, material, 1, rows - 2)
    arriving[2].wait()
    inner[0] = pot[first]
    outer[0] = pot[last - first]
    edge(0, pot, 0, rows - 1)
    arriving[3].wait()


def residual_kernel(
    place, source, potential, material, inner, outer, even, odd,
    residual, coarse, strip_even, strip_odd,
    wide, narrow, y_faces, mat, pot,
):
    low_x, low_y = place[0] == 1, place[1] == 1
    count, rows, depth = source.shape
    c1, r1 = count // 2, rows // 2
    pieces = depth // LANES

    def ordered(flag, a, b):
        return jnp.where(flag, a, b), jnp.where(flag, b, a)

    x_low, x_high = ordered(low_x, inner[...], outer[...])
    y_low, y_high = ordered(low_y, even[...], odd[...])
    row, lane = iota((rows, depth), 0), iota((rows, depth), 1)
    first, last = row == 0, row == rows - 1
    for n, ref in enumerate((y_low[0], y_high[0], y_low[1], y_high[1])):
        for i in range(count):
            y_faces[n, i] = jnp.broadcast_to(ref[i : i + 1], (8, depth))
    mat[0], mat[count + 1] = x_low[1], x_high[1]
    pot[0], pot[count + 1] = x_low[0], x_high[0]
    mat[pl.ds(1, count)] = material[...]
    pot[pl.ds(1, count)] = potential[...]
    step = 4
    outside = as_float(lane == 0) + as_float(lane == depth - 1)

    def edge_count(faces):
        return as_float(faces[:1, :1] <= 0.0)

    outside = outside + jnp.where(first, edge_count(y_low[1]), 0.0) + jnp.where(last, edge_count(y_high[1]), 0.0)

    def beside(ref, n, at):
        return jnp.broadcast_to(ref[n, at : at + step, :1], (step, rows, depth))

    for at in range(0, count, step):
        here = slice(at + 1, at + 1 + step)
        a, v = mat[here], pot[here]
        faces = harmonic(mat[at : at + step + 1], mat[at + 1 : at + step + 2], 1.0)
        down = jnp.where(first[None], beside(y_faces, 2, at), lower(a, 1))
        w_down = harmonic(a, down, 1.0)
        w_top = harmonic(a[:, rows - 1 :], y_faces[3, at : at + step, :1], 1.0)
        w_up = jnp.where(last[None], jnp.broadcast_to(w_top, a.shape), upper(w_down, 1))
        w_back = jnp.where(lane[None] == 0, 0.0, harmonic(a, lower(a, 2), 1.0))
        w_front = upper(w_back, 2)
        v_down = jnp.where(first[None], beside(y_faces, 0, at), lower(v, 1))
        v_up = jnp.where(last[None], beside(y_faces, 1, at), upper(v, 1))
        edges = jnp.broadcast_to(outside[None], a.shape)
        if at == 0:
            edges = edges + jnp.where(iota((step, 1, 1), 0) == 0, edge_count(x_low[1])[None], 0.0)
        if at == count - step:
            edges = edges + jnp.where(iota((step, 1, 1), 0) == step - 1, edge_count(x_high[1])[None], 0.0)
        diagonal = faces[:-1] + faces[1:] + w_down + w_up + w_back + w_front + a * edges
        off = faces[:-1] * pot[at : at + step] + faces[1:] * pot[at + 2 : at + 2 + step] + w_down * v_down + w_up * v_up
        off = off + w_back * lower(v, 2) + w_front * upper(v, 2)
        left = source[at : at + step] - diagonal * v + off
        residual[at : at + step] = left
        for n, x in enumerate((left, a)):
            pair = x.reshape(step // 2, 2, rows, depth)
            to = n * c1 * rows + at // 2 * rows
            wide[to : to + step // 2 * rows] = (pair[:, 0] + pair[:, 1]).reshape(step // 2 * rows, depth)
        low = jnp.concatenate([left[:, :4], a[:, :4]], axis=1)
        high = jnp.concatenate([left[:, rows - 4 :], a[:, rows - 4 :]], axis=1)
        for ref, strip in ((strip_even, jnp.where(low_y, low, high)), (strip_odd, jnp.where(low_y, high, low))):
            for k in range(step):
                for piece in range(pieces):
                    ref[(at + k) * pieces + piece] = strip[k, :, piece * LANES : (piece + 1) * LANES]
    base = 2 * c1 * rows
    for n, both in enumerate((x_low[1] + x_low[2], x_high[1] + x_high[2], y_low[1] + y_low[2], y_high[1] + y_high[2])):
        wide[base + n * rows : base + (n + 1) * rows] = both
    narrow[...] = select(wide[...], pair_matrix(depth)) * 0.125
    half = narrow.shape[0] // 2
    coarse[...] = narrow[pl.ds(0, half, 2)] + narrow[pl.ds(1, half, 2)]
    for k in range(c1):
        s, m = coarse[k * r1 : (k + 1) * r1], coarse[(c1 + k) * r1 : (c1 + k + 1) * r1]
        low = jnp.concatenate([s[:4], m[:4]], axis=0)
        high = jnp.concatenate([s[r1 - 4 :], m[r1 - 4 :]], axis=0)
        strip_even[count * pieces + k] = jnp.where(low_y, low, high)
        strip_odd[count * pieces + k] = jnp.where(low_y, high, low)


def payload_kernel(c1, r1, coarse, payload, wide, narrow, sheet, semaphore):
    c2 = c1 // 2
    depth = coarse.shape[1]
    shape = (c1, r1, depth)
    s, m = coarse[: c1 * r1].reshape(shape), coarse[c1 * r1 : 2 * c1 * r1].reshape(shape)
    base = 2 * c1 * r1
    m_xlow, m_xhigh = coarse[base : base + r1], coarse[base + r1 : base + 2 * r1]
    base += 2 * r1
    m_ylow = jnp.stack([coarse[base + k : base + k + 1] for k in range(c1)])
    m_yhigh = jnp.stack([coarse[base + r1 + k : base + r1 + k + 1] for k in range(c1)])
    row, lane = iota(shape, 1), iota(shape, 2)
    first, last = row == 0, row == r1 - 1
    around = jnp.concatenate([m_xlow[None], m, m_xhigh[None]], axis=0)
    faces = harmonic(around[:-1], around[1:], 0.25)
    down = jnp.where(first, jnp.broadcast_to(m_ylow, shape), lower(m, 1))
    up = jnp.where(last, jnp.broadcast_to(m_yhigh, shape), upper(m, 1))
    w_down = harmonic(m, down, 0.25)
    w_up = jnp.where(last, harmonic(m, up, 0.25), upper(w_down, 1))
    w_back = jnp.where(lane == 0, 0.0, harmonic(m, lower(m, 2), 0.25))
    w_front = upper(w_back, 2)
    outside = as_float(lane == 0) + as_float(lane == depth - 1)
    for b in (down, up, around[:-2], around[2:]):
        outside = outside + as_float(b <= 0.0)
    diagonal = faces[:-1] + faces[1:] + w_down + w_up + w_back + w_front + 0.25 * m * outside
    e = DAMPING * s * invert(diagonal)
    y_low, y_high = w_down * e, w_up * e
    t = KEPT * s + w_back * lower(e, 2) + w_front * upper(e, 2)
    t = t + jnp.where(first, 0.0, w_down * lower(e, 1)) + jnp.where(last, 0.0, w_up * upper(e, 1))
    nothing = jnp.zeros((1, r1, depth), F32)
    t = t + faces[:-1] * jnp.concatenate([nothing, e[:-1]], axis=0) + faces[1:] * jnp.concatenate([e[1:], nothing], axis=0)
    base = c2 // 2 * r1

    def pairs(x):
        x = x.reshape(c2, 2, r1, depth)
        return (x[:, 0] + x[:, 1]).reshape(c2 * r1, depth)

    t, m = pairs(t), pairs(m)
    for n in range(2):
        wide[n, :base] = t[n * base : (n + 1) * base]
        wide[n, base + 2 * r1 :] = m[n * base : (n + 1) * base]
    wide[0, base : base + r1] = faces[0] * e[0]
    wide[0, base + r1 : base + 2 * r1] = faces[c1] * e[c1 - 1]
    for k in range(c1):
        wide[1, base + k : base + k + 1] = y_low[k, :1]
        wide[1, base + r1 + k : base + r1 + k + 1] = y_high[k, r1 - 1 :]
    publish(wide[0], wide[1], narrow, sheet, payload, semaphore)


def packed(low, high, narrow):
    narrow[...] = (select(low, pair_matrix(LANES)) + select(high, pair_matrix(LANES, LANES // 2))) * 0.125
    half = narrow.shape[0] // 2
    return narrow[pl.ds(0, half, 2)] + narrow[pl.ds(1, half, 2)]


def publish(low, high, narrow, sheet, payload, semaphore):
    sheet[...] = jnp.broadcast_to(packed(low, high, narrow)[None], sheet.shape)
    leaving = pltpu.make_async_copy(sheet, payload, semaphore)
    leaving.start()
    leaving.wait()


def strips_kernel(place, residual, material, coarse, even, odd, inner, outer, long):
    low_x, low_y = place[0] == 1, place[1] == 1
    count, rows, depth = residual.shape
    pieces = depth // LANES
    c1, r1 = count // 2, rows // 2
    base = count * pieces

    def sides(at):
        a, b = even[at], odd[at]
        return jnp.where(low_y, a, b), jnp.where(low_y, b, a)

    for i in range(count):
        for piece in range(pieces):
            low, high = sides(i * pieces + piece)
            z = slice(piece * LANES, (piece + 1) * LANES)
            long[0, i, :, z] = jnp.concatenate([low[:4], residual[i, :, z], high[:4]], axis=0)
            long[1, i, :, z] = jnp.concatenate([low[4:], material[i, :, z], high[4:]], axis=0)
    for k in range(c1):
        low, high = sides(base + k)
        s, m = coarse[k * r1 : (k + 1) * r1], coarse[(c1 + k) * r1 : (c1 + k + 1) * r1]
        i, z = count + k // 2, slice(k % 2 * LANES, (k % 2 + 1) * LANES)
        long[0, i, : r1 + 8, z] = jnp.concatenate([low[:4], s, high[:4]], axis=0)
        long[1, i, : r1 + 8, z] = jnp.concatenate([low[4:], m, high[4:]], axis=0)

    def pack(out, flag):
        at = 0
        for n, planes in ((0, 3), (1, 4)):
            start = jnp.where(flag, 0, count - planes)
            for k in range(planes):
                for tile in range((rows + 8) // 8):
                    for piece in range(pieces):
                        out[at] = long[n, start + k, tile * 8 : tile * 8 + 8, piece * LANES : (piece + 1) * LANES]
                        at += 1
        for n, planes in ((0, 3), (1, 4)):
            for k in range(planes):
                low, high = k, c1 - planes + k
                for tile in range((r1 + 8) // 8):
                    y = slice(tile * 8, tile * 8 + 8)
                    a = long[n, count + low // 2, y, low % 2 * LANES : (low % 2 + 1) * LANES]
                    b = long[n, count + high // 2, y, high % 2 * LANES : (high % 2 + 1) * LANES]
                    out[at] = jnp.where(flag, a, b)
                    at += 1

    pack(inner, low_x)
    pack(outer, jnp.logical_not(low_x))


def unpack(source, flag, out, start, planes, tiles, pieces, at):
    for n in range(planes):
        for tile in range(tiles):
            for piece in range(pieces):
                value = jnp.where(flag, source[0][at], source[1][at])
                out[start + n, tile * 8 : tile * 8 + 8, piece * LANES : (piece + 1) * LANES] = value
                at += 1
    return at


def smooth_kernel(ends, place, potential_far, long, inner, outer, out, mat, res, x, d, fx, fy, fz, inv, potential, semaphore):
    arriving = pltpu.make_async_copy(potential_far, potential, semaphore)
    arriving.start()
    low_x = place[0] == 1
    count, rows, depth = potential.shape
    pieces, tiles = depth // LANES, (rows + 8) // 8
    both = (inner, outer)
    for flag, start_r, start_m in ((low_x, 1, 0), (jnp.logical_not(low_x), count + 4, count + 4)):
        at = unpack(both, flag, res, start_r, 3, tiles, pieces, 0)
        unpack(both, flag, mat, start_m, 4, tiles, pieces, at)
    res[pl.ds(4, count)] = long[0, :count]
    mat[pl.ds(4, count)] = long[1, :count]
    total, length = count + 8, rows + 8
    row, lane = iota((length, depth), 0), iota((length, depth), 1)
    outside = as_float(lane == 0) + as_float(lane == depth - 1)
    outside = outside + as_float((row == 4) & (place[3] == 0)) + as_float((row == rows + 3) & (place[3] == ends[1] - 1))
    low_end, high_end = place[2] == 0, place[2] == ends[0] - 1

    def chunks(first, last, step):
        return [(at, min(step, last - at)) for at in range(first, last, step)]

    for at, n in chunks(1, total - 1, SMOOTH_STEP):
        here = slice(at, at + n)
        a = mat[here]
        faces = harmonic(mat[at - 1 : at + n], mat[at : at + n + 1], 1.0)
        w_down = harmonic(a, lower(a, 1), 1.0)
        w_back = jnp.where(lane[None] == 0, 0.0, harmonic(a, lower(a, 2), 1.0))
        plane = at + iota((n, 1, 1), 0)
        edges = outside[None] + as_float((plane == 4) & low_end) + as_float((plane == count + 3) & high_end)
        diagonal = faces[:-1] + faces[1:] + w_down + upper(w_down, 1) + w_back + upper(w_back, 2) + a * edges
        inverse = jnp.where(a > 0.0, invert(jnp.maximum(diagonal, 1e-3)), 0.0)
        fx[at : at + n + 1], fy[here], fz[here], inv[here] = faces, w_down, w_back, inverse
        scaled = inverse * res[here]
        res[here] = scaled
        x[0, here] = scaled * (1.0 / THETA)
    rho = 1.0 / SIGMA
    for turn in range(DEG - 1):
        if turn == DEG - 2:
            arriving.wait()
        following = 1.0 / (2.0 * SIGMA - rho)
        old, new = turn % 2, (turn + 1) % 2
        keep, gain = following * rho, 2.0 * following / DELTA
        for at, n in chunks(2 + turn, total - 2 - turn, SMOOTH_STEP):
            here = slice(at, at + n)
            v = x[old, here]
            w_down, w_back = fy[here], fz[here]
            off = fx[here] * x[old, at - 1 : at + n - 1] + fx[at + 1 : at + n + 1] * x[old, at + 1 : at + n + 1]
            off = off + w_down * lower(v, 1) + upper(w_down * v, 1)
            off = off + w_back * lower(v, 2) + upper(w_back * v, 2)
            before = v * keep if turn == 0 else d[here] * keep
            change = before + gain * (res[here] - v + inv[here] * off)
            if turn == DEG - 2:
                out[at - 4 : at + n - 4] = potential[at - 4 : at + n - 4] + (v + change)[:, 4 : 4 + rows]
            else:
                d[here] = change
                x[new, here] = v + change
        rho = following


def each(count, body, most=8):
    step = min(count, most)
    if count // step <= 4:
        for n in range(count // step):
            body(n * step, step)
        return

    def run(n, _):
        body(n * step, step)
        return 0

    lax.fori_loop(0, count // step, run, 0)


def fill_table(mat, table, level, count, base, width):
    stride, scale = 2**level, 0.25 ** (level + 2)
    rows = mat.shape[1]
    row, lane = iota((rows, LANES), 0), iota((rows, LANES), 1)
    above, beyond = row >= stride, lane >= stride
    outside = as_float(row == 0) + as_float(row == rows - stride) + as_float(lane == 0) + as_float(lane == width - stride)

    def body(at, step):
        a, before, ahead = mat[pl.ds(at + 1, step)], mat[pl.ds(at, step)], mat[pl.ds(at + 2, step)]
        w_before, w_ahead = harmonic(a, before, scale), harmonic(a, ahead, scale)
        w_down = jnp.where(above[None], harmonic(a, lower(a, 1, stride), scale), 0.0)
        w_back = jnp.where(beyond[None], harmonic(a, lower(a, 2, stride), scale), 0.0)
        plane = at + iota((step, 1, 1), 0)
        edges = outside[None] + as_float(plane == 0) + as_float(plane == count - 1)
        diagonal = w_before + w_ahead + w_down + upper(w_down, 1, stride) + w_back + upper(w_back, 2, stride)
        diagonal = diagonal + scale * a * edges
        table[0, pl.ds(base + at, step)] = w_before
        table[1, pl.ds(base + at, step)] = w_down
        table[2, pl.ds(base + at, step)] = w_back
        table[3, pl.ds(base + at, step)] = jnp.where(a > 0.0, invert(jnp.maximum(diagonal, 1e-4)), 0.0)

    each(count, body)
    table[0, base + count] = jnp.zeros((rows, LANES), F32)


def fold(t, stride):
    a = t.reshape(t.shape[0] // 2, 2, *t.shape[1:])
    a = a[:, 0] + a[:, 1]
    a = a + upper(a, 1, stride)
    return a + upper(a, 2, stride)


def unfold(e, stride):
    e = e + lower(e, 1, stride)
    e = e + lower(e, 2, stride)
    return jnp.broadcast_to(e[:, None], (e.shape[0], 2, *e.shape[1:])).reshape(2 * e.shape[0], *e.shape[1:])


def off_diagonal(e, table, base, at, step, stride):
    v = e[pl.ds(at + 1, step)]
    total = table[0, pl.ds(base + at, step)] * e[pl.ds(at, step)]
    total = total + table[0, pl.ds(base + at + 1, step)] * e[pl.ds(at + 2, step)]
    fy, fz = table[1, pl.ds(base + at, step)], table[2, pl.ds(base + at, step)]
    total = total + fy * lower(v, 1, stride) + upper(fy * v, 1, stride)
    return v, total + fz * lower(v, 2, stride) + upper(fz * v, 2, stride)


def cycle(s, e, t, table, counts, bases, place, out, c2, r2, pad):
    zero = jnp.zeros(t.shape[1:], F32)
    for ref, count in zip(e, counts):
        ref[0] = zero
        ref[count + 1] = zero
    for level, (count, base) in enumerate(zip(counts, bases)):
        s_l, e_l, stride = s[level], e[level], 2**level

        def start(at, step):
            e_l[pl.ds(at + 1, step)] = DAMPING * s_l[pl.ds(at + 1, step)] * table[3, pl.ds(base + at, step)]

        each(count, start)
        if level == len(counts) - 1:
            break

        def remainder(at, step):
            _, off = off_diagonal(e_l, table, base, at, step, stride)
            left = KEPT * s_l[pl.ds(at + 1, step)] + off
            s[level + 1][pl.ds(at // 2 + 1, step // 2)] = 0.125 * fold(left, stride)

        each(count, remainder)

    def relax(s_l, source, target, base, count, stride):
        def sweep(at, step):
            v, off = off_diagonal(source, table, base, at, step, stride)
            inverse = table[3, pl.ds(base + at, step)]
            target[pl.ds(at + 1, step)] = KEPT * v + DAMPING * inverse * (s_l[pl.ds(at + 1, step)] + off)

        each(count, sweep)

    t[0] = zero
    t[counts[2] + 1] = zero
    now, other = e[2], t
    for _ in range(COARSE_SWEEPS - 1):
        relax(s[2], now, other, bases[2], counts[2], 4)
        now, other = other, now

    def add(at, step):
        e[1][pl.ds(2 * at + 1, 2 * step)] = e[1][pl.ds(2 * at + 1, 2 * step)] + unfold(now[pl.ds(at + 1, step)], 2)

    each(counts[2], add, 4)
    if now is t:
        now = e[2] = s[1]
    relax(s[1], e[1], t, bases[1], counts[1], 2)

    planes = c2 + 4
    begin = place[2] * c2 - 2
    inside = jnp.clip(begin, 0, counts[0] - planes)
    coarse = jnp.clip(place[2] * c2 // 2 - 2, 0, counts[1] - planes // 2 - 2)
    number = planes // 2 + 2
    at = pl.ds(2 * coarse + 1, 2 * number)
    e[0][at] = e[0][at] + unfold(t[pl.ds(coarse + 1, number)], 1)
    v, off = off_diagonal(e[0], table, bases[0], inside, planes, 1)
    inverse = table[3, pl.ds(bases[0] + inside, planes)]
    pad[...] = jnp.zeros(pad.shape, F32)
    rows = t.shape[1]
    value = KEPT * v + DAMPING * inverse * (s[0][pl.ds(inside + 1, planes)] + off)
    pad[pl.ds(2 + inside - begin, planes), 8 : 8 + rows, :] = value
    for n in range(planes):
        out[n] = pad[n + 2, pl.ds(place[3] * r2 + 6, r2 + 4), :]


def cycle_shapes(counts, rows, c2):
    out = [pltpu.VMEM((count + 2, rows, LANES), F32) for count in (*counts, *counts, counts[0])]
    return out + [pltpu.VMEM((c2 + 8, rows + 16, LANES), F32)]


def repeat(count, body):
    if count <= 8:
        for i in range(count):
            body(i)
    else:
        lax.fori_loop(0, count, lambda i, _: body(i), None)


def spread_blocks(blocks, outs, grid, c2, r2):
    gx, gy = grid
    length = c2 // 2 * r2
    low = iota((length, LANES), 1) < LANES // 2

    def column(i):
        for j in range(gy):
            for start, out in outs:
                block = blocks[i * gy + j, start : start + length]
                parts = (jnp.where(low, block, 0.0), jnp.where(low, pltpu.roll(block, LANES // 2, 1), 0.0))
                for k in range(c2):
                    n = k % (c2 // 2)
                    out[i * c2 + k + 1, j * r2 : (j + 1) * r2, :] = parts[k // (c2 // 2)][n * r2 : (n + 1) * r2]

    repeat(gx, column)


def clear_ends(refs, counts):
    for ref, count in zip(refs, counts):
        zero = jnp.zeros(ref.shape[1:], F32)
        ref[0] = zero
        ref[count + 1] = zero


def first_cycle_kernel(counts, bases, grid, c2, r2, width, place, blocks, out, table, *scratch):
    s, e, t, pad = scratch[0:3], list(scratch[3:6]), scratch[6], scratch[7]
    gx, gy = grid
    rows = gy * r2
    half = LANES // 2
    own = c2 // 2 * r2
    clear_ends((t, *s), (counts[0], *counts))
    spread_blocks(blocks, ((0, s[0]), (own + 2 * r2, t)), grid, c2, r2)
    face_y = e[0]
    low = iota((2 * c2, LANES), 1) < half

    def edges(i):
        for j in range(gy):
            faces = blocks[i * gy + j, own : own + 2 * r2]
            x_faces = jnp.where(low, faces, 0.0)
            y_faces = jnp.where(low, pltpu.roll(faces, half, 1), 0.0)
            here = slice(j * r2, (j + 1) * r2)
            s[0][i * c2, here, :] = s[0][i * c2, here, :] + x_faces[:r2]
            s[0][(i + 1) * c2 + 1, here, :] = s[0][(i + 1) * c2 + 1, here, :] + x_faces[r2:]
            for k in range(c2):
                at = i * c2 + k + 1
                if j > 0:
                    face_y[at, j * r2 - 1 : j * r2, :] = y_faces[k : k + 1]
                if j < gy - 1:
                    face_y[at, (j + 1) * r2 : (j + 1) * r2 + 1, :] = y_faces[c2 + k : c2 + k + 1]

    repeat(gx, edges)

    def join(at, step):
        now = pl.ds(at + 1, step)
        row = iota((rows, LANES), 0)
        edge = ((row % r2 == 0) & (row > 0)) | ((row % r2 == r2 - 1) & (row < rows - 1))
        s[0][now] = s[0][now] + jnp.where(edge[None], face_y[now], 0.0)

    each(counts[0], join)
    clear_ends(s[:1], counts)
    mats = (t, s[1], s[2])
    for level, (count, base) in enumerate(zip(counts, bases)):
        if level:

            def coarsen(at, step):
                whole = (iota((rows, LANES), 0) % 2**level == 0) & (iota((rows, LANES), 1) % 2**level == 0)
                mean = 0.125 * fold(mats[level - 1][pl.ds(at + 1, step)], 2 ** (level - 1))
                mats[level][pl.ds(at // 2 + 1, step // 2)] = jnp.where(whole[None], mean, 0.0)

            each(counts[level - 1], coarsen)
        fill_table(mats[level], table, level, count, base, width)
    cycle(s, e, t, table, counts, bases, place, out, c2, r2, pad)


def shifted(a):
    zero = jnp.zeros_like(a[:1])
    return jnp.concatenate([zero, a[:-1]], axis=0), jnp.concatenate([a[1:], zero], axis=0)


def apply_off(e, fx, fy, fz):
    before, ahead = shifted(e)
    out = fx[:-1] * before + fx[1:] * ahead
    out = out + fy * lower(e, 1) + upper(fy * e, 1)
    return out + fz * lower(e, 2) + upper(fz * e, 2)


def raise_window(window_ref, flat, out):
    planes, rows, _ = window_ref.shape
    values = select(window_ref[...].reshape(planes * rows, LANES), spread_matrix(LANES))
    flat[pl.ds(0, planes * rows, 2)] = values
    flat[pl.ds(1, planes * rows, 2)] = values
    v = flat[...].reshape(planes, 1, 2 * rows, LANES)
    out[...] = jnp.broadcast_to(v, (planes, 2, 2 * rows, LANES)).reshape(2 * planes, 2 * rows, LANES)


def level1_kernel(
    offset, place, long, inner, outer, window1, payload, state_far,
    src, mat, flat, prolonged, fx, fy, fz, diag, inv, err, c, state, wide, narrow, sheet, semaphores,
):
    low_x = place[0] == 1
    total, length, depth = src.shape
    count, rows = total - 8, length - 8
    both = (inner, outer)
    zero = jnp.zeros((length, depth), F32)
    src[0] = zero
    src[total - 1] = zero
    for flag, start_s, start_m in ((low_x, 1, 0), (jnp.logical_not(low_x), count + 4, count + 4)):
        at = unpack(both, flag, src, start_s, 3, length // 8, 1, offset)
        unpack(both, flag, mat, start_m, 4, length // 8, 1, at)
    for n, ref in enumerate((src, mat)):
        for k in range(count):
            ref[4 + k] = long[n, 2 * count + k // 2, :length, k % 2 * LANES : (k % 2 + 1) * LANES]
    raise_window(window1, flat, prolonged)
    row, lane = iota((length, depth), 0), iota((length, depth), 1)
    ends = as_float(lane == 0) + as_float(lane == depth - 1)
    def chunks(margin):
        first, last = margin, total - margin
        return [(at, min(LEVEL1_STEP, last - at)) for at in range(first, last, LEVEL1_STEP)]

    for at, n in chunks(1):
        here = slice(at, at + n)
        a, before, ahead = mat[here], mat[at - 1 : at + n - 1], mat[at + 1 : at + n + 1]
        down, up = lower(a, 1), upper(a, 1)
        f = harmonic(mat[at - 1 : at + n], mat[at : at + n + 1], 0.25)
        w_y = harmonic(a, down, 0.25)
        w_z = jnp.where(lane[None] == 0, 0.0, harmonic(a, lower(a, 2), 0.25))
        outside = ends[None] + as_float(before <= 0.0) + as_float(ahead <= 0.0) + as_float(down <= 0.0) + as_float(up <= 0.0)
        diagonal = f[:-1] + f[1:] + w_y + upper(w_y, 1) + w_z + upper(w_z, 2) + 0.25 * a * outside
        inverse = jnp.where(a > 0.0, invert(jnp.maximum(diagonal, 1e-4)), 0.0)
        fx[at : at + n + 1], fy[here], fz[here], diag[here], inv[here] = f, w_y, w_z, diagonal, inverse
        err[here] = DAMPING * inverse * src[here] + prolonged[here]

    def off(v, at, n):
        here = slice(at, at + n)
        mid, w_y, w_z = v[here], fy[here], fz[here]
        out = fx[here] * v[at - 1 : at + n - 1] + fx[at + 1 : at + n + 1] * v[at + 1 : at + n + 1]
        out = out + w_y * lower(mid, 1) + upper(w_y * mid, 1)
        return here, mid, out + w_z * lower(mid, 2) + upper(w_z * mid, 2)

    for at, n in chunks(2):
        here, mid, more = off(err, at, n)
        c[here] = KEPT * mid + DAMPING * inv[here] * (src[here] + more)
    for at, n in chunks(3):
        here, mid, more = off(c, at, n)
        left = src[here] - diag[here] * mid + more
        src[here] = left
        value = DAMPING * inv[here] * left
        err[here] = value
        state[at - 3 : at + n - 3] = value
    base = count + 2
    state[base : base + count + 1] = fx[4 : count + 5]
    base += count + 1
    for n, ref in enumerate((fy, fz, inv, c, src)):
        state[base + n * count : base + (n + 1) * count] = ref[4 : 4 + count]
    leaving = pltpu.make_async_copy(state, state_far, semaphores.at[0])
    leaving.start()
    here, _, more = off(err, 4, count)
    t = (KEPT * src[here] + more)[:, 4 : 4 + rows].reshape(count // 2, 2, rows, depth)
    wide[...] = (t[:, 0] + t[:, 1]).reshape(count // 2 * rows, depth)
    half = wide.shape[0] // 2
    publish(wide[:half], wide[half:], narrow, sheet, payload, semaphores.at[1])
    leaving.wait()


def last_cycle_kernel(counts, bases, grid, c2, r2, place, blocks, table, state_far, partial, out, *scratch):
    s, e, t, pad = scratch[0:3], list(scratch[3:6]), scratch[6], scratch[7]
    view, flat, prolonged, tall, coarse, state, semaphore, result, departures = scratch[8:17]
    arriving = pltpu.make_async_copy(state_far, state, semaphore)
    arriving.start()
    spread_blocks(blocks, ((0, s[0]),), grid, c2, r2)
    clear_ends(s, counts)
    cycle(s, e, t, table, counts, bases, place, view, c2, r2, pad)
    raise_window(view, flat, prolonged)
    count, rows, depth = partial.shape
    c1, r1 = count // 2, rows // 2
    arriving.wait()
    v = prolonged[3 : c1 + 5] + state[: c1 + 2]
    here = v[1:-1]
    base = 2 * c1 + 3
    w_x = state[c1 + 2 : base]
    w_y, w_z, inverse, before, left = (state[base + n * c1 : base + (n + 1) * c1] for n in range(5))
    off = w_x[:-1] * v[:-2] + w_x[1:] * v[2:]
    off = off + w_y * lower(here, 1) + upper(w_y * here, 1) + w_z * lower(here, 2) + upper(w_z * here, 2)
    total = before + KEPT * here + DAMPING * inverse * (left + off)
    coarse[...] = total[:, 4 : 4 + r1].reshape(c1 * r1, LANES)
    values = select(coarse[...], spread_matrix(depth))
    for piece in range(depth // LANES):
        z = slice(piece * LANES, (piece + 1) * LANES)
        tall[piece, pl.ds(0, c1 * r1, 2)] = values[:, z]
        tall[piece, pl.ds(1, c1 * r1, 2)] = values[:, z]
    leaving = []
    for k in range(c1):
        for piece in range(depth // LANES):
            z = slice(piece * LANES, (piece + 1) * LANES)
            more = tall[piece, k * rows : (k + 1) * rows]
            result[2 * k, :, z] = partial[2 * k, :, z] + more
            result[2 * k + 1, :, z] = partial[2 * k + 1, :, z] + more
        if k % 2 == 1:
            planes = pl.ds(2 * k - 2, 4)
            leaving.append(pltpu.make_async_copy(result.at[planes], out.at[planes], departures.at[k // 2]))
            leaving[-1].start()
    for copy in leaving:
        copy.wait()


def size_of(shape):
    lead = math.prod(shape[:-2])
    return 4 * lead * (-(-shape[-2] // 8) * 8) * (-(-shape[-1] // LANES) * LANES)


def call(kernel, name, inputs, outputs, scratch=(), apart=(), cost=None):
    streamed = 0

    def held(n, x):
        nonlocal streamed
        if n in apart:
            return pltpu.with_memory_space_constraint(x, pltpu.HBM)
        if x.ndim == 1:
            return x
        if size_of(x.shape) <= HELD:
            return pltpu.with_memory_space_constraint(x, pltpu.VMEM)
        streamed += size_of(x.shape)
        return x

    def result(shape):
        nonlocal streamed
        if isinstance(shape, jax.ShapeDtypeStruct):
            streamed += size_of(shape.shape)
            return shape
        if far(shape):
            return pltpu.HBM(shape[1], F32)
        if size_of(shape) <= HELD:
            return pltpu.VMEM(shape, F32)
        streamed += size_of(shape)
        return jax.ShapeDtypeStruct(shape, F32)

    def far(x):
        return isinstance(x, tuple) and x[0] == "far"

    def space(n, x):
        return pltpu.HBM if n in apart else pltpu.SMEM if x.ndim == 1 else pltpu.VMEM

    specs = [pl.BlockSpec(memory_space=space(n, x)) for n, x in enumerate(inputs)]
    inputs = [held(n, x) for n, x in enumerate(inputs)]
    results = [result(shape) for shape in outputs]
    need = streamed + sum(size_of(x.shape) for x in scratch if len(getattr(x, "shape", ())) > 1) + 3 * MIB
    return pl.pallas_call(
        kernel,
        out_shape=results,
        in_specs=specs,
        out_specs=[pl.BlockSpec(memory_space=pltpu.HBM if far(x) else pltpu.VMEM) for x in outputs],
        scratch_shapes=list(scratch),
        compiler_params=pltpu.CompilerParams(vmem_limit_bytes=max(need, 8 * MIB)),
        name=name,
        cost_estimate=None if cost is None else pl.CostEstimate(flops=cost, bytes_accessed=0, transcendentals=0),
    )(*inputs)


def swaps(count):
    inner = [(i, i + 1) for i in range(0, count - 1, 2)]
    outer = [(i, i + 1) for i in range(1, count - 1, 2)]
    return [pairs + [(b, a) for a, b in pairs] for pairs in (inner, outer)]


def local(right_side, potential, phase, permeability):
    gx, gy = lax.axis_size("gx"), lax.axis_size("gy")
    devices = gx * gy
    here_x, here_y = lax.axis_index("gx"), lax.axis_index("gy")
    place = jnp.stack([here_x % 2, here_y % 2, here_x, here_y]).astype(jnp.int32)
    count, rows, depth = right_side.shape
    c1, r1, d1 = count // 2, rows // 2, depth // 2
    c2, r2 = c1 // 2, r1 // 2
    pieces = depth // LANES
    swap_x, swap_y = swaps(gx), swaps(gy)
    VM = lambda *shape: pltpu.VMEM(shape, F32)

    brick = (count, rows, depth)
    face = (3, rows, depth)
    DMA = pltpu.SemaphoreType.DMA
    sheet = (devices, c2 // 2 * r2, LANES)
    sheet2 = (devices, c2 * r2 + 2 * r2, LANES)
    material, potential_here, source_here, inner, outer, even, odd = call(
        faces_kernel, "faces", (place, permeability, potential, phase, right_side),
        (brick, brick, brick, face, face, (3, count, depth), (3, count, depth)),
        (pltpu.VMEM(brick, jnp.int32), pltpu.SMEM(permeability.shape, F32), pltpu.SemaphoreType.DMA((4,))),
        apart=(1, 2, 3, 4),
    )
    even = lax.ppermute(even, "gy", swap_y[0])
    odd = lax.ppermute(odd, "gy", swap_y[1])
    outer = lax.ppermute(outer, "gx", swap_x[1])
    inner = lax.ppermute(inner, "gx", swap_x[0])

    strip = (count * pieces + c1, 8, LANES)
    total = 2 * c1 * rows + 4 * rows
    residual, coarse, even, odd = call(
        residual_kernel, "residual", (place, source_here, potential_here, material, inner, outer, even, odd),
        (brick, (total // 2, LANES), strip, strip),
        (
            VM(total, depth), VM(total, LANES), VM(4, count, 8, depth), VM(count + 2, rows, depth), VM(count + 2, rows, depth),
        ),
    )
    even = lax.ppermute(even, "gy", swap_y[0])
    odd = lax.ppermute(odd, "gy", swap_y[1])
    small = c2 * r1 + 2 * r1
    (payload,) = call(
        functools.partial(payload_kernel, c1, r1), "payload", (coarse,), (("far", sheet2),),
        (VM(2, small, d1), VM(small, LANES), VM(*sheet2), DMA),
    )
    blocks = lax.all_to_all(payload, ("gx", "gy"), 0, 0)
    tiles, tiles1 = (rows + 8) // 8, (r1 + 8) // 8
    strip = (7 * tiles * pieces + 7 * tiles1, 8, LANES)
    inner, outer, long = call(
        strips_kernel, "strips", (place, residual, material, coarse, even, odd),
        (strip, strip, (2, count + c1 // 2, rows + 8, depth)), cost=10**11,
    )
    outer = lax.ppermute(outer, "gx", swap_x[1])
    inner = lax.ppermute(inner, "gx", swap_x[0])

    counts = tuple(gx * c2 // k for k in (1, 2, 4))
    bases = (0, counts[0] + 1, counts[0] + counts[1] + 2)
    work = cycle_shapes(counts, gy * r2, c2)
    view = (c2 + 4, r2 + 4, LANES)
    window1, table = call(
        functools.partial(first_cycle_kernel, counts, bases, (gx, gy), c2, r2, d1 // 2), "cycle1", (place, blocks),
        (view, (4, sum(counts) + 3, gy * r2, LANES)), work,
    )
    frame = (c1 + 8, r1 + 8, d1)
    flat = VM((c2 + 4) * (r2 + 4) * 2, LANES)
    state = (7 * c1 + 3, r1 + 8, d1)
    tall = VM(c1 + 9, r1 + 8, d1)
    payload, held = call(
        functools.partial(level1_kernel, 7 * tiles * pieces), "level1", (place, long, inner, outer, window1), (("far", sheet), ("far", state)),
        (
            VM(*frame), VM(*frame), flat, VM(*frame), tall, VM(*frame), VM(*frame), VM(*frame), VM(*frame), VM(*frame),
            VM(*frame), VM(*state), VM(c1 // 2 * r1, d1), VM(c1 // 4 * r1, LANES), VM(*sheet), pltpu.SemaphoreType.DMA((2,)),
        ),
    )
    blocks = lax.all_to_all(payload, ("gx", "gy"), 0, 0)
    wide = (count + 8, rows + 8, depth)
    (partial,) = call(
        functools.partial(smooth_kernel, (gx, gy)), "smooth", (place, potential, long, inner, outer), (brick,),
        (
            VM(*wide), VM(*wide), VM(2, *wide), VM(*wide), VM(count + 9, rows + 8, depth), VM(*wide), VM(*wide), VM(*wide),
            VM(*brick), pltpu.SemaphoreType.DMA,
        ),
        apart=(1,),
    )
    (out,) = call(
        functools.partial(last_cycle_kernel, counts, bases, (gx, gy), c2, r2), "cycle2",
        (place, blocks, table, held, partial), (("far", brick),),
        (
            *work, VM(*view), flat, VM(*frame), VM(pieces, c1 * rows, LANES), VM(c1 * r1, LANES), VM(*state), DMA,
            VM(*brick), pltpu.SemaphoreType.DMA((c1 // 2,)),
        ),
        apart=(3,),
    )
    return out


def solution(mesh):
    placed = (P("gx", "gy", None), P("gx", "gy", None), P("gx", "gy", None), P())
    return jax.shard_map(local, mesh=mesh, in_specs=placed, out_specs=P("gx", "gy", None), check_vma=False)
```

```python
import functools
import math

import jax
import jax.numpy as jnp
from jax import lax
from jax.experimental import pallas as pl
from jax.experimental.pallas import tpu as pltpu
from jax.sharding import PartitionSpec as P

DEG = 4
COARSE_SWEEPS = 4
THETA = 1.15
DELTA = 0.85
SIGMA = 1.15 / 0.85
DAMPING = 0.6
KEPT = 1.0 - DAMPING
F32 = jnp.float32
LANES = 128
MIB = 1024 * 1024
HELD = 4 * MIB
SMOOTH_STEP = 4
LEVEL1_STEP = 7


def iota(shape, axis):
    return lax.broadcasted_iota(jnp.int32, shape, axis)


def invert(x):
    guess = pl.reciprocal(x, approx=True)
    return guess * (2.0 - x * guess)


def harmonic(a, b, scale):
    return (2.0 * scale) * a * b * invert(jnp.maximum(a + b, 1e-3))


def pair_matrix(size, offset=0):
    column = iota((size, LANES), 1)
    return ((column >= offset) & (iota((size, LANES), 0) // 2 == column - offset)).astype(jnp.bfloat16)


def spread_matrix(width):
    return (iota((LANES, width), 1) // 2 == iota((LANES, width), 0)).astype(jnp.bfloat16)


def select(values, matrix):
    high = values.astype(jnp.bfloat16)
    rest = (values - high.astype(F32)).astype(jnp.bfloat16)
    return jnp.dot(high, matrix, preferred_element_type=F32) + jnp.dot(rest, matrix, preferred_element_type=F32)


def lower(x, axis, stride=1):
    return pltpu.roll(x, stride, axis)


def upper(x, axis, stride=1):
    return pltpu.roll(x, x.shape[axis] - stride, axis)


def as_float(condition):
    return jnp.where(condition, 1.0, 0.0)


def faces_kernel(
    place, permeability, potential, phase, source,
    material, pot, src, inner, outer, even, odd,
    ids, values, semaphores,
):
    arriving = [
        pltpu.make_async_copy(a, b, semaphores.at[n])
        for n, (a, b) in enumerate(((permeability, values), (phase, ids), (potential, pot), (source, src)))
    ]
    for copy in arriving:
        copy.start()
    low_x, low_y = place[0] == 1, place[1] == 1
    count, rows = pot.shape[:2]
    arriving[0].wait()
    arriving[1].wait()
    p0, p1, p2 = values[0], values[1], values[2]
    for i in range(count):
        here = ids[i]
        material[i] = jnp.where(here == 0, p0, jnp.where(here == 1, p1, p2))
    last = count - 1
    first = jnp.where(low_x, 0, last)
    second = jnp.where(low_x, 1, last - 1)
    inner[1] = material[first]
    inner[2] = material[second]
    outer[1] = material[last - first]
    outer[2] = material[last - second]

    def edge(slot, ref, a, b):
        for i in range(count):
            low, high = ref[i, a : a + 1, :], ref[i, b : b + 1, :]
            even[slot, i : i + 1, :] = jnp.where(low_y, low, high)
            odd[slot, i : i + 1, :] = jnp.where(low_y, high, low)

    edge(1, material, 0, rows - 1)
    edge(2, material, 1, rows - 2)
    arriving[2].wait()
    inner[0] = pot[first]
    outer[0] = pot[last - first]
    edge(0, pot, 0, rows - 1)
    arriving[3].wait()


def residual_kernel(
    place, source, potential, material, inner, outer, even, odd,
    residual, coarse, strip_even, strip_odd,
    wide, narrow, y_faces, mat, pot,
):
    low_x, low_y = place[0] == 1, place[1] == 1
    count, rows, depth = source.shape
    c1, r1 = count // 2, rows // 2
    pieces = depth // LANES

    def ordered(flag, a, b):
        return jnp.where(flag, a, b), jnp.where(flag, b, a)

    x_low, x_high = ordered(low_x, inner[...], outer[...])
    y_low, y_high = ordered(low_y, even[...], odd[...])
    row, lane = iota((rows, depth), 0), iota((rows, depth), 1)
    first, last = row == 0, row == rows - 1
    for n, ref in enumerate((y_low[0], y_high[0], y_low[1], y_high[1])):
        for i in range(count):
            y_faces[n, i] = jnp.broadcast_to(ref[i : i + 1], (8, depth))
    mat[0], mat[count + 1] = x_low[1], x_high[1]
    pot[0], pot[count + 1] = x_low[0], x_high[0]
    mat[pl.ds(1, count)] = material[...]
    pot[pl.ds(1, count)] = potential[...]
    step = 4
    outside = as_float(lane == 0) + as_float(lane == depth - 1)

    def edge_count(faces):
        return as_float(faces[:1, :1] <= 0.0)

    outside = outside + jnp.where(first, edge_count(y_low[1]), 0.0) + jnp.where(last, edge_count(y_high[1]), 0.0)

    def beside(ref, n, at):
        return jnp.broadcast_to(ref[n, at : at + step, :1], (step, rows, depth))

    for at in range(0, count, step):
        here = slice(at + 1, at + 1 + step)
        a, v = mat[here], pot[here]
        faces = harmonic(mat[at : at + step + 1], mat[at + 1 : at + step + 2], 1.0)
        down = jnp.where(first[None], beside(y_faces, 2, at), lower(a, 1))
        w_down = harmonic(a, down, 1.0)
        w_top = harmonic(a[:, rows - 1 :], y_faces[3, at : at + step, :1], 1.0)
        w_up = jnp.where(last[None], jnp.broadcast_to(w_top, a.shape), upper(w_down, 1))
        w_back = jnp.where(lane[None] == 0, 0.0, harmonic(a, lower(a, 2), 1.0))
        w_front = upper(w_back, 2)
        v_down = jnp.where(first[None], beside(y_faces, 0, at), lower(v, 1))
        v_up = jnp.where(last[None], beside(y_faces, 1, at), upper(v, 1))
        edges = jnp.broadcast_to(outside[None], a.shape)
        if at == 0:
            edges = edges + jnp.where(iota((step, 1, 1), 0) == 0, edge_count(x_low[1])[None], 0.0)
        if at == count - step:
            edges = edges + jnp.where(iota((step, 1, 1), 0) == step - 1, edge_count(x_high[1])[None], 0.0)
        diagonal = faces[:-1] + faces[1:] + w_down + w_up + w_back + w_front + a * edges
        off = faces[:-1] * pot[at : at + step] + faces[1:] * pot[at + 2 : at + 2 + step] + w_down * v_down + w_up * v_up
        off = off + w_back * lower(v, 2) + w_front * upper(v, 2)
        left = source[at : at + step] - diagonal * v + off
        residual[at : at + step] = left
        for n, x in enumerate((left, a)):
            pair = x.reshape(step // 2, 2, rows, depth)
            to = n * c1 * rows + at // 2 * rows
            wide[to : to + step // 2 * rows] = (pair[:, 0] + pair[:, 1]).reshape(step // 2 * rows, depth)
        low = jnp.concatenate([left[:, :4], a[:, :4]], axis=1)
        high = jnp.concatenate([left[:, rows - 4 :], a[:, rows - 4 :]], axis=1)
        for ref, strip in ((strip_even, jnp.where(low_y, low, high)), (strip_odd, jnp.where(low_y, high, low))):
            for k in range(step):
                for piece in range(pieces):
                    ref[(at + k) * pieces + piece] = strip[k, :, piece * LANES : (piece + 1) * LANES]
    base = 2 * c1 * rows
    for n, both in enumerate((x_low[1] + x_low[2], x_high[1] + x_high[2], y_low[1] + y_low[2], y_high[1] + y_high[2])):
        wide[base + n * rows : base + (n + 1) * rows] = both
    narrow[...] = select(wide[...], pair_matrix(depth)) * 0.125
    half = narrow.shape[0] // 2
    coarse[...] = narrow[pl.ds(0, half, 2)] + narrow[pl.ds(1, half, 2)]
    for k in range(c1):
        s, m = coarse[k * r1 : (k + 1) * r1], coarse[(c1 + k) * r1 : (c1 + k + 1) * r1]
        low = jnp.concatenate([s[:4], m[:4]], axis=0)
        high = jnp.concatenate([s[r1 - 4 :], m[r1 - 4 :]], axis=0)
        strip_even[count * pieces + k] = jnp.where(low_y, low, high)
        strip_odd[count * pieces + k] = jnp.where(low_y, high, low)


def payload_kernel(c1, r1, coarse, payload, wide, narrow, sheet, semaphore):
    c2 = c1 // 2
    depth = coarse.shape[1]
    shape = (c1, r1, depth)
    s, m = coarse[: c1 * r1].reshape(shape), coarse[c1 * r1 : 2 * c1 * r1].reshape(shape)
    base = 2 * c1 * r1
    m_xlow, m_xhigh = coarse[base : base + r1], coarse[base + r1 : base + 2 * r1]
    base += 2 * r1
    m_ylow = jnp.stack([coarse[base + k : base + k + 1] for k in range(c1)])
    m_yhigh = jnp.stack([coarse[base + r1 + k : base + r1 + k + 1] for k in range(c1)])
    row, lane = iota(shape, 1), iota(shape, 2)
    first, last = row == 0, row == r1 - 1
    around = jnp.concatenate([m_xlow[None], m, m_xhigh[None]], axis=0)
    faces = harmonic(around[:-1], around[1:], 0.25)
    down = jnp.where(first, jnp.broadcast_to(m_ylow, shape), lower(m, 1))
    up = jnp.where(last, jnp.broadcast_to(m_yhigh, shape), upper(m, 1))
    w_down = harmonic(m, down, 0.25)
    w_up = jnp.where(last, harmonic(m, up, 0.25), upper(w_down, 1))
    w_back = jnp.where(lane == 0, 0.0, harmonic(m, lower(m, 2), 0.25))
    w_front = upper(w_back, 2)
    outside = as_float(lane == 0) + as_float(lane == depth - 1)
    for b in (down, up, around[:-2], around[2:]):
        outside = outside + as_float(b <= 0.0)
    diagonal = faces[:-1] + faces[1:] + w_down + w_up + w_back + w_front + 0.25 * m * outside
    e = DAMPING * s * invert(diagonal)
    y_low, y_high = w_down * e, w_up * e
    t = KEPT * s + w_back * lower(e, 2) + w_front * upper(e, 2)
    t = t + jnp.where(first, 0.0, w_down * lower(e, 1)) + jnp.where(last, 0.0, w_up * upper(e, 1))
    nothing = jnp.zeros((1, r1, depth), F32)
    t = t + faces[:-1] * jnp.concatenate([nothing, e[:-1]], axis=0) + faces[1:] * jnp.concatenate([e[1:], nothing], axis=0)
    base = c2 // 2 * r1

    def pairs(x):
        x = x.reshape(c2, 2, r1, depth)
        return (x[:, 0] + x[:, 1]).reshape(c2 * r1, depth)

    t, m = pairs(t), pairs(m)
    for n in range(2):
        wide[n, :base] = t[n * base : (n + 1) * base]
        wide[n, base + 2 * r1 :] = m[n * base : (n + 1) * base]
    wide[0, base : base + r1] = faces[0] * e[0]
    wide[0, base + r1 : base + 2 * r1] = faces[c1] * e[c1 - 1]
    for k in range(c1):
        wide[1, base + k : base + k + 1] = y_low[k, :1]
        wide[1, base + r1 + k : base + r1 + k + 1] = y_high[k, r1 - 1 :]
    publish(wide[0], wide[1], narrow, sheet, payload, semaphore)


def packed(low, high, narrow):
    narrow[...] = (select(low, pair_matrix(LANES)) + select(high, pair_matrix(LANES, LANES // 2))) * 0.125
    half = narrow.shape[0] // 2
    return narrow[pl.ds(0, half, 2)] + narrow[pl.ds(1, half, 2)]


def publish(low, high, narrow, sheet, payload, semaphore):
    sheet[...] = jnp.broadcast_to(packed(low, high, narrow)[None], sheet.shape)
    leaving = pltpu.make_async_copy(sheet, payload, semaphore)
    leaving.start()
    leaving.wait()


def strips_kernel(place, residual, material, coarse, even, odd, inner, outer, long_far, long1, long, semaphore):
    low_x, low_y = place[0] == 1, place[1] == 1
    count, rows, depth = residual.shape
    pieces = depth // LANES
    c1, r1 = count // 2, rows // 2
    base = count * pieces

    def sides(at):
        a, b = even[at], odd[at]
        return jnp.where(low_y, a, b), jnp.where(low_y, b, a)

    for i in range(count):
        for piece in range(pieces):
            low, high = sides(i * pieces + piece)
            z = slice(piece * LANES, (piece + 1) * LANES)
            long[0, i, :, z] = jnp.concatenate([low[:4], residual[i, :, z], high[:4]], axis=0)
            long[1, i, :, z] = jnp.concatenate([low[4:], material[i, :, z], high[4:]], axis=0)
    leaving = pltpu.make_async_copy(long, long_far, semaphore)
    leaving.start()
    for k in range(c1):
        low, high = sides(base + k)
        s, m = coarse[k * r1 : (k + 1) * r1], coarse[(c1 + k) * r1 : (c1 + k + 1) * r1]
        long1[0, k] = jnp.concatenate([low[:4], s, high[:4]], axis=0)
        long1[1, k] = jnp.concatenate([low[4:], m, high[4:]], axis=0)

    def pack(out, flag):
        at = 0
        for n, planes in ((0, 3), (1, 4)):
            start = jnp.where(flag, 0, count - planes)
            for k in range(planes):
                for tile in range((rows + 8) // 8):
                    for piece in range(pieces):
                        out[at] = long[n, start + k, tile * 8 : tile * 8 + 8, piece * LANES : (piece + 1) * LANES]
                        at += 1
        for n, planes in ((0, 3), (1, 4)):
            for k in range(planes):
                low, high = k, c1 - planes + k
                for tile in range((r1 + 8) // 8):
                    y = slice(tile * 8, tile * 8 + 8)
                    out[at] = jnp.where(flag, long1[n, low, y], long1[n, high, y])
                    at += 1

    pack(inner, low_x)
    pack(outer, jnp.logical_not(low_x))
    leaving.wait()


def unpack(source, flag, out, start, planes, tiles, pieces, at):
    for n in range(planes):
        for tile in range(tiles):
            for piece in range(pieces):
                value = jnp.where(flag, source[0][at], source[1][at])
                out[start + n, tile * 8 : tile * 8 + 8, piece * LANES : (piece + 1) * LANES] = value
                at += 1
    return at


def smooth_kernel(ends, place, potential_far, state_far, long, inner, outer, out, state, mat, res, x, d, fx, fy, fz, inv, potential, semaphores):
    arriving = pltpu.make_async_copy(potential_far, potential, semaphores.at[0])
    arriving.start()
    passing = pltpu.make_async_copy(state_far, state, semaphores.at[1])
    passing.start()
    count, rows, depth = potential.shape
    own = pl.ds(4, count)
    frames = [
        pltpu.make_async_copy(long.at[n], ref.at[own], semaphores.at[2 + n]) for n, ref in enumerate((res, mat))
    ]
    for copy in frames:
        copy.start()
    low_x = place[0] == 1
    count, rows, depth = potential.shape
    pieces, tiles = depth // LANES, (rows + 8) // 8
    both = (inner, outer)
    for flag, start_r, start_m in ((low_x, 1, 0), (jnp.logical_not(low_x), count + 4, count + 4)):
        at = unpack(both, flag, res, start_r, 3, tiles, pieces, 0)
        unpack(both, flag, mat, start_m, 4, tiles, pieces, at)
    for copy in frames:
        copy.wait()
    total, length = count + 8, rows + 8
    row, lane = iota((length, depth), 0), iota((length, depth), 1)
    outside = as_float(lane == 0) + as_float(lane == depth - 1)
    outside = outside + as_float((row == 4) & (place[3] == 0)) + as_float((row == rows + 3) & (place[3] == ends[1] - 1))
    low_end, high_end = place[2] == 0, place[2] == ends[0] - 1

    def chunks(first, last, step):
        return [(at, min(step, last - at)) for at in range(first, last, step)]

    for at, n in chunks(1, total - 1, SMOOTH_STEP):
        here = slice(at, at + n)
        a = mat[here]
        faces = harmonic(mat[at - 1 : at + n], mat[at : at + n + 1], 1.0)
        w_down = harmonic(a, lower(a, 1), 1.0)
        w_back = jnp.where(lane[None] == 0, 0.0, harmonic(a, lower(a, 2), 1.0))
        plane = at + iota((n, 1, 1), 0)
        edges = outside[None] + as_float((plane == 4) & low_end) + as_float((plane == count + 3) & high_end)
        diagonal = faces[:-1] + faces[1:] + w_down + upper(w_down, 1) + w_back + upper(w_back, 2) + a * edges
        inverse = jnp.where(a > 0.0, invert(jnp.maximum(diagonal, 1e-3)), 0.0)
        fx[at : at + n + 1], fy[here], fz[here], inv[here] = faces, w_down, w_back, inverse
        scaled = inverse * res[here]
        res[here] = scaled
        x[0, here] = scaled * (1.0 / THETA)
    rho = 1.0 / SIGMA
    for turn in range(DEG - 1):
        if turn == DEG - 2:
            arriving.wait()
        following = 1.0 / (2.0 * SIGMA - rho)
        old, new = turn % 2, (turn + 1) % 2
        keep, gain = following * rho, 2.0 * following / DELTA
        for at, n in chunks(2 + turn, total - 2 - turn, SMOOTH_STEP):
            here = slice(at, at + n)
            v = x[old, here]
            w_down, w_back = fy[here], fz[here]
            off = fx[here] * x[old, at - 1 : at + n - 1] + fx[at + 1 : at + n + 1] * x[old, at + 1 : at + n + 1]
            off = off + w_down * lower(v, 1) + upper(w_down * v, 1)
            off = off + w_back * lower(v, 2) + upper(w_back * v, 2)
            before = v * keep if turn == 0 else d[here] * keep
            change = before + gain * (res[here] - v + inv[here] * off)
            if turn == DEG - 2:
                out[at - 4 : at + n - 4] = potential[at - 4 : at + n - 4] + (v + change)[:, 4 : 4 + rows]
            else:
                d[here] = change
                x[new, here] = v + change
        rho = following
    passing.wait()


def each(count, body, most=8):
    step = min(count, most)
    if count // step <= 4:
        for n in range(count // step):
            body(n * step, step)
        return

    def run(n, _):
        body(n * step, step)
        return 0

    lax.fori_loop(0, count // step, run, 0)


def fill_table(mat, table, level, count, base, width):
    stride, scale = 2**level, 0.25 ** (level + 2)
    rows = mat.shape[1]
    row, lane = iota((rows, LANES), 0), iota((rows, LANES), 1)
    above, beyond = row >= stride, lane >= stride
    outside = as_float(row == 0) + as_float(row == rows - stride) + as_float(lane == 0) + as_float(lane == width - stride)

    def body(at, step):
        a, before, ahead = mat[pl.ds(at + 1, step)], mat[pl.ds(at, step)], mat[pl.ds(at + 2, step)]
        w_before, w_ahead = harmonic(a, before, scale), harmonic(a, ahead, scale)
        w_down = jnp.where(above[None], harmonic(a, lower(a, 1, stride), scale), 0.0)
        w_back = jnp.where(beyond[None], harmonic(a, lower(a, 2, stride), scale), 0.0)
        plane = at + iota((step, 1, 1), 0)
        edges = outside[None] + as_float(plane == 0) + as_float(plane == count - 1)
        diagonal = w_before + w_ahead + w_down + upper(w_down, 1, stride) + w_back + upper(w_back, 2, stride)
        diagonal = diagonal + scale * a * edges
        table[0, pl.ds(base + at, step)] = w_before
        table[1, pl.ds(base + at, step)] = w_down
        table[2, pl.ds(base + at, step)] = w_back
        table[3, pl.ds(base + at, step)] = jnp.where(a > 0.0, invert(jnp.maximum(diagonal, 1e-4)), 0.0)

    each(count, body)
    table[0, base + count] = jnp.zeros((rows, LANES), F32)


def fold(t, stride):
    a = t.reshape(t.shape[0] // 2, 2, *t.shape[1:])
    a = a[:, 0] + a[:, 1]
    a = a + upper(a, 1, stride)
    return a + upper(a, 2, stride)


def unfold(e, stride):
    e = e + lower(e, 1, stride)
    e = e + lower(e, 2, stride)
    return jnp.broadcast_to(e[:, None], (e.shape[0], 2, *e.shape[1:])).reshape(2 * e.shape[0], *e.shape[1:])


def off_diagonal(e, table, base, at, step, stride):
    v = e[pl.ds(at + 1, step)]
    total = table[0, pl.ds(base + at, step)] * e[pl.ds(at, step)]
    total = total + table[0, pl.ds(base + at + 1, step)] * e[pl.ds(at + 2, step)]
    fy, fz = table[1, pl.ds(base + at, step)], table[2, pl.ds(base + at, step)]
    total = total + fy * lower(v, 1, stride) + upper(fy * v, 1, stride)
    return v, total + fz * lower(v, 2, stride) + upper(fz * v, 2, stride)


def cycle(s, e, t, table, counts, bases, place, out, c2, r2, pad):
    zero = jnp.zeros(t.shape[1:], F32)
    for ref, count in zip(e, counts):
        ref[0] = zero
        ref[count + 1] = zero
    for level, (count, base) in enumerate(zip(counts, bases)):
        s_l, e_l, stride = s[level], e[level], 2**level

        def start(at, step):
            e_l[pl.ds(at + 1, step)] = DAMPING * s_l[pl.ds(at + 1, step)] * table[3, pl.ds(base + at, step)]

        each(count, start)
        if level == len(counts) - 1:
            break

        def remainder(at, step):
            _, off = off_diagonal(e_l, table, base, at, step, stride)
            left = KEPT * s_l[pl.ds(at + 1, step)] + off
            s[level + 1][pl.ds(at // 2 + 1, step // 2)] = 0.125 * fold(left, stride)

        each(count, remainder)

    def relax(s_l, source, target, base, count, stride):
        def sweep(at, step):
            v, off = off_diagonal(source, table, base, at, step, stride)
            inverse = table[3, pl.ds(base + at, step)]
            target[pl.ds(at + 1, step)] = KEPT * v + DAMPING * inverse * (s_l[pl.ds(at + 1, step)] + off)

        each(count, sweep)

    t[0] = zero
    t[counts[2] + 1] = zero
    now, other = e[2], t
    for _ in range(COARSE_SWEEPS - 1):
        relax(s[2], now, other, bases[2], counts[2], 4)
        now, other = other, now

    def add(at, step):
        e[1][pl.ds(2 * at + 1, 2 * step)] = e[1][pl.ds(2 * at + 1, 2 * step)] + unfold(now[pl.ds(at + 1, step)], 2)

    each(counts[2], add, 4)
    if now is t:
        now = e[2] = s[1]
    relax(s[1], e[1], t, bases[1], counts[1], 2)

    planes = c2 + 4
    begin = place[2] * c2 - 2
    inside = jnp.clip(begin, 0, counts[0] - planes)
    coarse = jnp.clip(place[2] * c2 // 2 - 2, 0, counts[1] - planes // 2 - 2)
    number = planes // 2 + 2
    at = pl.ds(2 * coarse + 1, 2 * number)
    e[0][at] = e[0][at] + unfold(t[pl.ds(coarse + 1, number)], 1)
    v, off = off_diagonal(e[0], table, bases[0], inside, planes, 1)
    inverse = table[3, pl.ds(bases[0] + inside, planes)]
    pad[...] = jnp.zeros(pad.shape, F32)
    rows = t.shape[1]
    value = KEPT * v + DAMPING * inverse * (s[0][pl.ds(inside + 1, planes)] + off)
    pad[pl.ds(2 + inside - begin, planes), 8 : 8 + rows, :] = value
    for n in range(planes):
        out[n] = pad[n + 2, pl.ds(place[3] * r2 + 6, r2 + 4), :]


def cycle_shapes(counts, rows, c2):
    out = [pltpu.VMEM((count + 2, rows, LANES), F32) for count in (*counts, *counts, counts[0])]
    return out + [pltpu.VMEM((c2 + 8, rows + 16, LANES), F32)]


def repeat(count, body):
    if count <= 8:
        for i in range(count):
            body(i, i % 2)
        return

    def two(n, _):
        body(2 * n, 0)
        body(2 * n + 1, 1)

    lax.fori_loop(0, count // 2, two, None)


def spread_blocks(fetch, outs, grid, c2, r2):
    gx, gy = grid
    length = c2 // 2 * r2
    low = iota((length, LANES), 1) < LANES // 2

    def column(i, parity):
        for j in range(gy):
            for start, out in outs:
                block = fetch(i, parity, j, slice(start, start + length))
                parts = (jnp.where(low, block, 0.0), jnp.where(low, pltpu.roll(block, LANES // 2, 1), 0.0))
                for k in range(c2):
                    n = k % (c2 // 2)
                    out[i * c2 + k + 1, j * r2 : (j + 1) * r2, :] = parts[k // (c2 // 2)][n * r2 : (n + 1) * r2]

    repeat(gx, column)


def clear_ends(refs, counts):
    for ref, count in zip(refs, counts):
        zero = jnp.zeros(ref.shape[1:], F32)
        ref[0] = zero
        ref[count + 1] = zero


def pass_kernel(blocks, _, out):
    out[...] = blocks[...]


def first_cycle_kernel(counts, bases, grid, c2, r2, width, place, mine, theirs, out, table, *scratch):
    s, e, t, pad = scratch[0:3], list(scratch[3:6]), scratch[6], scratch[7]
    gx, gy = grid
    rows = gy * r2
    half = LANES // 2
    own = c2 // 2 * r2
    clear_ends((t, *s), (counts[0], *counts))
    odd = place[0] == 1

    def fetch(i, parity, j, at):
        here = i // 2 * gy + j
        a, b = mine[here, at], theirs[here, at]
        return jnp.where(odd, b, a) if parity == 0 else jnp.where(odd, a, b)

    spread_blocks(fetch, ((0, s[0]), (own + 2 * r2, t)), grid, c2, r2)
    face_y = e[0]
    low = iota((2 * c2, LANES), 1) < half

    def edges(i, parity):
        for j in range(gy):
            faces = fetch(i, parity, j, slice(own, own + 2 * r2))
            x_faces = jnp.where(low, faces, 0.0)
            y_faces = jnp.where(low, pltpu.roll(faces, half, 1), 0.0)
            here = slice(j * r2, (j + 1) * r2)
            s[0][i * c2, here, :] = s[0][i * c2, here, :] + x_faces[:r2]
            s[0][(i + 1) * c2 + 1, here, :] = s[0][(i + 1) * c2 + 1, here, :] + x_faces[r2:]
            for k in range(c2):
                at = i * c2 + k + 1
                if j > 0:
                    face_y[at, j * r2 - 1 : j * r2, :] = y_faces[k : k + 1]
                if j < gy - 1:
                    face_y[at, (j + 1) * r2 : (j + 1) * r2 + 1, :] = y_faces[c2 + k : c2 + k + 1]

    repeat(gx, edges)

    def join(at, step):
        now = pl.ds(at + 1, step)
        row = iota((rows, LANES), 0)
        edge = ((row % r2 == 0) & (row > 0)) | ((row % r2 == r2 - 1) & (row < rows - 1))
        s[0][now] = s[0][now] + jnp.where(edge[None], face_y[now], 0.0)

    each(counts[0], join)
    clear_ends(s[:1], counts)
    mats = (t, s[1], s[2])
    for level, (count, base) in enumerate(zip(counts, bases)):
        if level:

            def coarsen(at, step):
                whole = (iota((rows, LANES), 0) % 2**level == 0) & (iota((rows, LANES), 1) % 2**level == 0)
                mean = 0.125 * fold(mats[level - 1][pl.ds(at + 1, step)], 2 ** (level - 1))
                mats[level][pl.ds(at // 2 + 1, step // 2)] = jnp.where(whole[None], mean, 0.0)

            each(counts[level - 1], coarsen)
        fill_table(mats[level], table, level, count, base, width)
    cycle(s, e, t, table, counts, bases, place, out, c2, r2, pad)


def shifted(a):
    zero = jnp.zeros_like(a[:1])
    return jnp.concatenate([zero, a[:-1]], axis=0), jnp.concatenate([a[1:], zero], axis=0)


def apply_off(e, fx, fy, fz):
    before, ahead = shifted(e)
    out = fx[:-1] * before + fx[1:] * ahead
    out = out + fy * lower(e, 1) + upper(fy * e, 1)
    return out + fz * lower(e, 2) + upper(fz * e, 2)


def raise_window(window_ref, flat, out):
    planes, rows, _ = window_ref.shape
    values = select(window_ref[...].reshape(planes * rows, LANES), spread_matrix(LANES))
    flat[pl.ds(0, planes * rows, 2)] = values
    flat[pl.ds(1, planes * rows, 2)] = values
    v = flat[...].reshape(planes, 1, 2 * rows, LANES)
    out[...] = jnp.broadcast_to(v, (planes, 2, 2 * rows, LANES)).reshape(2 * planes, 2 * rows, LANES)


def level1_kernel(
    offset, place, long1, inner, outer, window1, payload, state_far,
    src, mat, flat, prolonged, fx, fy, fz, diag, inv, err, c, state, wide, narrow, sheet, semaphores,
):
    low_x = place[0] == 1
    total, length, depth = src.shape
    count, rows = total - 8, length - 8
    both = (inner, outer)
    zero = jnp.zeros((length, depth), F32)
    src[0] = zero
    src[total - 1] = zero
    for flag, start_s, start_m in ((low_x, 1, 0), (jnp.logical_not(low_x), count + 4, count + 4)):
        at = unpack(both, flag, src, start_s, 3, length // 8, 1, offset)
        unpack(both, flag, mat, start_m, 4, length // 8, 1, at)
    for n, ref in enumerate((src, mat)):
        ref[pl.ds(4, count)] = long1[n]
    raise_window(window1, flat, prolonged)
    row, lane = iota((length, depth), 0), iota((length, depth), 1)
    ends = as_float(lane == 0) + as_float(lane == depth - 1)
    def chunks(margin):
        first, last = margin, total - margin
        return [(at, min(LEVEL1_STEP, last - at)) for at in range(first, last, LEVEL1_STEP)]

    for at, n in chunks(1):
        here = slice(at, at + n)
        a, before, ahead = mat[here], mat[at - 1 : at + n - 1], mat[at + 1 : at + n + 1]
        down, up = lower(a, 1), upper(a, 1)
        f = harmonic(mat[at - 1 : at + n], mat[at : at + n + 1], 0.25)
        w_y = harmonic(a, down, 0.25)
        w_z = jnp.where(lane[None] == 0, 0.0, harmonic(a, lower(a, 2), 0.25))
        outside = ends[None] + as_float(before <= 0.0) + as_float(ahead <= 0.0) + as_float(down <= 0.0) + as_float(up <= 0.0)
        diagonal = f[:-1] + f[1:] + w_y + upper(w_y, 1) + w_z + upper(w_z, 2) + 0.25 * a * outside
        inverse = jnp.where(a > 0.0, invert(jnp.maximum(diagonal, 1e-4)), 0.0)
        fx[at : at + n + 1], fy[here], fz[here], diag[here], inv[here] = f, w_y, w_z, diagonal, inverse
        err[here] = DAMPING * inverse * src[here] + prolonged[here]

    def off(v, at, n):
        here = slice(at, at + n)
        mid, w_y, w_z = v[here], fy[here], fz[here]
        out = fx[here] * v[at - 1 : at + n - 1] + fx[at + 1 : at + n + 1] * v[at + 1 : at + n + 1]
        out = out + w_y * lower(mid, 1) + upper(w_y * mid, 1)
        return here, mid, out + w_z * lower(mid, 2) + upper(w_z * mid, 2)

    for at, n in chunks(2):
        here, mid, more = off(err, at, n)
        c[here] = KEPT * mid + DAMPING * inv[here] * (src[here] + more)
    for at, n in chunks(3):
        here, mid, more = off(c, at, n)
        left = src[here] - diag[here] * mid + more
        src[here] = left
        value = DAMPING * inv[here] * left
        err[here] = value
        state[at - 3 : at + n - 3] = value
    base = count + 2
    state[base : base + count + 1] = fx[4 : count + 5]
    base += count + 1
    for n, ref in enumerate((fy, fz, inv, c, src)):
        state[base + n * count : base + (n + 1) * count] = ref[4 : 4 + count]
    leaving = pltpu.make_async_copy(state, state_far, semaphores.at[0])
    leaving.start()
    here, _, more = off(err, 4, count)
    t = (KEPT * src[here] + more)[:, 4 : 4 + rows].reshape(count // 2, 2, rows, depth)
    wide[...] = (t[:, 0] + t[:, 1]).reshape(count // 2 * rows, depth)
    half = wide.shape[0] // 2
    publish(wide[:half], wide[half:], narrow, sheet, payload, semaphores.at[1])
    leaving.wait()


def last_cycle_kernel(counts, bases, grid, c2, r2, place, blocks, table, state, partial, out, *scratch):
    s, e, t, pad = scratch[0:3], list(scratch[3:6]), scratch[6], scratch[7]
    view, flat, prolonged, tall, coarse, result, departures = scratch[8:15]
    spread_blocks(lambda i, _, j, at: blocks[i * grid[1] + j, at], ((0, s[0]),), grid, c2, r2)
    clear_ends(s, counts)
    cycle(s, e, t, table, counts, bases, place, view, c2, r2, pad)
    raise_window(view, flat, prolonged)
    count, rows, depth = partial.shape
    c1, r1 = count // 2, rows // 2
    v = prolonged[3 : c1 + 5] + state[: c1 + 2]
    here = v[1:-1]
    base = 2 * c1 + 3
    w_x = state[c1 + 2 : base]
    w_y, w_z, inverse, before, left = (state[base + n * c1 : base + (n + 1) * c1] for n in range(5))
    off = w_x[:-1] * v[:-2] + w_x[1:] * v[2:]
    off = off + w_y * lower(here, 1) + upper(w_y * here, 1) + w_z * lower(here, 2) + upper(w_z * here, 2)
    total = before + KEPT * here + DAMPING * inverse * (left + off)
    coarse[...] = total[:, 4 : 4 + r1].reshape(c1 * r1, LANES)
    values = select(coarse[...], spread_matrix(depth))
    for piece in range(depth // LANES):
        z = slice(piece * LANES, (piece + 1) * LANES)
        tall[piece, pl.ds(0, c1 * r1, 2)] = values[:, z]
        tall[piece, pl.ds(1, c1 * r1, 2)] = values[:, z]
    leaving = []
    for k in range(c1):
        for piece in range(depth // LANES):
            z = slice(piece * LANES, (piece + 1) * LANES)
            more = tall[piece, k * rows : (k + 1) * rows]
            result[2 * k, :, z] = partial[2 * k, :, z] + more
            result[2 * k + 1, :, z] = partial[2 * k + 1, :, z] + more
        if k % 2 == 1:
            planes = pl.ds(2 * k - 2, 4)
            leaving.append(pltpu.make_async_copy(result.at[planes], out.at[planes], departures.at[k // 2]))
            leaving[-1].start()
    for copy in leaving:
        copy.wait()


def size_of(shape):
    lead = math.prod(shape[:-2])
    return 4 * lead * (-(-shape[-2] // 8) * 8) * (-(-shape[-1] // LANES) * LANES)


def call(kernel, name, inputs, outputs, scratch=(), apart=(), cost=None):
    streamed = 0

    def held(n, x):
        nonlocal streamed
        if n in apart:
            return pltpu.with_memory_space_constraint(x, pltpu.HBM)
        if x.ndim == 1:
            return x
        if size_of(x.shape) <= HELD:
            return pltpu.with_memory_space_constraint(x, pltpu.VMEM)
        streamed += size_of(x.shape)
        return x

    def result(shape):
        nonlocal streamed
        if isinstance(shape, jax.ShapeDtypeStruct):
            streamed += size_of(shape.shape)
            return shape
        if far(shape):
            return pltpu.HBM(shape[1], F32)
        if size_of(shape) <= HELD:
            return pltpu.VMEM(shape, F32)
        streamed += size_of(shape)
        return jax.ShapeDtypeStruct(shape, F32)

    def far(x):
        return isinstance(x, tuple) and x[0] == "far"

    def space(n, x):
        return pltpu.HBM if n in apart else pltpu.SMEM if x.ndim == 1 else pltpu.VMEM

    specs = [pl.BlockSpec(memory_space=space(n, x)) for n, x in enumerate(inputs)]
    inputs = [held(n, x) for n, x in enumerate(inputs)]
    results = [result(shape) for shape in outputs]
    need = streamed + sum(size_of(x.shape) for x in scratch if len(getattr(x, "shape", ())) > 1) + 3 * MIB
    return pl.pallas_call(
        kernel,
        out_shape=results,
        in_specs=specs,
        out_specs=[pl.BlockSpec(memory_space=pltpu.HBM if far(x) else pltpu.VMEM) for x in outputs],
        scratch_shapes=list(scratch),
        compiler_params=pltpu.CompilerParams(vmem_limit_bytes=max(need, 8 * MIB)),
        name=name,
        cost_estimate=None if cost is None else pl.CostEstimate(flops=cost, bytes_accessed=0, transcendentals=0),
    )(*inputs)


def swaps(count):
    inner = [(i, i + 1) for i in range(0, count - 1, 2)]
    outer = [(i, i + 1) for i in range(1, count - 1, 2)]
    return [pairs + [(b, a) for a, b in pairs] for pairs in (inner, outer)]


def local(right_side, potential, phase, permeability):
    gx, gy = lax.axis_size("gx"), lax.axis_size("gy")
    devices = gx * gy
    here_x, here_y = lax.axis_index("gx"), lax.axis_index("gy")
    place = jnp.stack([here_x % 2, here_y % 2, here_x, here_y]).astype(jnp.int32)
    count, rows, depth = right_side.shape
    c1, r1, d1 = count // 2, rows // 2, depth // 2
    c2, r2 = c1 // 2, r1 // 2
    pieces = depth // LANES
    swap_x, swap_y = swaps(gx), swaps(gy)
    VM = lambda *shape: pltpu.VMEM(shape, F32)

    brick = (count, rows, depth)
    face = (3, rows, depth)
    DMA = pltpu.SemaphoreType.DMA
    sheet = (devices, c2 // 2 * r2, LANES)
    sheet2 = (devices // 2, c2 * r2 + 2 * r2, LANES)
    material, potential_here, source_here, inner, outer, even, odd = call(
        faces_kernel, "faces", (place, permeability, potential, phase, right_side),
        (brick, brick, brick, face, face, (3, count, depth), (3, count, depth)),
        (pltpu.VMEM(brick, jnp.int32), pltpu.SMEM(permeability.shape, F32), pltpu.SemaphoreType.DMA((4,))),
        apart=(1, 2, 3, 4),
    )
    even = lax.ppermute(even, "gy", swap_y[0])
    odd = lax.ppermute(odd, "gy", swap_y[1])
    outer = lax.ppermute(outer, "gx", swap_x[1])
    inner = lax.ppermute(inner, "gx", swap_x[0])

    strip = (count * pieces + c1, 8, LANES)
    total = 2 * c1 * rows + 4 * rows
    residual, coarse, even, odd = call(
        residual_kernel, "residual", (place, source_here, potential_here, material, inner, outer, even, odd),
        (brick, (total // 2, LANES), strip, strip),
        (
            VM(total, depth), VM(total, LANES), VM(4, count, 8, depth), VM(count + 2, rows, depth), VM(count + 2, rows, depth),
        ),
    )
    even = lax.ppermute(even, "gy", swap_y[0])
    odd = lax.ppermute(odd, "gy", swap_y[1])
    small = c2 * r1 + 2 * r1
    (payload,) = call(
        functools.partial(payload_kernel, c1, r1), "payload", (coarse,), (("far", sheet2),),
        (VM(2, small, d1), VM(small, LANES), VM(*sheet2), DMA),
    )
    groups = [[(2 * i + c) * gy + j for i in range(gx // 2) for j in range(gy)] for c in range(2)]
    blocks = lax.all_to_all(payload, ("gx", "gy"), 0, 0, axis_index_groups=groups)
    tiles, tiles1 = (rows + 8) // 8, (r1 + 8) // 8
    strip = (7 * tiles * pieces + 7 * tiles1, 8, LANES)
    long_shape = (2, count, rows + 8, depth)
    inner, outer, long, long1 = call(
        strips_kernel, "strips", (place, residual, material, coarse, even, odd),
        (strip, strip, ("far", long_shape), (2, c1, r1 + 8, d1)),
        (VM(*long_shape), DMA), cost=10**11,
    )
    outer = lax.ppermute(outer, "gx", swap_x[1])
    inner = lax.ppermute(inner, "gx", swap_x[0])

    (blocks,) = call(pass_kernel, "pass", (blocks, long1), (sheet2,))
    others = lax.ppermute(blocks, "gx", swap_x[0])
    counts = tuple(gx * c2 // k for k in (1, 2, 4))
    bases = (0, counts[0] + 1, counts[0] + counts[1] + 2)
    work = cycle_shapes(counts, gy * r2, c2)
    view = (c2 + 4, r2 + 4, LANES)
    window1, table = call(
        functools.partial(first_cycle_kernel, counts, bases, (gx, gy), c2, r2, d1 // 2), "cycle1", (place, blocks, others),
        (view, (4, sum(counts) + 3, gy * r2, LANES)), work,
    )
    frame = (c1 + 8, r1 + 8, d1)
    flat = VM((c2 + 4) * (r2 + 4) * 2, LANES)
    state = (7 * c1 + 3, r1 + 8, d1)
    tall = VM(c1 + 9, r1 + 8, d1)
    payload, held = call(
        functools.partial(level1_kernel, 7 * tiles * pieces), "level1", (place, long1, inner, outer, window1), (("far", sheet), ("far", state)),
        (
            VM(*frame), VM(*frame), flat, VM(*frame), tall, VM(*frame), VM(*frame), VM(*frame), VM(*frame), VM(*frame),
            VM(*frame), VM(*state), VM(c1 // 2 * r1, d1), VM(c1 // 4 * r1, LANES), VM(*sheet), pltpu.SemaphoreType.DMA((2,)),
        ),
    )
    blocks = lax.all_to_all(payload, ("gx", "gy"), 0, 0)
    wide = (count + 8, rows + 8, depth)
    partial, held = call(
        functools.partial(smooth_kernel, (gx, gy)), "smooth", (place, potential, held, long, inner, outer), (brick, state),
        (
            VM(*wide), VM(*wide), VM(2, *wide), VM(*wide), VM(count + 9, rows + 8, depth), VM(*wide), VM(*wide), VM(*wide),
            VM(*brick), pltpu.SemaphoreType.DMA((4,)),
        ),
        apart=(1, 2, 3),
    )
    (out,) = call(
        functools.partial(last_cycle_kernel, counts, bases, (gx, gy), c2, r2), "cycle2",
        (place, blocks, table, held, partial), (("far", brick),),
        (
            *work, VM(*view), flat, VM(*frame), VM(pieces, c1 * rows, LANES), VM(c1 * r1, LANES), VM(*brick),
            pltpu.SemaphoreType.DMA((c1 // 2,)),
        ),
    )
    return out


def solution(mesh):
    placed = (P("gx", "gy", None), P("gx", "gy", None), P("gx", "gy", None), P())
    return jax.shard_map(local, mesh=mesh, in_specs=placed, out_specs=P("gx", "gy", None), check_vma=False)
```

```python
import functools
import math

import jax
import jax.numpy as jnp
from jax import lax
from jax.experimental import pallas as pl
from jax.experimental.pallas import tpu as pltpu
from jax.sharding import PartitionSpec as P

DEG = 4
COARSE_SWEEPS = 4
THETA = 1.15
DELTA = 0.85
SIGMA = 1.15 / 0.85
DAMPING = 0.6
KEPT = 1.0 - DAMPING
F32 = jnp.float32
LANES = 128
MIB = 1024 * 1024
HELD = 4 * MIB
SMOOTH_STEP = 4
LEVEL1_STEP = 7


def iota(shape, axis):
    return lax.broadcasted_iota(jnp.int32, shape, axis)


def invert(x):
    guess = pl.reciprocal(x, approx=True)
    return guess * (2.0 - x * guess)


def harmonic(a, b, scale):
    return (2.0 * scale) * a * b * invert(jnp.maximum(a + b, 1e-3))


def pair_matrix(size, offset=0):
    column = iota((size, LANES), 1)
    return ((column >= offset) & (iota((size, LANES), 0) // 2 == column - offset)).astype(jnp.bfloat16)


def spread_matrix(width):
    return (iota((LANES, width), 1) // 2 == iota((LANES, width), 0)).astype(jnp.bfloat16)


def select(values, matrix):
    high = values.astype(jnp.bfloat16)
    rest = (values - high.astype(F32)).astype(jnp.bfloat16)
    return jnp.dot(high, matrix, preferred_element_type=F32) + jnp.dot(rest, matrix, preferred_element_type=F32)


def lower(x, axis, stride=1):
    return pltpu.roll(x, stride, axis)


def upper(x, axis, stride=1):
    return pltpu.roll(x, x.shape[axis] - stride, axis)


def as_float(condition):
    return jnp.where(condition, 1.0, 0.0)


def faces_kernel(
    place, permeability, potential, phase, source,
    material, pot, src, inner, outer, even, odd,
    ids, values, semaphores,
):
    arriving = [
        pltpu.make_async_copy(a, b, semaphores.at[n])
        for n, (a, b) in enumerate(((permeability, values), (phase, ids), (potential, pot), (source, src)))
    ]
    for copy in arriving:
        copy.start()
    low_x, low_y = place[0] == 1, place[1] == 1
    count, rows = pot.shape[:2]
    arriving[0].wait()
    arriving[1].wait()
    p0, p1, p2 = values[0], values[1], values[2]
    for i in range(count):
        here = ids[i]
        material[i] = jnp.where(here == 0, p0, jnp.where(here == 1, p1, p2))
    last = count - 1
    first = jnp.where(low_x, 0, last)
    second = jnp.where(low_x, 1, last - 1)
    inner[1] = material[first]
    inner[2] = material[second]
    outer[1] = material[last - first]
    outer[2] = material[last - second]

    def edge(slot, ref, a, b):
        for i in range(count):
            low, high = ref[i, a : a + 1, :], ref[i, b : b + 1, :]
            even[slot, i : i + 1, :] = jnp.where(low_y, low, high)
            odd[slot, i : i + 1, :] = jnp.where(low_y, high, low)

    edge(1, material, 0, rows - 1)
    edge(2, material, 1, rows - 2)
    arriving[2].wait()
    inner[0] = pot[first]
    outer[0] = pot[last - first]
    edge(0, pot, 0, rows - 1)
    arriving[3].wait()


def residual_kernel(
    place, source, potential, material, outer, even, odd, inner,
    residual, coarse, strip_even, strip_odd,
    wide, narrow, y_faces, mat, pot,
):
    low_x, low_y = place[0] == 1, place[1] == 1
    count, rows, depth = source.shape
    c1, r1 = count // 2, rows // 2
    pieces = depth // LANES

    def ordered(flag, a, b):
        return jnp.where(flag, a, b), jnp.where(flag, b, a)

    x_low, x_high = ordered(low_x, inner[...], outer[...])
    y_low, y_high = ordered(low_y, even[...], odd[...])
    row, lane = iota((rows, depth), 0), iota((rows, depth), 1)
    first, last = row == 0, row == rows - 1
    for n, ref in enumerate((y_low[0], y_high[0], y_low[1], y_high[1])):
        for i in range(count):
            y_faces[n, i] = jnp.broadcast_to(ref[i : i + 1], (8, depth))
    mat[0], mat[count + 1] = x_low[1], x_high[1]
    pot[0], pot[count + 1] = x_low[0], x_high[0]
    mat[pl.ds(1, count)] = material[...]
    pot[pl.ds(1, count)] = potential[...]
    step = 4
    outside = as_float(lane == 0) + as_float(lane == depth - 1)

    def edge_count(faces):
        return as_float(faces[:1, :1] <= 0.0)

    outside = outside + jnp.where(first, edge_count(y_low[1]), 0.0) + jnp.where(last, edge_count(y_high[1]), 0.0)

    def beside(ref, n, at):
        return jnp.broadcast_to(ref[n, at : at + step, :1], (step, rows, depth))

    for at in range(0, count, step):
        here = slice(at + 1, at + 1 + step)
        a, v = mat[here], pot[here]
        faces = harmonic(mat[at : at + step + 1], mat[at + 1 : at + step + 2], 1.0)
        down = jnp.where(first[None], beside(y_faces, 2, at), lower(a, 1))
        w_down = harmonic(a, down, 1.0)
        w_top = harmonic(a[:, rows - 1 :], y_faces[3, at : at + step, :1], 1.0)
        w_up = jnp.where(last[None], jnp.broadcast_to(w_top, a.shape), upper(w_down, 1))
        w_back = jnp.where(lane[None] == 0, 0.0, harmonic(a, lower(a, 2), 1.0))
        w_front = upper(w_back, 2)
        v_down = jnp.where(first[None], beside(y_faces, 0, at), lower(v, 1))
        v_up = jnp.where(last[None], beside(y_faces, 1, at), upper(v, 1))
        edges = jnp.broadcast_to(outside[None], a.shape)
        if at == 0:
            edges = edges + jnp.where(iota((step, 1, 1), 0) == 0, edge_count(x_low[1])[None], 0.0)
        if at == count - step:
            edges = edges + jnp.where(iota((step, 1, 1), 0) == step - 1, edge_count(x_high[1])[None], 0.0)
        diagonal = faces[:-1] + faces[1:] + w_down + w_up + w_back + w_front + a * edges
        off = faces[:-1] * pot[at : at + step] + faces[1:] * pot[at + 2 : at + 2 + step] + w_down * v_down + w_up * v_up
        off = off + w_back * lower(v, 2) + w_front * upper(v, 2)
        left = source[at : at + step] - diagonal * v + off
        residual[at : at + step] = left
        for n, x in enumerate((left, a)):
            pair = x.reshape(step // 2, 2, rows, depth)
            to = n * c1 * rows + at // 2 * rows
            wide[to : to + step // 2 * rows] = (pair[:, 0] + pair[:, 1]).reshape(step // 2 * rows, depth)
        low = jnp.concatenate([left[:, :4], a[:, :4]], axis=1)
        high = jnp.concatenate([left[:, rows - 4 :], a[:, rows - 4 :]], axis=1)
        for ref, strip in ((strip_even, jnp.where(low_y, low, high)), (strip_odd, jnp.where(low_y, high, low))):
            for k in range(step):
                for piece in range(pieces):
                    ref[(at + k) * pieces + piece] = strip[k, :, piece * LANES : (piece + 1) * LANES]
    base = 2 * c1 * rows
    for n, both in enumerate((x_low[1] + x_low[2], x_high[1] + x_high[2], y_low[1] + y_low[2], y_high[1] + y_high[2])):
        wide[base + n * rows : base + (n + 1) * rows] = both
    narrow[...] = select(wide[...], pair_matrix(depth)) * 0.125
    half = narrow.shape[0] // 2
    coarse[...] = narrow[pl.ds(0, half, 2)] + narrow[pl.ds(1, half, 2)]
    for k in range(c1):
        s, m = coarse[k * r1 : (k + 1) * r1], coarse[(c1 + k) * r1 : (c1 + k + 1) * r1]
        low = jnp.concatenate([s[:4], m[:4]], axis=0)
        high = jnp.concatenate([s[r1 - 4 :], m[r1 - 4 :]], axis=0)
        strip_even[count * pieces + k] = jnp.where(low_y, low, high)
        strip_odd[count * pieces + k] = jnp.where(low_y, high, low)


def payload_kernel(c1, r1, coarse, payload, wide, narrow, sheet, semaphore):
    c2 = c1 // 2
    depth = coarse.shape[1]
    shape = (c1, r1, depth)
    s, m = coarse[: c1 * r1].reshape(shape), coarse[c1 * r1 : 2 * c1 * r1].reshape(shape)
    base = 2 * c1 * r1
    m_xlow, m_xhigh = coarse[base : base + r1], coarse[base + r1 : base + 2 * r1]
    base += 2 * r1
    m_ylow = jnp.stack([coarse[base + k : base + k + 1] for k in range(c1)])
    m_yhigh = jnp.stack([coarse[base + r1 + k : base + r1 + k + 1] for k in range(c1)])
    row, lane = iota(shape, 1), iota(shape, 2)
    first, last = row == 0, row == r1 - 1
    around = jnp.concatenate([m_xlow[None], m, m_xhigh[None]], axis=0)
    faces = harmonic(around[:-1], around[1:], 0.25)
    down = jnp.where(first, jnp.broadcast_to(m_ylow, shape), lower(m, 1))
    up = jnp.where(last, jnp.broadcast_to(m_yhigh, shape), upper(m, 1))
    w_down = harmonic(m, down, 0.25)
    w_up = jnp.where(last, harmonic(m, up, 0.25), upper(w_down, 1))
    w_back = jnp.where(lane == 0, 0.0, harmonic(m, lower(m, 2), 0.25))
    w_front = upper(w_back, 2)
    outside = as_float(lane == 0) + as_float(lane == depth - 1)
    for b in (down, up, around[:-2], around[2:]):
        outside = outside + as_float(b <= 0.0)
    diagonal = faces[:-1] + faces[1:] + w_down + w_up + w_back + w_front + 0.25 * m * outside
    e = DAMPING * s * invert(diagonal)
    y_low, y_high = w_down * e, w_up * e
    t = KEPT * s + w_back * lower(e, 2) + w_front * upper(e, 2)
    t = t + jnp.where(first, 0.0, w_down * lower(e, 1)) + jnp.where(last, 0.0, w_up * upper(e, 1))
    nothing = jnp.zeros((1, r1, depth), F32)
    t = t + faces[:-1] * jnp.concatenate([nothing, e[:-1]], axis=0) + faces[1:] * jnp.concatenate([e[1:], nothing], axis=0)
    base = c2 // 2 * r1

    def pairs(x):
        x = x.reshape(c2, 2, r1, depth)
        return (x[:, 0] + x[:, 1]).reshape(c2 * r1, depth)

    t, m = pairs(t), pairs(m)
    for n in range(2):
        wide[n, :base] = t[n * base : (n + 1) * base]
        wide[n, base + 2 * r1 :] = m[n * base : (n + 1) * base]
    wide[0, base : base + r1] = faces[0] * e[0]
    wide[0, base + r1 : base + 2 * r1] = faces[c1] * e[c1 - 1]
    for k in range(c1):
        wide[1, base + k : base + k + 1] = y_low[k, :1]
        wide[1, base + r1 + k : base + r1 + k + 1] = y_high[k, r1 - 1 :]
    publish(wide[0], wide[1], narrow, sheet, payload, semaphore)


def packed(low, high, narrow):
    narrow[...] = (select(low, pair_matrix(LANES)) + select(high, pair_matrix(LANES, LANES // 2))) * 0.125
    half = narrow.shape[0] // 2
    return narrow[pl.ds(0, half, 2)] + narrow[pl.ds(1, half, 2)]


def publish(low, high, narrow, sheet, payload, semaphore):
    sheet[...] = jnp.broadcast_to(packed(low, high, narrow)[None], sheet.shape)
    leaving = pltpu.make_async_copy(sheet, payload, semaphore)
    leaving.start()
    leaving.wait()


def strips_kernel(place, residual, material, coarse, even, odd, inner, outer, long_far, long1, long, semaphore):
    low_x, low_y = place[0] == 1, place[1] == 1
    count, rows, depth = residual.shape
    pieces = depth // LANES
    c1, r1 = count // 2, rows // 2
    base = count * pieces

    def sides(at):
        a, b = even[at], odd[at]
        return jnp.where(low_y, a, b), jnp.where(low_y, b, a)

    for i in range(count):
        for piece in range(pieces):
            low, high = sides(i * pieces + piece)
            z = slice(piece * LANES, (piece + 1) * LANES)
            long[0, i, :, z] = jnp.concatenate([low[:4], residual[i, :, z], high[:4]], axis=0)
            long[1, i, :, z] = jnp.concatenate([low[4:], material[i, :, z], high[4:]], axis=0)
    leaving = pltpu.make_async_copy(long, long_far, semaphore)
    leaving.start()
    for k in range(c1):
        low, high = sides(base + k)
        s, m = coarse[k * r1 : (k + 1) * r1], coarse[(c1 + k) * r1 : (c1 + k + 1) * r1]
        long1[0, k] = jnp.concatenate([low[:4], s, high[:4]], axis=0)
        long1[1, k] = jnp.concatenate([low[4:], m, high[4:]], axis=0)

    def pack(out, flag):
        at = 0
        for n, planes in ((0, 3), (1, 4)):
            start = jnp.where(flag, 0, count - planes)
            for k in range(planes):
                for tile in range((rows + 8) // 8):
                    for piece in range(pieces):
                        out[at] = long[n, start + k, tile * 8 : tile * 8 + 8, piece * LANES : (piece + 1) * LANES]
                        at += 1
        for n, planes in ((0, 3), (1, 4)):
            for k in range(planes):
                low, high = k, c1 - planes + k
                for tile in range((r1 + 8) // 8):
                    y = slice(tile * 8, tile * 8 + 8)
                    out[at] = jnp.where(flag, long1[n, low, y], long1[n, high, y])
                    at += 1

    pack(inner, low_x)
    pack(outer, jnp.logical_not(low_x))
    leaving.wait()


def unpack(source, flag, out, start, planes, tiles, pieces, at):
    for n in range(planes):
        for tile in range(tiles):
            for piece in range(pieces):
                value = jnp.where(flag, source[0][at], source[1][at])
                out[start + n, tile * 8 : tile * 8 + 8, piece * LANES : (piece + 1) * LANES] = value
                at += 1
    return at


def smooth_kernel(ends, place, potential_far, state_far, long, outer, inner, out, state, mat, res, x, d, fx, fy, fz, inv, potential, semaphores):
    arriving = pltpu.make_async_copy(potential_far, potential, semaphores.at[0])
    arriving.start()
    passing = pltpu.make_async_copy(state_far, state, semaphores.at[1])
    passing.start()
    count, rows, depth = potential.shape
    own = pl.ds(4, count)
    frames = [
        pltpu.make_async_copy(long.at[n], ref.at[own], semaphores.at[2 + n]) for n, ref in enumerate((res, mat))
    ]
    for copy in frames:
        copy.start()
    low_x = place[0] == 1
    count, rows, depth = potential.shape
    pieces, tiles = depth // LANES, (rows + 8) // 8
    both = (inner, outer)
    for flag, start_r, start_m in ((low_x, 1, 0), (jnp.logical_not(low_x), count + 4, count + 4)):
        at = unpack(both, flag, res, start_r, 3, tiles, pieces, 0)
        unpack(both, flag, mat, start_m, 4, tiles, pieces, at)
    for copy in frames:
        copy.wait()
    total, length = count + 8, rows + 8
    row, lane = iota((length, depth), 0), iota((length, depth), 1)
    outside = as_float(lane == 0) + as_float(lane == depth - 1)
    outside = outside + as_float((row == 4) & (place[3] == 0)) + as_float((row == rows + 3) & (place[3] == ends[1] - 1))
    low_end, high_end = place[2] == 0, place[2] == ends[0] - 1

    def chunks(first, last, step):
        return [(at, min(step, last - at)) for at in range(first, last, step)]

    for at, n in chunks(1, total - 1, SMOOTH_STEP):
        here = slice(at, at + n)
        a = mat[here]
        faces = harmonic(mat[at - 1 : at + n], mat[at : at + n + 1], 1.0)
        w_down = harmonic(a, lower(a, 1), 1.0)
        w_back = jnp.where(lane[None] == 0, 0.0, harmonic(a, lower(a, 2), 1.0))
        plane = at + iota((n, 1, 1), 0)
        edges = outside[None] + as_float((plane == 4) & low_end) + as_float((plane == count + 3) & high_end)
        diagonal = faces[:-1] + faces[1:] + w_down + upper(w_down, 1) + w_back + upper(w_back, 2) + a * edges
        inverse = jnp.where(a > 0.0, invert(jnp.maximum(diagonal, 1e-3)), 0.0)
        fx[at : at + n + 1], fy[here], fz[here], inv[here] = faces, w_down, w_back, inverse
        scaled = inverse * res[here]
        res[here] = scaled
        x[0, here] = scaled * (1.0 / THETA)
    rho = 1.0 / SIGMA
    for turn in range(DEG - 1):
        if turn == DEG - 2:
            arriving.wait()
        following = 1.0 / (2.0 * SIGMA - rho)
        old, new = turn % 2, (turn + 1) % 2
        keep, gain = following * rho, 2.0 * following / DELTA
        for at, n in chunks(2 + turn, total - 2 - turn, SMOOTH_STEP):
            here = slice(at, at + n)
            v = x[old, here]
            w_down, w_back = fy[here], fz[here]
            off = fx[here] * x[old, at - 1 : at + n - 1] + fx[at + 1 : at + n + 1] * x[old, at + 1 : at + n + 1]
            off = off + w_down * lower(v, 1) + upper(w_down * v, 1)
            off = off + w_back * lower(v, 2) + upper(w_back * v, 2)
            before = v * keep if turn == 0 else d[here] * keep
            change = before + gain * (res[here] - v + inv[here] * off)
            if turn == DEG - 2:
                out[at - 4 : at + n - 4] = potential[at - 4 : at + n - 4] + (v + change)[:, 4 : 4 + rows]
            else:
                d[here] = change
                x[new, here] = v + change
        rho = following
    passing.wait()


def each(count, body, most=8):
    step = min(count, most)
    if count // step <= 4:
        for n in range(count // step):
            body(n * step, step)
        return

    def run(n, _):
        body(n * step, step)
        return 0

    lax.fori_loop(0, count // step, run, 0)


def fill_table(mat, table, level, count, base, width):
    stride, scale = 2**level, 0.25 ** (level + 2)
    rows = mat.shape[1]
    row, lane = iota((rows, LANES), 0), iota((rows, LANES), 1)
    above, beyond = row >= stride, lane >= stride
    outside = as_float(row == 0) + as_float(row == rows - stride) + as_float(lane == 0) + as_float(lane == width - stride)

    def body(at, step):
        a, before, ahead = mat[pl.ds(at + 1, step)], mat[pl.ds(at, step)], mat[pl.ds(at + 2, step)]
        w_before, w_ahead = harmonic(a, before, scale), harmonic(a, ahead, scale)
        w_down = jnp.where(above[None], harmonic(a, lower(a, 1, stride), scale), 0.0)
        w_back = jnp.where(beyond[None], harmonic(a, lower(a, 2, stride), scale), 0.0)
        plane = at + iota((step, 1, 1), 0)
        edges = outside[None] + as_float(plane == 0) + as_float(plane == count - 1)
        diagonal = w_before + w_ahead + w_down + upper(w_down, 1, stride) + w_back + upper(w_back, 2, stride)
        diagonal = diagonal + scale * a * edges
        table[0, pl.ds(base + at, step)] = w_before
        table[1, pl.ds(base + at, step)] = w_down
        table[2, pl.ds(base + at, step)] = w_back
        table[3, pl.ds(base + at, step)] = jnp.where(a > 0.0, invert(jnp.maximum(diagonal, 1e-4)), 0.0)

    each(count, body)
    table[0, base + count] = jnp.zeros((rows, LANES), F32)


def fold(t, stride):
    a = t.reshape(t.shape[0] // 2, 2, *t.shape[1:])
    a = a[:, 0] + a[:, 1]
    a = a + upper(a, 1, stride)
    return a + upper(a, 2, stride)


def unfold(e, stride):
    e = e + lower(e, 1, stride)
    e = e + lower(e, 2, stride)
    return jnp.broadcast_to(e[:, None], (e.shape[0], 2, *e.shape[1:])).reshape(2 * e.shape[0], *e.shape[1:])


def off_diagonal(e, table, base, at, step, stride):
    v = e[pl.ds(at + 1, step)]
    total = table[0, pl.ds(base + at, step)] * e[pl.ds(at, step)]
    total = total + table[0, pl.ds(base + at + 1, step)] * e[pl.ds(at + 2, step)]
    fy, fz = table[1, pl.ds(base + at, step)], table[2, pl.ds(base + at, step)]
    total = total + fy * lower(v, 1, stride) + upper(fy * v, 1, stride)
    return v, total + fz * lower(v, 2, stride) + upper(fz * v, 2, stride)


def cycle(s, e, t, table, counts, bases, place, out, c2, r2, pad):
    zero = jnp.zeros(t.shape[1:], F32)
    for ref, count in zip(e, counts):
        ref[0] = zero
        ref[count + 1] = zero
    for level, (count, base) in enumerate(zip(counts, bases)):
        s_l, e_l, stride = s[level], e[level], 2**level

        def start(at, step):
            e_l[pl.ds(at + 1, step)] = DAMPING * s_l[pl.ds(at + 1, step)] * table[3, pl.ds(base + at, step)]

        each(count, start)
        if level == len(counts) - 1:
            break

        def remainder(at, step):
            _, off = off_diagonal(e_l, table, base, at, step, stride)
            left = KEPT * s_l[pl.ds(at + 1, step)] + off
            s[level + 1][pl.ds(at // 2 + 1, step // 2)] = 0.125 * fold(left, stride)

        each(count, remainder)

    def relax(s_l, source, target, base, count, stride):
        def sweep(at, step):
            v, off = off_diagonal(source, table, base, at, step, stride)
            inverse = table[3, pl.ds(base + at, step)]
            target[pl.ds(at + 1, step)] = KEPT * v + DAMPING * inverse * (s_l[pl.ds(at + 1, step)] + off)

        each(count, sweep)

    t[0] = zero
    t[counts[2] + 1] = zero
    now, other = e[2], t
    for _ in range(COARSE_SWEEPS - 1):
        relax(s[2], now, other, bases[2], counts[2], 4)
        now, other = other, now

    def add(at, step):
        e[1][pl.ds(2 * at + 1, 2 * step)] = e[1][pl.ds(2 * at + 1, 2 * step)] + unfold(now[pl.ds(at + 1, step)], 2)

    each(counts[2], add, 4)
    if now is t:
        now = e[2] = s[1]
    relax(s[1], e[1], t, bases[1], counts[1], 2)

    planes = c2 + 4
    begin = place[2] * c2 - 2
    inside = jnp.clip(begin, 0, counts[0] - planes)
    coarse = jnp.clip(place[2] * c2 // 2 - 2, 0, counts[1] - planes // 2 - 2)
    number = planes // 2 + 2
    at = pl.ds(2 * coarse + 1, 2 * number)
    e[0][at] = e[0][at] + unfold(t[pl.ds(coarse + 1, number)], 1)
    v, off = off_diagonal(e[0], table, bases[0], inside, planes, 1)
    inverse = table[3, pl.ds(bases[0] + inside, planes)]
    pad[...] = jnp.zeros(pad.shape, F32)
    rows = t.shape[1]
    value = KEPT * v + DAMPING * inverse * (s[0][pl.ds(inside + 1, planes)] + off)
    pad[pl.ds(2 + inside - begin, planes), 8 : 8 + rows, :] = value
    for n in range(planes):
        out[n] = pad[n + 2, pl.ds(place[3] * r2 + 6, r2 + 4), :]


def cycle_shapes(counts, rows, c2):
    out = [pltpu.VMEM((count + 2, rows, LANES), F32) for count in (*counts, *counts, counts[0])]
    return out + [pltpu.VMEM((c2 + 8, rows + 16, LANES), F32)]


def repeat(count, body):
    if count <= 8:
        for i in range(count):
            body(i, i % 2)
        return

    def two(n, _):
        body(2 * n, 0)
        body(2 * n + 1, 1)

    lax.fori_loop(0, count // 2, two, None)


def spread_blocks(fetch, outs, grid, c2, r2):
    gx, gy = grid
    length = c2 // 2 * r2
    low = iota((length, LANES), 1) < LANES // 2

    def column(i, parity):
        for j in range(gy):
            for start, out in outs:
                block = fetch(i, parity, j, slice(start, start + length))
                parts = (jnp.where(low, block, 0.0), jnp.where(low, pltpu.roll(block, LANES // 2, 1), 0.0))
                for k in range(c2):
                    n = k % (c2 // 2)
                    out[i * c2 + k + 1, j * r2 : (j + 1) * r2, :] = parts[k // (c2 // 2)][n * r2 : (n + 1) * r2]

    repeat(gx, column)


def clear_ends(refs, counts):
    for ref, count in zip(refs, counts):
        zero = jnp.zeros(ref.shape[1:], F32)
        ref[0] = zero
        ref[count + 1] = zero


def pass_kernel(blocks, _, out):
    out[...] = blocks[...]


def first_cycle_kernel(counts, bases, grid, c2, r2, width, place, mine, theirs, out, table, *scratch):
    s, e, t, pad = scratch[0:3], list(scratch[3:6]), scratch[6], scratch[7]
    gx, gy = grid
    rows = gy * r2
    half = LANES // 2
    own = c2 // 2 * r2
    clear_ends((t, *s), (counts[0], *counts))
    odd = place[0] == 1

    def fetch(i, parity, j, at):
        here = i // 2 * gy + j
        a, b = mine[here, at], theirs[here, at]
        return jnp.where(odd, b, a) if parity == 0 else jnp.where(odd, a, b)

    spread_blocks(fetch, ((0, s[0]), (own + 2 * r2, t)), grid, c2, r2)
    face_y = e[0]
    low = iota((2 * c2, LANES), 1) < half

    def edges(i, parity):
        for j in range(gy):
            faces = fetch(i, parity, j, slice(own, own + 2 * r2))
            x_faces = jnp.where(low, faces, 0.0)
            y_faces = jnp.where(low, pltpu.roll(faces, half, 1), 0.0)
            here = slice(j * r2, (j + 1) * r2)
            s[0][i * c2, here, :] = s[0][i * c2, here, :] + x_faces[:r2]
            s[0][(i + 1) * c2 + 1, here, :] = s[0][(i + 1) * c2 + 1, here, :] + x_faces[r2:]
            for k in range(c2):
                at = i * c2 + k + 1
                if j > 0:
                    face_y[at, j * r2 - 1 : j * r2, :] = y_faces[k : k + 1]
                if j < gy - 1:
                    face_y[at, (j + 1) * r2 : (j + 1) * r2 + 1, :] = y_faces[c2 + k : c2 + k + 1]

    repeat(gx, edges)

    def join(at, step):
        now = pl.ds(at + 1, step)
        row = iota((rows, LANES), 0)
        edge = ((row % r2 == 0) & (row > 0)) | ((row % r2 == r2 - 1) & (row < rows - 1))
        s[0][now] = s[0][now] + jnp.where(edge[None], face_y[now], 0.0)

    each(counts[0], join)
    clear_ends(s[:1], counts)
    mats = (t, s[1], s[2])
    for level, (count, base) in enumerate(zip(counts, bases)):
        if level:

            def coarsen(at, step):
                whole = (iota((rows, LANES), 0) % 2**level == 0) & (iota((rows, LANES), 1) % 2**level == 0)
                mean = 0.125 * fold(mats[level - 1][pl.ds(at + 1, step)], 2 ** (level - 1))
                mats[level][pl.ds(at // 2 + 1, step // 2)] = jnp.where(whole[None], mean, 0.0)

            each(counts[level - 1], coarsen)
        fill_table(mats[level], table, level, count, base, width)
    cycle(s, e, t, table, counts, bases, place, out, c2, r2, pad)


def shifted(a):
    zero = jnp.zeros_like(a[:1])
    return jnp.concatenate([zero, a[:-1]], axis=0), jnp.concatenate([a[1:], zero], axis=0)


def apply_off(e, fx, fy, fz):
    before, ahead = shifted(e)
    out = fx[:-1] * before + fx[1:] * ahead
    out = out + fy * lower(e, 1) + upper(fy * e, 1)
    return out + fz * lower(e, 2) + upper(fz * e, 2)


def raise_window(window_ref, flat, out):
    planes, rows, _ = window_ref.shape
    values = select(window_ref[...].reshape(planes * rows, LANES), spread_matrix(LANES))
    flat[pl.ds(0, planes * rows, 2)] = values
    flat[pl.ds(1, planes * rows, 2)] = values
    v = flat[...].reshape(planes, 1, 2 * rows, LANES)
    out[...] = jnp.broadcast_to(v, (planes, 2, 2 * rows, LANES)).reshape(2 * planes, 2 * rows, LANES)


def level1_kernel(
    offset, place, long1, outer, inner, window1, payload, state_far,
    src, mat, flat, prolonged, fx, fy, fz, diag, inv, err, c, state, wide, narrow, sheet, semaphores,
):
    low_x = place[0] == 1
    total, length, depth = src.shape
    count, rows = total - 8, length - 8
    both = (inner, outer)
    zero = jnp.zeros((length, depth), F32)
    src[0] = zero
    src[total - 1] = zero
    for flag, start_s, start_m in ((low_x, 1, 0), (jnp.logical_not(low_x), count + 4, count + 4)):
        at = unpack(both, flag, src, start_s, 3, length // 8, 1, offset)
        unpack(both, flag, mat, start_m, 4, length // 8, 1, at)
    for n, ref in enumerate((src, mat)):
        ref[pl.ds(4, count)] = long1[n]
    raise_window(window1, flat, prolonged)
    row, lane = iota((length, depth), 0), iota((length, depth), 1)
    ends = as_float(lane == 0) + as_float(lane == depth - 1)
    def chunks(margin):
        first, last = margin, total - margin
        return [(at, min(LEVEL1_STEP, last - at)) for at in range(first, last, LEVEL1_STEP)]

    for at, n in chunks(1):
        here = slice(at, at + n)
        a, before, ahead = mat[here], mat[at - 1 : at + n - 1], mat[at + 1 : at + n + 1]
        down, up = lower(a, 1), upper(a, 1)
        f = harmonic(mat[at - 1 : at + n], mat[at : at + n + 1], 0.25)
        w_y = harmonic(a, down, 0.25)
        w_z = jnp.where(lane[None] == 0, 0.0, harmonic(a, lower(a, 2), 0.25))
        outside = ends[None] + as_float(before <= 0.0) + as_float(ahead <= 0.0) + as_float(down <= 0.0) + as_float(up <= 0.0)
        diagonal = f[:-1] + f[1:] + w_y + upper(w_y, 1) + w_z + upper(w_z, 2) + 0.25 * a * outside
        inverse = jnp.where(a > 0.0, invert(jnp.maximum(diagonal, 1e-4)), 0.0)
        fx[at : at + n + 1], fy[here], fz[here], diag[here], inv[here] = f, w_y, w_z, diagonal, inverse
        err[here] = DAMPING * inverse * src[here] + prolonged[here]

    def off(v, at, n):
        here = slice(at, at + n)
        mid, w_y, w_z = v[here], fy[here], fz[here]
        out = fx[here] * v[at - 1 : at + n - 1] + fx[at + 1 : at + n + 1] * v[at + 1 : at + n + 1]
        out = out + w_y * lower(mid, 1) + upper(w_y * mid, 1)
        return here, mid, out + w_z * lower(mid, 2) + upper(w_z * mid, 2)

    for at, n in chunks(2):
        here, mid, more = off(err, at, n)
        c[here] = KEPT * mid + DAMPING * inv[here] * (src[here] + more)
    for at, n in chunks(3):
        here, mid, more = off(c, at, n)
        left = src[here] - diag[here] * mid + more
        src[here] = left
        value = DAMPING * inv[here] * left
        err[here] = value
        state[at - 3 : at + n - 3] = value
    base = count + 2
    state[base : base + count + 1] = fx[4 : count + 5]
    base += count + 1
    for n, ref in enumerate((fy, fz, inv, c, src)):
        state[base + n * count : base + (n + 1) * count] = ref[4 : 4 + count]
    leaving = pltpu.make_async_copy(state, state_far, semaphores.at[0])
    leaving.start()
    here, _, more = off(err, 4, count)
    t = (KEPT * src[here] + more)[:, 4 : 4 + rows].reshape(count // 2, 2, rows, depth)
    wide[...] = (t[:, 0] + t[:, 1]).reshape(count // 2 * rows, depth)
    half = wide.shape[0] // 2
    publish(wide[:half], wide[half:], narrow, sheet, payload, semaphores.at[1])
    leaving.wait()


def last_cycle_kernel(counts, bases, grid, c2, r2, place, blocks, table, state, partial, out, *scratch):
    s, e, t, pad = scratch[0:3], list(scratch[3:6]), scratch[6], scratch[7]
    view, flat, prolonged, tall, coarse, result, departures = scratch[8:15]
    spread_blocks(lambda i, _, j, at: blocks[grid[0] * grid[1] - 1 - i * grid[1] - j, at], ((0, s[0]),), grid, c2, r2)
    clear_ends(s, counts)
    cycle(s, e, t, table, counts, bases, place, view, c2, r2, pad)
    raise_window(view, flat, prolonged)
    count, rows, depth = partial.shape
    c1, r1 = count // 2, rows // 2
    v = prolonged[3 : c1 + 5] + state[: c1 + 2]
    here = v[1:-1]
    base = 2 * c1 + 3
    w_x = state[c1 + 2 : base]
    w_y, w_z, inverse, before, left = (state[base + n * c1 : base + (n + 1) * c1] for n in range(5))
    off = w_x[:-1] * v[:-2] + w_x[1:] * v[2:]
    off = off + w_y * lower(here, 1) + upper(w_y * here, 1) + w_z * lower(here, 2) + upper(w_z * here, 2)
    total = before + KEPT * here + DAMPING * inverse * (left + off)
    coarse[...] = total[:, 4 : 4 + r1].reshape(c1 * r1, LANES)
    values = select(coarse[...], spread_matrix(depth))
    for piece in range(depth // LANES):
        z = slice(piece * LANES, (piece + 1) * LANES)
        tall[piece, pl.ds(0, c1 * r1, 2)] = values[:, z]
        tall[piece, pl.ds(1, c1 * r1, 2)] = values[:, z]
    leaving = []
    for k in range(c1):
        for piece in range(depth // LANES):
            z = slice(piece * LANES, (piece + 1) * LANES)
            more = tall[piece, k * rows : (k + 1) * rows]
            result[2 * k, :, z] = partial[2 * k, :, z] + more
            result[2 * k + 1, :, z] = partial[2 * k + 1, :, z] + more
        if k % 2 == 1:
            planes = pl.ds(2 * k - 2, 4)
            leaving.append(pltpu.make_async_copy(result.at[planes], out.at[planes], departures.at[k // 2]))
            leaving[-1].start()
    for copy in leaving:
        copy.wait()


def size_of(shape):
    lead = math.prod(shape[:-2])
    return 4 * lead * (-(-shape[-2] // 8) * 8) * (-(-shape[-1] // LANES) * LANES)


def call(kernel, name, inputs, outputs, scratch=(), apart=(), cost=None):
    streamed = 0

    def held(n, x):
        nonlocal streamed
        if n in apart:
            return pltpu.with_memory_space_constraint(x, pltpu.HBM)
        if x.ndim == 1:
            return x
        if size_of(x.shape) <= HELD:
            return pltpu.with_memory_space_constraint(x, pltpu.VMEM)
        streamed += size_of(x.shape)
        return x

    def result(shape):
        nonlocal streamed
        if isinstance(shape, jax.ShapeDtypeStruct):
            streamed += size_of(shape.shape)
            return shape
        if far(shape):
            return pltpu.HBM(shape[1], F32)
        if size_of(shape) <= HELD:
            return pltpu.VMEM(shape, F32)
        streamed += size_of(shape)
        return jax.ShapeDtypeStruct(shape, F32)

    def far(x):
        return isinstance(x, tuple) and x[0] == "far"

    def space(n, x):
        return pltpu.HBM if n in apart else pltpu.SMEM if x.ndim == 1 else pltpu.VMEM

    specs = [pl.BlockSpec(memory_space=space(n, x)) for n, x in enumerate(inputs)]
    inputs = [held(n, x) for n, x in enumerate(inputs)]
    results = [result(shape) for shape in outputs]
    need = streamed + sum(size_of(x.shape) for x in scratch if len(getattr(x, "shape", ())) > 1) + 3 * MIB
    return pl.pallas_call(
        kernel,
        out_shape=results,
        in_specs=specs,
        out_specs=[pl.BlockSpec(memory_space=pltpu.HBM if far(x) else pltpu.VMEM) for x in outputs],
        scratch_shapes=list(scratch),
        compiler_params=pltpu.CompilerParams(vmem_limit_bytes=max(need, 8 * MIB)),
        name=name,
        cost_estimate=None if cost is None else pl.CostEstimate(flops=cost, bytes_accessed=0, transcendentals=0),
    )(*inputs)


def swaps(count):
    inner = [(i, i + 1) for i in range(0, count - 1, 2)]
    outer = [(i, i + 1) for i in range(1, count - 1, 2)]
    return [pairs + [(b, a) for a, b in pairs] for pairs in (inner, outer)]


def local(right_side, potential, phase, permeability):
    gx, gy = lax.axis_size("gx"), lax.axis_size("gy")
    devices = gx * gy
    here_x, here_y = lax.axis_index("gx"), lax.axis_index("gy")
    place = jnp.stack([here_x % 2, here_y % 2, here_x, here_y]).astype(jnp.int32)
    count, rows, depth = right_side.shape
    c1, r1, d1 = count // 2, rows // 2, depth // 2
    c2, r2 = c1 // 2, r1 // 2
    pieces = depth // LANES
    swap_x, swap_y = swaps(gx), swaps(gy)
    VM = lambda *shape: pltpu.VMEM(shape, F32)

    brick = (count, rows, depth)
    face = (3, rows, depth)
    DMA = pltpu.SemaphoreType.DMA
    sheet = (devices, c2 // 2 * r2, LANES)
    sheet2 = (devices // 2, c2 * r2 + 2 * r2, LANES)
    material, potential_here, source_here, inner, outer, even, odd = call(
        faces_kernel, "faces", (place, permeability, potential, phase, right_side),
        (brick, brick, brick, face, face, (3, count, depth), (3, count, depth)),
        (pltpu.VMEM(brick, jnp.int32), pltpu.SMEM(permeability.shape, F32), pltpu.SemaphoreType.DMA((4,))),
        apart=(1, 2, 3, 4),
    )
    even = lax.ppermute(even, "gy", swap_y[0])
    odd = lax.ppermute(odd, "gy", swap_y[1])
    outer = lax.ppermute(outer, "gx", swap_x[1])
    inner = lax.ppermute(inner, "gx", swap_x[0])

    strip = (count * pieces + c1, 8, LANES)
    total = 2 * c1 * rows + 4 * rows
    residual, coarse, even, odd = call(
        residual_kernel, "residual", (place, source_here, potential_here, material, outer, even, odd, inner),
        (brick, (total // 2, LANES), strip, strip),
        (
            VM(total, depth), VM(total, LANES), VM(4, count, 8, depth), VM(count + 2, rows, depth), VM(count + 2, rows, depth),
        ),
    )
    even = lax.ppermute(even, "gy", swap_y[0])
    odd = lax.ppermute(odd, "gy", swap_y[1])
    small = c2 * r1 + 2 * r1
    (payload,) = call(
        functools.partial(payload_kernel, c1, r1), "payload", (coarse,), (("far", sheet2),),
        (VM(2, small, d1), VM(small, LANES), VM(*sheet2), DMA),
    )
    groups = [[(2 * i + c) * gy + j for i in range(gx // 2) for j in range(gy)] for c in range(2)]
    blocks = lax.all_to_all(payload, ("gx", "gy"), 0, 0, axis_index_groups=groups)
    tiles, tiles1 = (rows + 8) // 8, (r1 + 8) // 8
    strip = (7 * tiles * pieces + 7 * tiles1, 8, LANES)
    long_shape = (2, count, rows + 8, depth)
    inner, outer, long, long1 = call(
        strips_kernel, "strips", (place, residual, material, coarse, even, odd),
        (strip, strip, ("far", long_shape), (2, c1, r1 + 8, d1)),
        (VM(*long_shape), DMA), cost=10**11,
    )
    outer = lax.ppermute(outer, "gx", swap_x[1])
    inner = lax.ppermute(inner, "gx", swap_x[0])

    (blocks,) = call(pass_kernel, "pass", (blocks, long1), (sheet2,))
    others = lax.ppermute(blocks, "gx", swap_x[0])
    counts = tuple(gx * c2 // k for k in (1, 2, 4))
    bases = (0, counts[0] + 1, counts[0] + counts[1] + 2)
    work = cycle_shapes(counts, gy * r2, c2)
    view = (c2 + 4, r2 + 4, LANES)
    window1, table = call(
        functools.partial(first_cycle_kernel, counts, bases, (gx, gy), c2, r2, d1 // 2), "cycle1", (place, blocks, others),
        (view, (4, sum(counts) + 3, gy * r2, LANES)), work,
    )
    frame = (c1 + 8, r1 + 8, d1)
    flat = VM((c2 + 4) * (r2 + 4) * 2, LANES)
    state = (7 * c1 + 3, r1 + 8, d1)
    tall = VM(c1 + 9, r1 + 8, d1)
    payload, held = call(
        functools.partial(level1_kernel, 7 * tiles * pieces), "level1", (place, long1, outer, inner, window1), (("far", sheet), ("far", state)),
        (
            VM(*frame), VM(*frame), flat, VM(*frame), tall, VM(*frame), VM(*frame), VM(*frame), VM(*frame), VM(*frame),
            VM(*frame), VM(*state), VM(c1 // 2 * r1, d1), VM(c1 // 4 * r1, LANES), VM(*sheet), pltpu.SemaphoreType.DMA((2,)),
        ),
    )
    blocks = lax.all_to_all(payload, ("gx", "gy"), 0, 0, axis_index_groups=[list(range(devices))[::-1]])
    wide = (count + 8, rows + 8, depth)
    partial, held = call(
        functools.partial(smooth_kernel, (gx, gy)), "smooth", (place, potential, held, long, outer, inner), (brick, state),
        (
            VM(*wide), VM(*wide), VM(2, *wide), VM(*wide), VM(count + 9, rows + 8, depth), VM(*wide), VM(*wide), VM(*wide),
            VM(*brick), pltpu.SemaphoreType.DMA((4,)),
        ),
        apart=(1, 2, 3),
    )
    (out,) = call(
        functools.partial(last_cycle_kernel, counts, bases, (gx, gy), c2, r2), "cycle2",
        (place, blocks, table, held, partial), (("far", brick),),
        (
            *work, VM(*view), flat, VM(*frame), VM(pieces, c1 * rows, LANES), VM(c1 * r1, LANES), VM(*brick),
            pltpu.SemaphoreType.DMA((c1 // 2,)),
        ),
    )
    return out


def solution(mesh):
    placed = (P("gx", "gy", None), P("gx", "gy", None), P("gx", "gy", None), P())
    return jax.shard_map(local, mesh=mesh, in_specs=placed, out_specs=P("gx", "gy", None), check_vma=False)
```

```python
import functools
import math

import jax
import jax.numpy as jnp
from jax import lax
from jax.experimental import pallas as pl
from jax.experimental.pallas import tpu as pltpu
from jax.sharding import PartitionSpec as P

DEG = 4
COARSE_SWEEPS = 4
THETA = 1.15
DELTA = 0.85
SIGMA = 1.15 / 0.85
DAMPING = 0.6
KEPT = 1.0 - DAMPING
F32 = jnp.float32
LANES = 128
MIB = 1024 * 1024
HELD = 4 * MIB
SMOOTH_STEP = 4
LEVEL1_STEP = 7


def iota(shape, axis):
    return lax.broadcasted_iota(jnp.int32, shape, axis)


def invert(x):
    guess = pl.reciprocal(x, approx=True)
    return guess * (2.0 - x * guess)


def harmonic(a, b, scale):
    return (2.0 * scale) * a * b * invert(jnp.maximum(a + b, 1e-3))


def pair_matrix(size, offset=0):
    column = iota((size, LANES), 1)
    return ((column >= offset) & (iota((size, LANES), 0) // 2 == column - offset)).astype(jnp.bfloat16)


def spread_matrix(width):
    return (iota((LANES, width), 1) // 2 == iota((LANES, width), 0)).astype(jnp.bfloat16)


def select(values, matrix):
    high = values.astype(jnp.bfloat16)
    rest = (values - high.astype(F32)).astype(jnp.bfloat16)
    return jnp.dot(high, matrix, preferred_element_type=F32) + jnp.dot(rest, matrix, preferred_element_type=F32)


def lower(x, axis, stride=1):
    return pltpu.roll(x, stride, axis)


def upper(x, axis, stride=1):
    return pltpu.roll(x, x.shape[axis] - stride, axis)


def as_float(condition):
    return jnp.where(condition, 1.0, 0.0)


def faces_kernel(
    place, permeability, potential, phase, source,
    material, pot, src, inner, outer, even, odd,
    ids, values, semaphores,
):
    arriving = [
        pltpu.make_async_copy(a, b, semaphores.at[n])
        for n, (a, b) in enumerate(((permeability, values), (phase, ids), (potential, pot), (source, src)))
    ]
    for copy in arriving:
        copy.start()
    low_x, low_y = place[0] == 1, place[1] == 1
    count, rows = pot.shape[:2]
    arriving[0].wait()
    arriving[1].wait()
    p0, p1, p2 = values[0], values[1], values[2]
    for i in range(count):
        here = ids[i]
        material[i] = jnp.where(here == 0, p0, jnp.where(here == 1, p1, p2))
    last = count - 1
    first = jnp.where(low_x, 0, last)
    second = jnp.where(low_x, 1, last - 1)
    inner[1] = material[first]
    inner[2] = material[second]
    outer[1] = material[last - first]
    outer[2] = material[last - second]

    def edge(slot, ref, a, b):
        for i in range(count):
            low, high = ref[i, a : a + 1, :], ref[i, b : b + 1, :]
            even[slot, i : i + 1, :] = jnp.where(low_y, low, high)
            odd[slot, i : i + 1, :] = jnp.where(low_y, high, low)

    edge(1, material, 0, rows - 1)
    edge(2, material, 1, rows - 2)
    arriving[2].wait()
    inner[0] = pot[first]
    outer[0] = pot[last - first]
    edge(0, pot, 0, rows - 1)
    arriving[3].wait()


def residual_kernel(
    place, source, potential, material, outer, even, odd, inner,
    residual, coarse, strip_even, strip_odd,
    wide, narrow, y_faces, mat, pot,
):
    low_x, low_y = place[0] == 1, place[1] == 1
    count, rows, depth = source.shape
    c1, r1 = count // 2, rows // 2
    pieces = depth // LANES

    def ordered(flag, a, b):
        return jnp.where(flag, a, b), jnp.where(flag, b, a)

    x_low, x_high = ordered(low_x, inner[...], outer[...])
    y_low, y_high = ordered(low_y, even[...], odd[...])
    row, lane = iota((rows, depth), 0), iota((rows, depth), 1)
    first, last = row == 0, row == rows - 1
    for n, ref in enumerate((y_low[0], y_high[0], y_low[1], y_high[1])):
        for i in range(count):
            y_faces[n, i] = jnp.broadcast_to(ref[i : i + 1], (8, depth))
    mat[0], mat[count + 1] = x_low[1], x_high[1]
    pot[0], pot[count + 1] = x_low[0], x_high[0]
    mat[pl.ds(1, count)] = material[...]
    pot[pl.ds(1, count)] = potential[...]
    step = 4
    outside = as_float(lane == 0) + as_float(lane == depth - 1)

    def edge_count(faces):
        return as_float(faces[:1, :1] <= 0.0)

    outside = outside + jnp.where(first, edge_count(y_low[1]), 0.0) + jnp.where(last, edge_count(y_high[1]), 0.0)

    def beside(ref, n, at):
        return jnp.broadcast_to(ref[n, at : at + step, :1], (step, rows, depth))

    for at in range(0, count, step):
        here = slice(at + 1, at + 1 + step)
        a, v = mat[here], pot[here]
        faces = harmonic(mat[at : at + step + 1], mat[at + 1 : at + step + 2], 1.0)
        down = jnp.where(first[None], beside(y_faces, 2, at), lower(a, 1))
        w_down = harmonic(a, down, 1.0)
        w_top = harmonic(a[:, rows - 1 :], y_faces[3, at : at + step, :1], 1.0)
        w_up = jnp.where(last[None], jnp.broadcast_to(w_top, a.shape), upper(w_down, 1))
        w_back = jnp.where(lane[None] == 0, 0.0, harmonic(a, lower(a, 2), 1.0))
        w_front = upper(w_back, 2)
        v_down = jnp.where(first[None], beside(y_faces, 0, at), lower(v, 1))
        v_up = jnp.where(last[None], beside(y_faces, 1, at), upper(v, 1))
        edges = jnp.broadcast_to(outside[None], a.shape)
        if at == 0:
            edges = edges + jnp.where(iota((step, 1, 1), 0) == 0, edge_count(x_low[1])[None], 0.0)
        if at == count - step:
            edges = edges + jnp.where(iota((step, 1, 1), 0) == step - 1, edge_count(x_high[1])[None], 0.0)
        diagonal = faces[:-1] + faces[1:] + w_down + w_up + w_back + w_front + a * edges
        off = faces[:-1] * pot[at : at + step] + faces[1:] * pot[at + 2 : at + 2 + step] + w_down * v_down + w_up * v_up
        off = off + w_back * lower(v, 2) + w_front * upper(v, 2)
        left = source[at : at + step] - diagonal * v + off
        residual[at : at + step] = left
        for n, x in enumerate((left, a)):
            pair = x.reshape(step // 2, 2, rows, depth)
            to = n * c1 * rows + at // 2 * rows
            wide[to : to + step // 2 * rows] = (pair[:, 0] + pair[:, 1]).reshape(step // 2 * rows, depth)
        low = jnp.concatenate([left[:, :4], a[:, :4]], axis=1)
        high = jnp.concatenate([left[:, rows - 4 :], a[:, rows - 4 :]], axis=1)
        for ref, strip in ((strip_even, jnp.where(low_y, low, high)), (strip_odd, jnp.where(low_y, high, low))):
            for k in range(step):
                for piece in range(pieces):
                    ref[(at + k) * pieces + piece] = strip[k, :, piece * LANES : (piece + 1) * LANES]
    base = 2 * c1 * rows
    for n, both in enumerate((x_low[1] + x_low[2], x_high[1] + x_high[2], y_low[1] + y_low[2], y_high[1] + y_high[2])):
        wide[base + n * rows : base + (n + 1) * rows] = both
    narrow[...] = select(wide[...], pair_matrix(depth)) * 0.125
    half = narrow.shape[0] // 2
    coarse[...] = narrow[pl.ds(0, half, 2)] + narrow[pl.ds(1, half, 2)]
    for k in range(c1):
        s, m = coarse[k * r1 : (k + 1) * r1], coarse[(c1 + k) * r1 : (c1 + k + 1) * r1]
        low = jnp.concatenate([s[:4], m[:4]], axis=0)
        high = jnp.concatenate([s[r1 - 4 :], m[r1 - 4 :]], axis=0)
        strip_even[count * pieces + k] = jnp.where(low_y, low, high)
        strip_odd[count * pieces + k] = jnp.where(low_y, high, low)


def payload_kernel(c1, r1, coarse, payload, wide, narrow, sheet, semaphore):
    c2 = c1 // 2
    depth = coarse.shape[1]
    shape = (c1, r1, depth)
    s, m = coarse[: c1 * r1].reshape(shape), coarse[c1 * r1 : 2 * c1 * r1].reshape(shape)
    base = 2 * c1 * r1
    m_xlow, m_xhigh = coarse[base : base + r1], coarse[base + r1 : base + 2 * r1]
    base += 2 * r1
    m_ylow = jnp.stack([coarse[base + k : base + k + 1] for k in range(c1)])
    m_yhigh = jnp.stack([coarse[base + r1 + k : base + r1 + k + 1] for k in range(c1)])
    row, lane = iota(shape, 1), iota(shape, 2)
    first, last = row == 0, row == r1 - 1
    around = jnp.concatenate([m_xlow[None], m, m_xhigh[None]], axis=0)
    faces = harmonic(around[:-1], around[1:], 0.25)
    down = jnp.where(first, jnp.broadcast_to(m_ylow, shape), lower(m, 1))
    up = jnp.where(last, jnp.broadcast_to(m_yhigh, shape), upper(m, 1))
    w_down = harmonic(m, down, 0.25)
    w_up = jnp.where(last, harmonic(m, up, 0.25), upper(w_down, 1))
    w_back = jnp.where(lane == 0, 0.0, harmonic(m, lower(m, 2), 0.25))
    w_front = upper(w_back, 2)
    outside = as_float(lane == 0) + as_float(lane == depth - 1)
    for b in (down, up, around[:-2], around[2:]):
        outside = outside + as_float(b <= 0.0)
    diagonal = faces[:-1] + faces[1:] + w_down + w_up + w_back + w_front + 0.25 * m * outside
    e = DAMPING * s * invert(diagonal)
    y_low, y_high = w_down * e, w_up * e
    t = KEPT * s + w_back * lower(e, 2) + w_front * upper(e, 2)
    t = t + jnp.where(first, 0.0, w_down * lower(e, 1)) + jnp.where(last, 0.0, w_up * upper(e, 1))
    nothing = jnp.zeros((1, r1, depth), F32)
    t = t + faces[:-1] * jnp.concatenate([nothing, e[:-1]], axis=0) + faces[1:] * jnp.concatenate([e[1:], nothing], axis=0)
    base = c2 // 2 * r1

    def pairs(x):
        x = x.reshape(c2, 2, r1, depth)
        return (x[:, 0] + x[:, 1]).reshape(c2 * r1, depth)

    t, m = pairs(t), pairs(m)
    for n in range(2):
        wide[n, :base] = t[n * base : (n + 1) * base]
        wide[n, base + 2 * r1 :] = m[n * base : (n + 1) * base]
    wide[0, base : base + r1] = faces[0] * e[0]
    wide[0, base + r1 : base + 2 * r1] = faces[c1] * e[c1 - 1]
    for k in range(c1):
        wide[1, base + k : base + k + 1] = y_low[k, :1]
        wide[1, base + r1 + k : base + r1 + k + 1] = y_high[k, r1 - 1 :]
    publish(wide[0], wide[1], narrow, sheet, payload, semaphore)


def packed(low, high, narrow):
    narrow[...] = (select(low, pair_matrix(LANES)) + select(high, pair_matrix(LANES, LANES // 2))) * 0.125
    half = narrow.shape[0] // 2
    return narrow[pl.ds(0, half, 2)] + narrow[pl.ds(1, half, 2)]


def publish(low, high, narrow, sheet, payload, semaphore):
    sheet[...] = jnp.broadcast_to(packed(low, high, narrow)[None], sheet.shape)
    leaving = pltpu.make_async_copy(sheet, payload, semaphore)
    leaving.start()
    leaving.wait()


def strips_kernel(place, residual, material, coarse, even, odd, inner, outer, long_far, long1, long, semaphore):
    low_x, low_y = place[0] == 1, place[1] == 1
    count, rows, depth = residual.shape
    pieces = depth // LANES
    c1, r1 = count // 2, rows // 2
    base = count * pieces

    def sides(at):
        a, b = even[at], odd[at]
        return jnp.where(low_y, a, b), jnp.where(low_y, b, a)

    for i in range(count):
        for piece in range(pieces):
            low, high = sides(i * pieces + piece)
            z = slice(piece * LANES, (piece + 1) * LANES)
            long[0, i, :, z] = jnp.concatenate([low[:4], residual[i, :, z], high[:4]], axis=0)
            long[1, i, :, z] = jnp.concatenate([low[4:], material[i, :, z], high[4:]], axis=0)
    leaving = pltpu.make_async_copy(long, long_far, semaphore)
    leaving.start()
    for k in range(c1):
        low, high = sides(base + k)
        s, m = coarse[k * r1 : (k + 1) * r1], coarse[(c1 + k) * r1 : (c1 + k + 1) * r1]
        long1[0, k] = jnp.concatenate([low[:4], s, high[:4]], axis=0)
        long1[1, k] = jnp.concatenate([low[4:], m, high[4:]], axis=0)

    def pack(out, flag):
        at = 0
        for n, planes in ((0, 3), (1, 4)):
            start = jnp.where(flag, 0, count - planes)
            for k in range(planes):
                for tile in range((rows + 8) // 8):
                    for piece in range(pieces):
                        out[at] = long[n, start + k, tile * 8 : tile * 8 + 8, piece * LANES : (piece + 1) * LANES]
                        at += 1
        for n, planes in ((0, 3), (1, 4)):
            for k in range(planes):
                low, high = k, c1 - planes + k
                for tile in range((r1 + 8) // 8):
                    y = slice(tile * 8, tile * 8 + 8)
                    out[at] = jnp.where(flag, long1[n, low, y], long1[n, high, y])
                    at += 1

    pack(inner, low_x)
    pack(outer, jnp.logical_not(low_x))
    leaving.wait()


def unpack(source, flag, out, start, planes, tiles, pieces, at):
    for n in range(planes):
        for tile in range(tiles):
            for piece in range(pieces):
                value = jnp.where(flag, source[0][at], source[1][at])
                out[start + n, tile * 8 : tile * 8 + 8, piece * LANES : (piece + 1) * LANES] = value
                at += 1
    return at


def smooth_kernel(ends, place, potential_far, state_far, long, outer, inner, out, state, mat, res, x, d, fx, fy, fz, inv, potential, semaphores):
    arriving = pltpu.make_async_copy(potential_far, potential, semaphores.at[0])
    arriving.start()
    passing = pltpu.make_async_copy(state_far, state, semaphores.at[1])
    passing.start()
    count, rows, depth = potential.shape
    own = pl.ds(4, count)
    frames = [
        pltpu.make_async_copy(long.at[n], ref.at[own], semaphores.at[2 + n]) for n, ref in enumerate((res, mat))
    ]
    for copy in frames:
        copy.start()
    low_x = place[0] == 1
    count, rows, depth = potential.shape
    pieces, tiles = depth // LANES, (rows + 8) // 8
    both = (inner, outer)
    for flag, start_r, start_m in ((low_x, 1, 0), (jnp.logical_not(low_x), count + 4, count + 4)):
        at = unpack(both, flag, res, start_r, 3, tiles, pieces, 0)
        unpack(both, flag, mat, start_m, 4, tiles, pieces, at)
    for copy in frames:
        copy.wait()
    total, length = count + 8, rows + 8
    row, lane = iota((length, depth), 0), iota((length, depth), 1)
    outside = as_float(lane == 0) + as_float(lane == depth - 1)
    outside = outside + as_float((row == 4) & (place[3] == 0)) + as_float((row == rows + 3) & (place[3] == ends[1] - 1))
    low_end, high_end = place[2] == 0, place[2] == ends[0] - 1

    def chunks(first, last, step):
        return [(at, min(step, last - at)) for at in range(first, last, step)]

    for at, n in chunks(1, total - 1, SMOOTH_STEP):
        here = slice(at, at + n)
        a = mat[here]
        faces = harmonic(mat[at - 1 : at + n], mat[at : at + n + 1], 1.0)
        w_down = harmonic(a, lower(a, 1), 1.0)
        w_back = jnp.where(lane[None] == 0, 0.0, harmonic(a, lower(a, 2), 1.0))
        plane = at + iota((n, 1, 1), 0)
        edges = outside[None] + as_float((plane == 4) & low_end) + as_float((plane == count + 3) & high_end)
        diagonal = faces[:-1] + faces[1:] + w_down + upper(w_down, 1) + w_back + upper(w_back, 2) + a * edges
        inverse = jnp.where(a > 0.0, invert(jnp.maximum(diagonal, 1e-3)), 0.0)
        fx[at : at + n + 1], fy[here], fz[here], inv[here] = faces, w_down, w_back, inverse
        scaled = inverse * res[here]
        res[here] = scaled
        x[0, here] = scaled * (1.0 / THETA)
    rho = 1.0 / SIGMA
    for turn in range(DEG - 1):
        if turn == DEG - 2:
            arriving.wait()
        following = 1.0 / (2.0 * SIGMA - rho)
        old, new = turn % 2, (turn + 1) % 2
        keep, gain = following * rho, 2.0 * following / DELTA
        for at, n in chunks(2 + turn, total - 2 - turn, SMOOTH_STEP):
            here = slice(at, at + n)
            v = x[old, here]
            w_down, w_back = fy[here], fz[here]
            off = fx[here] * x[old, at - 1 : at + n - 1] + fx[at + 1 : at + n + 1] * x[old, at + 1 : at + n + 1]
            off = off + w_down * lower(v, 1) + upper(w_down * v, 1)
            off = off + w_back * lower(v, 2) + upper(w_back * v, 2)
            before = v * keep if turn == 0 else d[here] * keep
            change = before + gain * (res[here] - v + inv[here] * off)
            if turn == DEG - 2:
                out[at - 4 : at + n - 4] = potential[at - 4 : at + n - 4] + (v + change)[:, 4 : 4 + rows]
            else:
                d[here] = change
                x[new, here] = v + change
        rho = following
    passing.wait()


HALF = LANES // 2


def seal(ref, count):
    low = iota(ref.shape[1:], 1) < HALF
    ref[0] = jnp.where(low, 0.0, pltpu.roll(ref[count], HALF, 1))
    ref[count + 1] = jnp.where(low, pltpu.roll(ref[1], HALF, 1), 0.0)


def each(count, body, most=8):
    step = min(count, most)
    if count // step <= 4:
        for n in range(count // step):
            body(n * step, step)
        return

    def run(n, _):
        body(n * step, step)
        return 0

    lax.fori_loop(0, count // step, run, 0)


def fill_table(mat, table, level, count, base):
    stride, scale = 2**level, 0.25 ** (level + 2)
    rows = mat.shape[1]
    row, lane = iota((rows, LANES), 0), iota((rows, LANES), 1)
    depth = lane % HALF
    above, beyond = row >= stride, depth >= stride
    outside = as_float(row == 0) + as_float(row == rows - stride) + as_float(depth == 0) + as_float(depth == HALF - stride)

    def body(at, step):
        a, before, ahead = mat[pl.ds(at + 1, step)], mat[pl.ds(at, step)], mat[pl.ds(at + 2, step)]
        w_before, w_ahead = harmonic(a, before, scale), harmonic(a, ahead, scale)
        w_down = jnp.where(above[None], harmonic(a, lower(a, 1, stride), scale), 0.0)
        w_back = jnp.where(beyond[None], harmonic(a, lower(a, 2, stride), scale), 0.0)
        plane = at + iota((step, 1, 1), 0)
        low = (lane < HALF)[None]
        edges = outside[None] + as_float((plane == 0) & low) + as_float((plane == count - 1) & jnp.logical_not(low))
        diagonal = w_before + w_ahead + w_down + upper(w_down, 1, stride) + w_back + upper(w_back, 2, stride)
        diagonal = diagonal + scale * a * edges
        table[0, pl.ds(base + at, step)] = w_before
        table[1, pl.ds(base + at, step)] = w_down
        table[2, pl.ds(base + at, step)] = w_back
        table[3, pl.ds(base + at, step)] = jnp.where(a > 0.0, invert(jnp.maximum(diagonal, 1e-4)), 0.0)

    each(count, body)
    table[0, base + count] = harmonic(mat[count], mat[count + 1], scale)


def fold(t, stride):
    a = t.reshape(t.shape[0] // 2, 2, *t.shape[1:])
    a = a[:, 0] + a[:, 1]
    a = a + upper(a, 1, stride)
    return a + upper(a, 2, stride)


def unfold(e, stride):
    e = e + lower(e, 1, stride)
    e = e + lower(e, 2, stride)
    return jnp.broadcast_to(e[:, None], (e.shape[0], 2, *e.shape[1:])).reshape(2 * e.shape[0], *e.shape[1:])


def off_diagonal(e, table, base, at, step, stride):
    v = e[pl.ds(at + 1, step)]
    total = table[0, pl.ds(base + at, step)] * e[pl.ds(at, step)]
    total = total + table[0, pl.ds(base + at + 1, step)] * e[pl.ds(at + 2, step)]
    fy, fz = table[1, pl.ds(base + at, step)], table[2, pl.ds(base + at, step)]
    total = total + fy * lower(v, 1, stride) + upper(fy * v, 1, stride)
    return v, total + fz * lower(v, 2, stride) + upper(fz * v, 2, stride)


def cycle(s, e, t, table, counts, bases, place, out, c2, r2, pad):
    for level, (count, base) in enumerate(zip(counts, bases)):
        s_l, e_l, stride = s[level], e[level], 2**level

        def start(at, step):
            e_l[pl.ds(at + 1, step)] = DAMPING * s_l[pl.ds(at + 1, step)] * table[3, pl.ds(base + at, step)]

        each(count, start)
        seal(e_l, count)
        if level == len(counts) - 1:
            break

        def remainder(at, step):
            _, off = off_diagonal(e_l, table, base, at, step, stride)
            left = KEPT * s_l[pl.ds(at + 1, step)] + off
            s[level + 1][pl.ds(at // 2 + 1, step // 2)] = 0.125 * fold(left, stride)

        each(count, remainder)

    def relax(s_l, source, target, base, count, stride):
        def sweep(at, step):
            v, off = off_diagonal(source, table, base, at, step, stride)
            inverse = table[3, pl.ds(base + at, step)]
            target[pl.ds(at + 1, step)] = KEPT * v + DAMPING * inverse * (s_l[pl.ds(at + 1, step)] + off)

        each(count, sweep)

    now, other = e[2], t
    for _ in range(COARSE_SWEEPS - 1):
        relax(s[2], now, other, bases[2], counts[2], 4)
        seal(other, counts[2])
        now, other = other, now
    for level in (1, 0):
        coarser, e_l, stride = now, e[level], 2**level

        def add(at, step):
            here = pl.ds(2 * at + 1, 2 * step)
            e_l[here] = e_l[here] + unfold(coarser[pl.ds(at + 1, step)], stride)

        each(counts[level + 1], add, 4)
        seal(e_l, counts[level])
        now = s[level]
        relax(s[level], e_l, now, bases[level], counts[level], stride)

    rows = t.shape[1]
    low = iota((rows, LANES), 1) < HALF
    pad[...] = jnp.zeros(pad.shape, F32)
    for n in range(c2 + 4):
        at = place[2] * c2 + n - 2
        second = at >= counts[0]
        inside = (at >= 0) & (at < 2 * counts[0])
        value = now[jnp.clip(at - jnp.where(second, counts[0], 0), 0, counts[0] - 1) + 1]
        value = jnp.where(second, pltpu.roll(value, HALF, 1), value)
        pad[n, 8 : 8 + rows, :] = jnp.where(low & inside, value, 0.0)
        out[n] = pad[n, pl.ds(place[3] * r2 + 6, r2 + 4), :]


def cycle_shapes(counts, rows, c2):
    out = [pltpu.VMEM((count + 2, rows, LANES), F32) for count in (*counts, *counts, counts[0])]
    return out + [pltpu.VMEM((c2 + 4, rows + 16, LANES), F32)]


def repeat(count, body):
    if count <= 8:
        for i in range(count):
            body(i, i % 2)
        return

    def two(n, _):
        body(2 * n, 0)
        body(2 * n + 1, 1)

    lax.fori_loop(0, count // 2, two, None)


def spread_blocks(fetch, outs, grid, c2, r2):
    gx, gy = grid
    length = c2 // 2 * r2
    low = iota((length, LANES), 1) < HALF

    def column(i, parity):
        for j in range(gy):
            for start, out in outs:
                a, b = (fetch(n, parity, j, slice(start, start + length)) for n in (i, i + gx // 2))
                parts = jnp.where(low, a, pltpu.roll(b, HALF, 1)), jnp.where(low, pltpu.roll(a, HALF, 1), b)
                for k in range(c2):
                    n = k % (c2 // 2)
                    out[i * c2 + k + 1, j * r2 : (j + 1) * r2, :] = parts[k // (c2 // 2)][n * r2 : (n + 1) * r2]

    repeat(gx // 2, column)


def clear_ends(refs, counts):
    for ref, count in zip(refs, counts):
        zero = jnp.zeros(ref.shape[1:], F32)
        ref[0] = zero
        ref[count + 1] = zero


def pass_kernel(blocks, _, out):
    out[...] = blocks[...]


def first_cycle_kernel(counts, bases, grid, c2, r2, place, mine, theirs, out, table, *scratch):
    s, e, t, pad = scratch[0:3], list(scratch[3:6]), scratch[6], scratch[7]
    gx, gy = grid
    rows = gy * r2
    own = c2 // 2 * r2
    clear_ends(s[:1], counts)
    odd = place[0] == 1

    def fetch(i, parity, j, at):
        here = i // 2 * gy + j
        a, b = mine[here, at], theirs[here, at]
        return jnp.where(odd, b, a) if parity == 0 else jnp.where(odd, a, b)

    spread_blocks(fetch, ((0, s[0]), (own + 2 * r2, t)), grid, c2, r2)
    face_y = e[0]
    low = iota((2 * c2, LANES), 1) < HALF

    def edges(i, parity):
        for j in range(gy):
            a, b = (fetch(n, parity, j, slice(own, own + 2 * r2)) for n in (i, i + gx // 2))
            x_faces = jnp.where(low, a, pltpu.roll(b, HALF, 1))
            y_faces = jnp.where(low, pltpu.roll(a, HALF, 1), b)
            here = slice(j * r2, (j + 1) * r2)
            s[0][i * c2, here, :] = s[0][i * c2, here, :] + x_faces[:r2]
            s[0][(i + 1) * c2 + 1, here, :] = s[0][(i + 1) * c2 + 1, here, :] + x_faces[r2:]
            for k in range(c2):
                at = i * c2 + k + 1
                if j > 0:
                    face_y[at, j * r2 - 1 : j * r2, :] = y_faces[k : k + 1]
                if j < gy - 1:
                    face_y[at, (j + 1) * r2 : (j + 1) * r2 + 1, :] = y_faces[c2 + k : c2 + k + 1]

    repeat(gx // 2, edges)
    first, last = s[0][0], s[0][counts[0] + 1]
    low = iota(first.shape, 1) < HALF
    s[0][counts[0]] = s[0][counts[0]] + jnp.where(low, pltpu.roll(first, HALF, 1), 0.0)
    s[0][1] = s[0][1] + jnp.where(low, 0.0, pltpu.roll(last, HALF, 1))

    def join(at, step):
        now = pl.ds(at + 1, step)
        row = iota((rows, LANES), 0)
        edge = ((row % r2 == 0) & (row > 0)) | ((row % r2 == r2 - 1) & (row < rows - 1))
        s[0][now] = s[0][now] + jnp.where(edge[None], face_y[now], 0.0)

    each(counts[0], join)
    mats = (t, s[1], s[2])
    for level, (count, base) in enumerate(zip(counts, bases)):
        if level:

            def coarsen(at, step):
                whole = (iota((rows, LANES), 0) % 2**level == 0) & (iota((rows, LANES), 1) % 2**level == 0)
                mean = 0.125 * fold(mats[level - 1][pl.ds(at + 1, step)], 2 ** (level - 1))
                mats[level][pl.ds(at // 2 + 1, step // 2)] = jnp.where(whole[None], mean, 0.0)

            each(counts[level - 1], coarsen)
        seal(mats[level], count)
        fill_table(mats[level], table, level, count, base)
    cycle(s, e, t, table, counts, bases, place, out, c2, r2, pad)


def shifted(a):
    zero = jnp.zeros_like(a[:1])
    return jnp.concatenate([zero, a[:-1]], axis=0), jnp.concatenate([a[1:], zero], axis=0)


def apply_off(e, fx, fy, fz):
    before, ahead = shifted(e)
    out = fx[:-1] * before + fx[1:] * ahead
    out = out + fy * lower(e, 1) + upper(fy * e, 1)
    return out + fz * lower(e, 2) + upper(fz * e, 2)


def raise_window(window_ref, flat, out):
    planes, rows, _ = window_ref.shape
    values = select(window_ref[...].reshape(planes * rows, LANES), spread_matrix(LANES))
    flat[pl.ds(0, planes * rows, 2)] = values
    flat[pl.ds(1, planes * rows, 2)] = values
    v = flat[...].reshape(planes, 1, 2 * rows, LANES)
    out[...] = jnp.broadcast_to(v, (planes, 2, 2 * rows, LANES)).reshape(2 * planes, 2 * rows, LANES)


def level1_kernel(
    offset, place, long1, outer, inner, window1, payload, state_far,
    src, mat, flat, prolonged, fx, fy, fz, diag, inv, err, c, state, wide, narrow, sheet, semaphores,
):
    low_x = place[0] == 1
    total, length, depth = src.shape
    count, rows = total - 8, length - 8
    both = (inner, outer)
    zero = jnp.zeros((length, depth), F32)
    src[0] = zero
    src[total - 1] = zero
    for flag, start_s, start_m in ((low_x, 1, 0), (jnp.logical_not(low_x), count + 4, count + 4)):
        at = unpack(both, flag, src, start_s, 3, length // 8, 1, offset)
        unpack(both, flag, mat, start_m, 4, length // 8, 1, at)
    for n, ref in enumerate((src, mat)):
        ref[pl.ds(4, count)] = long1[n]
    raise_window(window1, flat, prolonged)
    row, lane = iota((length, depth), 0), iota((length, depth), 1)
    ends = as_float(lane == 0) + as_float(lane == depth - 1)
    def chunks(margin):
        first, last = margin, total - margin
        return [(at, min(LEVEL1_STEP, last - at)) for at in range(first, last, LEVEL1_STEP)]

    for at, n in chunks(1):
        here = slice(at, at + n)
        a, before, ahead = mat[here], mat[at - 1 : at + n - 1], mat[at + 1 : at + n + 1]
        down, up = lower(a, 1), upper(a, 1)
        f = harmonic(mat[at - 1 : at + n], mat[at : at + n + 1], 0.25)
        w_y = harmonic(a, down, 0.25)
        w_z = jnp.where(lane[None] == 0, 0.0, harmonic(a, lower(a, 2), 0.25))
        outside = ends[None] + as_float(before <= 0.0) + as_float(ahead <= 0.0) + as_float(down <= 0.0) + as_float(up <= 0.0)
        diagonal = f[:-1] + f[1:] + w_y + upper(w_y, 1) + w_z + upper(w_z, 2) + 0.25 * a * outside
        inverse = jnp.where(a > 0.0, invert(jnp.maximum(diagonal, 1e-4)), 0.0)
        fx[at : at + n + 1], fy[here], fz[here], diag[here], inv[here] = f, w_y, w_z, diagonal, inverse
        err[here] = DAMPING * inverse * src[here] + prolonged[here]

    def off(v, at, n):
        here = slice(at, at + n)
        mid, w_y, w_z = v[here], fy[here], fz[here]
        out = fx[here] * v[at - 1 : at + n - 1] + fx[at + 1 : at + n + 1] * v[at + 1 : at + n + 1]
        out = out + w_y * lower(mid, 1) + upper(w_y * mid, 1)
        return here, mid, out + w_z * lower(mid, 2) + upper(w_z * mid, 2)

    for at, n in chunks(2):
        here, mid, more = off(err, at, n)
        c[here] = KEPT * mid + DAMPING * inv[here] * (src[here] + more)
    for at, n in chunks(3):
        here, mid, more = off(c, at, n)
        left = src[here] - diag[here] * mid + more
        src[here] = left
        value = DAMPING * inv[here] * left
        err[here] = value
        state[at - 3 : at + n - 3] = value
    base = count + 2
    state[base : base + count + 1] = fx[4 : count + 5]
    base += count + 1
    for n, ref in enumerate((fy, fz, inv, c, src)):
        state[base + n * count : base + (n + 1) * count] = ref[4 : 4 + count]
    leaving = pltpu.make_async_copy(state, state_far, semaphores.at[0])
    leaving.start()
    here, _, more = off(err, 4, count)
    t = (KEPT * src[here] + more)[:, 4 : 4 + rows].reshape(count // 2, 2, rows, depth)
    wide[...] = (t[:, 0] + t[:, 1]).reshape(count // 2 * rows, depth)
    half = wide.shape[0] // 2
    publish(wide[:half], wide[half:], narrow, sheet, payload, semaphores.at[1])
    leaving.wait()


def last_cycle_kernel(counts, bases, grid, c2, r2, place, blocks, table, state, partial, out, *scratch):
    s, e, t, pad = scratch[0:3], list(scratch[3:6]), scratch[6], scratch[7]
    view, flat, prolonged, tall, coarse, result, departures = scratch[8:15]
    spread_blocks(lambda i, _, j, at: blocks[grid[0] * grid[1] - 1 - i * grid[1] - j, at], ((0, s[0]),), grid, c2, r2)
    cycle(s, e, t, table, counts, bases, place, view, c2, r2, pad)
    raise_window(view, flat, prolonged)
    count, rows, depth = partial.shape
    c1, r1 = count // 2, rows // 2
    v = prolonged[3 : c1 + 5] + state[: c1 + 2]
    here = v[1:-1]
    base = 2 * c1 + 3
    w_x = state[c1 + 2 : base]
    w_y, w_z, inverse, before, left = (state[base + n * c1 : base + (n + 1) * c1] for n in range(5))
    off = w_x[:-1] * v[:-2] + w_x[1:] * v[2:]
    off = off + w_y * lower(here, 1) + upper(w_y * here, 1) + w_z * lower(here, 2) + upper(w_z * here, 2)
    total = before + KEPT * here + DAMPING * inverse * (left + off)
    coarse[...] = total[:, 4 : 4 + r1].reshape(c1 * r1, LANES)
    values = select(coarse[...], spread_matrix(depth))
    for piece in range(depth // LANES):
        z = slice(piece * LANES, (piece + 1) * LANES)
        tall[piece, pl.ds(0, c1 * r1, 2)] = values[:, z]
        tall[piece, pl.ds(1, c1 * r1, 2)] = values[:, z]
    leaving = []
    for k in range(c1):
        for piece in range(depth // LANES):
            z = slice(piece * LANES, (piece + 1) * LANES)
            more = tall[piece, k * rows : (k + 1) * rows]
            result[2 * k, :, z] = partial[2 * k, :, z] + more
            result[2 * k + 1, :, z] = partial[2 * k + 1, :, z] + more
        if k % 2 == 1:
            planes = pl.ds(2 * k - 2, 4)
            leaving.append(pltpu.make_async_copy(result.at[planes], out.at[planes], departures.at[k // 2]))
            leaving[-1].start()
    for copy in leaving:
        copy.wait()


def size_of(shape):
    lead = math.prod(shape[:-2])
    return 4 * lead * (-(-shape[-2] // 8) * 8) * (-(-shape[-1] // LANES) * LANES)


def call(kernel, name, inputs, outputs, scratch=(), apart=(), cost=None):
    streamed = 0

    def held(n, x):
        nonlocal streamed
        if n in apart:
            return pltpu.with_memory_space_constraint(x, pltpu.HBM)
        if x.ndim == 1:
            return x
        if size_of(x.shape) <= HELD:
            return pltpu.with_memory_space_constraint(x, pltpu.VMEM)
        streamed += size_of(x.shape)
        return x

    def result(shape):
        nonlocal streamed
        if isinstance(shape, jax.ShapeDtypeStruct):
            streamed += size_of(shape.shape)
            return shape
        if far(shape):
            return pltpu.HBM(shape[1], F32)
        if size_of(shape) <= HELD:
            return pltpu.VMEM(shape, F32)
        streamed += size_of(shape)
        return jax.ShapeDtypeStruct(shape, F32)

    def far(x):
        return isinstance(x, tuple) and x[0] == "far"

    def space(n, x):
        return pltpu.HBM if n in apart else pltpu.SMEM if x.ndim == 1 else pltpu.VMEM

    specs = [pl.BlockSpec(memory_space=space(n, x)) for n, x in enumerate(inputs)]
    inputs = [held(n, x) for n, x in enumerate(inputs)]
    results = [result(shape) for shape in outputs]
    need = streamed + sum(size_of(x.shape) for x in scratch if len(getattr(x, "shape", ())) > 1) + 3 * MIB
    return pl.pallas_call(
        kernel,
        out_shape=results,
        in_specs=specs,
        out_specs=[pl.BlockSpec(memory_space=pltpu.HBM if far(x) else pltpu.VMEM) for x in outputs],
        scratch_shapes=list(scratch),
        compiler_params=pltpu.CompilerParams(vmem_limit_bytes=max(need, 8 * MIB)),
        name=name,
        cost_estimate=None if cost is None else pl.CostEstimate(flops=cost, bytes_accessed=0, transcendentals=0),
    )(*inputs)


def swaps(count):
    inner = [(i, i + 1) for i in range(0, count - 1, 2)]
    outer = [(i, i + 1) for i in range(1, count - 1, 2)]
    return [pairs + [(b, a) for a, b in pairs] for pairs in (inner, outer)]


def local(right_side, potential, phase, permeability):
    gx, gy = lax.axis_size("gx"), lax.axis_size("gy")
    devices = gx * gy
    here_x, here_y = lax.axis_index("gx"), lax.axis_index("gy")
    place = jnp.stack([here_x % 2, here_y % 2, here_x, here_y]).astype(jnp.int32)
    count, rows, depth = right_side.shape
    c1, r1, d1 = count // 2, rows // 2, depth // 2
    c2, r2 = c1 // 2, r1 // 2
    pieces = depth // LANES
    swap_x, swap_y = swaps(gx), swaps(gy)
    VM = lambda *shape: pltpu.VMEM(shape, F32)

    brick = (count, rows, depth)
    face = (3, rows, depth)
    DMA = pltpu.SemaphoreType.DMA
    sheet = (devices, c2 // 2 * r2, LANES)
    sheet2 = (devices // 2, c2 * r2 + 2 * r2, LANES)
    material, potential_here, source_here, inner, outer, even, odd = call(
        faces_kernel, "faces", (place, permeability, potential, phase, right_side),
        (brick, brick, brick, face, face, (3, count, depth), (3, count, depth)),
        (pltpu.VMEM(brick, jnp.int32), pltpu.SMEM(permeability.shape, F32), pltpu.SemaphoreType.DMA((4,))),
        apart=(1, 2, 3, 4),
    )
    even = lax.ppermute(even, "gy", swap_y[0])
    odd = lax.ppermute(odd, "gy", swap_y[1])
    outer = lax.ppermute(outer, "gx", swap_x[1])
    inner = lax.ppermute(inner, "gx", swap_x[0])

    strip = (count * pieces + c1, 8, LANES)
    total = 2 * c1 * rows + 4 * rows
    residual, coarse, even, odd = call(
        residual_kernel, "residual", (place, source_here, potential_here, material, outer, even, odd, inner),
        (brick, (total // 2, LANES), strip, strip),
        (
            VM(total, depth), VM(total, LANES), VM(4, count, 8, depth), VM(count + 2, rows, depth), VM(count + 2, rows, depth),
        ),
    )
    even = lax.ppermute(even, "gy", swap_y[0])
    odd = lax.ppermute(odd, "gy", swap_y[1])
    small = c2 * r1 + 2 * r1
    (payload,) = call(
        functools.partial(payload_kernel, c1, r1), "payload", (coarse,), (("far", sheet2),),
        (VM(2, small, d1), VM(small, LANES), VM(*sheet2), DMA),
    )
    groups = [[(2 * i + c) * gy + j for i in range(gx // 2) for j in range(gy)] for c in range(2)]
    blocks = lax.all_to_all(payload, ("gx", "gy"), 0, 0, axis_index_groups=groups)
    tiles, tiles1 = (rows + 8) // 8, (r1 + 8) // 8
    strip = (7 * tiles * pieces + 7 * tiles1, 8, LANES)
    long_shape = (2, count, rows + 8, depth)
    inner, outer, long, long1 = call(
        strips_kernel, "strips", (place, residual, material, coarse, even, odd),
        (strip, strip, ("far", long_shape), (2, c1, r1 + 8, d1)),
        (VM(*long_shape), DMA), cost=10**11,
    )
    outer = lax.ppermute(outer, "gx", swap_x[1])
    inner = lax.ppermute(inner, "gx", swap_x[0])

    (blocks,) = call(pass_kernel, "pass", (blocks, long1), (sheet2,))
    others = lax.ppermute(blocks, "gx", swap_x[0])
    counts = tuple(gx * c2 // 2 // k for k in (1, 2, 4))
    bases = (0, counts[0] + 1, counts[0] + counts[1] + 2)
    work = cycle_shapes(counts, gy * r2, c2)
    view = (c2 + 4, r2 + 4, LANES)
    window1, table = call(
        functools.partial(first_cycle_kernel, counts, bases, (gx, gy), c2, r2), "cycle1", (place, blocks, others),
        (view, (4, sum(counts) + 3, gy * r2, LANES)), work,
    )
    frame = (c1 + 8, r1 + 8, d1)
    flat = VM((c2 + 4) * (r2 + 4) * 2, LANES)
    state = (7 * c1 + 3, r1 + 8, d1)
    tall = VM(c1 + 9, r1 + 8, d1)
    payload, held = call(
        functools.partial(level1_kernel, 7 * tiles * pieces), "level1", (place, long1, outer, inner, window1), (("far", sheet), ("far", state)),
        (
            VM(*frame), VM(*frame), flat, VM(*frame), tall, VM(*frame), VM(*frame), VM(*frame), VM(*frame), VM(*frame),
            VM(*frame), VM(*state), VM(c1 // 2 * r1, d1), VM(c1 // 4 * r1, LANES), VM(*sheet), pltpu.SemaphoreType.DMA((2,)),
        ),
    )
    blocks = lax.all_to_all(payload, ("gx", "gy"), 0, 0, axis_index_groups=[list(range(devices))[::-1]])
    wide = (count + 8, rows + 8, depth)
    partial, held = call(
        functools.partial(smooth_kernel, (gx, gy)), "smooth", (place, potential, held, long, outer, inner), (brick, state),
        (
            VM(*wide), VM(*wide), VM(2, *wide), VM(*wide), VM(count + 9, rows + 8, depth), VM(*wide), VM(*wide), VM(*wide),
            VM(*brick), pltpu.SemaphoreType.DMA((4,)),
        ),
        apart=(1, 2, 3),
    )
    (out,) = call(
        functools.partial(last_cycle_kernel, counts, bases, (gx, gy), c2, r2), "cycle2",
        (place, blocks, table, held, partial), (("far", brick),),
        (
            *work, VM(*view), flat, VM(*frame), VM(pieces, c1 * rows, LANES), VM(c1 * r1, LANES), VM(*brick),
            pltpu.SemaphoreType.DMA((c1 // 2,)),
        ),
    )
    return out


def solution(mesh):
    placed = (P("gx", "gy", None), P("gx", "gy", None), P("gx", "gy", None), P())
    return jax.shard_map(local, mesh=mesh, in_specs=placed, out_specs=P("gx", "gy", None), check_vma=False)
```

```python
import functools
import math

import jax
import jax.numpy as jnp
from jax import lax
from jax.experimental import pallas as pl
from jax.experimental.pallas import tpu as pltpu
from jax.sharding import PartitionSpec as P

DEG = 4
COARSE_SWEEPS = 4
THETA = 1.15
DELTA = 0.85
SIGMA = 1.15 / 0.85
DAMPING = 0.6
KEPT = 1.0 - DAMPING
F32 = jnp.float32
LANES = 128
MIB = 1024 * 1024
HELD = 4 * MIB
SMOOTH_STEP = 4
LEVEL1_STEP = 7


def iota(shape, axis):
    return lax.broadcasted_iota(jnp.int32, shape, axis)


def invert(x):
    guess = pl.reciprocal(x, approx=True)
    return guess * (2.0 - x * guess)


def harmonic(a, b, scale):
    return (2.0 * scale) * a * b * invert(jnp.maximum(a + b, 1e-3))


def pair_matrix(size, offset=0):
    column = iota((size, LANES), 1)
    return ((column >= offset) & (iota((size, LANES), 0) // 2 == column - offset)).astype(jnp.bfloat16)


def spread_matrix(width):
    return (iota((LANES, width), 1) // 2 == iota((LANES, width), 0)).astype(jnp.bfloat16)


def select(values, matrix):
    high = values.astype(jnp.bfloat16)
    rest = (values - high.astype(F32)).astype(jnp.bfloat16)
    return jnp.dot(high, matrix, preferred_element_type=F32) + jnp.dot(rest, matrix, preferred_element_type=F32)


def lower(x, axis, stride=1):
    return pltpu.roll(x, stride, axis)


def upper(x, axis, stride=1):
    return pltpu.roll(x, x.shape[axis] - stride, axis)


def as_float(condition):
    return jnp.where(condition, 1.0, 0.0)


def faces_kernel(
    place, permeability, potential, phase, source,
    material, pot, src, inner, outer, even, odd,
    ids, values, semaphores,
):
    arriving = [
        pltpu.make_async_copy(a, b, semaphores.at[n])
        for n, (a, b) in enumerate(((permeability, values), (phase, ids), (potential, pot), (source, src)))
    ]
    for copy in arriving:
        copy.start()
    low_x, low_y = place[0] == 1, place[1] == 1
    count, rows = pot.shape[:2]
    arriving[0].wait()
    arriving[1].wait()
    p0, p1, p2 = values[0], values[1], values[2]
    for i in range(count):
        here = ids[i]
        material[i] = jnp.where(here == 0, p0, jnp.where(here == 1, p1, p2))
    last = count - 1
    first = jnp.where(low_x, 0, last)
    second = jnp.where(low_x, 1, last - 1)
    inner[1] = material[first]
    inner[2] = material[second]
    outer[1] = material[last - first]
    outer[2] = material[last - second]

    def edge(slot, ref, a, b):
        for i in range(count):
            low, high = ref[i, a : a + 1, :], ref[i, b : b + 1, :]
            even[slot, i : i + 1, :] = jnp.where(low_y, low, high)
            odd[slot, i : i + 1, :] = jnp.where(low_y, high, low)

    edge(1, material, 0, rows - 1)
    edge(2, material, 1, rows - 2)
    arriving[2].wait()
    inner[0] = pot[first]
    outer[0] = pot[last - first]
    edge(0, pot, 0, rows - 1)
    arriving[3].wait()


def residual_kernel(
    place, source, potential, material, outer, even, odd, inner,
    residual, coarse, strip_even, strip_odd,
    wide, narrow, y_faces, mat, pot,
):
    low_x, low_y = place[0] == 1, place[1] == 1
    count, rows, depth = source.shape
    c1, r1 = count // 2, rows // 2
    pieces = depth // LANES

    def ordered(flag, a, b):
        return jnp.where(flag, a, b), jnp.where(flag, b, a)

    x_low, x_high = ordered(low_x, inner[...], outer[...])
    y_low, y_high = ordered(low_y, even[...], odd[...])
    row, lane = iota((rows, depth), 0), iota((rows, depth), 1)
    first, last = row == 0, row == rows - 1
    for n, ref in enumerate((y_low[0], y_high[0], y_low[1], y_high[1])):
        for i in range(count):
            y_faces[n, i] = jnp.broadcast_to(ref[i : i + 1], (8, depth))
    mat[0], mat[count + 1] = x_low[1], x_high[1]
    pot[0], pot[count + 1] = x_low[0], x_high[0]
    mat[pl.ds(1, count)] = material[...]
    pot[pl.ds(1, count)] = potential[...]
    step = 4
    outside = as_float(lane == 0) + as_float(lane == depth - 1)

    def edge_count(faces):
        return as_float(faces[:1, :1] <= 0.0)

    outside = outside + jnp.where(first, edge_count(y_low[1]), 0.0) + jnp.where(last, edge_count(y_high[1]), 0.0)

    def beside(ref, n, at):
        return jnp.broadcast_to(ref[n, at : at + step, :1], (step, rows, depth))

    for at in range(0, count, step):
        here = slice(at + 1, at + 1 + step)
        a, v = mat[here], pot[here]
        faces = harmonic(mat[at : at + step + 1], mat[at + 1 : at + step + 2], 1.0)
        down = jnp.where(first[None], beside(y_faces, 2, at), lower(a, 1))
        w_down = harmonic(a, down, 1.0)
        w_top = harmonic(a[:, rows - 1 :], y_faces[3, at : at + step, :1], 1.0)
        w_up = jnp.where(last[None], jnp.broadcast_to(w_top, a.shape), upper(w_down, 1))
        w_back = jnp.where(lane[None] == 0, 0.0, harmonic(a, lower(a, 2), 1.0))
        w_front = upper(w_back, 2)
        v_down = jnp.where(first[None], beside(y_faces, 0, at), lower(v, 1))
        v_up = jnp.where(last[None], beside(y_faces, 1, at), upper(v, 1))
        edges = jnp.broadcast_to(outside[None], a.shape)
        if at == 0:
            edges = edges + jnp.where(iota((step, 1, 1), 0) == 0, edge_count(x_low[1])[None], 0.0)
        if at == count - step:
            edges = edges + jnp.where(iota((step, 1, 1), 0) == step - 1, edge_count(x_high[1])[None], 0.0)
        diagonal = faces[:-1] + faces[1:] + w_down + w_up + w_back + w_front + a * edges
        off = faces[:-1] * pot[at : at + step] + faces[1:] * pot[at + 2 : at + 2 + step] + w_down * v_down + w_up * v_up
        off = off + w_back * lower(v, 2) + w_front * upper(v, 2)
        left = source[at : at + step] - diagonal * v + off
        residual[at : at + step] = left
        for n, x in enumerate((left, a)):
            pair = x.reshape(step // 2, 2, rows, depth)
            to = n * c1 * rows + at // 2 * rows
            wide[to : to + step // 2 * rows] = (pair[:, 0] + pair[:, 1]).reshape(step // 2 * rows, depth)
        low = jnp.concatenate([left[:, :4], a[:, :4]], axis=1)
        high = jnp.concatenate([left[:, rows - 4 :], a[:, rows - 4 :]], axis=1)
        for ref, strip in ((strip_even, jnp.where(low_y, low, high)), (strip_odd, jnp.where(low_y, high, low))):
            for k in range(step):
                for piece in range(pieces):
                    ref[(at + k) * pieces + piece] = strip[k, :, piece * LANES : (piece + 1) * LANES]
    base = 2 * c1 * rows
    for n, both in enumerate((x_low[1] + x_low[2], x_high[1] + x_high[2], y_low[1] + y_low[2], y_high[1] + y_high[2])):
        wide[base + n * rows : base + (n + 1) * rows] = both
    narrow[...] = select(wide[...], pair_matrix(depth)) * 0.125
    half = narrow.shape[0] // 2
    coarse[...] = narrow[pl.ds(0, half, 2)] + narrow[pl.ds(1, half, 2)]
    for k in range(c1):
        s, m = coarse[k * r1 : (k + 1) * r1], coarse[(c1 + k) * r1 : (c1 + k + 1) * r1]
        low = jnp.concatenate([s[:4], m[:4]], axis=0)
        high = jnp.concatenate([s[r1 - 4 :], m[r1 - 4 :]], axis=0)
        strip_even[count * pieces + k] = jnp.where(low_y, low, high)
        strip_odd[count * pieces + k] = jnp.where(low_y, high, low)


def payload_kernel(c1, r1, coarse, payload, wide, narrow, sheet, semaphore):
    c2 = c1 // 2
    depth = coarse.shape[1]
    shape = (c1, r1, depth)
    s, m = coarse[: c1 * r1].reshape(shape), coarse[c1 * r1 : 2 * c1 * r1].reshape(shape)
    base = 2 * c1 * r1
    m_xlow, m_xhigh = coarse[base : base + r1], coarse[base + r1 : base + 2 * r1]
    base += 2 * r1
    m_ylow = jnp.stack([coarse[base + k : base + k + 1] for k in range(c1)])
    m_yhigh = jnp.stack([coarse[base + r1 + k : base + r1 + k + 1] for k in range(c1)])
    row, lane = iota(shape, 1), iota(shape, 2)
    first, last = row == 0, row == r1 - 1
    around = jnp.concatenate([m_xlow[None], m, m_xhigh[None]], axis=0)
    faces = harmonic(around[:-1], around[1:], 0.25)
    down = jnp.where(first, jnp.broadcast_to(m_ylow, shape), lower(m, 1))
    up = jnp.where(last, jnp.broadcast_to(m_yhigh, shape), upper(m, 1))
    w_down = harmonic(m, down, 0.25)
    w_up = jnp.where(last, harmonic(m, up, 0.25), upper(w_down, 1))
    w_back = jnp.where(lane == 0, 0.0, harmonic(m, lower(m, 2), 0.25))
    w_front = upper(w_back, 2)
    outside = as_float(lane == 0) + as_float(lane == depth - 1)
    for b in (down, up, around[:-2], around[2:]):
        outside = outside + as_float(b <= 0.0)
    diagonal = faces[:-1] + faces[1:] + w_down + w_up + w_back + w_front + 0.25 * m * outside
    e = DAMPING * s * invert(diagonal)
    y_low, y_high = w_down * e, w_up * e
    t = KEPT * s + w_back * lower(e, 2) + w_front * upper(e, 2)
    t = t + jnp.where(first, 0.0, w_down * lower(e, 1)) + jnp.where(last, 0.0, w_up * upper(e, 1))
    nothing = jnp.zeros((1, r1, depth), F32)
    t = t + faces[:-1] * jnp.concatenate([nothing, e[:-1]], axis=0) + faces[1:] * jnp.concatenate([e[1:], nothing], axis=0)
    base = c2 // 2 * r1

    def pairs(x):
        x = x.reshape(c2, 2, r1, depth)
        return (x[:, 0] + x[:, 1]).reshape(c2 * r1, depth)

    t, m = pairs(t), pairs(m)
    for n in range(2):
        wide[n, :base] = t[n * base : (n + 1) * base]
        wide[n, base + 2 * r1 :] = m[n * base : (n + 1) * base]
    wide[0, base : base + r1] = faces[0] * e[0]
    wide[0, base + r1 : base + 2 * r1] = faces[c1] * e[c1 - 1]
    for k in range(c1):
        wide[1, base + k : base + k + 1] = y_low[k, :1]
        wide[1, base + r1 + k : base + r1 + k + 1] = y_high[k, r1 - 1 :]
    publish(wide[0], wide[1], narrow, sheet, payload, semaphore)


def packed(low, high, narrow):
    narrow[...] = (select(low, pair_matrix(LANES)) + select(high, pair_matrix(LANES, LANES // 2))) * 0.125
    half = narrow.shape[0] // 2
    return narrow[pl.ds(0, half, 2)] + narrow[pl.ds(1, half, 2)]


def publish(low, high, narrow, sheet, payload, semaphore):
    sheet[...] = jnp.broadcast_to(packed(low, high, narrow)[None], sheet.shape)
    leaving = pltpu.make_async_copy(sheet, payload, semaphore)
    leaving.start()
    leaving.wait()


def strips_kernel(place, residual, material, coarse, even, odd, inner, outer, long_far, long1, long, semaphore):
    low_x, low_y = place[0] == 1, place[1] == 1
    count, rows, depth = residual.shape
    pieces = depth // LANES
    c1, r1 = count // 2, rows // 2
    base = count * pieces

    def sides(at):
        a, b = even[at], odd[at]
        return jnp.where(low_y, a, b), jnp.where(low_y, b, a)

    for i in range(count):
        for piece in range(pieces):
            low, high = sides(i * pieces + piece)
            z = slice(piece * LANES, (piece + 1) * LANES)
            long[0, i, :, z] = jnp.concatenate([low[:4], residual[i, :, z], high[:4]], axis=0)
            long[1, i, :, z] = jnp.concatenate([low[4:], material[i, :, z], high[4:]], axis=0)
    leaving = pltpu.make_async_copy(long, long_far, semaphore)
    leaving.start()
    for k in range(c1):
        low, high = sides(base + k)
        s, m = coarse[k * r1 : (k + 1) * r1], coarse[(c1 + k) * r1 : (c1 + k + 1) * r1]
        long1[0, k] = jnp.concatenate([low[:4], s, high[:4]], axis=0)
        long1[1, k] = jnp.concatenate([low[4:], m, high[4:]], axis=0)

    def pack(out, flag):
        at = 0
        for n, planes in ((0, 3), (1, 4)):
            for away in range(1, planes + 1):
                k = jnp.where(flag, away - 1, count - away)
                ref = long.at[n] if away < planes else (residual, material)[n]
                for tile in range(ref.shape[1] // 8):
                    for piece in range(pieces):
                        out[at] = ref[k, tile * 8 : tile * 8 + 8, piece * LANES : (piece + 1) * LANES]
                        at += 1
        for n, planes in ((0, 3), (1, 4)):
            for away in range(1, planes + 1):
                low, high = away - 1, c1 - away
                if away == planes:
                    low, high = (n * c1 + low) * r1, (n * c1 + high) * r1
                    out[at] = jnp.where(flag, coarse[low : low + r1], coarse[high : high + r1])
                    at += 1
                    continue
                for tile in range((r1 + 8) // 8):
                    y = slice(tile * 8, tile * 8 + 8)
                    out[at] = jnp.where(flag, long1[n, low, y], long1[n, high, y])
                    at += 1

    pack(inner, low_x)
    pack(outer, jnp.logical_not(low_x))
    leaving.wait()


def strip_length(rows, depth):
    return (5 * (rows + 8) + 2 * rows) // 8 * (depth // LANES)


def unpack(source, flag, out, base, side, planes, at):
    rows = out.shape[1]
    for away in range(1, planes + 1):
        to = base + side * away
        first = 0
        if away == planes:
            first = 4
            edge = jnp.zeros((4, out.shape[2]), F32)
            out[to, :4] = edge
            out[to, rows - 4 :] = edge
        for row in range(first, rows - first, 8):
            for z in range(0, out.shape[2], LANES):
                out[to, row : row + 8, z : z + LANES] = jnp.where(flag, source[0][at], source[1][at])
                at += 1
    return at


def smooth_kernel(ends, place, potential_far, state_far, long, outer, inner, out, state, mat, res, x, d, fx, fy, fz, inv, potential, semaphores):
    arriving = pltpu.make_async_copy(potential_far, potential, semaphores.at[0])
    arriving.start()
    passing = pltpu.make_async_copy(state_far, state, semaphores.at[1])
    passing.start()
    count, rows, depth = potential.shape
    own = pl.ds(4, count)
    frames = [
        pltpu.make_async_copy(long.at[n], ref.at[own], semaphores.at[2 + n]) for n, ref in enumerate((res, mat))
    ]
    for copy in frames:
        copy.start()
    low_x = place[0] == 1
    count, rows, depth = potential.shape
    both = (inner, outer)
    for flag, base, side in ((low_x, 4, -1), (jnp.logical_not(low_x), count + 3, 1)):
        unpack(both, flag, mat, base, side, 4, unpack(both, flag, res, base, side, 3, 0))
    for copy in frames:
        copy.wait()
    total, length = count + 8, rows + 8
    row, lane = iota((length, depth), 0), iota((length, depth), 1)
    outside = as_float(lane == 0) + as_float(lane == depth - 1)
    outside = outside + as_float((row == 4) & (place[3] == 0)) + as_float((row == rows + 3) & (place[3] == ends[1] - 1))
    low_end, high_end = place[2] == 0, place[2] == ends[0] - 1

    def chunks(first, last, step):
        return [(at, min(step, last - at)) for at in range(first, last, step)]

    for at, n in chunks(1, total - 1, SMOOTH_STEP):
        here = slice(at, at + n)
        a = mat[here]
        faces = harmonic(mat[at - 1 : at + n], mat[at : at + n + 1], 1.0)
        w_down = harmonic(a, lower(a, 1), 1.0)
        w_back = jnp.where(lane[None] == 0, 0.0, harmonic(a, lower(a, 2), 1.0))
        plane = at + iota((n, 1, 1), 0)
        edges = outside[None] + as_float((plane == 4) & low_end) + as_float((plane == count + 3) & high_end)
        diagonal = faces[:-1] + faces[1:] + w_down + upper(w_down, 1) + w_back + upper(w_back, 2) + a * edges
        inverse = jnp.where(a > 0.0, invert(jnp.maximum(diagonal, 1e-3)), 0.0)
        fx[at : at + n + 1], fy[here], fz[here], inv[here] = faces, w_down, w_back, inverse
        scaled = inverse * res[here]
        res[here] = scaled
        x[0, here] = scaled * (1.0 / THETA)
    rho = 1.0 / SIGMA
    for turn in range(DEG - 1):
        if turn == DEG - 2:
            arriving.wait()
        following = 1.0 / (2.0 * SIGMA - rho)
        old, new = turn % 2, (turn + 1) % 2
        keep, gain = following * rho, 2.0 * following / DELTA
        for at, n in chunks(2 + turn, total - 2 - turn, SMOOTH_STEP):
            here = slice(at, at + n)
            v = x[old, here]
            w_down, w_back = fy[here], fz[here]
            off = fx[here] * x[old, at - 1 : at + n - 1] + fx[at + 1 : at + n + 1] * x[old, at + 1 : at + n + 1]
            off = off + w_down * lower(v, 1) + upper(w_down * v, 1)
            off = off + w_back * lower(v, 2) + upper(w_back * v, 2)
            before = v * keep if turn == 0 else d[here] * keep
            change = before + gain * (res[here] - v + inv[here] * off)
            if turn == DEG - 2:
                out[at - 4 : at + n - 4] = potential[at - 4 : at + n - 4] + (v + change)[:, 4 : 4 + rows]
            else:
                d[here] = change
                x[new, here] = v + change
        rho = following
    passing.wait()


HALF = LANES // 2


def seal(ref, count):
    low = iota(ref.shape[1:], 1) < HALF
    ref[0] = jnp.where(low, 0.0, pltpu.roll(ref[count], HALF, 1))
    ref[count + 1] = jnp.where(low, pltpu.roll(ref[1], HALF, 1), 0.0)


def each(count, body, most=8):
    step = min(count, most)
    if count // step <= 4:
        for n in range(count // step):
            body(n * step, step)
        return

    def run(n, _):
        body(n * step, step)
        return 0

    lax.fori_loop(0, count // step, run, 0)


def fill_table(mat, table, level, count, base):
    stride, scale = 2**level, 0.25 ** (level + 2)
    rows = mat.shape[1]
    row, lane = iota((rows, LANES), 0), iota((rows, LANES), 1)
    depth = lane % HALF
    above, beyond = row >= stride, depth >= stride
    outside = as_float(row == 0) + as_float(row == rows - stride) + as_float(depth == 0) + as_float(depth == HALF - stride)

    def body(at, step):
        a, before, ahead = mat[pl.ds(at + 1, step)], mat[pl.ds(at, step)], mat[pl.ds(at + 2, step)]
        w_before, w_ahead = harmonic(a, before, scale), harmonic(a, ahead, scale)
        w_down = jnp.where(above[None], harmonic(a, lower(a, 1, stride), scale), 0.0)
        w_back = jnp.where(beyond[None], harmonic(a, lower(a, 2, stride), scale), 0.0)
        plane = at + iota((step, 1, 1), 0)
        low = (lane < HALF)[None]
        edges = outside[None] + as_float((plane == 0) & low) + as_float((plane == count - 1) & jnp.logical_not(low))
        diagonal = w_before + w_ahead + w_down + upper(w_down, 1, stride) + w_back + upper(w_back, 2, stride)
        diagonal = diagonal + scale * a * edges
        table[0, pl.ds(base + at, step)] = w_before
        table[1, pl.ds(base + at, step)] = w_down
        table[2, pl.ds(base + at, step)] = w_back
        table[3, pl.ds(base + at, step)] = jnp.where(a > 0.0, invert(jnp.maximum(diagonal, 1e-4)), 0.0)

    each(count, body)
    table[0, base + count] = harmonic(mat[count], mat[count + 1], scale)


def fold(t, stride):
    a = t.reshape(t.shape[0] // 2, 2, *t.shape[1:])
    a = a[:, 0] + a[:, 1]
    a = a + upper(a, 1, stride)
    return a + upper(a, 2, stride)


def unfold(e, stride):
    e = e + lower(e, 1, stride)
    e = e + lower(e, 2, stride)
    return jnp.broadcast_to(e[:, None], (e.shape[0], 2, *e.shape[1:])).reshape(2 * e.shape[0], *e.shape[1:])


def off_diagonal(e, table, base, at, step, stride):
    v = e[pl.ds(at + 1, step)]
    total = table[0, pl.ds(base + at, step)] * e[pl.ds(at, step)]
    total = total + table[0, pl.ds(base + at + 1, step)] * e[pl.ds(at + 2, step)]
    fy, fz = table[1, pl.ds(base + at, step)], table[2, pl.ds(base + at, step)]
    total = total + fy * lower(v, 1, stride) + upper(fy * v, 1, stride)
    return v, total + fz * lower(v, 2, stride) + upper(fz * v, 2, stride)


def cycle(s, e, t, table, counts, bases, place, out, c2, r2, pad):
    for level, (count, base) in enumerate(zip(counts, bases)):
        s_l, e_l, stride = s[level], e[level], 2**level

        def start(at, step):
            e_l[pl.ds(at + 1, step)] = DAMPING * s_l[pl.ds(at + 1, step)] * table[3, pl.ds(base + at, step)]

        each(count, start)
        seal(e_l, count)
        if level == len(counts) - 1:
            break

        def remainder(at, step):
            _, off = off_diagonal(e_l, table, base, at, step, stride)
            left = KEPT * s_l[pl.ds(at + 1, step)] + off
            s[level + 1][pl.ds(at // 2 + 1, step // 2)] = 0.125 * fold(left, stride)

        each(count, remainder)

    def relax(s_l, source, target, base, count, stride):
        def sweep(at, step):
            v, off = off_diagonal(source, table, base, at, step, stride)
            inverse = table[3, pl.ds(base + at, step)]
            target[pl.ds(at + 1, step)] = KEPT * v + DAMPING * inverse * (s_l[pl.ds(at + 1, step)] + off)

        each(count, sweep)

    now, other = e[2], t
    for _ in range(COARSE_SWEEPS - 1):
        relax(s[2], now, other, bases[2], counts[2], 4)
        seal(other, counts[2])
        now, other = other, now
    for level in (1, 0):
        coarser, e_l, stride = now, e[level], 2**level

        def add(at, step):
            here = pl.ds(2 * at + 1, 2 * step)
            e_l[here] = e_l[here] + unfold(coarser[pl.ds(at + 1, step)], stride)

        each(counts[level + 1], add, 4)
        seal(e_l, counts[level])
        now = s[level]
        relax(s[level], e_l, now, bases[level], counts[level], stride)

    rows = t.shape[1]
    low = iota((rows, LANES), 1) < HALF
    pad[...] = jnp.zeros(pad.shape, F32)
    for n in range(c2 + 4):
        at = place[2] * c2 + n - 2
        second = at >= counts[0]
        inside = (at >= 0) & (at < 2 * counts[0])
        value = now[jnp.clip(at - jnp.where(second, counts[0], 0), 0, counts[0] - 1) + 1]
        value = jnp.where(second, pltpu.roll(value, HALF, 1), value)
        pad[n, 8 : 8 + rows, :] = jnp.where(low & inside, value, 0.0)
        out[n] = pad[n, pl.ds(place[3] * r2 + 6, r2 + 4), :]


def cycle_shapes(counts, rows, c2):
    out = [pltpu.VMEM((count + 2, rows, LANES), F32) for count in (*counts, *counts, counts[0])]
    return out + [pltpu.VMEM((c2 + 4, rows + 16, LANES), F32)]


def repeat(count, body):
    if count <= 8:
        for i in range(count):
            body(i, i % 2)
        return

    def two(n, _):
        body(2 * n, 0)
        body(2 * n + 1, 1)

    lax.fori_loop(0, count // 2, two, None)


def spread_blocks(fetch, outs, grid, c2, r2):
    gx, gy = grid
    length = c2 // 2 * r2
    low = iota((length, LANES), 1) < HALF

    def column(i, parity):
        for j in range(gy):
            for start, out in outs:
                a, b = (fetch(n, parity, j, slice(start, start + length)) for n in (i, i + gx // 2))
                parts = jnp.where(low, a, pltpu.roll(b, HALF, 1)), jnp.where(low, pltpu.roll(a, HALF, 1), b)
                for k in range(c2):
                    n = k % (c2 // 2)
                    out[i * c2 + k + 1, j * r2 : (j + 1) * r2, :] = parts[k // (c2 // 2)][n * r2 : (n + 1) * r2]

    repeat(gx // 2, column)


def clear_ends(refs, counts):
    for ref, count in zip(refs, counts):
        zero = jnp.zeros(ref.shape[1:], F32)
        ref[0] = zero
        ref[count + 1] = zero


def pass_kernel(blocks, _, out):
    out[...] = blocks[...]


def first_cycle_kernel(counts, bases, grid, c2, r2, place, mine, theirs, out, table, *scratch):
    s, e, t, pad = scratch[0:3], list(scratch[3:6]), scratch[6], scratch[7]
    gx, gy = grid
    rows = gy * r2
    own = c2 // 2 * r2
    clear_ends(s[:1], counts)
    odd = place[0] == 1

    def fetch(i, parity, j, at):
        here = i // 2 * gy + j
        a, b = mine[here, at], theirs[here, at]
        return jnp.where(odd, b, a) if parity == 0 else jnp.where(odd, a, b)

    spread_blocks(fetch, ((0, s[0]), (own + 2 * r2, t)), grid, c2, r2)
    face_y = e[0]
    low = iota((2 * c2, LANES), 1) < HALF

    def edges(i, parity):
        for j in range(gy):
            a, b = (fetch(n, parity, j, slice(own, own + 2 * r2)) for n in (i, i + gx // 2))
            x_faces = jnp.where(low, a, pltpu.roll(b, HALF, 1))
            y_faces = jnp.where(low, pltpu.roll(a, HALF, 1), b)
            here = slice(j * r2, (j + 1) * r2)
            s[0][i * c2, here, :] = s[0][i * c2, here, :] + x_faces[:r2]
            s[0][(i + 1) * c2 + 1, here, :] = s[0][(i + 1) * c2 + 1, here, :] + x_faces[r2:]
            for k in range(c2):
                at = i * c2 + k + 1
                if j > 0:
                    face_y[at, j * r2 - 1 : j * r2, :] = y_faces[k : k + 1]
                if j < gy - 1:
                    face_y[at, (j + 1) * r2 : (j + 1) * r2 + 1, :] = y_faces[c2 + k : c2 + k + 1]

    repeat(gx // 2, edges)
    first, last = s[0][0], s[0][counts[0] + 1]
    low = iota(first.shape, 1) < HALF
    s[0][counts[0]] = s[0][counts[0]] + jnp.where(low, pltpu.roll(first, HALF, 1), 0.0)
    s[0][1] = s[0][1] + jnp.where(low, 0.0, pltpu.roll(last, HALF, 1))

    def join(at, step):
        now = pl.ds(at + 1, step)
        row = iota((rows, LANES), 0)
        edge = ((row % r2 == 0) & (row > 0)) | ((row % r2 == r2 - 1) & (row < rows - 1))
        s[0][now] = s[0][now] + jnp.where(edge[None], face_y[now], 0.0)

    each(counts[0], join)
    mats = (t, s[1], s[2])
    for level, (count, base) in enumerate(zip(counts, bases)):
        if level:

            def coarsen(at, step):
                whole = (iota((rows, LANES), 0) % 2**level == 0) & (iota((rows, LANES), 1) % 2**level == 0)
                mean = 0.125 * fold(mats[level - 1][pl.ds(at + 1, step)], 2 ** (level - 1))
                mats[level][pl.ds(at // 2 + 1, step // 2)] = jnp.where(whole[None], mean, 0.0)

            each(counts[level - 1], coarsen)
        seal(mats[level], count)
        fill_table(mats[level], table, level, count, base)
    cycle(s, e, t, table, counts, bases, place, out, c2, r2, pad)


def shifted(a):
    zero = jnp.zeros_like(a[:1])
    return jnp.concatenate([zero, a[:-1]], axis=0), jnp.concatenate([a[1:], zero], axis=0)


def apply_off(e, fx, fy, fz):
    before, ahead = shifted(e)
    out = fx[:-1] * before + fx[1:] * ahead
    out = out + fy * lower(e, 1) + upper(fy * e, 1)
    return out + fz * lower(e, 2) + upper(fz * e, 2)


def raise_window(window_ref, flat, out):
    planes, rows, _ = window_ref.shape
    values = select(window_ref[...].reshape(planes * rows, LANES), spread_matrix(LANES))
    flat[pl.ds(0, planes * rows, 2)] = values
    flat[pl.ds(1, planes * rows, 2)] = values
    v = flat[...].reshape(planes, 1, 2 * rows, LANES)
    out[...] = jnp.broadcast_to(v, (planes, 2, 2 * rows, LANES)).reshape(2 * planes, 2 * rows, LANES)


def level1_kernel(
    offset, place, long1, outer, inner, window1, payload, state_far,
    src, mat, flat, prolonged, fx, fy, fz, diag, inv, err, c, state, wide, narrow, sheet, semaphores,
):
    low_x = place[0] == 1
    total, length, depth = src.shape
    count, rows = total - 8, length - 8
    both = (inner, outer)
    zero = jnp.zeros((length, depth), F32)
    src[0] = zero
    src[total - 1] = zero
    for flag, base, side in ((low_x, 4, -1), (jnp.logical_not(low_x), count + 3, 1)):
        unpack(both, flag, mat, base, side, 4, unpack(both, flag, src, base, side, 3, offset))
    for n, ref in enumerate((src, mat)):
        ref[pl.ds(4, count)] = long1[n]
    raise_window(window1, flat, prolonged)
    row, lane = iota((length, depth), 0), iota((length, depth), 1)
    ends = as_float(lane == 0) + as_float(lane == depth - 1)
    def chunks(margin):
        first, last = margin, total - margin
        return [(at, min(LEVEL1_STEP, last - at)) for at in range(first, last, LEVEL1_STEP)]

    for at, n in chunks(1):
        here = slice(at, at + n)
        a, before, ahead = mat[here], mat[at - 1 : at + n - 1], mat[at + 1 : at + n + 1]
        down, up = lower(a, 1), upper(a, 1)
        f = harmonic(mat[at - 1 : at + n], mat[at : at + n + 1], 0.25)
        w_y = harmonic(a, down, 0.25)
        w_z = jnp.where(lane[None] == 0, 0.0, harmonic(a, lower(a, 2), 0.25))
        outside = ends[None] + as_float(before <= 0.0) + as_float(ahead <= 0.0) + as_float(down <= 0.0) + as_float(up <= 0.0)
        diagonal = f[:-1] + f[1:] + w_y + upper(w_y, 1) + w_z + upper(w_z, 2) + 0.25 * a * outside
        inverse = jnp.where(a > 0.0, invert(jnp.maximum(diagonal, 1e-4)), 0.0)
        fx[at : at + n + 1], fy[here], fz[here], diag[here], inv[here] = f, w_y, w_z, diagonal, inverse
        err[here] = DAMPING * inverse * src[here] + prolonged[here]

    def off(v, at, n):
        here = slice(at, at + n)
        mid, w_y, w_z = v[here], fy[here], fz[here]
        out = fx[here] * v[at - 1 : at + n - 1] + fx[at + 1 : at + n + 1] * v[at + 1 : at + n + 1]
        out = out + w_y * lower(mid, 1) + upper(w_y * mid, 1)
        return here, mid, out + w_z * lower(mid, 2) + upper(w_z * mid, 2)

    for at, n in chunks(2):
        here, mid, more = off(err, at, n)
        c[here] = KEPT * mid + DAMPING * inv[here] * (src[here] + more)
    for at, n in chunks(3):
        here, mid, more = off(c, at, n)
        left = src[here] - diag[here] * mid + more
        src[here] = left
        value = DAMPING * inv[here] * left
        err[here] = value
        state[at - 3 : at + n - 3] = value
    base = count + 2
    state[base : base + count + 1] = fx[4 : count + 5]
    base += count + 1
    for n, ref in enumerate((fy, fz, inv, c, src)):
        state[base + n * count : base + (n + 1) * count] = ref[4 : 4 + count]
    leaving = pltpu.make_async_copy(state, state_far, semaphores.at[0])
    leaving.start()
    here, _, more = off(err, 4, count)
    t = (KEPT * src[here] + more)[:, 4 : 4 + rows].reshape(count // 2, 2, rows, depth)
    wide[...] = (t[:, 0] + t[:, 1]).reshape(count // 2 * rows, depth)
    half = wide.shape[0] // 2
    publish(wide[:half], wide[half:], narrow, sheet, payload, semaphores.at[1])
    leaving.wait()


def last_cycle_kernel(counts, bases, grid, c2, r2, place, blocks, table, state, partial, out, *scratch):
    s, e, t, pad = scratch[0:3], list(scratch[3:6]), scratch[6], scratch[7]
    view, flat, prolonged, tall, coarse, result, departures = scratch[8:15]
    spread_blocks(lambda i, _, j, at: blocks[grid[0] * grid[1] - 1 - i * grid[1] - j, at], ((0, s[0]),), grid, c2, r2)
    cycle(s, e, t, table, counts, bases, place, view, c2, r2, pad)
    raise_window(view, flat, prolonged)
    count, rows, depth = partial.shape
    c1, r1 = count // 2, rows // 2
    v = prolonged[3 : c1 + 5] + state[: c1 + 2]
    here = v[1:-1]
    base = 2 * c1 + 3
    w_x = state[c1 + 2 : base]
    w_y, w_z, inverse, before, left = (state[base + n * c1 : base + (n + 1) * c1] for n in range(5))
    off = w_x[:-1] * v[:-2] + w_x[1:] * v[2:]
    off = off + w_y * lower(here, 1) + upper(w_y * here, 1) + w_z * lower(here, 2) + upper(w_z * here, 2)
    total = before + KEPT * here + DAMPING * inverse * (left + off)
    coarse[...] = total[:, 4 : 4 + r1].reshape(c1 * r1, LANES)
    values = select(coarse[...], spread_matrix(depth))
    for piece in range(depth // LANES):
        z = slice(piece * LANES, (piece + 1) * LANES)
        tall[piece, pl.ds(0, c1 * r1, 2)] = values[:, z]
        tall[piece, pl.ds(1, c1 * r1, 2)] = values[:, z]
    leaving = []
    for k in range(c1):
        for piece in range(depth // LANES):
            z = slice(piece * LANES, (piece + 1) * LANES)
            more = tall[piece, k * rows : (k + 1) * rows]
            result[2 * k, :, z] = partial[2 * k, :, z] + more
            result[2 * k + 1, :, z] = partial[2 * k + 1, :, z] + more
        if k % 2 == 1:
            planes = pl.ds(2 * k - 2, 4)
            leaving.append(pltpu.make_async_copy(result.at[planes], out.at[planes], departures.at[k // 2]))
            leaving[-1].start()
    for copy in leaving:
        copy.wait()


def size_of(shape):
    lead = math.prod(shape[:-2])
    return 4 * lead * (-(-shape[-2] // 8) * 8) * (-(-shape[-1] // LANES) * LANES)


def call(kernel, name, inputs, outputs, scratch=(), apart=(), cost=None):
    streamed = 0

    def held(n, x):
        nonlocal streamed
        if n in apart:
            return pltpu.with_memory_space_constraint(x, pltpu.HBM)
        if x.ndim == 1:
            return x
        if size_of(x.shape) <= HELD:
            return pltpu.with_memory_space_constraint(x, pltpu.VMEM)
        streamed += size_of(x.shape)
        return x

    def result(shape):
        nonlocal streamed
        if isinstance(shape, jax.ShapeDtypeStruct):
            streamed += size_of(shape.shape)
            return shape
        if far(shape):
            return pltpu.HBM(shape[1], F32)
        if size_of(shape) <= HELD:
            return pltpu.VMEM(shape, F32)
        streamed += size_of(shape)
        return jax.ShapeDtypeStruct(shape, F32)

    def far(x):
        return isinstance(x, tuple) and x[0] == "far"

    def space(n, x):
        return pltpu.HBM if n in apart else pltpu.SMEM if x.ndim == 1 else pltpu.VMEM

    specs = [pl.BlockSpec(memory_space=space(n, x)) for n, x in enumerate(inputs)]
    inputs = [held(n, x) for n, x in enumerate(inputs)]
    results = [result(shape) for shape in outputs]
    need = streamed + sum(size_of(x.shape) for x in scratch if len(getattr(x, "shape", ())) > 1) + 3 * MIB
    return pl.pallas_call(
        kernel,
        out_shape=results,
        in_specs=specs,
        out_specs=[pl.BlockSpec(memory_space=pltpu.HBM if far(x) else pltpu.VMEM) for x in outputs],
        scratch_shapes=list(scratch),
        compiler_params=pltpu.CompilerParams(vmem_limit_bytes=max(need, 8 * MIB)),
        name=name,
        cost_estimate=None if cost is None else pl.CostEstimate(flops=cost, bytes_accessed=0, transcendentals=0),
    )(*inputs)


def swaps(count):
    inner = [(i, i + 1) for i in range(0, count - 1, 2)]
    outer = [(i, i + 1) for i in range(1, count - 1, 2)]
    return [pairs + [(b, a) for a, b in pairs] for pairs in (inner, outer)]


def local(right_side, potential, phase, permeability):
    gx, gy = lax.axis_size("gx"), lax.axis_size("gy")
    devices = gx * gy
    here_x, here_y = lax.axis_index("gx"), lax.axis_index("gy")
    place = jnp.stack([here_x % 2, here_y % 2, here_x, here_y]).astype(jnp.int32)
    count, rows, depth = right_side.shape
    c1, r1, d1 = count // 2, rows // 2, depth // 2
    c2, r2 = c1 // 2, r1 // 2
    pieces = depth // LANES
    swap_x, swap_y = swaps(gx), swaps(gy)
    VM = lambda *shape: pltpu.VMEM(shape, F32)

    brick = (count, rows, depth)
    face = (3, rows, depth)
    DMA = pltpu.SemaphoreType.DMA
    sheet = (devices, c2 // 2 * r2, LANES)
    sheet2 = (devices // 2, c2 * r2 + 2 * r2, LANES)
    material, potential_here, source_here, inner, outer, even, odd = call(
        faces_kernel, "faces", (place, permeability, potential, phase, right_side),
        (brick, brick, brick, face, face, (3, count, depth), (3, count, depth)),
        (pltpu.VMEM(brick, jnp.int32), pltpu.SMEM(permeability.shape, F32), pltpu.SemaphoreType.DMA((4,))),
        apart=(1, 2, 3, 4),
    )
    even = lax.ppermute(even, "gy", swap_y[0])
    odd = lax.ppermute(odd, "gy", swap_y[1])
    outer = lax.ppermute(outer, "gx", swap_x[1])
    inner = lax.ppermute(inner, "gx", swap_x[0])

    strip = (count * pieces + c1, 8, LANES)
    total = 2 * c1 * rows + 4 * rows
    residual, coarse, even, odd = call(
        residual_kernel, "residual", (place, source_here, potential_here, material, outer, even, odd, inner),
        (brick, (total // 2, LANES), strip, strip),
        (
            VM(total, depth), VM(total, LANES), VM(4, count, 8, depth), VM(count + 2, rows, depth), VM(count + 2, rows, depth),
        ),
    )
    even = lax.ppermute(even, "gy", swap_y[0])
    odd = lax.ppermute(odd, "gy", swap_y[1])
    small = c2 * r1 + 2 * r1
    (payload,) = call(
        functools.partial(payload_kernel, c1, r1), "payload", (coarse,), (("far", sheet2),),
        (VM(2, small, d1), VM(small, LANES), VM(*sheet2), DMA),
    )
    groups = [[(2 * i + c) * gy + j for i in range(gx // 2) for j in range(gy)] for c in range(2)]
    blocks = lax.all_to_all(payload, ("gx", "gy"), 0, 0, axis_index_groups=groups)
    strip = (strip_length(rows, depth) + strip_length(r1, d1), 8, LANES)
    long_shape = (2, count, rows + 8, depth)
    inner, outer, long, long1 = call(
        strips_kernel, "strips", (place, residual, material, coarse, even, odd),
        (strip, strip, ("far", long_shape), (2, c1, r1 + 8, d1)),
        (VM(*long_shape), DMA), cost=10**11,
    )
    outer = lax.ppermute(outer, "gx", swap_x[1])
    inner = lax.ppermute(inner, "gx", swap_x[0])

    (blocks,) = call(pass_kernel, "pass", (blocks, long1), (sheet2,))
    others = lax.ppermute(blocks, "gx", swap_x[0])
    counts = tuple(gx * c2 // 2 // k for k in (1, 2, 4))
    bases = (0, counts[0] + 1, counts[0] + counts[1] + 2)
    work = cycle_shapes(counts, gy * r2, c2)
    view = (c2 + 4, r2 + 4, LANES)
    window1, table = call(
        functools.partial(first_cycle_kernel, counts, bases, (gx, gy), c2, r2), "cycle1", (place, blocks, others),
        (view, (4, sum(counts) + 3, gy * r2, LANES)), work,
    )
    frame = (c1 + 8, r1 + 8, d1)
    flat = VM((c2 + 4) * (r2 + 4) * 2, LANES)
    state = (7 * c1 + 3, r1 + 8, d1)
    tall = VM(c1 + 9, r1 + 8, d1)
    payload, held = call(
        functools.partial(level1_kernel, strip_length(rows, depth)), "level1", (place, long1, outer, inner, window1), (("far", sheet), ("far", state)),
        (
            VM(*frame), VM(*frame), flat, VM(*frame), tall, VM(*frame), VM(*frame), VM(*frame), VM(*frame), VM(*frame),
            VM(*frame), VM(*state), VM(c1 // 2 * r1, d1), VM(c1 // 4 * r1, LANES), VM(*sheet), pltpu.SemaphoreType.DMA((2,)),
        ),
    )
    blocks = lax.all_to_all(payload, ("gx", "gy"), 0, 0, axis_index_groups=[list(range(devices))[::-1]])
    wide = (count + 8, rows + 8, depth)
    partial, held = call(
        functools.partial(smooth_kernel, (gx, gy)), "smooth", (place, potential, held, long, outer, inner), (brick, state),
        (
            VM(*wide), VM(*wide), VM(2, *wide), VM(*wide), VM(count + 9, rows + 8, depth), VM(*wide), VM(*wide), VM(*wide),
            VM(*brick), pltpu.SemaphoreType.DMA((4,)),
        ),
        apart=(1, 2, 3),
    )
    (out,) = call(
        functools.partial(last_cycle_kernel, counts, bases, (gx, gy), c2, r2), "cycle2",
        (place, blocks, table, held, partial), (("far", brick),),
        (
            *work, VM(*view), flat, VM(*frame), VM(pieces, c1 * rows, LANES), VM(c1 * r1, LANES), VM(*brick),
            pltpu.SemaphoreType.DMA((c1 // 2,)),
        ),
    )
    return out


def solution(mesh):
    placed = (P("gx", "gy", None), P("gx", "gy", None), P("gx", "gy", None), P())
    return jax.shard_map(local, mesh=mesh, in_specs=placed, out_specs=P("gx", "gy", None), check_vma=False)
```

```python
import functools
import math

import jax
import jax.numpy as jnp
from jax import lax
from jax.experimental import pallas as pl
from jax.experimental.pallas import tpu as pltpu
from jax.sharding import PartitionSpec as P

DEG = 4
COARSE_SWEEPS = 4
THETA = 1.15
DELTA = 0.85
SIGMA = 1.15 / 0.85
DAMPING = 0.6
KEPT = 1.0 - DAMPING
F32 = jnp.float32
LANES = 128
MIB = 1024 * 1024
HELD = 4 * MIB
SMOOTH_STEP = 4
LEVEL1_STEP = 7


def iota(shape, axis):
    return lax.broadcasted_iota(jnp.int32, shape, axis)


def invert(x):
    guess = pl.reciprocal(x, approx=True)
    return guess * (2.0 - x * guess)


def harmonic(a, b, scale):
    return (2.0 * scale) * a * b * invert(jnp.maximum(a + b, 1e-3))


def pair_matrix(size, offset=0):
    column = iota((size, LANES), 1)
    return ((column >= offset) & (iota((size, LANES), 0) // 2 == column - offset)).astype(jnp.bfloat16)


def spread_matrix(width):
    return (iota((LANES, width), 1) // 2 == iota((LANES, width), 0)).astype(jnp.bfloat16)


def select(values, matrix):
    high = values.astype(jnp.bfloat16)
    rest = (values - high.astype(F32)).astype(jnp.bfloat16)
    return jnp.dot(high, matrix, preferred_element_type=F32) + jnp.dot(rest, matrix, preferred_element_type=F32)


def lower(x, axis, stride=1):
    return pltpu.roll(x, stride, axis)


def upper(x, axis, stride=1):
    return pltpu.roll(x, x.shape[axis] - stride, axis)


def as_float(condition):
    return jnp.where(condition, 1.0, 0.0)


def faces_kernel(
    place, permeability, potential, phase, source,
    material, pot, src, inner, outer, even, odd,
    ids, values, semaphores,
):
    arriving = [
        pltpu.make_async_copy(a, b, semaphores.at[n])
        for n, (a, b) in enumerate(((permeability, values), (phase, ids), (potential, pot), (source, src)))
    ]
    for copy in arriving:
        copy.start()
    low_x, low_y = place[0] == 1, place[1] == 1
    count, rows = pot.shape[:2]
    arriving[0].wait()
    arriving[1].wait()
    p0, p1, p2 = values[0], values[1], values[2]
    for i in range(count):
        here = ids[i]
        material[i] = jnp.where(here == 0, p0, jnp.where(here == 1, p1, p2))
    last = count - 1
    first = jnp.where(low_x, 0, last)
    second = jnp.where(low_x, 1, last - 1)
    inner[1] = material[first]
    inner[2] = material[second]
    outer[1] = material[last - first]
    outer[2] = material[last - second]

    def edge(slot, ref, a, b):
        for i in range(count):
            low, high = ref[i, a : a + 1, :], ref[i, b : b + 1, :]
            even[slot, i : i + 1, :] = jnp.where(low_y, low, high)
            odd[slot, i : i + 1, :] = jnp.where(low_y, high, low)

    edge(1, material, 0, rows - 1)
    edge(2, material, 1, rows - 2)
    arriving[2].wait()
    inner[0] = pot[first]
    outer[0] = pot[last - first]
    edge(0, pot, 0, rows - 1)
    arriving[3].wait()


def residual_kernel(
    place, source, potential, material, outer, even, odd, inner,
    residual, coarse, strip_even, strip_odd,
    wide, narrow, y_faces, mat, pot,
):
    low_x, low_y = place[0] == 1, place[1] == 1
    count, rows, depth = source.shape
    c1, r1 = count // 2, rows // 2
    pieces = depth // LANES

    def ordered(flag, a, b):
        return jnp.where(flag, a, b), jnp.where(flag, b, a)

    x_low, x_high = ordered(low_x, inner[...], outer[...])
    y_low, y_high = ordered(low_y, even[...], odd[...])
    row, lane = iota((rows, depth), 0), iota((rows, depth), 1)
    first, last = row == 0, row == rows - 1
    for n, ref in enumerate((y_low[0], y_high[0], y_low[1], y_high[1])):
        for i in range(count):
            y_faces[n, i] = jnp.broadcast_to(ref[i : i + 1], (8, depth))
    mat[0], mat[count + 1] = x_low[1], x_high[1]
    pot[0], pot[count + 1] = x_low[0], x_high[0]
    mat[pl.ds(1, count)] = material[...]
    pot[pl.ds(1, count)] = potential[...]
    step = 4
    outside = as_float(lane == 0) + as_float(lane == depth - 1)

    def edge_count(faces):
        return as_float(faces[:1, :1] <= 0.0)

    outside = outside + jnp.where(first, edge_count(y_low[1]), 0.0) + jnp.where(last, edge_count(y_high[1]), 0.0)

    def beside(ref, n, at):
        return jnp.broadcast_to(ref[n, at : at + step, :1], (step, rows, depth))

    for at in range(0, count, step):
        here = slice(at + 1, at + 1 + step)
        a, v = mat[here], pot[here]
        faces = harmonic(mat[at : at + step + 1], mat[at + 1 : at + step + 2], 1.0)
        down = jnp.where(first[None], beside(y_faces, 2, at), lower(a, 1))
        w_down = harmonic(a, down, 1.0)
        w_top = harmonic(a[:, rows - 1 :], y_faces[3, at : at + step, :1], 1.0)
        w_up = jnp.where(last[None], jnp.broadcast_to(w_top, a.shape), upper(w_down, 1))
        w_back = jnp.where(lane[None] == 0, 0.0, harmonic(a, lower(a, 2), 1.0))
        w_front = upper(w_back, 2)
        v_down = jnp.where(first[None], beside(y_faces, 0, at), lower(v, 1))
        v_up = jnp.where(last[None], beside(y_faces, 1, at), upper(v, 1))
        edges = jnp.broadcast_to(outside[None], a.shape)
        if at == 0:
            edges = edges + jnp.where(iota((step, 1, 1), 0) == 0, edge_count(x_low[1])[None], 0.0)
        if at == count - step:
            edges = edges + jnp.where(iota((step, 1, 1), 0) == step - 1, edge_count(x_high[1])[None], 0.0)
        diagonal = faces[:-1] + faces[1:] + w_down + w_up + w_back + w_front + a * edges
        off = faces[:-1] * pot[at : at + step] + faces[1:] * pot[at + 2 : at + 2 + step] + w_down * v_down + w_up * v_up
        off = off + w_back * lower(v, 2) + w_front * upper(v, 2)
        left = source[at : at + step] - diagonal * v + off
        residual[at : at + step] = left
        for n, x in enumerate((left, a)):
            pair = x.reshape(step // 2, 2, rows, depth)
            to = n * c1 * rows + at // 2 * rows
            wide[to : to + step // 2 * rows] = (pair[:, 0] + pair[:, 1]).reshape(step // 2 * rows, depth)
        low = jnp.concatenate([left[:, :4], a[:, :4]], axis=1)
        high = jnp.concatenate([left[:, rows - 4 :], a[:, rows - 4 :]], axis=1)
        for ref, strip in ((strip_even, jnp.where(low_y, low, high)), (strip_odd, jnp.where(low_y, high, low))):
            for k in range(step):
                for piece in range(pieces):
                    ref[(at + k) * pieces + piece] = strip[k, :, piece * LANES : (piece + 1) * LANES]
    base = 2 * c1 * rows
    for n, both in enumerate((x_low[1] + x_low[2], x_high[1] + x_high[2], y_low[1] + y_low[2], y_high[1] + y_high[2])):
        wide[base + n * rows : base + (n + 1) * rows] = both
    narrow[...] = select(wide[...], pair_matrix(depth)) * 0.125
    half = narrow.shape[0] // 2
    coarse[...] = narrow[pl.ds(0, half, 2)] + narrow[pl.ds(1, half, 2)]
    for k in range(c1):
        s, m = coarse[k * r1 : (k + 1) * r1], coarse[(c1 + k) * r1 : (c1 + k + 1) * r1]
        low = jnp.concatenate([s[:4], m[:4]], axis=0)
        high = jnp.concatenate([s[r1 - 4 :], m[r1 - 4 :]], axis=0)
        strip_even[count * pieces + k] = jnp.where(low_y, low, high)
        strip_odd[count * pieces + k] = jnp.where(low_y, high, low)


def payload_kernel(c1, r1, coarse, payload, wide, narrow, sheet, semaphore):
    c2 = c1 // 2
    depth = coarse.shape[1]
    shape = (c1, r1, depth)
    s, m = coarse[: c1 * r1].reshape(shape), coarse[c1 * r1 : 2 * c1 * r1].reshape(shape)
    base = 2 * c1 * r1
    m_xlow, m_xhigh = coarse[base : base + r1], coarse[base + r1 : base + 2 * r1]
    base += 2 * r1
    m_ylow = jnp.stack([coarse[base + k : base + k + 1] for k in range(c1)])
    m_yhigh = jnp.stack([coarse[base + r1 + k : base + r1 + k + 1] for k in range(c1)])
    row, lane = iota(shape, 1), iota(shape, 2)
    first, last = row == 0, row == r1 - 1
    around = jnp.concatenate([m_xlow[None], m, m_xhigh[None]], axis=0)
    faces = harmonic(around[:-1], around[1:], 0.25)
    down = jnp.where(first, jnp.broadcast_to(m_ylow, shape), lower(m, 1))
    up = jnp.where(last, jnp.broadcast_to(m_yhigh, shape), upper(m, 1))
    w_down = harmonic(m, down, 0.25)
    w_up = jnp.where(last, harmonic(m, up, 0.25), upper(w_down, 1))
    w_back = jnp.where(lane == 0, 0.0, harmonic(m, lower(m, 2), 0.25))
    w_front = upper(w_back, 2)
    outside = as_float(lane == 0) + as_float(lane == depth - 1)
    for b in (down, up, around[:-2], around[2:]):
        outside = outside + as_float(b <= 0.0)
    diagonal = faces[:-1] + faces[1:] + w_down + w_up + w_back + w_front + 0.25 * m * outside
    e = DAMPING * s * invert(diagonal)
    y_low, y_high = w_down * e, w_up * e
    t = KEPT * s + w_back * lower(e, 2) + w_front * upper(e, 2)
    t = t + jnp.where(first, 0.0, w_down * lower(e, 1)) + jnp.where(last, 0.0, w_up * upper(e, 1))
    nothing = jnp.zeros((1, r1, depth), F32)
    t = t + faces[:-1] * jnp.concatenate([nothing, e[:-1]], axis=0) + faces[1:] * jnp.concatenate([e[1:], nothing], axis=0)
    base = c2 // 2 * r1

    def pairs(x):
        x = x.reshape(c2, 2, r1, depth)
        return (x[:, 0] + x[:, 1]).reshape(c2 * r1, depth)

    t, m = pairs(t), pairs(m)
    for n in range(2):
        wide[n, :base] = t[n * base : (n + 1) * base]
        wide[n, base + 2 * r1 :] = m[n * base : (n + 1) * base]
    wide[0, base : base + r1] = faces[0] * e[0]
    wide[0, base + r1 : base + 2 * r1] = faces[c1] * e[c1 - 1]
    for k in range(c1):
        wide[1, base + k : base + k + 1] = y_low[k, :1]
        wide[1, base + r1 + k : base + r1 + k + 1] = y_high[k, r1 - 1 :]
    block = packed(wide[0], wide[1], narrow)
    for parity in range(2):
        for n in range(block.shape[0] // 8):
            value = block[8 * n + 4 * parity : 8 * n + 4 * parity + 4]
            sheet[:, parity, :, n] = jnp.broadcast_to(value[None, None], (sheet.shape[0], sheet.shape[2], *value.shape))
    leaving = pltpu.make_async_copy(sheet, payload, semaphore)
    leaving.start()
    leaving.wait()


def packed(low, high, narrow):
    narrow[...] = (select(low, pair_matrix(LANES)) + select(high, pair_matrix(LANES, LANES // 2))) * 0.125
    half = narrow.shape[0] // 2
    return narrow[pl.ds(0, half, 2)] + narrow[pl.ds(1, half, 2)]


def publish(low, high, narrow, sheet, payload, semaphore):
    sheet[...] = jnp.broadcast_to(packed(low, high, narrow)[None], sheet.shape)
    leaving = pltpu.make_async_copy(sheet, payload, semaphore)
    leaving.start()
    leaving.wait()


def strips_kernel(place, residual, material, coarse, even, odd, inner, outer, long_far, long1, long, semaphore):
    low_x, low_y = place[0] == 1, place[1] == 1
    count, rows, depth = residual.shape
    pieces = depth // LANES
    c1, r1 = count // 2, rows // 2
    base = count * pieces

    def sides(at):
        a, b = even[at], odd[at]
        return jnp.where(low_y, a, b), jnp.where(low_y, b, a)

    for i in range(count):
        for piece in range(pieces):
            low, high = sides(i * pieces + piece)
            z = slice(piece * LANES, (piece + 1) * LANES)
            long[0, i, :, z] = jnp.concatenate([low[:4], residual[i, :, z], high[:4]], axis=0)
            long[1, i, :, z] = jnp.concatenate([low[4:], material[i, :, z], high[4:]], axis=0)
    leaving = pltpu.make_async_copy(long, long_far, semaphore)
    leaving.start()
    for k in range(c1):
        low, high = sides(base + k)
        s, m = coarse[k * r1 : (k + 1) * r1], coarse[(c1 + k) * r1 : (c1 + k + 1) * r1]
        long1[0, k] = jnp.concatenate([low[:4], s, high[:4]], axis=0)
        long1[1, k] = jnp.concatenate([low[4:], m, high[4:]], axis=0)

    def pack(out, flag):
        at = 0
        for n, planes in ((0, 3), (1, 4)):
            for away in range(1, planes + 1):
                k = jnp.where(flag, away - 1, count - away)
                ref = long.at[n] if away < planes else (residual, material)[n]
                for tile in range(ref.shape[1] // 8):
                    for piece in range(pieces):
                        out[at] = ref[k, tile * 8 : tile * 8 + 8, piece * LANES : (piece + 1) * LANES]
                        at += 1
        for n, planes in ((0, 3), (1, 4)):
            for away in range(1, planes + 1):
                low, high = away - 1, c1 - away
                if away == planes:
                    low, high = (n * c1 + low) * r1, (n * c1 + high) * r1
                    out[at] = jnp.where(flag, coarse[low : low + r1], coarse[high : high + r1])
                    at += 1
                    continue
                for tile in range((r1 + 8) // 8):
                    y = slice(tile * 8, tile * 8 + 8)
                    out[at] = jnp.where(flag, long1[n, low, y], long1[n, high, y])
                    at += 1

    pack(inner, low_x)
    pack(outer, jnp.logical_not(low_x))
    leaving.wait()


def strip_length(rows, depth):
    return (5 * (rows + 8) + 2 * rows) // 8 * (depth // LANES)


def unpack(source, flag, out, base, side, planes, at):
    rows = out.shape[1]
    for away in range(1, planes + 1):
        to = base + side * away
        first = 0
        if away == planes:
            first = 4
            edge = jnp.zeros((4, out.shape[2]), F32)
            out[to, :4] = edge
            out[to, rows - 4 :] = edge
        for row in range(first, rows - first, 8):
            for z in range(0, out.shape[2], LANES):
                out[to, row : row + 8, z : z + LANES] = jnp.where(flag, source[0][at], source[1][at])
                at += 1
    return at


def smooth_kernel(ends, place, potential_far, state_far, long, outer, inner, out, state, mat, res, x, d, fx, fy, fz, inv, potential, semaphores):
    arriving = pltpu.make_async_copy(potential_far, potential, semaphores.at[0])
    arriving.start()
    passing = pltpu.make_async_copy(state_far, state, semaphores.at[1])
    passing.start()
    count, rows, depth = potential.shape
    own = pl.ds(4, count)
    frames = [
        pltpu.make_async_copy(long.at[n], ref.at[own], semaphores.at[2 + n]) for n, ref in enumerate((res, mat))
    ]
    for copy in frames:
        copy.start()
    low_x = place[0] == 1
    count, rows, depth = potential.shape
    both = (inner, outer)
    for flag, base, side in ((low_x, 4, -1), (jnp.logical_not(low_x), count + 3, 1)):
        unpack(both, flag, mat, base, side, 4, unpack(both, flag, res, base, side, 3, 0))
    for copy in frames:
        copy.wait()
    total, length = count + 8, rows + 8
    row, lane = iota((length, depth), 0), iota((length, depth), 1)
    outside = as_float(lane == 0) + as_float(lane == depth - 1)
    outside = outside + as_float((row == 4) & (place[3] == 0)) + as_float((row == rows + 3) & (place[3] == ends[1] - 1))
    low_end, high_end = place[2] == 0, place[2] == ends[0] - 1

    def chunks(first, last, step):
        return [(at, min(step, last - at)) for at in range(first, last, step)]

    for at, n in chunks(1, total - 1, SMOOTH_STEP):
        here = slice(at, at + n)
        a = mat[here]
        faces = harmonic(mat[at - 1 : at + n], mat[at : at + n + 1], 1.0)
        w_down = harmonic(a, lower(a, 1), 1.0)
        w_back = jnp.where(lane[None] == 0, 0.0, harmonic(a, lower(a, 2), 1.0))
        plane = at + iota((n, 1, 1), 0)
        edges = outside[None] + as_float((plane == 4) & low_end) + as_float((plane == count + 3) & high_end)
        diagonal = faces[:-1] + faces[1:] + w_down + upper(w_down, 1) + w_back + upper(w_back, 2) + a * edges
        inverse = jnp.where(a > 0.0, invert(jnp.maximum(diagonal, 1e-3)), 0.0)
        fx[at : at + n + 1], fy[here], fz[here], inv[here] = faces, w_down, w_back, inverse
        scaled = inverse * res[here]
        res[here] = scaled
        x[0, here] = scaled * (1.0 / THETA)
    rho = 1.0 / SIGMA
    for turn in range(DEG - 1):
        if turn == DEG - 2:
            arriving.wait()
        following = 1.0 / (2.0 * SIGMA - rho)
        old, new = turn % 2, (turn + 1) % 2
        keep, gain = following * rho, 2.0 * following / DELTA
        for at, n in chunks(2 + turn, total - 2 - turn, SMOOTH_STEP):
            here = slice(at, at + n)
            v = x[old, here]
            w_down, w_back = fy[here], fz[here]
            off = fx[here] * x[old, at - 1 : at + n - 1] + fx[at + 1 : at + n + 1] * x[old, at + 1 : at + n + 1]
            off = off + w_down * lower(v, 1) + upper(w_down * v, 1)
            off = off + w_back * lower(v, 2) + upper(w_back * v, 2)
            before = v * keep if turn == 0 else d[here] * keep
            change = before + gain * (res[here] - v + inv[here] * off)
            if turn == DEG - 2:
                out[at - 4 : at + n - 4] = potential[at - 4 : at + n - 4] + (v + change)[:, 4 : 4 + rows]
            else:
                d[here] = change
                x[new, here] = v + change
        rho = following
    passing.wait()


HALF = LANES // 2


def seal(ref, count):
    low = iota(ref.shape[1:], 1) < HALF
    ref[0] = jnp.where(low, 0.0, pltpu.roll(ref[count], HALF, 1))
    ref[count + 1] = jnp.where(low, pltpu.roll(ref[1], HALF, 1), 0.0)


def each(count, body, most=8):
    step = min(count, most)
    if count // step <= 4:
        for n in range(count // step):
            body(n * step, step)
        return

    def run(n, _):
        body(n * step, step)
        return 0

    lax.fori_loop(0, count // step, run, 0)


def fill_table(mat, table, level, count, base):
    stride, scale = 2**level, 0.25 ** (level + 2)
    rows = mat.shape[1]
    row, lane = iota((rows, LANES), 0), iota((rows, LANES), 1)
    depth = lane % HALF
    above, beyond = row >= stride, depth >= stride
    outside = as_float(row == 0) + as_float(row == rows - stride) + as_float(depth == 0) + as_float(depth == HALF - stride)

    def body(at, step):
        a, before, ahead = mat[pl.ds(at + 1, step)], mat[pl.ds(at, step)], mat[pl.ds(at + 2, step)]
        w_before, w_ahead = harmonic(a, before, scale), harmonic(a, ahead, scale)
        w_down = jnp.where(above[None], harmonic(a, lower(a, 1, stride), scale), 0.0)
        w_back = jnp.where(beyond[None], harmonic(a, lower(a, 2, stride), scale), 0.0)
        plane = at + iota((step, 1, 1), 0)
        low = (lane < HALF)[None]
        edges = outside[None] + as_float((plane == 0) & low) + as_float((plane == count - 1) & jnp.logical_not(low))
        diagonal = w_before + w_ahead + w_down + upper(w_down, 1, stride) + w_back + upper(w_back, 2, stride)
        diagonal = diagonal + scale * a * edges
        table[0, pl.ds(base + at, step)] = w_before
        table[1, pl.ds(base + at, step)] = w_down
        table[2, pl.ds(base + at, step)] = w_back
        table[3, pl.ds(base + at, step)] = jnp.where(a > 0.0, invert(jnp.maximum(diagonal, 1e-4)), 0.0)

    each(count, body)
    table[0, base + count] = harmonic(mat[count], mat[count + 1], scale)


def fold(t, stride):
    a = t.reshape(t.shape[0] // 2, 2, *t.shape[1:])
    a = a[:, 0] + a[:, 1]
    a = a + upper(a, 1, stride)
    return a + upper(a, 2, stride)


def unfold(e, stride):
    e = e + lower(e, 1, stride)
    e = e + lower(e, 2, stride)
    return jnp.broadcast_to(e[:, None], (e.shape[0], 2, *e.shape[1:])).reshape(2 * e.shape[0], *e.shape[1:])


def off_diagonal(e, table, base, at, step, stride):
    v = e[pl.ds(at + 1, step)]
    total = table[0, pl.ds(base + at, step)] * e[pl.ds(at, step)]
    total = total + table[0, pl.ds(base + at + 1, step)] * e[pl.ds(at + 2, step)]
    fy, fz = table[1, pl.ds(base + at, step)], table[2, pl.ds(base + at, step)]
    total = total + fy * lower(v, 1, stride) + upper(fy * v, 1, stride)
    return v, total + fz * lower(v, 2, stride) + upper(fz * v, 2, stride)


def cycle(s, e, t, table, counts, bases, place, out, c2, r2, pad):
    for level, (count, base) in enumerate(zip(counts, bases)):
        s_l, e_l, stride = s[level], e[level], 2**level

        def start(at, step):
            e_l[pl.ds(at + 1, step)] = DAMPING * s_l[pl.ds(at + 1, step)] * table[3, pl.ds(base + at, step)]

        each(count, start)
        seal(e_l, count)
        if level == len(counts) - 1:
            break

        def remainder(at, step):
            _, off = off_diagonal(e_l, table, base, at, step, stride)
            left = KEPT * s_l[pl.ds(at + 1, step)] + off
            s[level + 1][pl.ds(at // 2 + 1, step // 2)] = 0.125 * fold(left, stride)

        each(count, remainder)

    def relax(s_l, source, target, base, count, stride):
        def sweep(at, step):
            v, off = off_diagonal(source, table, base, at, step, stride)
            inverse = table[3, pl.ds(base + at, step)]
            target[pl.ds(at + 1, step)] = KEPT * v + DAMPING * inverse * (s_l[pl.ds(at + 1, step)] + off)

        each(count, sweep)

    now, other = e[2], t
    for _ in range(COARSE_SWEEPS - 1):
        relax(s[2], now, other, bases[2], counts[2], 4)
        seal(other, counts[2])
        now, other = other, now
    for level in (1, 0):
        coarser, e_l, stride = now, e[level], 2**level

        def add(at, step):
            here = pl.ds(2 * at + 1, 2 * step)
            e_l[here] = e_l[here] + unfold(coarser[pl.ds(at + 1, step)], stride)

        each(counts[level + 1], add, 4)
        seal(e_l, counts[level])
        now = s[level]
        relax(s[level], e_l, now, bases[level], counts[level], stride)

    rows = t.shape[1]
    low = iota((rows, LANES), 1) < HALF
    pad[...] = jnp.zeros(pad.shape, F32)
    for n in range(c2 + 4):
        at = place[2] * c2 + n - 2
        second = at >= counts[0]
        inside = (at >= 0) & (at < 2 * counts[0])
        value = now[jnp.clip(at - jnp.where(second, counts[0], 0), 0, counts[0] - 1) + 1]
        value = jnp.where(second, pltpu.roll(value, HALF, 1), value)
        pad[n, 8 : 8 + rows, :] = jnp.where(low & inside, value, 0.0)
        out[n] = pad[n, pl.ds(place[3] * r2 + 6, r2 + 4), :]


def cycle_shapes(counts, rows, c2):
    out = [pltpu.VMEM((count + 2, rows, LANES), F32) for count in (*counts, *counts, counts[0])]
    return out + [pltpu.VMEM((c2 + 4, rows + 16, LANES), F32)]


def repeat(count, body):
    if count <= 8:
        for i in range(count):
            body(i, i % 2)
        return

    def two(n, _):
        body(2 * n, 0)
        body(2 * n + 1, 1)

    lax.fori_loop(0, count // 2, two, None)


def spread_blocks(fetch, outs, grid, c2, r2):
    gx, gy = grid
    length = c2 // 2 * r2
    low = iota((length, LANES), 1) < HALF

    def column(i, parity):
        for j in range(gy):
            for start, out in outs:
                a, b = (fetch(n, parity, j, slice(start, start + length)) for n in (i, i + gx // 2))
                parts = jnp.where(low, a, pltpu.roll(b, HALF, 1)), jnp.where(low, pltpu.roll(a, HALF, 1), b)
                for k in range(c2):
                    n = k % (c2 // 2)
                    out[i * c2 + k + 1, j * r2 : (j + 1) * r2, :] = parts[k // (c2 // 2)][n * r2 : (n + 1) * r2]

    repeat(gx // 2, column)


def clear_ends(refs, counts):
    for ref, count in zip(refs, counts):
        zero = jnp.zeros(ref.shape[1:], F32)
        ref[0] = zero
        ref[count + 1] = zero


def pass_kernel(blocks, _, out):
    out[...] = blocks[...]


def first_cycle_kernel(counts, bases, grid, c2, r2, place, mine, theirs, out, table, *scratch):
    s, e, t, pad = scratch[0:3], list(scratch[3:6]), scratch[6], scratch[7]
    gx, gy = grid
    rows = gy * r2
    own = c2 // 2 * r2
    clear_ends(s[:1], counts)
    odd = place[0] == 1

    def fetch(i, _, j, at):
        here = i * gy + j
        rows = []
        for n in range(at.start // 8, at.stop // 8):
            a, b = mine[here, n], theirs[here, n]
            rows += [jnp.where(odd, b, a), jnp.where(odd, a, b)]
        return jnp.concatenate(rows, axis=0)

    spread_blocks(fetch, ((0, s[0]), (own + 2 * r2, t)), grid, c2, r2)
    face_y = e[0]
    low = iota((2 * c2, LANES), 1) < HALF

    def edges(i, parity):
        for j in range(gy):
            a, b = (fetch(n, parity, j, slice(own, own + 2 * r2)) for n in (i, i + gx // 2))
            x_faces = jnp.where(low, a, pltpu.roll(b, HALF, 1))
            y_faces = jnp.where(low, pltpu.roll(a, HALF, 1), b)
            here = slice(j * r2, (j + 1) * r2)
            s[0][i * c2, here, :] = s[0][i * c2, here, :] + x_faces[:r2]
            s[0][(i + 1) * c2 + 1, here, :] = s[0][(i + 1) * c2 + 1, here, :] + x_faces[r2:]
            for k in range(c2):
                at = i * c2 + k + 1
                if j > 0:
                    face_y[at, j * r2 - 1 : j * r2, :] = y_faces[k : k + 1]
                if j < gy - 1:
                    face_y[at, (j + 1) * r2 : (j + 1) * r2 + 1, :] = y_faces[c2 + k : c2 + k + 1]

    repeat(gx // 2, edges)
    first, last = s[0][0], s[0][counts[0] + 1]
    low = iota(first.shape, 1) < HALF
    s[0][counts[0]] = s[0][counts[0]] + jnp.where(low, pltpu.roll(first, HALF, 1), 0.0)
    s[0][1] = s[0][1] + jnp.where(low, 0.0, pltpu.roll(last, HALF, 1))

    def join(at, step):
        now = pl.ds(at + 1, step)
        row = iota((rows, LANES), 0)
        edge = ((row % r2 == 0) & (row > 0)) | ((row % r2 == r2 - 1) & (row < rows - 1))
        s[0][now] = s[0][now] + jnp.where(edge[None], face_y[now], 0.0)

    each(counts[0], join)
    mats = (t, s[1], s[2])
    for level, (count, base) in enumerate(zip(counts, bases)):
        if level:

            def coarsen(at, step):
                whole = (iota((rows, LANES), 0) % 2**level == 0) & (iota((rows, LANES), 1) % 2**level == 0)
                mean = 0.125 * fold(mats[level - 1][pl.ds(at + 1, step)], 2 ** (level - 1))
                mats[level][pl.ds(at // 2 + 1, step // 2)] = jnp.where(whole[None], mean, 0.0)

            each(counts[level - 1], coarsen)
        seal(mats[level], count)
        fill_table(mats[level], table, level, count, base)
    cycle(s, e, t, table, counts, bases, place, out, c2, r2, pad)


def shifted(a):
    zero = jnp.zeros_like(a[:1])
    return jnp.concatenate([zero, a[:-1]], axis=0), jnp.concatenate([a[1:], zero], axis=0)


def apply_off(e, fx, fy, fz):
    before, ahead = shifted(e)
    out = fx[:-1] * before + fx[1:] * ahead
    out = out + fy * lower(e, 1) + upper(fy * e, 1)
    return out + fz * lower(e, 2) + upper(fz * e, 2)


def raise_window(window_ref, flat, out):
    planes, rows, _ = window_ref.shape
    values = select(window_ref[...].reshape(planes * rows, LANES), spread_matrix(LANES))
    flat[pl.ds(0, planes * rows, 2)] = values
    flat[pl.ds(1, planes * rows, 2)] = values
    v = flat[...].reshape(planes, 1, 2 * rows, LANES)
    out[...] = jnp.broadcast_to(v, (planes, 2, 2 * rows, LANES)).reshape(2 * planes, 2 * rows, LANES)


def level1_kernel(
    offset, place, long1, outer, inner, window1, payload, state_far,
    src, mat, flat, prolonged, fx, fy, fz, diag, inv, err, c, state, wide, narrow, sheet, semaphores,
):
    low_x = place[0] == 1
    total, length, depth = src.shape
    count, rows = total - 8, length - 8
    both = (inner, outer)
    zero = jnp.zeros((length, depth), F32)
    src[0] = zero
    src[total - 1] = zero
    for flag, base, side in ((low_x, 4, -1), (jnp.logical_not(low_x), count + 3, 1)):
        unpack(both, flag, mat, base, side, 4, unpack(both, flag, src, base, side, 3, offset))
    for n, ref in enumerate((src, mat)):
        ref[pl.ds(4, count)] = long1[n]
    raise_window(window1, flat, prolonged)
    row, lane = iota((length, depth), 0), iota((length, depth), 1)
    ends = as_float(lane == 0) + as_float(lane == depth - 1)
    def chunks(margin):
        first, last = margin, total - margin
        return [(at, min(LEVEL1_STEP, last - at)) for at in range(first, last, LEVEL1_STEP)]

    for at, n in chunks(1):
        here = slice(at, at + n)
        a, before, ahead = mat[here], mat[at - 1 : at + n - 1], mat[at + 1 : at + n + 1]
        down, up = lower(a, 1), upper(a, 1)
        f = harmonic(mat[at - 1 : at + n], mat[at : at + n + 1], 0.25)
        w_y = harmonic(a, down, 0.25)
        w_z = jnp.where(lane[None] == 0, 0.0, harmonic(a, lower(a, 2), 0.25))
        outside = ends[None] + as_float(before <= 0.0) + as_float(ahead <= 0.0) + as_float(down <= 0.0) + as_float(up <= 0.0)
        diagonal = f[:-1] + f[1:] + w_y + upper(w_y, 1) + w_z + upper(w_z, 2) + 0.25 * a * outside
        inverse = jnp.where(a > 0.0, invert(jnp.maximum(diagonal, 1e-4)), 0.0)
        fx[at : at + n + 1], fy[here], fz[here], diag[here], inv[here] = f, w_y, w_z, diagonal, inverse
        err[here] = DAMPING * inverse * src[here] + prolonged[here]

    def off(v, at, n):
        here = slice(at, at + n)
        mid, w_y, w_z = v[here], fy[here], fz[here]
        out = fx[here] * v[at - 1 : at + n - 1] + fx[at + 1 : at + n + 1] * v[at + 1 : at + n + 1]
        out = out + w_y * lower(mid, 1) + upper(w_y * mid, 1)
        return here, mid, out + w_z * lower(mid, 2) + upper(w_z * mid, 2)

    for at, n in chunks(2):
        here, mid, more = off(err, at, n)
        c[here] = KEPT * mid + DAMPING * inv[here] * (src[here] + more)
    for at, n in chunks(3):
        here, mid, more = off(c, at, n)
        left = src[here] - diag[here] * mid + more
        src[here] = left
        value = DAMPING * inv[here] * left
        err[here] = value
        state[at - 3 : at + n - 3] = value
    base = count + 2
    state[base : base + count + 1] = fx[4 : count + 5]
    base += count + 1
    for n, ref in enumerate((fy, fz, inv, c, src)):
        state[base + n * count : base + (n + 1) * count] = ref[4 : 4 + count]
    leaving = pltpu.make_async_copy(state, state_far, semaphores.at[0])
    leaving.start()
    here, _, more = off(err, 4, count)
    t = (KEPT * src[here] + more)[:, 4 : 4 + rows].reshape(count // 2, 2, rows, depth)
    wide[...] = (t[:, 0] + t[:, 1]).reshape(count // 2 * rows, depth)
    half = wide.shape[0] // 2
    publish(wide[:half], wide[half:], narrow, sheet, payload, semaphores.at[1])
    leaving.wait()


def last_cycle_kernel(counts, bases, grid, c2, r2, place, blocks, table, state, partial, out, *scratch):
    s, e, t, pad = scratch[0:3], list(scratch[3:6]), scratch[6], scratch[7]
    view, flat, prolonged, tall, coarse, result, departures = scratch[8:15]
    spread_blocks(lambda i, _, j, at: blocks[grid[0] * grid[1] - 1 - i * grid[1] - j, at], ((0, s[0]),), grid, c2, r2)
    cycle(s, e, t, table, counts, bases, place, view, c2, r2, pad)
    raise_window(view, flat, prolonged)
    count, rows, depth = partial.shape
    c1, r1 = count // 2, rows // 2
    v = prolonged[3 : c1 + 5] + state[: c1 + 2]
    here = v[1:-1]
    base = 2 * c1 + 3
    w_x = state[c1 + 2 : base]
    w_y, w_z, inverse, before, left = (state[base + n * c1 : base + (n + 1) * c1] for n in range(5))
    off = w_x[:-1] * v[:-2] + w_x[1:] * v[2:]
    off = off + w_y * lower(here, 1) + upper(w_y * here, 1) + w_z * lower(here, 2) + upper(w_z * here, 2)
    total = before + KEPT * here + DAMPING * inverse * (left + off)
    coarse[...] = total[:, 4 : 4 + r1].reshape(c1 * r1, LANES)
    values = select(coarse[...], spread_matrix(depth))
    for piece in range(depth // LANES):
        z = slice(piece * LANES, (piece + 1) * LANES)
        tall[piece, pl.ds(0, c1 * r1, 2)] = values[:, z]
        tall[piece, pl.ds(1, c1 * r1, 2)] = values[:, z]
    leaving = []
    for k in range(c1):
        for piece in range(depth // LANES):
            z = slice(piece * LANES, (piece + 1) * LANES)
            more = tall[piece, k * rows : (k + 1) * rows]
            result[2 * k, :, z] = partial[2 * k, :, z] + more
            result[2 * k + 1, :, z] = partial[2 * k + 1, :, z] + more
        if k % 2 == 1:
            planes = pl.ds(2 * k - 2, 4)
            leaving.append(pltpu.make_async_copy(result.at[planes], out.at[planes], departures.at[k // 2]))
            leaving[-1].start()
    for copy in leaving:
        copy.wait()


def size_of(shape):
    lead = math.prod(shape[:-2])
    return 4 * lead * (-(-shape[-2] // 8) * 8) * (-(-shape[-1] // LANES) * LANES)


def call(kernel, name, inputs, outputs, scratch=(), apart=(), cost=None):
    streamed = 0

    def held(n, x):
        nonlocal streamed
        if n in apart:
            return pltpu.with_memory_space_constraint(x, pltpu.HBM)
        if x.ndim == 1:
            return x
        if size_of(x.shape) <= HELD:
            return pltpu.with_memory_space_constraint(x, pltpu.VMEM)
        streamed += size_of(x.shape)
        return x

    def result(shape):
        nonlocal streamed
        if isinstance(shape, jax.ShapeDtypeStruct):
            streamed += size_of(shape.shape)
            return shape
        if far(shape):
            return pltpu.HBM(shape[1], F32)
        if size_of(shape) <= HELD:
            return pltpu.VMEM(shape, F32)
        streamed += size_of(shape)
        return jax.ShapeDtypeStruct(shape, F32)

    def far(x):
        return isinstance(x, tuple) and x[0] == "far"

    def space(n, x):
        return pltpu.HBM if n in apart else pltpu.SMEM if x.ndim == 1 else pltpu.VMEM

    specs = [pl.BlockSpec(memory_space=space(n, x)) for n, x in enumerate(inputs)]
    inputs = [held(n, x) for n, x in enumerate(inputs)]
    results = [result(shape) for shape in outputs]
    need = streamed + sum(size_of(x.shape) for x in scratch if len(getattr(x, "shape", ())) > 1) + 3 * MIB
    return pl.pallas_call(
        kernel,
        out_shape=results,
        in_specs=specs,
        out_specs=[pl.BlockSpec(memory_space=pltpu.HBM if far(x) else pltpu.VMEM) for x in outputs],
        scratch_shapes=list(scratch),
        compiler_params=pltpu.CompilerParams(vmem_limit_bytes=max(need, 8 * MIB)),
        name=name,
        cost_estimate=None if cost is None else pl.CostEstimate(flops=cost, bytes_accessed=0, transcendentals=0),
    )(*inputs)


def swaps(count):
    inner = [(i, i + 1) for i in range(0, count - 1, 2)]
    outer = [(i, i + 1) for i in range(1, count - 1, 2)]
    return [pairs + [(b, a) for a, b in pairs] for pairs in (inner, outer)]


def local(right_side, potential, phase, permeability):
    gx, gy = lax.axis_size("gx"), lax.axis_size("gy")
    devices = gx * gy
    here_x, here_y = lax.axis_index("gx"), lax.axis_index("gy")
    place = jnp.stack([here_x % 2, here_y % 2, here_x, here_y]).astype(jnp.int32)
    count, rows, depth = right_side.shape
    c1, r1, d1 = count // 2, rows // 2, depth // 2
    c2, r2 = c1 // 2, r1 // 2
    pieces = depth // LANES
    swap_x, swap_y = swaps(gx), swaps(gy)
    VM = lambda *shape: pltpu.VMEM(shape, F32)

    brick = (count, rows, depth)
    face = (3, rows, depth)
    DMA = pltpu.SemaphoreType.DMA
    sheet = (devices, c2 // 2 * r2, LANES)
    sheet2 = (gx // 2, 2, gy, (c2 * r2 + 2 * r2) // 8, 4, LANES)
    material, potential_here, source_here, inner, outer, even, odd = call(
        faces_kernel, "faces", (place, permeability, potential, phase, right_side),
        (brick, brick, brick, face, face, (3, count, depth), (3, count, depth)),
        (pltpu.VMEM(brick, jnp.int32), pltpu.SMEM(permeability.shape, F32), pltpu.SemaphoreType.DMA((4,))),
        apart=(1, 2, 3, 4),
    )
    even = lax.ppermute(even, "gy", swap_y[0])
    odd = lax.ppermute(odd, "gy", swap_y[1])
    outer = lax.ppermute(outer, "gx", swap_x[1])
    inner = lax.ppermute(inner, "gx", swap_x[0])

    strip = (count * pieces + c1, 8, LANES)
    total = 2 * c1 * rows + 4 * rows
    residual, coarse, even, odd = call(
        residual_kernel, "residual", (place, source_here, potential_here, material, outer, even, odd, inner),
        (brick, (total // 2, LANES), strip, strip),
        (
            VM(total, depth), VM(total, LANES), VM(4, count, 8, depth), VM(count + 2, rows, depth), VM(count + 2, rows, depth),
        ),
    )
    even = lax.ppermute(even, "gy", swap_y[0])
    odd = lax.ppermute(odd, "gy", swap_y[1])
    small = c2 * r1 + 2 * r1
    (payload,) = call(
        functools.partial(payload_kernel, c1, r1), "payload", (coarse,), (("far", sheet2),),
        (VM(2, small, d1), VM(small, LANES), VM(*sheet2), DMA),
    )
    blocks = lax.all_to_all(payload.reshape(devices, *sheet2[3:]), ("gx", "gy"), 0, 0)
    strip = (strip_length(rows, depth) + strip_length(r1, d1), 8, LANES)
    long_shape = (2, count, rows + 8, depth)
    inner, outer, long, long1 = call(
        strips_kernel, "strips", (place, residual, material, coarse, even, odd),
        (strip, strip, ("far", long_shape), (2, c1, r1 + 8, d1)),
        (VM(*long_shape), DMA), cost=10**11,
    )
    outer = lax.ppermute(outer, "gx", swap_x[1])
    inner = lax.ppermute(inner, "gx", swap_x[0])

    others = lax.ppermute(blocks, "gx", swap_x[0])
    counts = tuple(gx * c2 // 2 // k for k in (1, 2, 4))
    bases = (0, counts[0] + 1, counts[0] + counts[1] + 2)
    work = cycle_shapes(counts, gy * r2, c2)
    view = (c2 + 4, r2 + 4, LANES)
    window1, table = call(
        functools.partial(first_cycle_kernel, counts, bases, (gx, gy), c2, r2), "cycle1", (place, blocks, others),
        (view, (4, sum(counts) + 3, gy * r2, LANES)), work,
    )
    frame = (c1 + 8, r1 + 8, d1)
    flat = VM((c2 + 4) * (r2 + 4) * 2, LANES)
    state = (7 * c1 + 3, r1 + 8, d1)
    tall = VM(c1 + 9, r1 + 8, d1)
    payload, held = call(
        functools.partial(level1_kernel, strip_length(rows, depth)), "level1", (place, long1, outer, inner, window1), (("far", sheet), ("far", state)),
        (
            VM(*frame), VM(*frame), flat, VM(*frame), tall, VM(*frame), VM(*frame), VM(*frame), VM(*frame), VM(*frame),
            VM(*frame), VM(*state), VM(c1 // 2 * r1, d1), VM(c1 // 4 * r1, LANES), VM(*sheet), pltpu.SemaphoreType.DMA((2,)),
        ),
    )
    blocks = lax.all_to_all(payload, ("gx", "gy"), 0, 0, axis_index_groups=[list(range(devices))[::-1]])
    wide = (count + 8, rows + 8, depth)
    partial, held = call(
        functools.partial(smooth_kernel, (gx, gy)), "smooth", (place, potential, held, long, outer, inner), (brick, state),
        (
            VM(*wide), VM(*wide), VM(2, *wide), VM(*wide), VM(count + 9, rows + 8, depth), VM(*wide), VM(*wide), VM(*wide),
            VM(*brick), pltpu.SemaphoreType.DMA((4,)),
        ),
        apart=(1, 2, 3),
    )
    (out,) = call(
        functools.partial(last_cycle_kernel, counts, bases, (gx, gy), c2, r2), "cycle2",
        (place, blocks, table, held, partial), (("far", brick),),
        (
            *work, VM(*view), flat, VM(*frame), VM(pieces, c1 * rows, LANES), VM(c1 * r1, LANES), VM(*brick),
            pltpu.SemaphoreType.DMA((c1 // 2,)),
        ),
    )
    return out


def solution(mesh):
    placed = (P("gx", "gy", None), P("gx", "gy", None), P("gx", "gy", None), P())
    return jax.shard_map(local, mesh=mesh, in_specs=placed, out_specs=P("gx", "gy", None), check_vma=False)
```

```python
import functools
import math

import jax
import jax.numpy as jnp
from jax import lax
from jax.experimental import pallas as pl
from jax.experimental.pallas import tpu as pltpu
from jax.sharding import PartitionSpec as P

DEG = 4
COARSE_SWEEPS = 4
THETA = 1.15
DELTA = 0.85
SIGMA = 1.15 / 0.85
DAMPING = 0.6
KEPT = 1.0 - DAMPING
F32 = jnp.float32
LANES = 128
MIB = 1024 * 1024
HELD = 4 * MIB
SMOOTH_STEP = 4
LEVEL1_STEP = 7


def iota(shape, axis):
    return lax.broadcasted_iota(jnp.int32, shape, axis)


def invert(x):
    guess = pl.reciprocal(x, approx=True)
    return guess * (2.0 - x * guess)


def harmonic(a, b, scale):
    return (2.0 * scale) * a * b * invert(jnp.maximum(a + b, 1e-3))


def pair_matrix(size, offset=0):
    column = iota((size, LANES), 1)
    return ((column >= offset) & (iota((size, LANES), 0) // 2 == column - offset)).astype(jnp.bfloat16)


def spread_matrix(width):
    return (iota((LANES, width), 1) // 2 == iota((LANES, width), 0)).astype(jnp.bfloat16)


def select(values, matrix):
    high = values.astype(jnp.bfloat16)
    rest = (values - high.astype(F32)).astype(jnp.bfloat16)
    return jnp.dot(high, matrix, preferred_element_type=F32) + jnp.dot(rest, matrix, preferred_element_type=F32)


def lower(x, axis, stride=1):
    return pltpu.roll(x, stride, axis)


def upper(x, axis, stride=1):
    return pltpu.roll(x, x.shape[axis] - stride, axis)


def as_float(condition):
    return jnp.where(condition, 1.0, 0.0)


def faces_kernel(
    place, permeability, potential, phase, source,
    material, pot, src, inner, outer, even, odd,
    ids, values, semaphores,
):
    arriving = [
        pltpu.make_async_copy(a, b, semaphores.at[n])
        for n, (a, b) in enumerate(((permeability, values), (phase, ids), (potential, pot), (source, src)))
    ]
    for copy in arriving:
        copy.start()
    low_x, low_y = place[0] == 1, place[1] == 1
    count, rows = pot.shape[:2]
    arriving[0].wait()
    arriving[1].wait()
    p0, p1, p2 = values[0], values[1], values[2]
    for i in range(count):
        here = ids[i]
        material[i] = jnp.where(here == 0, p0, jnp.where(here == 1, p1, p2))
    last = count - 1
    first = jnp.where(low_x, 0, last)
    second = jnp.where(low_x, 1, last - 1)
    inner[1] = material[first]
    inner[2] = material[second]
    outer[1] = material[last - first]
    outer[2] = material[last - second]

    def edge(slot, ref, a, b):
        for i in range(count):
            low, high = ref[i, a : a + 1, :], ref[i, b : b + 1, :]
            even[slot, i : i + 1, :] = jnp.where(low_y, low, high)
            odd[slot, i : i + 1, :] = jnp.where(low_y, high, low)

    edge(1, material, 0, rows - 1)
    edge(2, material, 1, rows - 2)
    arriving[2].wait()
    inner[0] = pot[first]
    outer[0] = pot[last - first]
    edge(0, pot, 0, rows - 1)
    arriving[3].wait()


def residual_kernel(
    place, source, potential, material, outer, even, odd, inner,
    residual, coarse, strip_even, strip_odd,
    wide, narrow, y_faces, mat, pot,
):
    low_x, low_y = place[0] == 1, place[1] == 1
    count, rows, depth = source.shape
    c1, r1 = count // 2, rows // 2
    pieces = depth // LANES

    def ordered(flag, a, b):
        return jnp.where(flag, a, b), jnp.where(flag, b, a)

    x_low, x_high = ordered(low_x, inner[...], outer[...])
    y_low, y_high = ordered(low_y, even[...], odd[...])
    row, lane = iota((rows, depth), 0), iota((rows, depth), 1)
    first, last = row == 0, row == rows - 1
    for n, ref in enumerate((y_low[0], y_high[0], y_low[1], y_high[1])):
        for i in range(count):
            y_faces[n, i] = jnp.broadcast_to(ref[i : i + 1], (8, depth))
    mat[0], mat[count + 1] = x_low[1], x_high[1]
    pot[0], pot[count + 1] = x_low[0], x_high[0]
    mat[pl.ds(1, count)] = material[...]
    pot[pl.ds(1, count)] = potential[...]
    step = 4
    outside = as_float(lane == 0) + as_float(lane == depth - 1)

    def edge_count(faces):
        return as_float(faces[:1, :1] <= 0.0)

    outside = outside + jnp.where(first, edge_count(y_low[1]), 0.0) + jnp.where(last, edge_count(y_high[1]), 0.0)

    def beside(ref, n, at):
        return jnp.broadcast_to(ref[n, at : at + step, :1], (step, rows, depth))

    for at in range(0, count, step):
        here = slice(at + 1, at + 1 + step)
        a, v = mat[here], pot[here]
        faces = harmonic(mat[at : at + step + 1], mat[at + 1 : at + step + 2], 1.0)
        down = jnp.where(first[None], beside(y_faces, 2, at), lower(a, 1))
        w_down = harmonic(a, down, 1.0)
        w_top = harmonic(a[:, rows - 1 :], y_faces[3, at : at + step, :1], 1.0)
        w_up = jnp.where(last[None], jnp.broadcast_to(w_top, a.shape), upper(w_down, 1))
        w_back = jnp.where(lane[None] == 0, 0.0, harmonic(a, lower(a, 2), 1.0))
        w_front = upper(w_back, 2)
        v_down = jnp.where(first[None], beside(y_faces, 0, at), lower(v, 1))
        v_up = jnp.where(last[None], beside(y_faces, 1, at), upper(v, 1))
        edges = jnp.broadcast_to(outside[None], a.shape)
        if at == 0:
            edges = edges + jnp.where(iota((step, 1, 1), 0) == 0, edge_count(x_low[1])[None], 0.0)
        if at == count - step:
            edges = edges + jnp.where(iota((step, 1, 1), 0) == step - 1, edge_count(x_high[1])[None], 0.0)
        diagonal = faces[:-1] + faces[1:] + w_down + w_up + w_back + w_front + a * edges
        off = faces[:-1] * pot[at : at + step] + faces[1:] * pot[at + 2 : at + 2 + step] + w_down * v_down + w_up * v_up
        off = off + w_back * lower(v, 2) + w_front * upper(v, 2)
        left = source[at : at + step] - diagonal * v + off
        residual[at : at + step] = left
        for n, x in enumerate((left, a)):
            pair = x.reshape(step // 2, 2, rows, depth)
            to = n * c1 * rows + at // 2 * rows
            wide[to : to + step // 2 * rows] = (pair[:, 0] + pair[:, 1]).reshape(step // 2 * rows, depth)
        low = jnp.concatenate([left[:, :4], a[:, :4]], axis=1)
        high = jnp.concatenate([left[:, rows - 4 :], a[:, rows - 4 :]], axis=1)
        for ref, strip in ((strip_even, jnp.where(low_y, low, high)), (strip_odd, jnp.where(low_y, high, low))):
            for k in range(step):
                for piece in range(pieces):
                    ref[(at + k) * pieces + piece] = strip[k, :, piece * LANES : (piece + 1) * LANES]
    base = 2 * c1 * rows
    for n, both in enumerate((x_low[1] + x_low[2], x_high[1] + x_high[2], y_low[1] + y_low[2], y_high[1] + y_high[2])):
        wide[base + n * rows : base + (n + 1) * rows] = both
    narrow[...] = select(wide[...], pair_matrix(depth)) * 0.125
    half = narrow.shape[0] // 2
    coarse[...] = narrow[pl.ds(0, half, 2)] + narrow[pl.ds(1, half, 2)]
    for k in range(c1):
        s, m = coarse[k * r1 : (k + 1) * r1], coarse[(c1 + k) * r1 : (c1 + k + 1) * r1]
        low = jnp.concatenate([s[:4], m[:4]], axis=0)
        high = jnp.concatenate([s[r1 - 4 :], m[r1 - 4 :]], axis=0)
        strip_even[count * pieces + k] = jnp.where(low_y, low, high)
        strip_odd[count * pieces + k] = jnp.where(low_y, high, low)


def payload_kernel(c1, r1, coarse, payload, wide, narrow, sheet, semaphore):
    c2 = c1 // 2
    depth = coarse.shape[1]
    shape = (c1, r1, depth)
    s, m = coarse[: c1 * r1].reshape(shape), coarse[c1 * r1 : 2 * c1 * r1].reshape(shape)
    base = 2 * c1 * r1
    m_xlow, m_xhigh = coarse[base : base + r1], coarse[base + r1 : base + 2 * r1]
    base += 2 * r1
    m_ylow = jnp.stack([coarse[base + k : base + k + 1] for k in range(c1)])
    m_yhigh = jnp.stack([coarse[base + r1 + k : base + r1 + k + 1] for k in range(c1)])
    row, lane = iota(shape, 1), iota(shape, 2)
    first, last = row == 0, row == r1 - 1
    around = jnp.concatenate([m_xlow[None], m, m_xhigh[None]], axis=0)
    faces = harmonic(around[:-1], around[1:], 0.25)
    down = jnp.where(first, jnp.broadcast_to(m_ylow, shape), lower(m, 1))
    up = jnp.where(last, jnp.broadcast_to(m_yhigh, shape), upper(m, 1))
    w_down = harmonic(m, down, 0.25)
    w_up = jnp.where(last, harmonic(m, up, 0.25), upper(w_down, 1))
    w_back = jnp.where(lane == 0, 0.0, harmonic(m, lower(m, 2), 0.25))
    w_front = upper(w_back, 2)
    outside = as_float(lane == 0) + as_float(lane == depth - 1)
    for b in (down, up, around[:-2], around[2:]):
        outside = outside + as_float(b <= 0.0)
    diagonal = faces[:-1] + faces[1:] + w_down + w_up + w_back + w_front + 0.25 * m * outside
    e = DAMPING * s * invert(diagonal)
    y_low, y_high = w_down * e, w_up * e
    t = KEPT * s + w_back * lower(e, 2) + w_front * upper(e, 2)
    t = t + jnp.where(first, 0.0, w_down * lower(e, 1)) + jnp.where(last, 0.0, w_up * upper(e, 1))
    nothing = jnp.zeros((1, r1, depth), F32)
    t = t + faces[:-1] * jnp.concatenate([nothing, e[:-1]], axis=0) + faces[1:] * jnp.concatenate([e[1:], nothing], axis=0)
    base = c2 // 2 * r1

    def pairs(x):
        x = x.reshape(c2, 2, r1, depth)
        return (x[:, 0] + x[:, 1]).reshape(c2 * r1, depth)

    t, m = pairs(t), pairs(m)
    for n in range(2):
        wide[n, :base] = t[n * base : (n + 1) * base]
        wide[n, base + 2 * r1 :] = m[n * base : (n + 1) * base]
    wide[0, base : base + r1] = faces[0] * e[0]
    wide[0, base + r1 : base + 2 * r1] = faces[c1] * e[c1 - 1]
    for k in range(c1):
        wide[1, base + k : base + k + 1] = y_low[k, :1]
        wide[1, base + r1 + k : base + r1 + k + 1] = y_high[k, r1 - 1 :]
    block = packed(wide[0], wide[1], narrow)
    for parity in range(2):
        for n in range(block.shape[0] // 8):
            value = block[8 * n + 4 * parity : 8 * n + 4 * parity + 4]
            sheet[:, parity, :, n] = jnp.broadcast_to(value[None, None], (sheet.shape[0], sheet.shape[2], *value.shape))
    leaving = pltpu.make_async_copy(sheet, payload, semaphore)
    leaving.start()
    leaving.wait()


def packed(low, high, narrow):
    narrow[...] = (select(low, pair_matrix(LANES)) + select(high, pair_matrix(LANES, LANES // 2))) * 0.125
    half = narrow.shape[0] // 2
    return narrow[pl.ds(0, half, 2)] + narrow[pl.ds(1, half, 2)]


def publish(low, high, narrow, sheet, payload, semaphore):
    sheet[...] = jnp.broadcast_to(packed(low, high, narrow)[None], sheet.shape)
    leaving = pltpu.make_async_copy(sheet, payload, semaphore)
    leaving.start()
    leaving.wait()


def strips_kernel(place, residual, material, coarse, even, odd, inner, outer, long, long1):
    low_x, low_y = place[0] == 1, place[1] == 1
    count, rows, depth = residual.shape
    pieces = depth // LANES
    c1, r1 = count // 2, rows // 2
    base = count * pieces

    def sides(at):
        a, b = even[at], odd[at]
        return jnp.where(low_y, a, b), jnp.where(low_y, b, a)

    for i in range(count):
        for piece in range(pieces):
            low, high = sides(i * pieces + piece)
            z = slice(piece * LANES, (piece + 1) * LANES)
            long[0, i, :, z] = jnp.concatenate([low[:4], residual[i, :, z], high[:4]], axis=0)
            long[1, i, :, z] = jnp.concatenate([low[4:], material[i, :, z], high[4:]], axis=0)
    for k in range(c1):
        low, high = sides(base + k)
        s, m = coarse[k * r1 : (k + 1) * r1], coarse[(c1 + k) * r1 : (c1 + k + 1) * r1]
        long1[0, k] = jnp.concatenate([low[:4], s, high[:4]], axis=0)
        long1[1, k] = jnp.concatenate([low[4:], m, high[4:]], axis=0)

    def pack(out, flag):
        at = 0
        for n, planes in ((0, 3), (1, 4)):
            for away in range(1, planes + 1):
                k = jnp.where(flag, away - 1, count - away)
                ref = long.at[n] if away < planes else (residual, material)[n]
                for tile in range(ref.shape[1] // 8):
                    for piece in range(pieces):
                        out[at] = ref[k, tile * 8 : tile * 8 + 8, piece * LANES : (piece + 1) * LANES]
                        at += 1
        for n, planes in ((0, 3), (1, 4)):
            for away in range(1, planes + 1):
                low, high = away - 1, c1 - away
                if away == planes:
                    low, high = (n * c1 + low) * r1, (n * c1 + high) * r1
                    out[at] = jnp.where(flag, coarse[low : low + r1], coarse[high : high + r1])
                    at += 1
                    continue
                for tile in range((r1 + 8) // 8):
                    y = slice(tile * 8, tile * 8 + 8)
                    out[at] = jnp.where(flag, long1[n, low, y], long1[n, high, y])
                    at += 1

    pack(inner, low_x)
    pack(outer, jnp.logical_not(low_x))


def strip_length(rows, depth):
    return (5 * (rows + 8) + 2 * rows) // 8 * (depth // LANES)


def unpack(source, flag, out, base, side, planes, at):
    rows = out.shape[1]
    for away in range(1, planes + 1):
        to = base + side * away
        first = 0
        if away == planes:
            first = 4
            edge = jnp.zeros((4, out.shape[2]), F32)
            out[to, :4] = edge
            out[to, rows - 4 :] = edge
        for row in range(first, rows - first, 8):
            for z in range(0, out.shape[2], LANES):
                out[to, row : row + 8, z : z + LANES] = jnp.where(flag, source[0][at], source[1][at])
                at += 1
    return at


def smooth_kernel(ends, place, potential_far, long, outer, inner, out, mat, res, x, d, fx, fy, fz, inv, potential, semaphores):
    arriving = pltpu.make_async_copy(potential_far, potential, semaphores.at[0])
    arriving.start()
    count, rows, depth = potential.shape
    res[pl.ds(4, count)] = long[0]
    mat[pl.ds(4, count)] = long[1]
    low_x = place[0] == 1
    count, rows, depth = potential.shape
    both = (inner, outer)
    for flag, base, side in ((low_x, 4, -1), (jnp.logical_not(low_x), count + 3, 1)):
        unpack(both, flag, mat, base, side, 4, unpack(both, flag, res, base, side, 3, 0))
    total, length = count + 8, rows + 8
    row, lane = iota((length, depth), 0), iota((length, depth), 1)
    outside = as_float(lane == 0) + as_float(lane == depth - 1)
    outside = outside + as_float((row == 4) & (place[3] == 0)) + as_float((row == rows + 3) & (place[3] == ends[1] - 1))
    low_end, high_end = place[2] == 0, place[2] == ends[0] - 1

    def chunks(first, last, step):
        return [(at, min(step, last - at)) for at in range(first, last, step)]

    for at, n in chunks(1, total - 1, SMOOTH_STEP):
        here = slice(at, at + n)
        a = mat[here]
        faces = harmonic(mat[at - 1 : at + n], mat[at : at + n + 1], 1.0)
        w_down = harmonic(a, lower(a, 1), 1.0)
        w_back = jnp.where(lane[None] == 0, 0.0, harmonic(a, lower(a, 2), 1.0))
        plane = at + iota((n, 1, 1), 0)
        edges = outside[None] + as_float((plane == 4) & low_end) + as_float((plane == count + 3) & high_end)
        diagonal = faces[:-1] + faces[1:] + w_down + upper(w_down, 1) + w_back + upper(w_back, 2) + a * edges
        inverse = jnp.where(a > 0.0, invert(jnp.maximum(diagonal, 1e-3)), 0.0)
        fx[at : at + n + 1], fy[here], fz[here], inv[here] = faces, w_down, w_back, inverse
        scaled = inverse * res[here]
        res[here] = scaled
        x[0, here] = scaled * (1.0 / THETA)
    rho = 1.0 / SIGMA
    for turn in range(DEG - 1):
        if turn == DEG - 2:
            arriving.wait()
        following = 1.0 / (2.0 * SIGMA - rho)
        old, new = turn % 2, (turn + 1) % 2
        keep, gain = following * rho, 2.0 * following / DELTA
        for at, n in chunks(2 + turn, total - 2 - turn, SMOOTH_STEP):
            here = slice(at, at + n)
            v = x[old, here]
            w_down, w_back = fy[here], fz[here]
            off = fx[here] * x[old, at - 1 : at + n - 1] + fx[at + 1 : at + n + 1] * x[old, at + 1 : at + n + 1]
            off = off + w_down * lower(v, 1) + upper(w_down * v, 1)
            off = off + w_back * lower(v, 2) + upper(w_back * v, 2)
            before = v * keep if turn == 0 else d[here] * keep
            change = before + gain * (res[here] - v + inv[here] * off)
            if turn == DEG - 2:
                out[at - 4 : at + n - 4] = potential[at - 4 : at + n - 4] + (v + change)[:, 4 : 4 + rows]
            else:
                d[here] = change
                x[new, here] = v + change
        rho = following


HALF = LANES // 2


def seal(ref, count):
    low = iota(ref.shape[1:], 1) < HALF
    ref[0] = jnp.where(low, 0.0, pltpu.roll(ref[count], HALF, 1))
    ref[count + 1] = jnp.where(low, pltpu.roll(ref[1], HALF, 1), 0.0)


def each(count, body, most=8):
    step = min(count, most)
    if count // step <= 4:
        for n in range(count // step):
            body(n * step, step)
        return

    def run(n, _):
        body(n * step, step)
        return 0

    lax.fori_loop(0, count // step, run, 0)


def fill_table(mat, table, level, count, base):
    stride, scale = 2**level, 0.25 ** (level + 2)
    rows = mat.shape[1]
    row, lane = iota((rows, LANES), 0), iota((rows, LANES), 1)
    depth = lane % HALF
    above, beyond = row >= stride, depth >= stride
    outside = as_float(row == 0) + as_float(row == rows - stride) + as_float(depth == 0) + as_float(depth == HALF - stride)

    def body(at, step):
        a, before, ahead = mat[pl.ds(at + 1, step)], mat[pl.ds(at, step)], mat[pl.ds(at + 2, step)]
        w_before, w_ahead = harmonic(a, before, scale), harmonic(a, ahead, scale)
        w_down = jnp.where(above[None], harmonic(a, lower(a, 1, stride), scale), 0.0)
        w_back = jnp.where(beyond[None], harmonic(a, lower(a, 2, stride), scale), 0.0)
        plane = at + iota((step, 1, 1), 0)
        low = (lane < HALF)[None]
        edges = outside[None] + as_float((plane == 0) & low) + as_float((plane == count - 1) & jnp.logical_not(low))
        diagonal = w_before + w_ahead + w_down + upper(w_down, 1, stride) + w_back + upper(w_back, 2, stride)
        diagonal = diagonal + scale * a * edges
        table[0, pl.ds(base + at, step)] = w_before
        table[1, pl.ds(base + at, step)] = w_down
        table[2, pl.ds(base + at, step)] = w_back
        table[3, pl.ds(base + at, step)] = jnp.where(a > 0.0, invert(jnp.maximum(diagonal, 1e-4)), 0.0)

    each(count, body)
    table[0, base + count] = harmonic(mat[count], mat[count + 1], scale)


def fold(t, stride):
    a = t.reshape(t.shape[0] // 2, 2, *t.shape[1:])
    a = a[:, 0] + a[:, 1]
    a = a + upper(a, 1, stride)
    return a + upper(a, 2, stride)


def unfold(e, stride):
    e = e + lower(e, 1, stride)
    e = e + lower(e, 2, stride)
    return jnp.broadcast_to(e[:, None], (e.shape[0], 2, *e.shape[1:])).reshape(2 * e.shape[0], *e.shape[1:])


def off_diagonal(e, table, base, at, step, stride):
    v = e[pl.ds(at + 1, step)]
    total = table[0, pl.ds(base + at, step)] * e[pl.ds(at, step)]
    total = total + table[0, pl.ds(base + at + 1, step)] * e[pl.ds(at + 2, step)]
    fy, fz = table[1, pl.ds(base + at, step)], table[2, pl.ds(base + at, step)]
    total = total + fy * lower(v, 1, stride) + upper(fy * v, 1, stride)
    return v, total + fz * lower(v, 2, stride) + upper(fz * v, 2, stride)


def cycle(s, e, t, table, counts, bases, place, out, c2, r2, pad):
    for level, (count, base) in enumerate(zip(counts, bases)):
        s_l, e_l, stride = s[level], e[level], 2**level

        def start(at, step):
            e_l[pl.ds(at + 1, step)] = DAMPING * s_l[pl.ds(at + 1, step)] * table[3, pl.ds(base + at, step)]

        each(count, start)
        seal(e_l, count)
        if level == len(counts) - 1:
            break

        def remainder(at, step):
            _, off = off_diagonal(e_l, table, base, at, step, stride)
            left = KEPT * s_l[pl.ds(at + 1, step)] + off
            s[level + 1][pl.ds(at // 2 + 1, step // 2)] = 0.125 * fold(left, stride)

        each(count, remainder)

    def relax(s_l, source, target, base, count, stride):
        def sweep(at, step):
            v, off = off_diagonal(source, table, base, at, step, stride)
            inverse = table[3, pl.ds(base + at, step)]
            target[pl.ds(at + 1, step)] = KEPT * v + DAMPING * inverse * (s_l[pl.ds(at + 1, step)] + off)

        each(count, sweep)

    now, other = e[2], t
    for _ in range(COARSE_SWEEPS - 1):
        relax(s[2], now, other, bases[2], counts[2], 4)
        seal(other, counts[2])
        now, other = other, now
    for level in (1, 0):
        coarser, e_l, stride = now, e[level], 2**level

        def add(at, step):
            here = pl.ds(2 * at + 1, 2 * step)
            e_l[here] = e_l[here] + unfold(coarser[pl.ds(at + 1, step)], stride)

        each(counts[level + 1], add, 4)
        seal(e_l, counts[level])
        now = s[level]
        relax(s[level], e_l, now, bases[level], counts[level], stride)

    rows = t.shape[1]
    low = iota((rows, LANES), 1) < HALF
    pad[...] = jnp.zeros(pad.shape, F32)
    for n in range(c2 + 4):
        at = place[2] * c2 + n - 2
        second = at >= counts[0]
        inside = (at >= 0) & (at < 2 * counts[0])
        value = now[jnp.clip(at - jnp.where(second, counts[0], 0), 0, counts[0] - 1) + 1]
        value = jnp.where(second, pltpu.roll(value, HALF, 1), value)
        pad[n, 8 : 8 + rows, :] = jnp.where(low & inside, value, 0.0)
        out[n] = pad[n, pl.ds(place[3] * r2 + 6, r2 + 4), :]


def cycle_shapes(counts, rows, c2):
    out = [pltpu.VMEM((count + 2, rows, LANES), F32) for count in (*counts, *counts, counts[0])]
    return out + [pltpu.VMEM((c2 + 4, rows + 16, LANES), F32)]


def repeat(count, body):
    if count <= 8:
        for i in range(count):
            body(i, i % 2)
        return

    def two(n, _):
        body(2 * n, 0)
        body(2 * n + 1, 1)

    lax.fori_loop(0, count // 2, two, None)


def spread_blocks(fetch, outs, grid, c2, r2):
    gx, gy = grid
    length = c2 // 2 * r2
    low = iota((length, LANES), 1) < HALF

    def column(i, parity):
        for j in range(gy):
            for start, out in outs:
                a, b = (fetch(n, parity, j, slice(start, start + length)) for n in (i, i + gx // 2))
                parts = jnp.where(low, a, pltpu.roll(b, HALF, 1)), jnp.where(low, pltpu.roll(a, HALF, 1), b)
                for k in range(c2):
                    n = k % (c2 // 2)
                    out[i * c2 + k + 1, j * r2 : (j + 1) * r2, :] = parts[k // (c2 // 2)][n * r2 : (n + 1) * r2]

    repeat(gx // 2, column)


def clear_ends(refs, counts):
    for ref, count in zip(refs, counts):
        zero = jnp.zeros(ref.shape[1:], F32)
        ref[0] = zero
        ref[count + 1] = zero


def pass_kernel(blocks, _, out):
    out[...] = blocks[...]


def first_cycle_kernel(counts, bases, grid, c2, r2, place, mine, theirs, out, table, *scratch):
    s, e, t, pad = scratch[0:3], list(scratch[3:6]), scratch[6], scratch[7]
    gx, gy = grid
    rows = gy * r2
    own = c2 // 2 * r2
    clear_ends(s[:1], counts)
    odd = place[0] == 1

    def fetch(i, _, j, at):
        here = i * gy + j
        rows = []
        for n in range(at.start // 8, at.stop // 8):
            a, b = mine[here, n], theirs[here, n]
            rows += [jnp.where(odd, b, a), jnp.where(odd, a, b)]
        return jnp.concatenate(rows, axis=0)

    spread_blocks(fetch, ((0, s[0]), (own + 2 * r2, t)), grid, c2, r2)
    face_y = e[0]
    low = iota((2 * c2, LANES), 1) < HALF

    def edges(i, parity):
        for j in range(gy):
            a, b = (fetch(n, parity, j, slice(own, own + 2 * r2)) for n in (i, i + gx // 2))
            x_faces = jnp.where(low, a, pltpu.roll(b, HALF, 1))
            y_faces = jnp.where(low, pltpu.roll(a, HALF, 1), b)
            here = slice(j * r2, (j + 1) * r2)
            s[0][i * c2, here, :] = s[0][i * c2, here, :] + x_faces[:r2]
            s[0][(i + 1) * c2 + 1, here, :] = s[0][(i + 1) * c2 + 1, here, :] + x_faces[r2:]
            for k in range(c2):
                at = i * c2 + k + 1
                if j > 0:
                    face_y[at, j * r2 - 1 : j * r2, :] = y_faces[k : k + 1]
                if j < gy - 1:
                    face_y[at, (j + 1) * r2 : (j + 1) * r2 + 1, :] = y_faces[c2 + k : c2 + k + 1]

    repeat(gx // 2, edges)
    first, last = s[0][0], s[0][counts[0] + 1]
    low = iota(first.shape, 1) < HALF
    s[0][counts[0]] = s[0][counts[0]] + jnp.where(low, pltpu.roll(first, HALF, 1), 0.0)
    s[0][1] = s[0][1] + jnp.where(low, 0.0, pltpu.roll(last, HALF, 1))

    def join(at, step):
        now = pl.ds(at + 1, step)
        row = iota((rows, LANES), 0)
        edge = ((row % r2 == 0) & (row > 0)) | ((row % r2 == r2 - 1) & (row < rows - 1))
        s[0][now] = s[0][now] + jnp.where(edge[None], face_y[now], 0.0)

    each(counts[0], join)
    mats = (t, s[1], s[2])
    for level, (count, base) in enumerate(zip(counts, bases)):
        if level:

            def coarsen(at, step):
                whole = (iota((rows, LANES), 0) % 2**level == 0) & (iota((rows, LANES), 1) % 2**level == 0)
                mean = 0.125 * fold(mats[level - 1][pl.ds(at + 1, step)], 2 ** (level - 1))
                mats[level][pl.ds(at // 2 + 1, step // 2)] = jnp.where(whole[None], mean, 0.0)

            each(counts[level - 1], coarsen)
        seal(mats[level], count)
        fill_table(mats[level], table, level, count, base)
    cycle(s, e, t, table, counts, bases, place, out, c2, r2, pad)


def shifted(a):
    zero = jnp.zeros_like(a[:1])
    return jnp.concatenate([zero, a[:-1]], axis=0), jnp.concatenate([a[1:], zero], axis=0)


def apply_off(e, fx, fy, fz):
    before, ahead = shifted(e)
    out = fx[:-1] * before + fx[1:] * ahead
    out = out + fy * lower(e, 1) + upper(fy * e, 1)
    return out + fz * lower(e, 2) + upper(fz * e, 2)


def raise_window(window_ref, flat, out):
    planes, rows, _ = window_ref.shape
    values = select(window_ref[...].reshape(planes * rows, LANES), spread_matrix(LANES))
    flat[pl.ds(0, planes * rows, 2)] = values
    flat[pl.ds(1, planes * rows, 2)] = values
    v = flat[...].reshape(planes, 1, 2 * rows, LANES)
    out[...] = jnp.broadcast_to(v, (planes, 2, 2 * rows, LANES)).reshape(2 * planes, 2 * rows, LANES)


def level1_kernel(
    offset, place, long1, outer, inner, window1, payload, state,
    src, mat, flat, prolonged, fx, fy, fz, diag, inv, err, c, wide, narrow, sheet, semaphore,
):
    low_x = place[0] == 1
    total, length, depth = src.shape
    count, rows = total - 8, length - 8
    both = (inner, outer)
    zero = jnp.zeros((length, depth), F32)
    src[0] = zero
    src[total - 1] = zero
    for flag, base, side in ((low_x, 4, -1), (jnp.logical_not(low_x), count + 3, 1)):
        unpack(both, flag, mat, base, side, 4, unpack(both, flag, src, base, side, 3, offset))
    for n, ref in enumerate((src, mat)):
        ref[pl.ds(4, count)] = long1[n]
    raise_window(window1, flat, prolonged)
    row, lane = iota((length, depth), 0), iota((length, depth), 1)
    ends = as_float(lane == 0) + as_float(lane == depth - 1)
    def chunks(margin):
        first, last = margin, total - margin
        return [(at, min(LEVEL1_STEP, last - at)) for at in range(first, last, LEVEL1_STEP)]

    for at, n in chunks(1):
        here = slice(at, at + n)
        a, before, ahead = mat[here], mat[at - 1 : at + n - 1], mat[at + 1 : at + n + 1]
        down, up = lower(a, 1), upper(a, 1)
        f = harmonic(mat[at - 1 : at + n], mat[at : at + n + 1], 0.25)
        w_y = harmonic(a, down, 0.25)
        w_z = jnp.where(lane[None] == 0, 0.0, harmonic(a, lower(a, 2), 0.25))
        outside = ends[None] + as_float(before <= 0.0) + as_float(ahead <= 0.0) + as_float(down <= 0.0) + as_float(up <= 0.0)
        diagonal = f[:-1] + f[1:] + w_y + upper(w_y, 1) + w_z + upper(w_z, 2) + 0.25 * a * outside
        inverse = jnp.where(a > 0.0, invert(jnp.maximum(diagonal, 1e-4)), 0.0)
        fx[at : at + n + 1], fy[here], fz[here], diag[here], inv[here] = f, w_y, w_z, diagonal, inverse
        err[here] = DAMPING * inverse * src[here] + prolonged[here]

    def off(v, at, n):
        here = slice(at, at + n)
        mid, w_y, w_z = v[here], fy[here], fz[here]
        out = fx[here] * v[at - 1 : at + n - 1] + fx[at + 1 : at + n + 1] * v[at + 1 : at + n + 1]
        out = out + w_y * lower(mid, 1) + upper(w_y * mid, 1)
        return here, mid, out + w_z * lower(mid, 2) + upper(w_z * mid, 2)

    for at, n in chunks(2):
        here, mid, more = off(err, at, n)
        c[here] = KEPT * mid + DAMPING * inv[here] * (src[here] + more)
    for at, n in chunks(3):
        here, mid, more = off(c, at, n)
        left = src[here] - diag[here] * mid + more
        src[here] = left
        value = DAMPING * inv[here] * left
        err[here] = value
        state[at - 3 : at + n - 3] = value
    base = count + 2
    state[base : base + count + 1] = fx[4 : count + 5]
    base += count + 1
    for n, ref in enumerate((fy, fz, inv, c, src)):
        state[base + n * count : base + (n + 1) * count] = ref[4 : 4 + count]
    here, _, more = off(err, 4, count)
    t = (KEPT * src[here] + more)[:, 4 : 4 + rows].reshape(count // 2, 2, rows, depth)
    wide[...] = (t[:, 0] + t[:, 1]).reshape(count // 2 * rows, depth)
    half = wide.shape[0] // 2
    publish(wide[:half], wide[half:], narrow, sheet, payload, semaphore)


def last_cycle_kernel(counts, bases, grid, c2, r2, place, blocks, table, state, partial, out, *scratch):
    s, e, t, pad = scratch[0:3], list(scratch[3:6]), scratch[6], scratch[7]
    view, flat, prolonged, tall, coarse, result, departures = scratch[8:15]
    spread_blocks(lambda i, _, j, at: blocks[grid[0] * grid[1] - 1 - i * grid[1] - j, at], ((0, s[0]),), grid, c2, r2)
    cycle(s, e, t, table, counts, bases, place, view, c2, r2, pad)
    raise_window(view, flat, prolonged)
    count, rows, depth = partial.shape
    c1, r1 = count // 2, rows // 2
    v = prolonged[3 : c1 + 5] + state[: c1 + 2]
    here = v[1:-1]
    base = 2 * c1 + 3
    w_x = state[c1 + 2 : base]
    w_y, w_z, inverse, before, left = (state[base + n * c1 : base + (n + 1) * c1] for n in range(5))
    off = w_x[:-1] * v[:-2] + w_x[1:] * v[2:]
    off = off + w_y * lower(here, 1) + upper(w_y * here, 1) + w_z * lower(here, 2) + upper(w_z * here, 2)
    total = before + KEPT * here + DAMPING * inverse * (left + off)
    coarse[...] = total[:, 4 : 4 + r1].reshape(c1 * r1, LANES)
    values = select(coarse[...], spread_matrix(depth))
    for piece in range(depth // LANES):
        z = slice(piece * LANES, (piece + 1) * LANES)
        tall[piece, pl.ds(0, c1 * r1, 2)] = values[:, z]
        tall[piece, pl.ds(1, c1 * r1, 2)] = values[:, z]
    leaving = []
    for k in range(c1):
        for piece in range(depth // LANES):
            z = slice(piece * LANES, (piece + 1) * LANES)
            more = tall[piece, k * rows : (k + 1) * rows]
            result[2 * k, :, z] = partial[2 * k, :, z] + more
            result[2 * k + 1, :, z] = partial[2 * k + 1, :, z] + more
        if k % 2 == 1:
            planes = pl.ds(2 * k - 2, 4)
            leaving.append(pltpu.make_async_copy(result.at[planes], out.at[planes], departures.at[k // 2]))
            leaving[-1].start()
    for copy in leaving:
        copy.wait()


def size_of(shape):
    lead = math.prod(shape[:-2])
    return 4 * lead * (-(-shape[-2] // 8) * 8) * (-(-shape[-1] // LANES) * LANES)


def call(kernel, name, inputs, outputs, scratch=(), apart=(), cost=None):
    streamed = 0

    def held(n, x):
        nonlocal streamed
        if n in apart:
            return pltpu.with_memory_space_constraint(x, pltpu.HBM)
        if x.ndim == 1:
            return x
        if size_of(x.shape) <= HELD:
            return pltpu.with_memory_space_constraint(x, pltpu.VMEM)
        streamed += size_of(x.shape)
        return x

    def result(shape):
        nonlocal streamed
        if isinstance(shape, jax.ShapeDtypeStruct):
            streamed += size_of(shape.shape)
            return shape
        if far(shape):
            return pltpu.HBM(shape[1], F32)
        if size_of(shape) <= HELD:
            return pltpu.VMEM(shape, F32)
        streamed += size_of(shape)
        return jax.ShapeDtypeStruct(shape, F32)

    def far(x):
        return isinstance(x, tuple) and x[0] == "far"

    def space(n, x):
        return pltpu.HBM if n in apart else pltpu.SMEM if x.ndim == 1 else pltpu.VMEM

    specs = [pl.BlockSpec(memory_space=space(n, x)) for n, x in enumerate(inputs)]
    inputs = [held(n, x) for n, x in enumerate(inputs)]
    results = [result(shape) for shape in outputs]
    need = streamed + sum(size_of(x.shape) for x in scratch if len(getattr(x, "shape", ())) > 1) + 3 * MIB
    return pl.pallas_call(
        kernel,
        out_shape=results,
        in_specs=specs,
        out_specs=[pl.BlockSpec(memory_space=pltpu.HBM if far(x) else pltpu.VMEM) for x in outputs],
        scratch_shapes=list(scratch),
        compiler_params=pltpu.CompilerParams(vmem_limit_bytes=max(need, 8 * MIB)),
        name=name,
        cost_estimate=None if cost is None else pl.CostEstimate(flops=cost, bytes_accessed=0, transcendentals=0),
    )(*inputs)


def swaps(count):
    inner = [(i, i + 1) for i in range(0, count - 1, 2)]
    outer = [(i, i + 1) for i in range(1, count - 1, 2)]
    return [pairs + [(b, a) for a, b in pairs] for pairs in (inner, outer)]


def local(right_side, potential, phase, permeability):
    gx, gy = lax.axis_size("gx"), lax.axis_size("gy")
    devices = gx * gy
    here_x, here_y = lax.axis_index("gx"), lax.axis_index("gy")
    place = jnp.stack([here_x % 2, here_y % 2, here_x, here_y]).astype(jnp.int32)
    count, rows, depth = right_side.shape
    c1, r1, d1 = count // 2, rows // 2, depth // 2
    c2, r2 = c1 // 2, r1 // 2
    pieces = depth // LANES
    swap_x, swap_y = swaps(gx), swaps(gy)
    VM = lambda *shape: pltpu.VMEM(shape, F32)

    brick = (count, rows, depth)
    face = (3, rows, depth)
    DMA = pltpu.SemaphoreType.DMA
    sheet = (devices, c2 // 2 * r2, LANES)
    sheet2 = (gx // 2, 2, gy, (c2 * r2 + 2 * r2) // 8, 4, LANES)
    material, potential_here, source_here, inner, outer, even, odd = call(
        faces_kernel, "faces", (place, permeability, potential, phase, right_side),
        (brick, brick, brick, face, face, (3, count, depth), (3, count, depth)),
        (pltpu.VMEM(brick, jnp.int32), pltpu.SMEM(permeability.shape, F32), pltpu.SemaphoreType.DMA((4,))),
        apart=(1, 2, 3, 4),
    )
    even = lax.ppermute(even, "gy", swap_y[0])
    odd = lax.ppermute(odd, "gy", swap_y[1])
    outer = lax.ppermute(outer, "gx", swap_x[1])
    inner = lax.ppermute(inner, "gx", swap_x[0])

    strip = (count * pieces + c1, 8, LANES)
    total = 2 * c1 * rows + 4 * rows
    residual, coarse, even, odd = call(
        residual_kernel, "residual", (place, source_here, potential_here, material, outer, even, odd, inner),
        (brick, (total // 2, LANES), strip, strip),
        (
            VM(total, depth), VM(total, LANES), VM(4, count, 8, depth), VM(count + 2, rows, depth), VM(count + 2, rows, depth),
        ),
    )
    even = lax.ppermute(even, "gy", swap_y[0])
    odd = lax.ppermute(odd, "gy", swap_y[1])
    small = c2 * r1 + 2 * r1
    (payload,) = call(
        functools.partial(payload_kernel, c1, r1), "payload", (coarse,), (("far", sheet2),),
        (VM(2, small, d1), VM(small, LANES), VM(*sheet2), DMA),
    )
    blocks = lax.all_to_all(payload.reshape(devices, *sheet2[3:]), ("gx", "gy"), 0, 0)
    strip = (strip_length(rows, depth) + strip_length(r1, d1), 8, LANES)
    long_shape = (2, count, rows + 8, depth)
    inner, outer, long, long1 = call(
        strips_kernel, "strips", (place, residual, material, coarse, even, odd),
        (strip, strip, long_shape, (2, c1, r1 + 8, d1)), cost=10**11,
    )
    outer = lax.ppermute(outer, "gx", swap_x[1])
    inner = lax.ppermute(inner, "gx", swap_x[0])

    others = lax.ppermute(blocks, "gx", swap_x[0])
    counts = tuple(gx * c2 // 2 // k for k in (1, 2, 4))
    bases = (0, counts[0] + 1, counts[0] + counts[1] + 2)
    work = cycle_shapes(counts, gy * r2, c2)
    view = (c2 + 4, r2 + 4, LANES)
    window1, table = call(
        functools.partial(first_cycle_kernel, counts, bases, (gx, gy), c2, r2), "cycle1", (place, blocks, others),
        (view, (4, sum(counts) + 3, gy * r2, LANES)), work,
    )
    frame = (c1 + 8, r1 + 8, d1)
    flat = VM((c2 + 4) * (r2 + 4) * 2, LANES)
    state = (7 * c1 + 3, r1 + 8, d1)
    tall = VM(c1 + 9, r1 + 8, d1)
    payload, held = call(
        functools.partial(level1_kernel, strip_length(rows, depth)), "level1", (place, long1, outer, inner, window1), (("far", sheet), state),
        (
            VM(*frame), VM(*frame), flat, VM(*frame), tall, VM(*frame), VM(*frame), VM(*frame), VM(*frame), VM(*frame),
            VM(*frame), VM(c1 // 2 * r1, d1), VM(c1 // 4 * r1, LANES), VM(*sheet), DMA,
        ),
    )
    blocks = lax.all_to_all(payload, ("gx", "gy"), 0, 0, axis_index_groups=[list(range(devices))[::-1]])
    wide = (count + 8, rows + 8, depth)
    (partial,) = call(
        functools.partial(smooth_kernel, (gx, gy)), "smooth", (place, potential, long, outer, inner), (brick,),
        (
            VM(*wide), VM(*wide), VM(2, *wide), VM(*wide), VM(count + 9, rows + 8, depth), VM(*wide), VM(*wide), VM(*wide),
            VM(*brick), pltpu.SemaphoreType.DMA((1,)),
        ),
        apart=(1,),
    )
    (out,) = call(
        functools.partial(last_cycle_kernel, counts, bases, (gx, gy), c2, r2), "cycle2",
        (place, blocks, table, held, partial), (("far", brick),),
        (
            *work, VM(*view), flat, VM(*frame), VM(pieces, c1 * rows, LANES), VM(c1 * r1, LANES), VM(*brick),
            pltpu.SemaphoreType.DMA((c1 // 2,)),
        ),
    )
    return out


def solution(mesh):
    placed = (P("gx", "gy", None), P("gx", "gy", None), P("gx", "gy", None), P())
    return jax.shard_map(local, mesh=mesh, in_specs=placed, out_specs=P("gx", "gy", None), check_vma=False)
```
